32 devices in a mesh: groups: 2 (over y), ka: 16 (over z, x, core).
Axes of the slice: x: 2, y: 2, z: 4, core: 2. Of those that a mesh axis runs over, the one named last changes fastest.
Arguments:
- coeffs: bfloat16 [64, 32, 32, 1024], P(('groups', 'ka')), parts along dimension 0, may hold values from -6 to 6
- g_cond: bfloat16 [64, 2, 32, 32], P(('groups', 'ka')), parts along dimension 0, may hold values from -1 to 1
- g_val: bfloat16 [64, 2, 32, 32], P(('groups', 'ka')), parts along dimension 0, may hold values from -1 to 1
- k_plus_q: int32 [64], P(('groups', 'ka')), parts along dimension 0, may hold values from 0 to 31, as said below
- band_first: int32 [4, 2], P('groups'), parts along dimension 0, may hold values from 0 to 15
Outputs:
- coupling: float32 [2048, 2, 1024], P(('groups', 'ka')), parts along dimension 0
The draws below stay inside these ranges and needn't reach their ends.
There are 2 independent parts, one for each index of `groups`. The reference program is written for one: setup_inputs(seed, part) draws one part's arguments, and reference() takes and returns one part's arrays. A program takes and returns all parts, laid end to end along the dimension named above; each array names one. Nothing has to cross between parts.
Inputs may be any that keep to these rules, and one draw needn't show every extreme that they name: Taking the k-points in aligned blocks of 2, k_plus_q[k] lies in the block of k or in the following block, the last block being followed by the first.
All inputs are finite; a program needn't handle non-finite values.
Results may differ from the reference program's by a relative error of at most 0.0029.
Values may be sent and summed in bfloat16 or wider, within the bound.
No kernel may reach another device: no remote copies, remote signals or barrier semaphores. Data moves between devices by JAX's collectives and lax.ppermute only.
A program may use at most 64 MiB of HBM per device.

```python
import math
import jax
import jax.numpy as jnp
from jax import lax

NC = 32
NV = 32
NX = 1024
MODES = 2
K_DEV = 2
NK = 32


def draw_k_plus_q(key, part):
    key = jax.random.fold_in(key, 7)
    offsets = jax.random.randint(key, (NK,), 0, 2 * K_DEV)
    points = jnp.arange(NK, dtype=jnp.int32)
    offsets = offsets.at[NK - 2 * K_DEV].set(2 * K_DEV - 1)
    offsets = offsets.at[NK - K_DEV].set(K_DEV)
    starts = points - points % K_DEV
    return ((starts + offsets) % NK).astype(jnp.int32)


def set_ends(entries, key, smallest, top_value):
    place = [jax.random.randint(jax.random.fold_in(key, axis), (), 0, length) for axis, length in enumerate(entries.shape)]
    main_axis = entries.shape.index(max(entries.shape))
    next_to = place[:main_axis] + [(place[main_axis] + 1) % entries.shape[main_axis]] + place[main_axis + 1:]
    return entries.at[tuple(place)].set(smallest).at[tuple(next_to)].set(top_value)


def strengthened(entries, key, source, target, shards_of, factor):
    owner, partner = [(jnp.arange(entries.shape[position]) // (entries.shape[position] // shards_of)).reshape([-1 if axis == position else 1 for axis in range(entries.ndim)]) for position in (source, target)]
    chosen = jax.random.permutation(key, shards_of)[partner]
    strong = (owner == chosen) | (owner == (partner + shards_of // 2) % shards_of)
    return jnp.where(strong, factor * entries, entries)


def levels(key, shape, pieces, low, top_value):
    loudness = 1.0
    for position, blocks in pieces:
        steps = jax.random.uniform(jax.random.fold_in(jax.random.fold_in(key, 6), position), (blocks,), jnp.float32, low / len(pieces), top_value / len(pieces))
        loudness = loudness * jnp.repeat(jnp.exp(steps), shape[position] // blocks).reshape((-1,) + (1,) * (len(shape) - 1 - position))
    return loudness


def bell_draw(rng, shape, width, reach, shards=(), held_as=jnp.bfloat16):
    array = width * jax.random.normal(rng, shape, jnp.float32)
    if shards:
        array = array * levels(rng, shape, shards, -0.22, 0.18)
    return jnp.clip(array, -reach, reach).astype(held_as)


def noise_with(rng, dims, scale, limit, cuts, heavy, held_as=jnp.bfloat16):
    entries = scale * jax.random.normal(rng, dims, jnp.float32)
    if cuts:
        entries = entries * levels(rng, dims, cuts, -0.22, 0.18)
    return jnp.clip(strengthened(entries, jax.random.fold_in(rng, 3), *heavy), -limit, limit).astype(held_as)


def setup_inputs(seed: int = 0, part: int = 0) -> dict:
    streams_of = jax.random.split(jax.random.key(seed), 6)
    part_splits = jax.random.split(jax.random.fold_in(streams_of[5], part), 6)
    return {
        "coeffs": noise_with(part_splits[0], (NK, NC, NV, NX), 1.0, 6.0, ((0, 16),), (0, 3, 16, 2.0)),
        "g_cond": bell_draw(part_splits[1], (NK, MODES, NC, NC), NC ** -0.5, 1.0, ((0, 16),)),
        "g_val": bell_draw(part_splits[2], (NK, MODES, NV, NV), NV ** -0.5, 1.0, ((0, 16),)),
        "k_plus_q": draw_k_plus_q(jax.random.fold_in(jax.random.fold_in(streams_of[5], part), 71), part),
        "band_first": set_ends(jax.random.randint(part_splits[4], (MODES, 2), 0, min(NC, NV) // 2), jax.random.fold_in(part_splits[4], 1), 0, (min(NC, NV) // 2) - 1).astype(jnp.int32),
    }


def reference(coeffs, g_cond, g_val, k_plus_q, band_first):
    bands_c = jnp.arange(NC, dtype=jnp.int32)
    bands_v = jnp.arange(NV, dtype=jnp.int32)
    mask_cond = (bands_c[None, :] >= band_first[:, 0:1]).astype(g_cond.dtype)
    mask_val = (bands_v[None, :] >= band_first[:, 1:2]).astype(g_val.dtype)
    cond_masked = g_cond * mask_cond[None, :, :, None]
    val_masked = g_val * mask_val[None, :, None, :]
    norm_factor = 1.0 / math.sqrt(NC * NV * NK)

    def advance(running, inputs):
        block, cond_block, val_block, target = inputs
        wide = block.astype(jnp.float32)
        electron = jnp.einsum('mxc,cvs->xvms', cond_block.astype(jnp.float32), wide)
        hole_term = jnp.einsum('mvw,cvs->cwms', val_block.astype(jnp.float32), wide)
        products = (electron - hole_term).astype(jnp.bfloat16).reshape(NC * NV, MODES * NX)
        partner = lax.dynamic_index_in_dim(coeffs, target.astype(jnp.int32), 0, keepdims=False)
        partner = partner.reshape(NC * NV, NX)
        term = jnp.dot(partner.T.astype(jnp.float32), products.astype(jnp.float32), preferred_element_type=jnp.float32)
        return (running + term, None)
    start = jnp.zeros((NX, MODES * NX), jnp.float32)
    running, unused = lax.scan(advance, start, (coeffs, cond_masked, val_masked, k_plus_q))
    return (running * norm_factor).reshape(NX, MODES, NX)
```

```python
import functools
import math

import jax
import jax.numpy as jnp
from jax import lax
from jax.experimental import pallas as pl
from jax.experimental.pallas import tpu as pltpu
from jax.sharding import PartitionSpec as P

MIB = 1024 * 1024


def permute(x, target):
    size = lax.axis_size("ka")
    pairs = [(i, target(i)) for i in range(size)]
    return lax.ppermute(x, "ka", [(i, j % size) for i, j in pairs if j is not None])


def nt_dot(a, b):
    return lax.dot_general(a, b, (((1,), (1,)), ((), ())), preferred_element_type=jnp.float32)


def spread(rows, count, group, by_rest):
    row = lax.broadcasted_iota(jnp.int32, (rows, count), 0)
    col = lax.broadcasted_iota(jnp.int32, (rows, count), 1)
    return jnp.where((row % count if by_rest else row // group) == col, 1.0, 0.0).astype(jnp.bfloat16)


def products_kernel(first_ref, coeffs_ref, cond_ref, val_ref, out_ref, we_ref, wh_ref):
    _, bands_c, bands_v, tile = coeffs_ref.shape
    modes = cond_ref.shape[1]
    part_v, part_c = bands_v // 2, 8
    rows_e, rows_h = bands_c * part_v, part_c * bands_v

    @pl.when(pl.program_id(1) == 0)
    def _():
        take = spread(rows_e, bands_c, part_v, False)
        row = lax.broadcasted_iota(jnp.int32, (rows_e, rows_e), 0)
        col = lax.broadcasted_iota(jnp.int32, (rows_e, rows_e), 1)
        for m in range(modes):
            part = jnp.dot(take, cond_ref[0, m], preferred_element_type=jnp.float32)
            full = nt_dot(part.astype(jnp.bfloat16), take)
            keep = (row % part_v == col % part_v) & (row // part_v >= first_ref[m, 0])
            we_ref[m * rows_e:(m + 1) * rows_e, :] = jnp.where(keep, full, 0.0).astype(jnp.bfloat16)
        take = spread(rows_h, bands_v, 0, True)
        row = lax.broadcasted_iota(jnp.int32, (rows_h, rows_h), 0)
        col = lax.broadcasted_iota(jnp.int32, (rows_h, rows_h), 1)
        for m in range(modes):
            part = nt_dot(take, val_ref[0, m])
            full = nt_dot(part.astype(jnp.bfloat16), take)
            keep = (row // bands_v == col // bands_v) & (row % bands_v >= first_ref[m, 1])
            wh_ref[m * rows_h:(m + 1) * rows_h, :] = jnp.where(keep, full, 0.0).astype(jnp.bfloat16)

    electron = []
    for h in range(2):
        x = coeffs_ref[0, :, h * part_v:(h + 1) * part_v, :].reshape(rows_e, tile)
        e = jnp.dot(we_ref[...], x, preferred_element_type=jnp.float32)
        electron.append(e.reshape(modes, bands_c, part_v, tile))
    for q in range(bands_c // part_c):
        own = slice(q * part_c, (q + 1) * part_c)
        y = coeffs_ref[0, own].reshape(rows_h, tile)
        hole = jnp.dot(wh_ref[...], y, preferred_element_type=jnp.float32)
        hole = hole.reshape(modes, part_c, bands_v, tile)
        for m in range(modes):
            for h in range(2):
                cols = slice(h * part_v, (h + 1) * part_v)
                value = electron[h][m, own] - hole[m, :, cols]
                out_ref[0, m, own, cols, :] = value.astype(jnp.bfloat16)


def products_of(coeffs, g_cond, g_val, band_first):
    k_local, bands_c, bands_v, excitons = coeffs.shape
    modes = g_cond.shape[1]
    tile = 256
    rows_e, rows_h = bands_c * bands_v // 2, 8 * bands_v
    flops = 2 * k_local * modes * excitons * bands_c * bands_v * (rows_e + rows_h)
    out = pl.pallas_call(
        products_kernel,
        out_shape=jax.ShapeDtypeStruct((k_local, modes, bands_c, bands_v, excitons), jnp.bfloat16),
        grid=(k_local, excitons // tile),
        in_specs=[
            pl.BlockSpec(memory_space=pltpu.SMEM),
            pl.BlockSpec((1, bands_c, bands_v, tile), lambda k, s: (k, 0, 0, s)),
            pl.BlockSpec((1, modes, bands_c, bands_c), lambda k, s: (k, 0, 0, 0)),
            pl.BlockSpec((1, modes, bands_v, bands_v), lambda k, s: (k, 0, 0, 0)),
        ],
        out_specs=pl.BlockSpec((1, modes, bands_c, bands_v, tile), lambda k, s: (k, 0, 0, 0, s)),
        scratch_shapes=[
            pltpu.VMEM((modes * rows_e, rows_e), jnp.bfloat16),
            pltpu.VMEM((modes * rows_h, rows_h), jnp.bfloat16),
        ],
        compiler_params=pltpu.CompilerParams(vmem_limit_bytes=32 * MIB),
        cost_estimate=pl.CostEstimate(
            flops=flops, bytes_accessed=2 * coeffs.size * (1 + modes), transcendentals=0
        ),
    )(band_first, coeffs, g_cond, g_val)
    return out.reshape(k_local, modes, bands_c * bands_v, excitons)


def rows_kernel(adds, last, *refs):
    pick_ref, own_ref, sib_ref, next_ref, p_own_ref, p_sib_ref = refs[:6]
    arrived = refs[6:6 + adds]
    outs, left = refs[6 + adds:-1], refs[-1]
    k_local = own_ref.shape[0]

    @pl.when(pl.program_id(0) == 0)
    def _():
        for k in range(2 * k_local):
            which, place = pick_ref[2 * k], pick_ref[2 * k + 1]
            for source, ref in enumerate((own_ref, sib_ref, next_ref)):
                @pl.when(which == source)
                def _():
                    left[k] = ref[place].T

    total = None
    for k in range(2 * k_local):
        right = p_own_ref if k < k_local else p_sib_ref
        term = jnp.dot(left[k], right[k % k_local, 0], preferred_element_type=jnp.float32)
        total = term if total is None else total + term
    for ref in arrived:
        total = total + ref[...].astype(jnp.float32)
    if not last:
        outs[0][...] = total.astype(jnp.bfloat16)
        return
    half = total.shape[0] // 2
    low, high = total[:half], total[half:]
    core, first = pick_ref[4 * k_local + 1], pick_ref[4 * k_local + 2]
    outs[0][...] = jnp.where(core == 0, low, high)
    outs[1][...] = jnp.where(first == 0, low, high).astype(jnp.bfloat16)
    outs[2][...] = jnp.where(first == 0, high, low).astype(jnp.bfloat16)


def rows_of(pick, own, sib, following, p_own, p_sib, arrived, last, width):
    k_local, depth, excitons = own.shape
    modes = p_own.shape[1]
    tile = 512
    per_mode = excitons // tile
    columns = modes * excitons
    if last:
        half = width // 2
        outs = [((half, columns), jnp.float32)] + 2 * [((half, columns), jnp.bfloat16)]
    else:
        outs = [((width, columns), jnp.bfloat16)]
    block = lambda j, pick: (0, 0, pick[4 * k_local])
    right = pl.BlockSpec((k_local, 1, depth, tile), lambda j, pick: (0, j // per_mode, 0, j % per_mode))
    return pl.pallas_call(
        functools.partial(rows_kernel, len(arrived), last),
        out_shape=[jax.ShapeDtypeStruct(*o) for o in outs],
        grid_spec=pltpu.PrefetchScalarGridSpec(
            num_scalar_prefetch=1,
            grid=(modes * per_mode,),
            in_specs=[
                pl.BlockSpec((k_local, depth, width), block),
                pl.BlockSpec((k_local, depth, width), block),
                pl.BlockSpec((k_local, depth, width), lambda j, pick: (0, 0, 0)),
                right,
                right,
            ] + [pl.BlockSpec((width, tile), lambda j, pick: (0, j)) for _ in arrived],
            out_specs=[pl.BlockSpec((o[0][0], tile), lambda j, pick: (0, j)) for o in outs],
            scratch_shapes=[pltpu.VMEM((2 * k_local, width, depth), jnp.bfloat16)],
        ),
        compiler_params=pltpu.CompilerParams(vmem_limit_bytes=32 * MIB),
        cost_estimate=pl.CostEstimate(
            flops=4 * k_local * depth * width * columns,
            bytes_accessed=4 * k_local * depth * columns,
            transcendentals=0,
        ),
    )(pick, own, sib, following, p_own, p_sib, *arrived)


def on_two_by_four(coeffs, g_cond, g_val, k_plus_q, band_first, norm_factor):
    k_local, bands_c, bands_v, excitons = coeffs.shape
    modes = g_cond.shape[1]
    size = lax.axis_size("ka")
    chips = size // 2
    width = excitons // chips
    me = lax.axis_index("ka")
    core, x, z = me % 2, me // 2 % 2, me // 4
    flat = coeffs.reshape(k_local, bands_c * bands_v, excitons)

    offsets = jnp.mod(k_plus_q - me * k_local, k_local * size)
    small = jnp.concatenate(
        (g_cond.reshape(-1), g_val.reshape(-1), offsets.astype(jnp.bfloat16))
    )
    sib_small = permute(small, lambda i: i ^ 1)
    sib = permute(flat, lambda i: i ^ 1)

    def cut(array, block):
        return lax.dynamic_slice_in_dim(array, block * width, width, 2)

    behind_z = jnp.mod(me // 2 - 1, chips) // 2
    following = []
    for step in range(4):
        block = 2 * (behind_z ^ (3 - step))
        if step == 0:
            to_first = permute(cut(flat, block), lambda i: i - 2 if i % 2 == 0 else i)
            to_second = permute(cut(flat, block + 1), lambda i: i - 1 if i % 2 == 0 else i - 1)
            following.append(jnp.where(core == 0, to_first, to_second))
        else:
            sent = jnp.where(core == 0, cut(flat, block), cut(sib, block + 1))
            following.append(permute(sent, lambda i: i - 2))

    sib_cond = sib_small[:g_cond.size].reshape(g_cond.shape)
    sib_val = sib_small[g_cond.size:g_cond.size + g_val.size].reshape(g_val.shape)
    sib_offsets = sib_small[g_cond.size + g_val.size:].astype(jnp.int32)
    p_own = products_of(coeffs, g_cond, g_val, band_first)
    p_sib = products_of(sib.reshape(coeffs.shape), sib_cond, sib_val, band_first)

    places = jnp.concatenate((offsets + core * k_local, sib_offsets + (1 - core) * k_local))
    of_block = places // k_local
    which = jnp.where(of_block == 2, 2, of_block ^ core)
    picks = jnp.stack((which, places % k_local), 1).reshape(-1).astype(jnp.int32)
    keeper = core == x
    first = jnp.where(keeper, 1 - core, core)

    def rows(step, arrived, last=False):
        block = 2 * (z ^ (3 - step)) + core
        pick = jnp.concatenate((picks, jnp.stack((block, core, first)).astype(jnp.int32)))
        return rows_of(pick, flat, sib, following[step], p_own, p_sib, arrived, last, width)

    far = permute(rows(0, [])[0], lambda i: i ^ 4)
    pair = permute(rows(1, [far])[0], lambda i: i ^ 8)
    near = permute(rows(2, [])[0], lambda i: i ^ 4)
    mine, sent_a, sent_b = rows(3, [pair, near], True)
    is_keeper = lambda i: i % 2 == i // 2 % 2
    got_a = permute(sent_a, lambda i: i ^ 1 if is_keeper(i) else i ^ 2)
    got_b = permute(sent_b, lambda i: i if is_keeper(i) else i ^ 3)
    total = got_a.astype(jnp.float32) + jnp.where(keeper, mine, got_b.astype(jnp.float32))
    return (total * norm_factor).reshape(width // 2, modes, excitons)


def on_any(coeffs, g_cond, g_val, k_plus_q, band_first, norm_factor):
    k_local, bands_c, bands_v, excitons = coeffs.shape
    modes = g_cond.shape[1]
    size = lax.axis_size("ka")
    depth = bands_c * bands_v
    flat = coeffs.reshape(k_local, depth, excitons)
    blocks = jnp.concatenate((flat, permute(flat, lambda i: i - 1)), 0)
    offsets = jnp.mod(k_plus_q - lax.axis_index("ka") * k_local, k_local * size)
    products = products_of(coeffs, g_cond, g_val, band_first)
    partners = [
        lax.dynamic_index_in_dim(blocks, offsets[k], 0, keepdims=False) for k in range(k_local)
    ]
    running = jnp.einsum(
        "kds,kmdt->smt", jnp.stack(partners), products, preferred_element_type=jnp.float32
    )
    return lax.psum_scatter(running * norm_factor, "ka", scatter_dimension=0, tiled=True)


def shards(coeffs, g_cond, g_val, k_plus_q, band_first):
    k_local, bands_c, bands_v, excitons = coeffs.shape
    size = lax.axis_size("ka")
    norm_factor = 1.0 / math.sqrt(bands_c * bands_v * k_local * size)
    whole_tiles = excitons % (size // 2 * 128) == 0
    plan = on_two_by_four if size == 16 and whole_tiles else on_any
    return plan(coeffs, g_cond, g_val, k_plus_q, band_first, norm_factor)


def solution(mesh):
    in_specs = (
        P(("groups", "ka"), None, None, None),
        P(("groups", "ka"), None, None, None),
        P(("groups", "ka"), None, None, None),
        P(("groups", "ka")),
        P("groups", None),
    )
    out_specs = P(("groups", "ka"), None, None)
    return jax.shard_map(shards, mesh=mesh, in_specs=in_specs, out_specs=out_specs, check_vma=False)
```

```python
import functools
import math

import jax
import jax.numpy as jnp
from jax import lax
from jax.experimental import pallas as pl
from jax.experimental.pallas import tpu as pltpu
from jax.sharding import PartitionSpec as P

MIB = 1024 * 1024


def permute(x, target):
    size = lax.axis_size("ka")
    pairs = [(i, target(i)) for i in range(size)]
    return lax.ppermute(x, "ka", [(i, j % size) for i, j in pairs if j is not None])


def nt_dot(a, b):
    return lax.dot_general(a, b, (((1,), (1,)), ((), ())), preferred_element_type=jnp.float32)


def spread(rows, count, group, by_rest):
    row = lax.broadcasted_iota(jnp.int32, (rows, count), 0)
    col = lax.broadcasted_iota(jnp.int32, (rows, count), 1)
    return jnp.where((row % count if by_rest else row // group) == col, 1.0, 0.0).astype(jnp.bfloat16)


def products_kernel(first_ref, coeffs_ref, cond_ref, val_ref, out_ref, we_ref, wh_ref):
    _, bands_c, bands_v, tile = coeffs_ref.shape
    modes = cond_ref.shape[1]
    part_v, part_c = bands_v // 2, 8
    rows_e, rows_h = bands_c * part_v, part_c * bands_v

    @pl.when(pl.program_id(1) == 0)
    def _():
        take = spread(rows_e, bands_c, part_v, False)
        row = lax.broadcasted_iota(jnp.int32, (rows_e, rows_e), 0)
        col = lax.broadcasted_iota(jnp.int32, (rows_e, rows_e), 1)
        for m in range(modes):
            part = jnp.dot(take, cond_ref[0, m], preferred_element_type=jnp.float32)
            full = nt_dot(part.astype(jnp.bfloat16), take)
            keep = (row % part_v == col % part_v) & (row // part_v >= first_ref[m, 0])
            we_ref[m * rows_e:(m + 1) * rows_e, :] = jnp.where(keep, full, 0.0).astype(jnp.bfloat16)
        take = spread(rows_h, bands_v, 0, True)
        row = lax.broadcasted_iota(jnp.int32, (rows_h, rows_h), 0)
        col = lax.broadcasted_iota(jnp.int32, (rows_h, rows_h), 1)
        for m in range(modes):
            part = nt_dot(take, val_ref[0, m])
            full = nt_dot(part.astype(jnp.bfloat16), take)
            keep = (row // bands_v == col // bands_v) & (row % bands_v >= first_ref[m, 1])
            wh_ref[m * rows_h:(m + 1) * rows_h, :] = jnp.where(keep, full, 0.0).astype(jnp.bfloat16)

    electron = []
    for h in range(2):
        x = coeffs_ref[0, :, h * part_v:(h + 1) * part_v, :].reshape(rows_e, tile)
        e = jnp.dot(we_ref[...], x, preferred_element_type=jnp.float32)
        electron.append(e.reshape(modes, bands_c, part_v, tile))
    for q in range(bands_c // part_c):
        own = slice(q * part_c, (q + 1) * part_c)
        y = coeffs_ref[0, own].reshape(rows_h, tile)
        hole = jnp.dot(wh_ref[...], y, preferred_element_type=jnp.float32)
        hole = hole.reshape(modes, part_c, bands_v, tile)
        for m in range(modes):
            for h in range(2):
                cols = slice(h * part_v, (h + 1) * part_v)
                value = electron[h][m, own] - hole[m, :, cols]
                out_ref[0, m, own, cols, :] = value.astype(jnp.bfloat16)


def products_of(coeffs, g_cond, g_val, band_first):
    k_local, bands_c, bands_v, excitons = coeffs.shape
    modes = g_cond.shape[1]
    tile = 256
    rows_e, rows_h = bands_c * bands_v // 2, 8 * bands_v
    flops = 2 * k_local * modes * excitons * bands_c * bands_v * (rows_e + rows_h)
    out = pl.pallas_call(
        products_kernel,
        out_shape=jax.ShapeDtypeStruct((k_local, modes, bands_c, bands_v, excitons), jnp.bfloat16),
        grid=(k_local, excitons // tile),
        in_specs=[
            pl.BlockSpec(memory_space=pltpu.SMEM),
            pl.BlockSpec((1, bands_c, bands_v, tile), lambda k, s: (k, 0, 0, s)),
            pl.BlockSpec((1, modes, bands_c, bands_c), lambda k, s: (k, 0, 0, 0)),
            pl.BlockSpec((1, modes, bands_v, bands_v), lambda k, s: (k, 0, 0, 0)),
        ],
        out_specs=pl.BlockSpec((1, modes, bands_c, bands_v, tile), lambda k, s: (k, 0, 0, 0, s)),
        scratch_shapes=[
            pltpu.VMEM((modes * rows_e, rows_e), jnp.bfloat16),
            pltpu.VMEM((modes * rows_h, rows_h), jnp.bfloat16),
        ],
        compiler_params=pltpu.CompilerParams(vmem_limit_bytes=32 * MIB),
        cost_estimate=pl.CostEstimate(
            flops=flops, bytes_accessed=2 * coeffs.size * (1 + modes), transcendentals=0
        ),
    )(band_first, coeffs, g_cond, g_val)
    return out.reshape(k_local, modes, bands_c * bands_v, excitons)


def rows_kernel(pick_ref, own_ref, next_ref, right_ref, keep_ref, send_ref, left):
    k_local = own_ref.shape[0]

    @pl.when(pl.program_id(0) == 0)
    def _():
        for k in range(k_local):
            place = pick_ref[k]

            @pl.when(place < k_local)
            def _():
                left[k] = own_ref[place].T

            @pl.when(place >= k_local)
            def _():
                left[k] = next_ref[place - k_local].T

    total = None
    for k in range(k_local):
        term = jnp.dot(left[k], right_ref[k, 0], preferred_element_type=jnp.float32)
        total = term if total is None else total + term
    core = pick_ref[k_local + 1]
    width, tile = total.shape
    parts = total.reshape(2, 2, width // 4, tile)
    low, high = parts[:, 0].reshape(width // 2, tile), parts[:, 1].reshape(width // 2, tile)
    keep_ref[...] = jnp.where(core == 0, low, high)
    send_ref[...] = jnp.where(core == 0, high, low).astype(jnp.bfloat16)


def rows_of(pick, own, following, products, width):
    k_local, depth, excitons = own.shape
    modes = products.shape[1]
    tile = 512
    per_mode = excitons // tile
    columns = modes * excitons
    return pl.pallas_call(
        rows_kernel,
        out_shape=[
            jax.ShapeDtypeStruct((width // 2, columns), jnp.float32),
            jax.ShapeDtypeStruct((width // 2, columns), jnp.bfloat16),
        ],
        grid_spec=pltpu.PrefetchScalarGridSpec(
            num_scalar_prefetch=1,
            grid=(modes * per_mode,),
            in_specs=[
                pl.BlockSpec((k_local, depth, width), lambda j, pick: (0, 0, pick[k_local])),
                pl.BlockSpec((k_local, depth, width), lambda j, pick: (0, 0, 0)),
                pl.BlockSpec(
                    (k_local, 1, depth, tile), lambda j, pick: (0, j // per_mode, 0, j % per_mode)
                ),
            ],
            out_specs=[pl.BlockSpec((width // 2, tile), lambda j, pick: (0, j))] * 2,
            scratch_shapes=[pltpu.VMEM((k_local, width, depth), jnp.bfloat16)],
        ),
        compiler_params=pltpu.CompilerParams(vmem_limit_bytes=32 * MIB),
        cost_estimate=pl.CostEstimate(
            flops=2 * k_local * depth * width * columns,
            bytes_accessed=2 * k_local * depth * columns,
            transcendentals=0,
        ),
    )(pick, own, following, products)


def on_two_by_four(coeffs, g_cond, g_val, k_plus_q, band_first, norm_factor):
    k_local, bands_c, bands_v, excitons = coeffs.shape
    modes = g_cond.shape[1]
    size = lax.axis_size("ka")
    width = excitons // 4
    me = lax.axis_index("ka")
    core, x, z = me & 1, me >> 1 & 1, me >> 2
    flat = coeffs.reshape(k_local, bands_c * bands_v, excitons)

    behind_z = (me + size - 1) % size >> 2
    following, source = [], flat
    for step in range(4):
        piece = lax.dynamic_slice_in_dim(source, (behind_z ^ (3 - step)) * width, width, 2)
        following.append(permute(piece, lambda i: i - 1))
        source, piece = lax.optimization_barrier((source, piece))

    products = products_of(coeffs, g_cond, g_val, band_first)
    places = jnp.mod(k_plus_q - me * k_local, k_local * size)

    def rows(step):
        pick = jnp.concatenate((places, jnp.stack((z ^ (3 - step), core))))
        keep, send = rows_of(pick, flat, following[step], products, width)
        return keep, permute(send, lambda i: i ^ 1).astype(jnp.float32)

    keep, other = rows(0)
    far = permute((keep + other).astype(jnp.bfloat16), lambda i: i ^ 4)
    keep, other = rows(1)
    pair = permute((keep + other + far.astype(jnp.float32)).astype(jnp.bfloat16), lambda i: i ^ 8)
    keep, other = rows(2)
    near = permute((keep + other).astype(jnp.bfloat16), lambda i: i ^ 4)
    keep, other = rows(3)
    total = keep + other + near.astype(jnp.float32) + pair.astype(jnp.float32)
    total = total.reshape(2, width // 4, modes * excitons)
    mine = lax.dynamic_index_in_dim(total, x, 0, keepdims=False)
    sent = lax.dynamic_index_in_dim(total, 1 - x, 0, keepdims=False).astype(jnp.bfloat16)
    total = mine + permute(sent, lambda i: i ^ 2).astype(jnp.float32)
    return (total * norm_factor).reshape(width // 4, modes, excitons)


def on_any(coeffs, g_cond, g_val, k_plus_q, band_first, norm_factor):
    k_local, bands_c, bands_v, excitons = coeffs.shape
    modes = g_cond.shape[1]
    size = lax.axis_size("ka")
    depth = bands_c * bands_v
    flat = coeffs.reshape(k_local, depth, excitons)
    blocks = jnp.concatenate((flat, permute(flat, lambda i: i - 1)), 0)
    offsets = jnp.mod(k_plus_q - lax.axis_index("ka") * k_local, k_local * size)
    products = products_of(coeffs, g_cond, g_val, band_first)
    partners = [
        lax.dynamic_index_in_dim(blocks, offsets[k], 0, keepdims=False) for k in range(k_local)
    ]
    running = jnp.einsum(
        "kds,kmdt->smt", jnp.stack(partners), products, preferred_element_type=jnp.float32
    )
    return lax.psum_scatter(running * norm_factor, "ka", scatter_dimension=0, tiled=True)


def shards(coeffs, g_cond, g_val, k_plus_q, band_first):
    k_local, bands_c, bands_v, excitons = coeffs.shape
    size = lax.axis_size("ka")
    norm_factor = 1.0 / math.sqrt(bands_c * bands_v * k_local * size)
    whole_tiles = excitons % (4 * 128) == 0
    plan = on_two_by_four if size == 16 and whole_tiles else on_any
    return plan(coeffs, g_cond, g_val, k_plus_q, band_first, norm_factor)


def solution(mesh):
    in_specs = (
        P(("groups", "ka"), None, None, None),
        P(("groups", "ka"), None, None, None),
        P(("groups", "ka"), None, None, None),
        P(("groups", "ka")),
        P("groups", None),
    )
    out_specs = P(("groups", "ka"), None, None)
    return jax.shard_map(shards, mesh=mesh, in_specs=in_specs, out_specs=out_specs, check_vma=False)
```

```python
import functools
import math

import jax
import jax.numpy as jnp
from jax import lax
from jax.experimental import pallas as pl
from jax.experimental.pallas import tpu as pltpu
from jax.sharding import PartitionSpec as P

VMEM = 60 * 1024 * 1024


def permute(x, target):
    size = lax.axis_size("ka")
    pairs = [(i, target(i)) for i in range(size)]
    return lax.ppermute(x, "ka", [(i, j % size) for i, j in pairs if j is not None])


def nt_dot(a, b):
    return lax.dot_general(a, b, (((1,), (1,)), ((), ())), preferred_element_type=jnp.float32)


def iotas(rows, cols):
    shape = (rows, cols)
    return lax.broadcasted_iota(jnp.int32, shape, 0), lax.broadcasted_iota(jnp.int32, shape, 1)


def ones_where(condition):
    return jnp.where(condition, 1.0, 0.0).astype(jnp.bfloat16)


PART_C, PART_V = 8, 16


def fill_weights(first_ref, cond_ref, val_ref, we_ref, wh_ref):
    _, modes, bands_c, _ = cond_ref.shape
    bands_v = val_ref.shape[2]
    rows_e, part = bands_c * PART_V, PART_C * PART_V
    row, col = iotas(rows_e, bands_c)
    take = ones_where(row // PART_V == col)
    row, col = iotas(rows_e, rows_e)
    for m in range(modes):
        half = jnp.dot(take, cond_ref[0, m], preferred_element_type=jnp.float32)
        full = nt_dot(half.astype(jnp.bfloat16), take)
        keep = (row % PART_V == col % PART_V) & (row // PART_V >= first_ref[m, 0])
        full = jnp.where(keep, full, 0.0).astype(jnp.bfloat16)
        for q in range(bands_c // PART_C):
            we_ref[q, m * part:(m + 1) * part, :] = full[q * part:(q + 1) * part]
    row, col = iotas(PART_C * bands_v, bands_v)
    take_cols = ones_where(row % bands_v == col)
    for h in range(bands_v // PART_V):
        row, col = iotas(part, bands_v)
        take = ones_where(row % PART_V + h * PART_V == col)
        row, col = iotas(part, PART_C * bands_v)
        for m in range(modes):
            half = nt_dot(take, val_ref[0, m])
            full = nt_dot(half.astype(jnp.bfloat16), take_cols)
            keep = (row // PART_V == col // bands_v) & (
                row % PART_V + h * PART_V >= first_ref[m, 1]
            )
            wh_ref[h, m * part:(m + 1) * part, :] = jnp.where(keep, -full, 0.0).astype(jnp.bfloat16)


def products_kernel(order_ref, first_ref, coeffs_ref, cond_ref, val_ref, out_ref, *refs):
    *turned, we_ref, wh_ref = refs
    _, bands_c, bands_v, tile = coeffs_ref.shape
    modes = cond_ref.shape[1]

    @pl.when(pl.program_id(1) == 0)
    def _():
        fill_weights(first_ref, cond_ref, val_ref, we_ref, wh_ref)

    if turned:
        block = coeffs_ref[0].reshape(bands_c * bands_v, tile).T
        turned[0][0, 0] = block
        for step in range(1, len(turned)):
            @pl.when(pl.program_id(1) == step)
            def _():
                turned[step][0] = block

    for h in range(bands_v // PART_V):
        own_v = slice(h * PART_V, (h + 1) * PART_V)
        x = coeffs_ref[0, :, own_v, :].reshape(bands_c * PART_V, tile)
        for q in range(bands_c // PART_C):
            own_c = slice(q * PART_C, (q + 1) * PART_C)
            y = coeffs_ref[0, own_c].reshape(PART_C * bands_v, tile)
            left = jnp.concatenate((we_ref[q], wh_ref[h]), 1)
            value = jnp.dot(left, jnp.concatenate((x, y), 0), preferred_element_type=jnp.float32)
            value = value.reshape(modes, PART_C, PART_V, tile).astype(jnp.bfloat16)
            out_ref[0, :, own_c, own_v, :] = value


def products_of(coeffs, g_cond, g_val, band_first, order=None):
    k_local, bands_c, bands_v, excitons = coeffs.shape
    modes = g_cond.shape[1]
    tile = 256
    tiles, depth = excitons // tile, bands_c * bands_v
    rows_e, rows_h = bands_c * PART_V, PART_C * bands_v
    rows = modes * PART_C * PART_V
    out_shape = [jax.ShapeDtypeStruct((k_local, modes, bands_c, bands_v, excitons), jnp.bfloat16)]
    out_specs = [
        pl.BlockSpec(
            (1, modes, bands_c, bands_v, tile), lambda k, s, order: (k, 0, 0, 0, order[s])
        )
    ]
    if order is None:
        order = jnp.arange(tiles, dtype=jnp.int32)
    else:
        out_shape += [jax.ShapeDtypeStruct((tiles, k_local, tile, depth), jnp.bfloat16)]
        out_specs += [pl.BlockSpec((1, 1, tile, depth), lambda k, s, order: (order[s], k, 0, 0))]
        out_shape += [jax.ShapeDtypeStruct((k_local, tile, depth), jnp.bfloat16)] * (tiles - 1)
        out_specs += [pl.BlockSpec((1, tile, depth), lambda k, s, order: (k, 0, 0))] * (tiles - 1)
    return pl.pallas_call(
        products_kernel,
        out_shape=out_shape,
        grid_spec=pltpu.PrefetchScalarGridSpec(
            num_scalar_prefetch=1,
            grid=(k_local, tiles),
            in_specs=[
                pl.BlockSpec(memory_space=pltpu.SMEM),
                pl.BlockSpec((1, bands_c, bands_v, tile), lambda k, s, order: (k, 0, 0, order[s])),
                pl.BlockSpec((1, modes, bands_c, bands_c), lambda k, s, order: (k, 0, 0, 0)),
                pl.BlockSpec((1, modes, bands_v, bands_v), lambda k, s, order: (k, 0, 0, 0)),
            ],
            out_specs=out_specs,
            scratch_shapes=[
                pltpu.VMEM((bands_c // PART_C, rows, rows_e), jnp.bfloat16),
                pltpu.VMEM((bands_v // PART_V, rows, rows_h), jnp.bfloat16),
            ],
        ),
        compiler_params=pltpu.CompilerParams(vmem_limit_bytes=VMEM),
        cost_estimate=pl.CostEstimate(
            flops=2 * k_local * modes * excitons * depth * (rows_e + rows_h),
            bytes_accessed=2 * coeffs.size * (3 + modes),
            transcendentals=0,
        ),
    )(order, band_first, coeffs, g_cond, g_val)


def turn_kernel(block_ref, coeffs_ref, out_ref):
    out_ref[0] = coeffs_ref[0].T


def turned_piece(flat, block, width):
    k_local, depth, _ = flat.shape
    parts = 2
    return pl.pallas_call(
        turn_kernel,
        out_shape=jax.ShapeDtypeStruct((k_local, width, depth), jnp.bfloat16),
        grid_spec=pltpu.PrefetchScalarGridSpec(
            num_scalar_prefetch=1,
            grid=(k_local, parts),
            in_specs=[
                pl.BlockSpec((1, depth // parts, width), lambda k, d, block: (k, d, block[0]))
            ],
            out_specs=pl.BlockSpec((1, width, depth // parts), lambda k, d, block: (k, 0, d)),
        ),
        compiler_params=pltpu.CompilerParams(vmem_limit_bytes=VMEM),
        cost_estimate=pl.CostEstimate(
            flops=0, bytes_accessed=4 * k_local * depth * width, transcendentals=0
        ),
    )(block, flat)


def rows_kernel(pick_ref, own_ref, next_ref, right_ref, keep_ref, send_ref, left):
    _, k_local, width, depth = own_ref.shape

    @pl.when(pl.program_id(0) == 0)
    def _():
        for k in range(k_local):
            place = pick_ref[k]

            @pl.when(place < k_local)
            def _():
                left[:, k * depth:(k + 1) * depth] = own_ref[0, place]

            @pl.when(place >= k_local)
            def _():
                left[:, k * depth:(k + 1) * depth] = next_ref[place - k_local]

    tile = right_ref.shape[3]
    right = right_ref[:, 0].reshape(k_local * depth, tile)
    total = jnp.dot(left[...], right, preferred_element_type=jnp.float32)
    core = pick_ref[k_local + 1]
    parts = total.reshape(2, 2, width // 4, tile)
    low, high = parts[:, 0].reshape(width // 2, tile), parts[:, 1].reshape(width // 2, tile)
    keep_ref[...] = jnp.where(core == 0, low, high)
    send_ref[...] = jnp.where(core == 0, high, low).astype(jnp.bfloat16)


def rows_of(pick, own, following, products):
    _, k_local, width, depth = own.shape
    modes, excitons = products.shape[1], products.shape[3]
    tile = 512
    per_mode = excitons // tile
    columns = modes * excitons
    return pl.pallas_call(
        rows_kernel,
        out_shape=[
            jax.ShapeDtypeStruct((width // 2, columns), jnp.float32),
            jax.ShapeDtypeStruct((width // 2, columns), jnp.bfloat16),
        ],
        grid_spec=pltpu.PrefetchScalarGridSpec(
            num_scalar_prefetch=1,
            grid=(modes * per_mode,),
            in_specs=[
                pl.BlockSpec(
                    (1, k_local, width, depth), lambda j, pick: (pick[k_local], 0, 0, 0)
                ),
                pl.BlockSpec((k_local, width, depth), lambda j, pick: (0, 0, 0)),
                pl.BlockSpec(
                    (k_local, 1, depth, tile), lambda j, pick: (0, j // per_mode, 0, j % per_mode)
                ),
            ],
            out_specs=[pl.BlockSpec((width // 2, tile), lambda j, pick: (0, j))] * 2,
            scratch_shapes=[pltpu.VMEM((width, k_local * depth), jnp.bfloat16)],
        ),
        compiler_params=pltpu.CompilerParams(vmem_limit_bytes=VMEM),
        cost_estimate=pl.CostEstimate(
            flops=2 * k_local * depth * width * columns,
            bytes_accessed=2 * k_local * depth * columns,
            transcendentals=0,
        ),
    )(pick, own, following, products)


def on_two_by_four(coeffs, g_cond, g_val, k_plus_q, band_first, norm_factor):
    k_local, bands_c, bands_v, excitons = coeffs.shape
    modes = g_cond.shape[1]
    size = lax.axis_size("ka")
    width = excitons // 4
    me = lax.axis_index("ka")
    core, x, z = me & 1, me >> 1 & 1, me >> 2
    flat = coeffs.reshape(k_local, bands_c * bands_v, excitons)

    behind_z = (me + size - 1) % size >> 2
    order = behind_z ^ jnp.arange(3, -1, -1, dtype=jnp.int32)
    pieces = [turned_piece(flat, order[:1], width)]
    following = [permute(pieces[0], lambda i: i - 1)]
    products, own, *pieces = products_of(coeffs, g_cond, g_val, band_first, order)
    products = products.reshape(k_local, modes, bands_c * bands_v, excitons)
    following += [permute(piece, lambda i: i - 1) for piece in pieces]
    places = jnp.mod(k_plus_q - me * k_local, k_local * size)
    picks = [jnp.concatenate((places, jnp.stack((z ^ (3 - step), core)))) for step in range(4)]

    def rows(step):
        keep, send = rows_of(picks[step], own, following[step], products)
        return keep, permute(send, lambda i: i ^ 1).astype(jnp.float32)

    keep, other = rows(0)
    send = (keep + other).astype(jnp.bfloat16)
    send, picks[1] = lax.optimization_barrier((send, picks[1]))
    far = permute(send, lambda i: i ^ 4)
    keep, other = rows(1)
    pair = permute((keep + other + far.astype(jnp.float32)).astype(jnp.bfloat16), lambda i: i ^ 8)
    keep, other = rows(2)
    near = permute((keep + other).astype(jnp.bfloat16), lambda i: i ^ 4)
    keep, other = rows(3)
    total = keep + other + near.astype(jnp.float32) + pair.astype(jnp.float32)
    total = total.reshape(2, width // 4, modes * excitons)
    mine = lax.dynamic_index_in_dim(total, x, 0, keepdims=False)
    sent = lax.dynamic_index_in_dim(total, 1 - x, 0, keepdims=False).astype(jnp.bfloat16)
    total = mine + permute(sent, lambda i: i ^ 2).astype(jnp.float32)
    return (total * norm_factor).reshape(width // 4, modes, excitons)


def on_any(coeffs, g_cond, g_val, k_plus_q, band_first, norm_factor):
    k_local, bands_c, bands_v, excitons = coeffs.shape
    modes = g_cond.shape[1]
    size = lax.axis_size("ka")
    depth = bands_c * bands_v
    flat = coeffs.reshape(k_local, depth, excitons)
    blocks = jnp.concatenate((flat, permute(flat, lambda i: i - 1)), 0)
    offsets = jnp.mod(k_plus_q - lax.axis_index("ka") * k_local, k_local * size)
    products = products_of(coeffs, g_cond, g_val, band_first)[0]
    products = products.reshape(k_local, modes, depth, excitons)
    partners = [
        lax.dynamic_index_in_dim(blocks, offsets[k], 0, keepdims=False) for k in range(k_local)
    ]
    running = jnp.einsum(
        "kds,kmdt->smt", jnp.stack(partners), products, preferred_element_type=jnp.float32
    )
    return lax.psum_scatter(running * norm_factor, "ka", scatter_dimension=0, tiled=True)


def shards(coeffs, g_cond, g_val, k_plus_q, band_first):
    k_local, bands_c, bands_v, excitons = coeffs.shape
    size = lax.axis_size("ka")
    norm_factor = 1.0 / math.sqrt(bands_c * bands_v * k_local * size)
    whole_tiles = excitons % (4 * 128) == 0
    plan = on_two_by_four if size == 16 and whole_tiles else on_any
    return plan(coeffs, g_cond, g_val, k_plus_q, band_first, norm_factor)


def solution(mesh):
    in_specs = (
        P(("groups", "ka"), None, None, None),
        P(("groups", "ka"), None, None, None),
        P(("groups", "ka"), None, None, None),
        P(("groups", "ka")),
        P("groups", None),
    )
    out_specs = P(("groups", "ka"), None, None)
    return jax.shard_map(shards, mesh=mesh, in_specs=in_specs, out_specs=out_specs, check_vma=False)
```

```python
import functools
import math

import jax
import jax.numpy as jnp
from jax import lax
from jax.experimental import pallas as pl
from jax.experimental.pallas import tpu as pltpu
from jax.sharding import PartitionSpec as P

VMEM = 16 * 1024 * 1024


def permute(x, target):
    size = lax.axis_size("ka")
    pairs = [(i, target(i)) for i in range(size)]
    return lax.ppermute(x, "ka", [(i, j % size) for i, j in pairs if j is not None])


def nt_dot(a, b):
    return lax.dot_general(a, b, (((1,), (1,)), ((), ())), preferred_element_type=jnp.float32)


def iotas(rows, cols):
    shape = (rows, cols)
    return lax.broadcasted_iota(jnp.int32, shape, 0), lax.broadcasted_iota(jnp.int32, shape, 1)


def ones_where(condition):
    return jnp.where(condition, 1.0, 0.0).astype(jnp.bfloat16)


PART_C, PART_V = 8, 16


def fill_weights(first_ref, cond_ref, val_ref, we_ref, wh_ref):
    _, modes, bands_c, _ = cond_ref.shape
    bands_v = val_ref.shape[2]
    rows_e, part = bands_c * PART_V, PART_C * PART_V
    row, col = iotas(rows_e, bands_c)
    take = ones_where(row // PART_V == col)
    row, col = iotas(rows_e, rows_e)
    for m in range(modes):
        half = jnp.dot(take, cond_ref[0, m], preferred_element_type=jnp.float32)
        full = nt_dot(half.astype(jnp.bfloat16), take)
        keep = (row % PART_V == col % PART_V) & (row // PART_V >= first_ref[m, 0])
        full = jnp.where(keep, full, 0.0).astype(jnp.bfloat16)
        for q in range(bands_c // PART_C):
            we_ref[q, m * part:(m + 1) * part, :] = full[q * part:(q + 1) * part]
    row, col = iotas(PART_C * bands_v, bands_v)
    take_cols = ones_where(row % bands_v == col)
    for h in range(bands_v // PART_V):
        row, col = iotas(part, bands_v)
        take = ones_where(row % PART_V + h * PART_V == col)
        row, col = iotas(part, PART_C * bands_v)
        for m in range(modes):
            half = nt_dot(take, val_ref[0, m])
            full = nt_dot(half.astype(jnp.bfloat16), take_cols)
            keep = (row // PART_V == col // bands_v) & (
                row % PART_V + h * PART_V >= first_ref[m, 1]
            )
            wh_ref[h, m * part:(m + 1) * part, :] = jnp.where(keep, -full, 0.0).astype(jnp.bfloat16)


def tile_copy(order_ref, coeffs_ref, held, sems, step, tiles, tile):
    columns = pl.ds(pl.multiple_of(order_ref[step % tiles] * tile, tile), tile)
    slot = step % 2
    return pltpu.make_async_copy(
        coeffs_ref.at[step // tiles, :, :, columns], held.at[slot], sems.at[slot]
    )


def products_kernel(order_ref, first_ref, coeffs_ref, cond_ref, val_ref, out_ref, *refs):
    *turned, we_ref, wh_ref, held, sems = refs
    _, bands_c, bands_v, tile = held.shape
    k, s, tiles = pl.program_id(0), pl.program_id(1), pl.num_programs(1)
    step = k * tiles + s
    copy = functools.partial(
        tile_copy, order_ref, coeffs_ref, held, sems, tiles=tiles, tile=tile
    )

    @pl.when(step == 0)
    def _():
        copy(step=step).start()

    @pl.when(step + 1 < tiles * pl.num_programs(0))
    def _():
        copy(step=step + 1).start()

    @pl.when(s == 0)
    def _():
        fill_weights(first_ref, cond_ref, val_ref, we_ref, wh_ref)

    copy(step=step).wait()
    block_ref = held.at[step % 2]
    if turned:
        block = block_ref[...].reshape(bands_c * bands_v, tile).T
        turned[0][0, 0] = block
        for place in range(1, len(turned)):
            @pl.when(s == place)
            def _():
                turned[place][0] = block

    for h in range(bands_v // PART_V):
        own_v = slice(h * PART_V, (h + 1) * PART_V)
        x = block_ref[:, own_v, :].reshape(bands_c * PART_V, tile)
        for q in range(bands_c // PART_C):
            own_c = slice(q * PART_C, (q + 1) * PART_C)
            y = block_ref[own_c].reshape(PART_C * bands_v, tile)
            left = jnp.concatenate((we_ref[q], wh_ref[h]), 1)
            value = jnp.dot(left, jnp.concatenate((x, y), 0), preferred_element_type=jnp.float32)
            value = value.reshape(-1, PART_C, PART_V, tile).astype(jnp.bfloat16)
            out_ref[0, :, own_c, own_v, :] = value


def products_of(coeffs, g_cond, g_val, band_first, order=None):
    k_local, bands_c, bands_v, excitons = coeffs.shape
    modes = g_cond.shape[1]
    tile = 256
    tiles, depth = excitons // tile, bands_c * bands_v
    rows_e, rows_h = bands_c * PART_V, PART_C * bands_v
    rows = modes * PART_C * PART_V
    out_shape = [jax.ShapeDtypeStruct((k_local, modes, bands_c, bands_v, excitons), jnp.bfloat16)]
    out_specs = [
        pl.BlockSpec(
            (1, modes, bands_c, bands_v, tile), lambda k, s, order: (k, 0, 0, 0, order[s])
        )
    ]
    if order is None:
        order = jnp.arange(tiles, dtype=jnp.int32)
    else:
        out_shape += [jax.ShapeDtypeStruct((tiles, k_local, tile, depth), jnp.bfloat16)]
        out_specs += [pl.BlockSpec((1, 1, tile, depth), lambda k, s, order: (order[s], k, 0, 0))]
        out_shape += [jax.ShapeDtypeStruct((k_local, tile, depth), jnp.bfloat16)] * (tiles - 1)
        out_specs += [pl.BlockSpec((1, tile, depth), lambda k, s, order: (k, 0, 0))] * (tiles - 1)
    return pl.pallas_call(
        products_kernel,
        out_shape=out_shape,
        grid_spec=pltpu.PrefetchScalarGridSpec(
            num_scalar_prefetch=1,
            grid=(k_local, tiles),
            in_specs=[
                pl.BlockSpec(memory_space=pltpu.SMEM),
                pl.BlockSpec(memory_space=pltpu.HBM),
                pl.BlockSpec((1, modes, bands_c, bands_c), lambda k, s, order: (k, 0, 0, 0)),
                pl.BlockSpec((1, modes, bands_v, bands_v), lambda k, s, order: (k, 0, 0, 0)),
            ],
            out_specs=out_specs,
            scratch_shapes=[
                pltpu.VMEM((bands_c // PART_C, rows, rows_e), jnp.bfloat16),
                pltpu.VMEM((bands_v // PART_V, rows, rows_h), jnp.bfloat16),
                pltpu.VMEM((2, bands_c, bands_v, tile), jnp.bfloat16),
                pltpu.SemaphoreType.DMA((2,)),
            ],
        ),
        compiler_params=pltpu.CompilerParams(vmem_limit_bytes=VMEM),
        cost_estimate=pl.CostEstimate(
            flops=2 * k_local * modes * excitons * depth * (rows_e + rows_h),
            bytes_accessed=2 * coeffs.size * (3 + modes),
            transcendentals=0,
        ),
    )(order, band_first, coeffs, g_cond, g_val)


def turn_kernel(block_ref, coeffs_ref, out_ref, held, sems):
    k_local, parts, rows, width = held.shape
    columns = pl.ds(pl.multiple_of(block_ref[0] * width, width), width)
    copies = {}
    for k in range(k_local):
        for p in range(parts):
            copies[k, p] = pltpu.make_async_copy(
                coeffs_ref.at[k, pl.ds(p * rows, rows), columns], held.at[k, p], sems.at[k, p]
            )
            copies[k, p].start()
    for k in range(k_local):
        for p in range(parts):
            copies[k, p].wait()
            out_ref[k, :, p * rows:(p + 1) * rows] = held[k, p].T


def turned_piece(flat, block, width):
    k_local, depth, _ = flat.shape
    parts = 2
    return pl.pallas_call(
        turn_kernel,
        out_shape=jax.ShapeDtypeStruct((k_local, width, depth), jnp.bfloat16),
        in_specs=[
            pl.BlockSpec(memory_space=pltpu.SMEM),
            pl.BlockSpec(memory_space=pltpu.HBM),
        ],
        out_specs=pl.BlockSpec(memory_space=pltpu.VMEM),
        scratch_shapes=[
            pltpu.VMEM((k_local, parts, depth // parts, width), jnp.bfloat16),
            pltpu.SemaphoreType.DMA((k_local, parts)),
        ],
        compiler_params=pltpu.CompilerParams(vmem_limit_bytes=VMEM),
        cost_estimate=pl.CostEstimate(
            flops=0, bytes_accessed=4 * k_local * depth * width, transcendentals=0
        ),
    )(block, flat)


def rows_kernel(pick_ref, own_ref, next_ref, right_ref, keep_ref, send_ref, left):
    _, k_local, width, depth = own_ref.shape
    _, modes, _, excitons = right_ref.shape
    block, core = pick_ref[k_local], pick_ref[k_local + 1]
    for k in range(k_local):
        place = pick_ref[k]

        @pl.when(place < k_local)
        def _():
            left[:, k * depth:(k + 1) * depth] = own_ref[block, place]

        @pl.when(place >= k_local)
        def _():
            left[:, k * depth:(k + 1) * depth] = next_ref[place - k_local]

    tile = 512
    for m in range(modes):
        for s in range(0, excitons, tile):
            right = right_ref[:, m, :, s:s + tile].reshape(k_local * depth, tile)
            total = jnp.dot(left[...], right, preferred_element_type=jnp.float32)
            parts = total.reshape(2, 2, width // 4, tile)
            low = parts[:, 0].reshape(width // 2, tile)
            high = parts[:, 1].reshape(width // 2, tile)
            columns = slice(m * excitons + s, m * excitons + s + tile)
            keep_ref[:, columns] = jnp.where(core == 0, low, high)
            send_ref[:, columns] = jnp.where(core == 0, high, low).astype(jnp.bfloat16)


def rows_of(pick, own, following, products):
    _, k_local, width, depth = own.shape
    modes, excitons = products.shape[1], products.shape[3]
    columns = modes * excitons
    return pl.pallas_call(
        rows_kernel,
        out_shape=[
            jax.ShapeDtypeStruct((width // 2, columns), jnp.float32),
            jax.ShapeDtypeStruct((width // 2, columns), jnp.bfloat16),
        ],
        in_specs=[pl.BlockSpec(memory_space=pltpu.SMEM)]
        + [pl.BlockSpec(memory_space=pltpu.VMEM)] * 3,
        out_specs=[pl.BlockSpec(memory_space=pltpu.VMEM)] * 2,
        scratch_shapes=[pltpu.VMEM((width, k_local * depth), jnp.bfloat16)],
        compiler_params=pltpu.CompilerParams(vmem_limit_bytes=VMEM),
        cost_estimate=pl.CostEstimate(
            flops=2 * k_local * depth * width * columns,
            bytes_accessed=2 * k_local * depth * columns,
            transcendentals=0,
        ),
    )(pick, own, following, products)


def on_two_by_four(coeffs, g_cond, g_val, k_plus_q, band_first, norm_factor):
    k_local, bands_c, bands_v, excitons = coeffs.shape
    modes = g_cond.shape[1]
    size = lax.axis_size("ka")
    width = excitons // 4
    me = lax.axis_index("ka")
    core, x, z = me & 1, me >> 1 & 1, me >> 2
    flat = coeffs.reshape(k_local, bands_c * bands_v, excitons)

    behind_z = (me + size - 1) % size >> 2
    order = behind_z ^ jnp.arange(3, -1, -1, dtype=jnp.int32)
    pieces = [turned_piece(flat, order[:1], width)]
    following = [permute(pieces[0], lambda i: i - 1)]
    products, own, *pieces = products_of(coeffs, g_cond, g_val, band_first, order)
    products = products.reshape(k_local, modes, bands_c * bands_v, excitons)
    following += [permute(piece, lambda i: i - 1) for piece in pieces]
    places = jnp.mod(k_plus_q - me * k_local, k_local * size)
    picks = [jnp.concatenate((places, jnp.stack((z ^ (3 - step), core)))) for step in range(4)]

    def rows(step, after):
        pick, _ = lax.optimization_barrier((picks[step], after))
        keep, send = rows_of(pick, own, following[step], products)
        return keep, permute(send, lambda i: i ^ 1).astype(jnp.float32)

    keep, other = rows(0, products)
    send_far = (keep + other).astype(jnp.bfloat16)
    far = permute(send_far, lambda i: i ^ 4)
    keep_1, other_1 = rows(1, send_far)
    keep, other = rows(2, keep_1)
    send_pair = (keep_1 + other_1 + far.astype(jnp.float32)).astype(jnp.bfloat16)
    pair = permute(send_pair, lambda i: i ^ 8)
    send_near = (keep + other).astype(jnp.bfloat16)
    near = permute(send_near, lambda i: i ^ 4)
    keep, other = rows(3, (send_pair, send_near))
    total = keep + other + near.astype(jnp.float32) + pair.astype(jnp.float32)
    total = total.reshape(2, width // 4, modes * excitons)
    mine = lax.dynamic_index_in_dim(total, x, 0, keepdims=False)
    sent = lax.dynamic_index_in_dim(total, 1 - x, 0, keepdims=False).astype(jnp.bfloat16)
    total = mine + permute(sent, lambda i: i ^ 2).astype(jnp.float32)
    return (total * norm_factor).reshape(width // 4, modes, excitons)


def on_any(coeffs, g_cond, g_val, k_plus_q, band_first, norm_factor):
    k_local, bands_c, bands_v, excitons = coeffs.shape
    modes = g_cond.shape[1]
    size = lax.axis_size("ka")
    depth = bands_c * bands_v
    flat = coeffs.reshape(k_local, depth, excitons)
    blocks = jnp.concatenate((flat, permute(flat, lambda i: i - 1)), 0)
    offsets = jnp.mod(k_plus_q - lax.axis_index("ka") * k_local, k_local * size)
    products = products_of(coeffs, g_cond, g_val, band_first)[0]
    products = products.reshape(k_local, modes, depth, excitons)
    partners = [
        lax.dynamic_index_in_dim(blocks, offsets[k], 0, keepdims=False) for k in range(k_local)
    ]
    running = jnp.einsum(
        "kds,kmdt->smt", jnp.stack(partners), products, preferred_element_type=jnp.float32
    )
    return lax.psum_scatter(running * norm_factor, "ka", scatter_dimension=0, tiled=True)


def shards(coeffs, g_cond, g_val, k_plus_q, band_first):
    k_local, bands_c, bands_v, excitons = coeffs.shape
    size = lax.axis_size("ka")
    norm_factor = 1.0 / math.sqrt(bands_c * bands_v * k_local * size)
    whole_tiles = excitons % (4 * 128) == 0
    plan = on_two_by_four if size == 16 and whole_tiles else on_any
    return plan(coeffs, g_cond, g_val, k_plus_q, band_first, norm_factor)


def solution(mesh):
    in_specs = (
        P(("groups", "ka"), None, None, None),
        P(("groups", "ka"), None, None, None),
        P(("groups", "ka"), None, None, None),
        P(("groups", "ka")),
        P("groups", None),
    )
    out_specs = P(("groups", "ka"), None, None)
    return jax.shard_map(shards, mesh=mesh, in_specs=in_specs, out_specs=out_specs, check_vma=False)
```

```python
import functools
import math

import jax
import jax.numpy as jnp
from jax import lax
from jax.experimental import pallas as pl
from jax.experimental.pallas import tpu as pltpu
from jax.sharding import PartitionSpec as P

MIB = 1024 * 1024


def permute(x, target):
    size = lax.axis_size("ka")
    pairs = [(i, target(i)) for i in range(size)]
    return lax.ppermute(x, "ka", [(i, j % size) for i, j in pairs if j is not None])


def nt_dot(a, b):
    return lax.dot_general(a, b, (((1,), (1,)), ((), ())), preferred_element_type=jnp.float32)


def iotas(rows, cols):
    shape = (rows, cols)
    return lax.broadcasted_iota(jnp.int32, shape, 0), lax.broadcasted_iota(jnp.int32, shape, 1)


def ones_where(condition):
    return jnp.where(condition, 1.0, 0.0).astype(jnp.bfloat16)


PART_C, PART_V = 8, 16


def fill_weights(first_ref, cond_ref, val_ref, we_ref, wh_ref):
    _, modes, bands_c, _ = cond_ref.shape
    bands_v = val_ref.shape[2]
    rows_e, rows_h = bands_c * PART_V, PART_C * bands_v
    row, col = iotas(rows_e, bands_c)
    take = ones_where(row // PART_V == col)
    row, col = iotas(rows_e, rows_e)
    for m in range(modes):
        half = jnp.dot(take, cond_ref[0, m], preferred_element_type=jnp.float32)
        full = nt_dot(half.astype(jnp.bfloat16), take)
        keep = (row % PART_V == col % PART_V) & (row // PART_V >= first_ref[m, 0])
        we_ref[m * rows_e:(m + 1) * rows_e, :] = jnp.where(keep, full, 0.0).astype(jnp.bfloat16)
    row, col = iotas(rows_h, bands_v)
    take = ones_where(row % bands_v == col)
    row, col = iotas(rows_h, rows_h)
    for m in range(modes):
        half = nt_dot(take, val_ref[0, m])
        full = nt_dot(half.astype(jnp.bfloat16), take)
        keep = (row // bands_v == col // bands_v) & (row % bands_v >= first_ref[m, 1])
        wh_ref[m * rows_h:(m + 1) * rows_h, :] = jnp.where(keep, full, 0.0).astype(jnp.bfloat16)


def products_kernel(first_ref, coeffs_ref, cond_ref, val_ref, out_ref, we_ref, wh_ref):
    _, bands_c, bands_v, tile = coeffs_ref.shape
    modes = cond_ref.shape[1]
    rows_e, rows_h = bands_c * PART_V, PART_C * bands_v

    @pl.when(pl.program_id(1) == 0)
    def _():
        fill_weights(first_ref, cond_ref, val_ref, we_ref, wh_ref)

    electron = []
    for h in range(bands_v // PART_V):
        x = coeffs_ref[0, :, h * PART_V:(h + 1) * PART_V, :].reshape(rows_e, tile)
        e = jnp.dot(we_ref[...], x, preferred_element_type=jnp.float32)
        electron.append(e.reshape(modes, bands_c, PART_V, tile))
    for q in range(bands_c // PART_C):
        own = slice(q * PART_C, (q + 1) * PART_C)
        y = coeffs_ref[0, own].reshape(rows_h, tile)
        hole = jnp.dot(wh_ref[...], y, preferred_element_type=jnp.float32)
        hole = hole.reshape(modes, PART_C, bands_v, tile)
        for m in range(modes):
            for h in range(bands_v // PART_V):
                cols = slice(h * PART_V, (h + 1) * PART_V)
                value = electron[h][m, own] - hole[m, :, cols]
                out_ref[0, m, own, cols, :] = value.astype(jnp.bfloat16)


def products_of(coeffs, g_cond, g_val, band_first):
    k_local, bands_c, bands_v, excitons = coeffs.shape
    modes = g_cond.shape[1]
    tile = 256
    rows_e, rows_h = bands_c * PART_V, PART_C * bands_v
    depth = bands_c * bands_v
    return pl.pallas_call(
        products_kernel,
        out_shape=jax.ShapeDtypeStruct((k_local, modes, bands_c, bands_v, excitons), jnp.bfloat16),
        grid=(k_local, excitons // tile),
        in_specs=[
            pl.BlockSpec(memory_space=pltpu.SMEM),
            pl.BlockSpec((1, bands_c, bands_v, tile), lambda k, s: (k, 0, 0, s)),
            pl.BlockSpec((1, modes, bands_c, bands_c), lambda k, s: (k, 0, 0, 0)),
            pl.BlockSpec((1, modes, bands_v, bands_v), lambda k, s: (k, 0, 0, 0)),
        ],
        out_specs=pl.BlockSpec((1, modes, bands_c, bands_v, tile), lambda k, s: (k, 0, 0, 0, s)),
        scratch_shapes=[
            pltpu.VMEM((modes * rows_e, rows_e), jnp.bfloat16),
            pltpu.VMEM((modes * rows_h, rows_h), jnp.bfloat16),
        ],
        compiler_params=pltpu.CompilerParams(vmem_limit_bytes=60 * MIB),
        cost_estimate=pl.CostEstimate(
            flops=2 * k_local * modes * excitons * depth * (rows_e + rows_h),
            bytes_accessed=2 * coeffs.size * (1 + modes),
            transcendentals=0,
        ),
    )(band_first, coeffs, g_cond, g_val)


def turn_kernel(blocks_ref, coeffs_ref, *refs):
    *out_refs, held, sems = refs
    pieces, k_local, parts, rows, width = held.shape

    def copy(i, k, p):
        columns = pl.ds(pl.multiple_of(blocks_ref[i] * width, width), width)
        source = coeffs_ref.at[k, pl.ds(p * rows, rows), columns]
        return pltpu.make_async_copy(source, held.at[i, k, p], sems.at[i, k, p])

    steps = [(i, k, p) for i in range(pieces) for k in range(k_local) for p in range(parts)]
    for step in steps:
        copy(*step).start()
    for step in steps:
        i, k, p = step
        copy(*step).wait()
        out_refs[i][k, :, p * rows:(p + 1) * rows] = held[i, k, p].T


def turned_pieces(flat, blocks, width):
    k_local, depth, _ = flat.shape
    pieces, parts = blocks.shape[0], 2
    return pl.pallas_call(
        turn_kernel,
        out_shape=[jax.ShapeDtypeStruct((k_local, width, depth), jnp.bfloat16)] * pieces,
        in_specs=[
            pl.BlockSpec(memory_space=pltpu.SMEM),
            pl.BlockSpec(memory_space=pl.ANY),
        ],
        out_specs=[pl.BlockSpec(memory_space=pltpu.VMEM)] * pieces,
        scratch_shapes=[
            pltpu.VMEM((pieces, k_local, parts, depth // parts, width), jnp.bfloat16),
            pltpu.SemaphoreType.DMA((pieces, k_local, parts)),
        ],
        compiler_params=pltpu.CompilerParams(vmem_limit_bytes=60 * MIB),
        cost_estimate=pl.CostEstimate(
            flops=0, bytes_accessed=4 * pieces * k_local * depth * width, transcendentals=0
        ),
    )(blocks, flat)


def rows_kernel(pick_ref, own_ref, next_ref, right_ref, keep_ref, send_ref, *refs):
    own_held, next_held, held, left, own_sems, next_sems, sems = refs
    k_local, depth, width = own_held.shape
    tiles, _, _, tile = held.shape
    per_mode = right_ref.shape[3] // tile
    core = pick_ref[k_local + 1]
    columns = pl.ds(pl.multiple_of(pick_ref[k_local] * width, width), width)
    near = [pick_ref[k] < k_local for k in range(k_local)]

    def copy_own(k):
        source = own_ref.at[jnp.minimum(pick_ref[k], k_local - 1), :, columns]
        return pltpu.make_async_copy(source, own_held.at[k], own_sems.at[k])

    def copy_next(k):
        source = next_ref.at[jnp.maximum(pick_ref[k] - k_local, 0)]
        return pltpu.make_async_copy(source, next_held.at[k], next_sems.at[k])

    def copy_right(t, k):
        source = right_ref.at[k, t // per_mode, :, pl.ds(t % per_mode * tile, tile)]
        return pltpu.make_async_copy(source, held.at[t, k], sems.at[t, k])

    for k in range(k_local):
        copy_own(k).start()
        copy_next(k).start()
    for t in range(tiles):
        for k in range(k_local):
            copy_right(t, k).start()
    for k in range(k_local):
        copy_own(k).wait()
        copy_next(k).wait()

        @pl.when(near[k])
        def _():
            left[:, k * depth:(k + 1) * depth] = own_held[k].T

        @pl.when(jnp.logical_not(near[k]))
        def _():
            left[:, k * depth:(k + 1) * depth] = next_held[k]

    for t in range(tiles):
        for k in range(k_local):
            copy_right(t, k).wait()
        right = held[t].reshape(k_local * depth, tile)
        total = jnp.dot(left[...], right, preferred_element_type=jnp.float32)
        parts = total.reshape(2, 2, width // 4, tile)
        low = parts[:, 0].reshape(width // 2, tile)
        high = parts[:, 1].reshape(width // 2, tile)
        place = slice(t * tile, (t + 1) * tile)
        keep_ref[:, place] = jnp.where(core == 0, low, high)
        send_ref[:, place] = jnp.where(core == 0, high, low).astype(jnp.bfloat16)


def rows_of(pick, own, following, products):
    k_local, width, depth = following.shape
    modes, excitons = products.shape[1], products.shape[3]
    columns, tile = modes * excitons, 512
    tiles = columns // tile
    return pl.pallas_call(
        rows_kernel,
        out_shape=[
            jax.ShapeDtypeStruct((width // 2, columns), jnp.float32),
            jax.ShapeDtypeStruct((width // 2, columns), jnp.bfloat16),
        ],
        in_specs=[pl.BlockSpec(memory_space=pltpu.SMEM)]
        + [pl.BlockSpec(memory_space=pl.ANY)] * 3,
        out_specs=[pl.BlockSpec(memory_space=pltpu.VMEM)] * 2,
        scratch_shapes=[
            pltpu.VMEM((k_local, depth, width), jnp.bfloat16),
            pltpu.VMEM((k_local, width, depth), jnp.bfloat16),
            pltpu.VMEM((tiles, k_local, depth, tile), jnp.bfloat16),
            pltpu.VMEM((width, k_local * depth), jnp.bfloat16),
            pltpu.SemaphoreType.DMA((k_local,)),
            pltpu.SemaphoreType.DMA((k_local,)),
            pltpu.SemaphoreType.DMA((tiles, k_local)),
        ],
        compiler_params=pltpu.CompilerParams(vmem_limit_bytes=50 * MIB),
        cost_estimate=pl.CostEstimate(
            flops=2 * k_local * depth * width * columns,
            bytes_accessed=2 * k_local * depth * columns,
            transcendentals=0,
        ),
    )(pick, own, following, products)


def on_two_by_four(coeffs, g_cond, g_val, k_plus_q, band_first, norm_factor):
    k_local, bands_c, bands_v, excitons = coeffs.shape
    modes = g_cond.shape[1]
    size = lax.axis_size("ka")
    width = excitons // 4
    me = lax.axis_index("ka")
    core, x, z = me & 1, me >> 1 & 1, me >> 2
    flat = coeffs.reshape(k_local, bands_c * bands_v, excitons)

    behind_z = (me + size - 1) % size >> 2
    order = behind_z ^ jnp.arange(3, -1, -1, dtype=jnp.int32)
    pieces = turned_pieces(flat, order[:1], width)
    others, _ = lax.optimization_barrier((order[1:], pieces))
    pieces += turned_pieces(flat, others, width)
    following = [permute(piece, lambda i: i - 1) for piece in pieces]
    products = products_of(coeffs, g_cond, g_val, band_first)
    products = products.reshape(k_local, modes, bands_c * bands_v, excitons)
    places = jnp.mod(k_plus_q - me * k_local, k_local * size)
    picks = [jnp.concatenate((places, jnp.stack((z ^ (3 - step), core)))) for step in range(4)]

    def rows(step, after):
        pick, _ = lax.optimization_barrier((picks[step], after))
        keep, send = rows_of(pick, flat, following[step], products)
        return keep, permute(send, lambda i: i ^ 1).astype(jnp.float32)

    keep, other = rows(0, products)
    send_far = (keep + other).astype(jnp.bfloat16)
    far = permute(send_far, lambda i: i ^ 4)
    keep_1, other_1 = rows(1, send_far)
    keep, other = rows(2, keep_1)
    send_pair = (keep_1 + other_1 + far.astype(jnp.float32)).astype(jnp.bfloat16)
    pair = permute(send_pair, lambda i: i ^ 8)
    send_near = (keep + other).astype(jnp.bfloat16)
    near = permute(send_near, lambda i: i ^ 4)
    keep, other = rows(3, (send_pair, send_near))
    total = keep + other + near.astype(jnp.float32) + pair.astype(jnp.float32)
    total = total.reshape(2, width // 4, modes * excitons)
    mine = lax.dynamic_index_in_dim(total, x, 0, keepdims=False)
    sent = lax.dynamic_index_in_dim(total, 1 - x, 0, keepdims=False).astype(jnp.bfloat16)
    total = mine + permute(sent, lambda i: i ^ 2).astype(jnp.float32)
    return (total * norm_factor).reshape(width // 4, modes, excitons)


def on_any(coeffs, g_cond, g_val, k_plus_q, band_first, norm_factor):
    k_local, bands_c, bands_v, excitons = coeffs.shape
    modes = g_cond.shape[1]
    size = lax.axis_size("ka")
    depth = bands_c * bands_v
    flat = coeffs.reshape(k_local, depth, excitons)
    blocks = jnp.concatenate((flat, permute(flat, lambda i: i - 1)), 0)
    offsets = jnp.mod(k_plus_q - lax.axis_index("ka") * k_local, k_local * size)
    products = products_of(coeffs, g_cond, g_val, band_first)
    products = products.reshape(k_local, modes, depth, excitons)
    partners = [
        lax.dynamic_index_in_dim(blocks, offsets[k], 0, keepdims=False) for k in range(k_local)
    ]
    running = jnp.einsum(
        "kds,kmdt->smt", jnp.stack(partners), products, preferred_element_type=jnp.float32
    )
    return lax.psum_scatter(running * norm_factor, "ka", scatter_dimension=0, tiled=True)


def shards(coeffs, g_cond, g_val, k_plus_q, band_first):
    k_local, bands_c, bands_v, excitons = coeffs.shape
    size = lax.axis_size("ka")
    norm_factor = 1.0 / math.sqrt(bands_c * bands_v * k_local * size)
    whole_tiles = excitons % (4 * 128) == 0
    plan = on_two_by_four if size == 16 and whole_tiles else on_any
    return plan(coeffs, g_cond, g_val, k_plus_q, band_first, norm_factor)


def solution(mesh):
    in_specs = (
        P(("groups", "ka"), None, None, None),
        P(("groups", "ka"), None, None, None),
        P(("groups", "ka"), None, None, None),
        P(("groups", "ka")),
        P("groups", None),
    )
    out_specs = P(("groups", "ka"), None, None)
    return jax.shard_map(shards, mesh=mesh, in_specs=in_specs, out_specs=out_specs, check_vma=False)
```

```python
import functools
import math

import jax
import jax.numpy as jnp
from jax import lax
from jax.experimental import pallas as pl
from jax.experimental.pallas import tpu as pltpu
from jax.sharding import PartitionSpec as P

MIB = 1024 * 1024


def permute(x, target):
    size = lax.axis_size("ka")
    pairs = [(i, target(i)) for i in range(size)]
    return lax.ppermute(x, "ka", [(i, j % size) for i, j in pairs if j is not None])


def nt_dot(a, b):
    return lax.dot_general(a, b, (((1,), (1,)), ((), ())), preferred_element_type=jnp.float32)


def iotas(rows, cols):
    shape = (rows, cols)
    return lax.broadcasted_iota(jnp.int32, shape, 0), lax.broadcasted_iota(jnp.int32, shape, 1)


def ones_where(condition):
    return jnp.where(condition, 1.0, 0.0).astype(jnp.bfloat16)


PART_C, PART_V = 8, 16


def fill_weights(first_ref, cond_ref, val_ref, we_ref, wh_ref):
    _, modes, bands_c, _ = cond_ref.shape
    bands_v = val_ref.shape[2]
    rows_e, rows_h = bands_c * PART_V, PART_C * bands_v
    row, col = iotas(rows_e, bands_c)
    take = ones_where(row // PART_V == col)
    row, col = iotas(rows_e, rows_e)
    for m in range(modes):
        half = jnp.dot(take, cond_ref[0, m], preferred_element_type=jnp.float32)
        full = nt_dot(half.astype(jnp.bfloat16), take)
        keep = (row % PART_V == col % PART_V) & (row // PART_V >= first_ref[m, 0])
        we_ref[m * rows_e:(m + 1) * rows_e, :] = jnp.where(keep, full, 0.0).astype(jnp.bfloat16)
    row, col = iotas(rows_h, bands_v)
    take = ones_where(row % bands_v == col)
    row, col = iotas(rows_h, rows_h)
    for m in range(modes):
        half = nt_dot(take, val_ref[0, m])
        full = nt_dot(half.astype(jnp.bfloat16), take)
        keep = (row // bands_v == col // bands_v) & (row % bands_v >= first_ref[m, 1])
        wh_ref[m * rows_h:(m + 1) * rows_h, :] = jnp.where(keep, full, 0.0).astype(jnp.bfloat16)


def products_kernel(first_ref, coeffs_ref, cond_ref, val_ref, out_ref, we_ref, wh_ref):
    _, bands_c, bands_v, tile = coeffs_ref.shape
    modes = cond_ref.shape[1]
    rows_e, rows_h = bands_c * PART_V, PART_C * bands_v

    @pl.when(pl.program_id(1) == 0)
    def _():
        fill_weights(first_ref, cond_ref, val_ref, we_ref, wh_ref)

    electron = []
    for h in range(bands_v // PART_V):
        x = coeffs_ref[0, :, h * PART_V:(h + 1) * PART_V, :].reshape(rows_e, tile)
        e = jnp.dot(we_ref[...], x, preferred_element_type=jnp.float32)
        electron.append(e.reshape(modes, bands_c, PART_V, tile))
    for q in range(bands_c // PART_C):
        own = slice(q * PART_C, (q + 1) * PART_C)
        y = coeffs_ref[0, own].reshape(rows_h, tile)
        hole = jnp.dot(wh_ref[...], y, preferred_element_type=jnp.float32)
        hole = hole.reshape(modes, PART_C, bands_v, tile)
        for m in range(modes):
            for h in range(bands_v // PART_V):
                cols = slice(h * PART_V, (h + 1) * PART_V)
                value = electron[h][m, own] - hole[m, :, cols]
                out_ref[0, m, own, cols, :] = value.astype(jnp.bfloat16)


def products_of(coeffs, g_cond, g_val, band_first):
    k_local, bands_c, bands_v, excitons = coeffs.shape
    modes = g_cond.shape[1]
    tile = 256
    rows_e, rows_h = bands_c * PART_V, PART_C * bands_v
    depth = bands_c * bands_v
    return pl.pallas_call(
        products_kernel,
        out_shape=jax.ShapeDtypeStruct((k_local, modes, bands_c, bands_v, excitons), jnp.bfloat16),
        grid=(k_local, excitons // tile),
        in_specs=[
            pl.BlockSpec(memory_space=pltpu.SMEM),
            pl.BlockSpec((1, bands_c, bands_v, tile), lambda k, s: (k, 0, 0, s)),
            pl.BlockSpec((1, modes, bands_c, bands_c), lambda k, s: (k, 0, 0, 0)),
            pl.BlockSpec((1, modes, bands_v, bands_v), lambda k, s: (k, 0, 0, 0)),
        ],
        out_specs=pl.BlockSpec((1, modes, bands_c, bands_v, tile), lambda k, s: (k, 0, 0, 0, s)),
        scratch_shapes=[
            pltpu.VMEM((modes * rows_e, rows_e), jnp.bfloat16),
            pltpu.VMEM((modes * rows_h, rows_h), jnp.bfloat16),
        ],
        compiler_params=pltpu.CompilerParams(vmem_limit_bytes=60 * MIB),
        cost_estimate=pl.CostEstimate(
            flops=2 * k_local * modes * excitons * depth * (rows_e + rows_h),
            bytes_accessed=2 * coeffs.size * (1 + modes),
            transcendentals=0,
        ),
    )(band_first, coeffs, g_cond, g_val)


def turn_kernel(first, order_ref, coeffs_ref, *refs):
    *out_refs, held, sems = refs
    pieces, k_local, parts, rows, width = held.shape

    def copy(i, k, p):
        columns = pl.ds(pl.multiple_of(order_ref[first + i] * width, width), width)
        source = coeffs_ref.at[k, pl.ds(p * rows, rows), columns]
        return pltpu.make_async_copy(source, held.at[i, k, p], sems.at[i, k, p])

    steps = [(i, k, p) for i in range(pieces) for k in range(k_local) for p in range(parts)]
    for step in steps:
        copy(*step).start()
    for step in steps:
        i, k, p = step
        copy(*step).wait()
        out_refs[i][k, :, p * rows:(p + 1) * rows] = held[i, k, p].T


def turned_pieces(flat, order, first, pieces, width):
    k_local, depth, _ = flat.shape
    parts = 2
    return pl.pallas_call(
        functools.partial(turn_kernel, first),
        out_shape=[jax.ShapeDtypeStruct((k_local, width, depth), jnp.bfloat16)] * pieces,
        in_specs=[
            pl.BlockSpec(memory_space=pltpu.SMEM),
            pl.BlockSpec(memory_space=pl.ANY),
        ],
        out_specs=[pl.BlockSpec(memory_space=pltpu.VMEM)] * pieces,
        scratch_shapes=[
            pltpu.VMEM((pieces, k_local, parts, depth // parts, width), jnp.bfloat16),
            pltpu.SemaphoreType.DMA((pieces, k_local, parts)),
        ],
        compiler_params=pltpu.CompilerParams(vmem_limit_bytes=60 * MIB),
        cost_estimate=pl.CostEstimate(
            flops=0, bytes_accessed=4 * pieces * k_local * depth * width, transcendentals=0
        ),
    )(order, flat)


def rows_kernel(pick_ref, own_ref, next_ref, right_ref, mine_ref, other_ref, send_ref, *refs):
    own_held, next_held, held, left, own_sems, next_sems, sems = refs
    k_local, depth, width = own_held.shape
    tiles, _, _, tile = held.shape
    per_mode = right_ref.shape[3] // tile
    core, x = pick_ref[k_local + 1], pick_ref[k_local + 2]
    columns = pl.ds(pl.multiple_of(pick_ref[k_local] * width, width), width)
    near = [pick_ref[k] < k_local for k in range(k_local)]

    def copy_own(k):
        source = own_ref.at[jnp.minimum(pick_ref[k], k_local - 1), :, columns]
        return pltpu.make_async_copy(source, own_held.at[k], own_sems.at[k])

    def copy_next(k):
        source = next_ref.at[jnp.maximum(pick_ref[k] - k_local, 0)]
        return pltpu.make_async_copy(source, next_held.at[k], next_sems.at[k])

    def copy_right(t, k):
        source = right_ref.at[k, t // per_mode, :, pl.ds(t % per_mode * tile, tile)]
        return pltpu.make_async_copy(source, held.at[t, k], sems.at[t, k])

    for k in range(k_local):
        copy_own(k).start()
        copy_next(k).start()
    for t in range(tiles):
        for k in range(k_local):
            copy_right(t, k).start()
    for k in range(k_local):
        copy_own(k).wait()
        copy_next(k).wait()

        @pl.when(near[k])
        def _():
            left[:, k * depth:(k + 1) * depth] = own_held[k].T

        @pl.when(jnp.logical_not(near[k]))
        def _():
            left[:, k * depth:(k + 1) * depth] = next_held[k]

    for t in range(tiles):
        for k in range(k_local):
            copy_right(t, k).wait()
        right = held[t].reshape(k_local * depth, tile)
        total = jnp.dot(left[...], right, preferred_element_type=jnp.float32)
        parts = total.reshape(2, 2, width // 4, tile)
        mine = jnp.where(x == 0, parts[0], parts[1])
        other = jnp.where(x == 0, parts[1], parts[0])
        place = slice(t * tile, (t + 1) * tile)
        mine_ref[:, place] = jnp.where(core == 0, mine[0], mine[1])
        other_ref[:, place] = jnp.where(core == 0, other[0], other[1])
        send_ref[:width // 4, place] = jnp.where(core == 0, mine[1], mine[0]).astype(jnp.bfloat16)
        send_ref[width // 4:, place] = jnp.where(core == 0, other[1], other[0]).astype(jnp.bfloat16)


def rows_of(pick, own, following, products):
    k_local, width, depth = following.shape
    modes, excitons = products.shape[1], products.shape[3]
    columns, tile = modes * excitons, 512
    tiles = columns // tile
    return pl.pallas_call(
        rows_kernel,
        out_shape=[
            jax.ShapeDtypeStruct((width // 4, columns), jnp.float32),
            jax.ShapeDtypeStruct((width // 4, columns), jnp.float32),
            jax.ShapeDtypeStruct((width // 2, columns), jnp.bfloat16),
        ],
        in_specs=[pl.BlockSpec(memory_space=pltpu.SMEM)]
        + [pl.BlockSpec(memory_space=pl.ANY)] * 3,
        out_specs=[pl.BlockSpec(memory_space=pltpu.VMEM)] * 3,
        scratch_shapes=[
            pltpu.VMEM((k_local, depth, width), jnp.bfloat16),
            pltpu.VMEM((k_local, width, depth), jnp.bfloat16),
            pltpu.VMEM((tiles, k_local, depth, tile), jnp.bfloat16),
            pltpu.VMEM((width, k_local * depth), jnp.bfloat16),
            pltpu.SemaphoreType.DMA((k_local,)),
            pltpu.SemaphoreType.DMA((k_local,)),
            pltpu.SemaphoreType.DMA((tiles, k_local)),
        ],
        compiler_params=pltpu.CompilerParams(vmem_limit_bytes=50 * MIB),
        cost_estimate=pl.CostEstimate(
            flops=2 * k_local * depth * width * columns,
            bytes_accessed=2 * k_local * depth * columns,
            transcendentals=0,
        ),
    )(pick, own, following, products)


def on_two_by_four(coeffs, g_cond, g_val, k_plus_q, band_first, norm_factor):
    k_local, bands_c, bands_v, excitons = coeffs.shape
    modes = g_cond.shape[1]
    size = lax.axis_size("ka")
    width = excitons // 4
    me = lax.axis_index("ka")
    core, x, z = me & 1, me >> 1 & 1, me >> 2
    flat = coeffs.reshape(k_local, bands_c * bands_v, excitons)

    behind_z = (me + size - 1) % size >> 2
    order = behind_z ^ jnp.arange(3, -1, -1, dtype=jnp.int32)
    pieces = turned_pieces(flat, order, 0, 1, width)
    order, _ = lax.optimization_barrier((order, pieces))
    pieces += turned_pieces(flat, order, 1, 3, width)
    following = [permute(piece, lambda i: i - 1) for piece in pieces]
    products = products_of(coeffs, g_cond, g_val, band_first)
    products = products.reshape(k_local, modes, bands_c * bands_v, excitons)
    places = jnp.mod(k_plus_q - me * k_local, k_local * size)

    def rows(step, after):
        pick = jnp.concatenate((places, jnp.stack((z ^ (3 - step), core, x))))
        pick, _ = lax.optimization_barrier((pick, after))
        mine, other, send = rows_of(pick, flat, following[step], products)
        return mine, other, permute(send, lambda i: i ^ 1)

    def for_x(step, from_core):
        return (step[1] + from_core[width // 4:].astype(jnp.float32)).astype(jnp.bfloat16)

    steps = [rows(0, products)]
    for step in (1, 2):
        steps.append(rows(step, steps[-1][0]))
    from_cores = [step[2] for step in steps]
    from_cores, following[3] = lax.optimization_barrier((from_cores, following[3]))
    sends = [for_x(*both) for both in zip(steps, from_cores)]
    steps.append(rows(3, sends))
    from_cores.append(steps[3][2])
    sends.append(for_x(steps[3], from_cores[3]))

    def summed(step):
        from_x = permute(sends[step], lambda i: i ^ 2).astype(jnp.float32)
        return steps[step][0] + from_cores[step][:width // 4].astype(jnp.float32) + from_x

    def over(value, bit):
        return permute(value.astype(jnp.bfloat16), lambda i: i ^ bit).astype(jnp.float32)

    far = over(summed(0), 4)
    pair = over(summed(1) + far, 8)
    near = over(summed(2), 4)
    total = summed(3) + near + pair
    return (total * norm_factor).reshape(width // 4, modes, excitons)


def on_any(coeffs, g_cond, g_val, k_plus_q, band_first, norm_factor):
    k_local, bands_c, bands_v, excitons = coeffs.shape
    modes = g_cond.shape[1]
    size = lax.axis_size("ka")
    depth = bands_c * bands_v
    flat = coeffs.reshape(k_local, depth, excitons)
    blocks = jnp.concatenate((flat, permute(flat, lambda i: i - 1)), 0)
    offsets = jnp.mod(k_plus_q - lax.axis_index("ka") * k_local, k_local * size)
    products = products_of(coeffs, g_cond, g_val, band_first)
    products = products.reshape(k_local, modes, depth, excitons)
    partners = [
        lax.dynamic_index_in_dim(blocks, offsets[k], 0, keepdims=False) for k in range(k_local)
    ]
    running = jnp.einsum(
        "kds,kmdt->smt", jnp.stack(partners), products, preferred_element_type=jnp.float32
    )
    return lax.psum_scatter(running * norm_factor, "ka", scatter_dimension=0, tiled=True)


def shards(coeffs, g_cond, g_val, k_plus_q, band_first):
    k_local, bands_c, bands_v, excitons = coeffs.shape
    size = lax.axis_size("ka")
    norm_factor = 1.0 / math.sqrt(bands_c * bands_v * k_local * size)
    whole_tiles = excitons % (4 * 128) == 0
    plan = on_two_by_four if size == 16 and whole_tiles else on_any
    return plan(coeffs, g_cond, g_val, k_plus_q, band_first, norm_factor)


def solution(mesh):
    in_specs = (
        P(("groups", "ka"), None, None, None),
        P(("groups", "ka"), None, None, None),
        P(("groups", "ka"), None, None, None),
        P(("groups", "ka")),
        P("groups", None),
    )
    out_specs = P(("groups", "ka"), None, None)
    return jax.shard_map(shards, mesh=mesh, in_specs=in_specs, out_specs=out_specs, check_vma=False)
```

```python
import functools
import math

import jax
import jax.numpy as jnp
from jax import lax
from jax.experimental import pallas as pl
from jax.experimental.pallas import tpu as pltpu
from jax.sharding import PartitionSpec as P

MIB = 1024 * 1024


def permute(x, target):
    size = lax.axis_size("ka")
    pairs = [(i, target(i)) for i in range(size)]
    return lax.ppermute(x, "ka", [(i, j % size) for i, j in pairs if j is not None])


def nt_dot(a, b):
    return lax.dot_general(a, b, (((1,), (1,)), ((), ())), preferred_element_type=jnp.float32)


def iotas(rows, cols):
    shape = (rows, cols)
    return lax.broadcasted_iota(jnp.int32, shape, 0), lax.broadcasted_iota(jnp.int32, shape, 1)


def ones_where(condition):
    return jnp.where(condition, 1.0, 0.0).astype(jnp.bfloat16)


PART_C, PART_V = 8, 16


def fill_weights(first_ref, cond_ref, val_ref, we_ref, wh_ref):
    _, modes, bands_c, _ = cond_ref.shape
    bands_v = val_ref.shape[2]
    rows_e, rows_h = bands_c * PART_V, PART_C * bands_v
    row, col = iotas(rows_e, bands_c)
    take = ones_where(row // PART_V == col)
    row, col = iotas(rows_e, rows_e)
    for m in range(modes):
        half = jnp.dot(take, cond_ref[0, m], preferred_element_type=jnp.float32)
        full = nt_dot(half.astype(jnp.bfloat16), take)
        keep = (row % PART_V == col % PART_V) & (row // PART_V >= first_ref[m, 0])
        we_ref[m * rows_e:(m + 1) * rows_e, :] = jnp.where(keep, full, 0.0).astype(jnp.bfloat16)
    row, col = iotas(rows_h, bands_v)
    take = ones_where(row % bands_v == col)
    row, col = iotas(rows_h, rows_h)
    for m in range(modes):
        half = nt_dot(take, val_ref[0, m])
        full = nt_dot(half.astype(jnp.bfloat16), take)
        keep = (row // bands_v == col // bands_v) & (row % bands_v >= first_ref[m, 1])
        wh_ref[m * rows_h:(m + 1) * rows_h, :] = jnp.where(keep, full, 0.0).astype(jnp.bfloat16)


def products_kernel(first_ref, coeffs_ref, cond_ref, val_ref, out_ref, we_ref, wh_ref):
    _, bands_c, bands_v, tile = coeffs_ref.shape
    modes = cond_ref.shape[1]
    rows_e, rows_h = bands_c * PART_V, PART_C * bands_v

    @pl.when(pl.program_id(1) == 0)
    def _():
        fill_weights(first_ref, cond_ref, val_ref, we_ref, wh_ref)

    electron = []
    for h in range(bands_v // PART_V):
        x = coeffs_ref[0, :, h * PART_V:(h + 1) * PART_V, :].reshape(rows_e, tile)
        e = jnp.dot(we_ref[...], x, preferred_element_type=jnp.float32)
        electron.append(e.reshape(modes, bands_c, PART_V, tile))
    for q in range(bands_c // PART_C):
        own = slice(q * PART_C, (q + 1) * PART_C)
        y = coeffs_ref[0, own].reshape(rows_h, tile)
        hole = jnp.dot(wh_ref[...], y, preferred_element_type=jnp.float32)
        hole = hole.reshape(modes, PART_C, bands_v, tile)
        for m in range(modes):
            for h in range(bands_v // PART_V):
                cols = slice(h * PART_V, (h + 1) * PART_V)
                value = electron[h][m, own] - hole[m, :, cols]
                out_ref[0, m, own, cols, :] = value.astype(jnp.bfloat16)


def products_of(coeffs, g_cond, g_val, band_first):
    k_local, bands_c, bands_v, excitons = coeffs.shape
    modes = g_cond.shape[1]
    tile = 256
    rows_e, rows_h = bands_c * PART_V, PART_C * bands_v
    depth = bands_c * bands_v
    return pl.pallas_call(
        products_kernel,
        out_shape=jax.ShapeDtypeStruct((k_local, modes, bands_c, bands_v, excitons), jnp.bfloat16),
        grid=(k_local, excitons // tile),
        in_specs=[
            pl.BlockSpec(memory_space=pltpu.SMEM),
            pl.BlockSpec((1, bands_c, bands_v, tile), lambda k, s: (k, 0, 0, s)),
            pl.BlockSpec((1, modes, bands_c, bands_c), lambda k, s: (k, 0, 0, 0)),
            pl.BlockSpec((1, modes, bands_v, bands_v), lambda k, s: (k, 0, 0, 0)),
        ],
        out_specs=pl.BlockSpec((1, modes, bands_c, bands_v, tile), lambda k, s: (k, 0, 0, 0, s)),
        scratch_shapes=[
            pltpu.VMEM((modes * rows_e, rows_e), jnp.bfloat16),
            pltpu.VMEM((modes * rows_h, rows_h), jnp.bfloat16),
        ],
        compiler_params=pltpu.CompilerParams(vmem_limit_bytes=60 * MIB),
        cost_estimate=pl.CostEstimate(
            flops=2 * k_local * modes * excitons * depth * (rows_e + rows_h),
            bytes_accessed=2 * coeffs.size * (1 + modes),
            transcendentals=0,
        ),
    )(band_first, coeffs, g_cond, g_val)


def turn_kernel(first, order_ref, coeffs_ref, *refs):
    *out_refs, held, sems = refs
    pieces, k_local, parts, rows, width = held.shape

    def copy(i, k, p):
        columns = pl.ds(pl.multiple_of(order_ref[first + i] * width, width), width)
        source = coeffs_ref.at[k, pl.ds(p * rows, rows), columns]
        return pltpu.make_async_copy(source, held.at[i, k, p], sems.at[i, k, p])

    steps = [(i, k, p) for i in range(pieces) for k in range(k_local) for p in range(parts)]
    for step in steps:
        copy(*step).start()
    for step in steps:
        i, k, p = step
        copy(*step).wait()
        out_refs[i][k, :, p * rows:(p + 1) * rows] = held[i, k, p].T


def turned_pieces(flat, order, first, pieces, width):
    k_local, depth, _ = flat.shape
    parts = 2
    return pl.pallas_call(
        functools.partial(turn_kernel, first),
        out_shape=[jax.ShapeDtypeStruct((k_local, width, depth), jnp.bfloat16)] * pieces,
        in_specs=[
            pl.BlockSpec(memory_space=pltpu.SMEM),
            pl.BlockSpec(memory_space=pl.ANY),
        ],
        out_specs=[pl.BlockSpec(memory_space=pltpu.VMEM)] * pieces,
        scratch_shapes=[
            pltpu.VMEM((pieces, k_local, parts, depth // parts, width), jnp.bfloat16),
            pltpu.SemaphoreType.DMA((pieces, k_local, parts)),
        ],
        compiler_params=pltpu.CompilerParams(vmem_limit_bytes=60 * MIB),
        cost_estimate=pl.CostEstimate(
            flops=0, bytes_accessed=4 * pieces * k_local * depth * width, transcendentals=0
        ),
    )(order, flat)


def rows_kernel(pick_ref, own_ref, next_ref, right_ref, mine_ref, other_ref, send_ref, *refs):
    own_held, next_held, held, left, own_sems, next_sems, sems = refs
    k_local, depth, width = own_held.shape
    tiles, _, _, tile = held.shape
    per_mode = right_ref.shape[3] // tile
    core, x = pick_ref[k_local + 1], pick_ref[k_local + 2]
    columns = pl.ds(pl.multiple_of(pick_ref[k_local] * width, width), width)
    near = [pick_ref[k] < k_local for k in range(k_local)]

    def copy_own(k):
        source = own_ref.at[jnp.minimum(pick_ref[k], k_local - 1), :, columns]
        return pltpu.make_async_copy(source, own_held.at[k], own_sems.at[k])

    def copy_next(k):
        source = next_ref.at[jnp.maximum(pick_ref[k] - k_local, 0)]
        return pltpu.make_async_copy(source, next_held.at[k], next_sems.at[k])

    def copy_right(t, k):
        source = right_ref.at[k, t // per_mode, :, pl.ds(t % per_mode * tile, tile)]
        return pltpu.make_async_copy(source, held.at[t, k], sems.at[t, k])

    for k in range(k_local):
        copy_own(k).start()
        copy_next(k).start()
    for t in range(tiles):
        for k in range(k_local):
            copy_right(t, k).start()
    for k in range(k_local):
        copy_own(k).wait()
        copy_next(k).wait()

        @pl.when(near[k])
        def _():
            left[:, k * depth:(k + 1) * depth] = own_held[k].T

        @pl.when(jnp.logical_not(near[k]))
        def _():
            left[:, k * depth:(k + 1) * depth] = next_held[k]

    for t in range(tiles):
        for k in range(k_local):
            copy_right(t, k).wait()
        right = held[t].reshape(k_local * depth, tile)
        total = jnp.dot(left[...], right, preferred_element_type=jnp.float32)
        parts = total.reshape(2, 2, width // 4, tile)
        mine = jnp.where(x == 0, parts[0], parts[1])
        other = jnp.where(x == 0, parts[1], parts[0])
        place = slice(t * tile, (t + 1) * tile)
        mine_ref[:, place] = jnp.where(core == 0, mine[0], mine[1])
        other_ref[:, place] = jnp.where(core == 0, other[0], other[1])
        send_ref[:width // 4, place] = jnp.where(core == 0, mine[1], mine[0]).astype(jnp.bfloat16)
        send_ref[width // 4:, place] = jnp.where(core == 0, other[1], other[0]).astype(jnp.bfloat16)


def rows_of(pick, own, following, products):
    k_local, width, depth = following.shape
    modes, excitons = products.shape[1], products.shape[3]
    columns, tile = modes * excitons, 512
    tiles = columns // tile
    return pl.pallas_call(
        rows_kernel,
        out_shape=[
            jax.ShapeDtypeStruct((width // 4, columns), jnp.float32),
            jax.ShapeDtypeStruct((width // 4, columns), jnp.float32),
            jax.ShapeDtypeStruct((width // 2, columns), jnp.bfloat16),
        ],
        in_specs=[pl.BlockSpec(memory_space=pltpu.SMEM)]
        + [pl.BlockSpec(memory_space=pl.ANY)] * 3,
        out_specs=[pl.BlockSpec(memory_space=pltpu.VMEM)] * 3,
        scratch_shapes=[
            pltpu.VMEM((k_local, depth, width), jnp.bfloat16),
            pltpu.VMEM((k_local, width, depth), jnp.bfloat16),
            pltpu.VMEM((tiles, k_local, depth, tile), jnp.bfloat16),
            pltpu.VMEM((width, k_local * depth), jnp.bfloat16),
            pltpu.SemaphoreType.DMA((k_local,)),
            pltpu.SemaphoreType.DMA((k_local,)),
            pltpu.SemaphoreType.DMA((tiles, k_local)),
        ],
        compiler_params=pltpu.CompilerParams(vmem_limit_bytes=50 * MIB),
        cost_estimate=pl.CostEstimate(
            flops=2 * k_local * depth * width * columns,
            bytes_accessed=2 * k_local * depth * columns,
            transcendentals=0,
        ),
    )(pick, own, following, products)


def on_two_by_four(coeffs, g_cond, g_val, k_plus_q, band_first, norm_factor):
    k_local, bands_c, bands_v, excitons = coeffs.shape
    modes = g_cond.shape[1]
    size = lax.axis_size("ka")
    width = excitons // 4
    me = lax.axis_index("ka")
    core, x, z = me & 1, me >> 1 & 1, me >> 2
    flat = coeffs.reshape(k_local, bands_c * bands_v, excitons)

    behind_z = (me + size - 1) % size >> 2
    order = behind_z ^ jnp.arange(3, -1, -1, dtype=jnp.int32)
    pieces = turned_pieces(flat, order, 0, 1, width)
    order, _ = lax.optimization_barrier((order, pieces))
    pieces += turned_pieces(flat, order, 1, 3, width)
    following = [permute(piece, lambda i: i - 1) for piece in pieces]
    products = products_of(coeffs, g_cond, g_val, band_first)
    products = products.reshape(k_local, modes, bands_c * bands_v, excitons)
    places = jnp.mod(k_plus_q - me * k_local, k_local * size)

    def rows(step, after):
        pick = jnp.concatenate((places, jnp.stack((z ^ (3 - step), core, x))))
        pick, _ = lax.optimization_barrier((pick, after))
        mine, other, send = rows_of(pick, flat, following[step], products)
        return mine, other, permute(send, lambda i: i ^ 1)

    def for_x(step, from_core):
        return (step[1] + from_core[width // 4:].astype(jnp.float32)).astype(jnp.bfloat16)

    def from_x(send):
        return permute(send, lambda i: i ^ 2).astype(jnp.float32)

    def own_sum(step, from_core, across):
        return step[0] + from_core[:width // 4].astype(jnp.float32) + across

    def over(value, bit):
        return permute(value, lambda i: i ^ bit).astype(jnp.float32)

    step_0 = rows(0, products)
    step_1 = rows(1, step_0[0])
    core_0, following[2], _ = lax.optimization_barrier((step_0[2], following[2], step_1[0]))
    send_0 = for_x(step_0, core_0)
    across_0 = from_x(send_0)
    step_2 = rows(2, (step_1[0], send_0))
    core_1, core_2, following[3] = lax.optimization_barrier((step_1[2], step_2[2], following[3]))
    send_1, send_2 = for_x(step_1, core_1), for_x(step_2, core_2)
    across_1, across_2 = from_x(send_1), from_x(send_2)
    far = own_sum(step_0, core_0, across_0).astype(jnp.bfloat16)
    step_3 = rows(3, (send_1, send_2, far))
    far = over(far, 4)
    pair = (own_sum(step_1, core_1, across_1) + far).astype(jnp.bfloat16)
    send_3 = for_x(step_3, step_3[2])
    across_2, _ = lax.optimization_barrier((across_2, (pair, send_3)))
    pair = over(pair, 8)
    near = over(own_sum(step_2, core_2, across_2).astype(jnp.bfloat16), 4)
    across_3 = from_x(send_3)
    total = own_sum(step_3, step_3[2], across_3) + near + pair
    return (total * norm_factor).reshape(width // 4, modes, excitons)


def on_any(coeffs, g_cond, g_val, k_plus_q, band_first, norm_factor):
    k_local, bands_c, bands_v, excitons = coeffs.shape
    modes = g_cond.shape[1]
    size = lax.axis_size("ka")
    depth = bands_c * bands_v
    flat = coeffs.reshape(k_local, depth, excitons)
    blocks = jnp.concatenate((flat, permute(flat, lambda i: i - 1)), 0)
    offsets = jnp.mod(k_plus_q - lax.axis_index("ka") * k_local, k_local * size)
    products = products_of(coeffs, g_cond, g_val, band_first)
    products = products.reshape(k_local, modes, depth, excitons)
    partners = [
        lax.dynamic_index_in_dim(blocks, offsets[k], 0, keepdims=False) for k in range(k_local)
    ]
    running = jnp.einsum(
        "kds,kmdt->smt", jnp.stack(partners), products, preferred_element_type=jnp.float32
    )
    return lax.psum_scatter(running * norm_factor, "ka", scatter_dimension=0, tiled=True)


def shards(coeffs, g_cond, g_val, k_plus_q, band_first):
    k_local, bands_c, bands_v, excitons = coeffs.shape
    size = lax.axis_size("ka")
    norm_factor = 1.0 / math.sqrt(bands_c * bands_v * k_local * size)
    whole_tiles = excitons % (4 * 128) == 0
    plan = on_two_by_four if size == 16 and whole_tiles else on_any
    return plan(coeffs, g_cond, g_val, k_plus_q, band_first, norm_factor)


def solution(mesh):
    in_specs = (
        P(("groups", "ka"), None, None, None),
        P(("groups", "ka"), None, None, None),
        P(("groups", "ka"), None, None, None),
        P(("groups", "ka")),
        P("groups", None),
    )
    out_specs = P(("groups", "ka"), None, None)
    return jax.shard_map(shards, mesh=mesh, in_specs=in_specs, out_specs=out_specs, check_vma=False)
```

```python
import functools
import math

import jax
import jax.numpy as jnp
from jax import lax
from jax.experimental import pallas as pl
from jax.experimental.pallas import tpu as pltpu
from jax.sharding import PartitionSpec as P

MIB = 1024 * 1024


def permute(x, target):
    size = lax.axis_size("ka")
    pairs = [(i, target(i)) for i in range(size)]
    return lax.ppermute(x, "ka", [(i, j % size) for i, j in pairs if j is not None])


def nt_dot(a, b):
    return lax.dot_general(a, b, (((1,), (1,)), ((), ())), preferred_element_type=jnp.float32)


def iotas(rows, cols):
    shape = (rows, cols)
    return lax.broadcasted_iota(jnp.int32, shape, 0), lax.broadcasted_iota(jnp.int32, shape, 1)


def ones_where(condition):
    return jnp.where(condition, 1.0, 0.0).astype(jnp.bfloat16)


PART_C, PART_V = 8, 16


def fill_weights(first_ref, cond_ref, val_ref, we_ref, wh_ref):
    _, modes, bands_c, _ = cond_ref.shape
    bands_v = val_ref.shape[2]
    rows_e, rows_h = bands_c * PART_V, PART_C * bands_v
    row, col = iotas(rows_e, bands_c)
    take = ones_where(row // PART_V == col)
    row, col = iotas(rows_e, rows_e)
    for m in range(modes):
        half = jnp.dot(take, cond_ref[0, m], preferred_element_type=jnp.float32)
        full = nt_dot(half.astype(jnp.bfloat16), take)
        keep = (row % PART_V == col % PART_V) & (row // PART_V >= first_ref[m, 0])
        we_ref[m * rows_e:(m + 1) * rows_e, :] = jnp.where(keep, full, 0.0).astype(jnp.bfloat16)
    row, col = iotas(rows_h, bands_v)
    take = ones_where(row % bands_v == col)
    row, col = iotas(rows_h, rows_h)
    for m in range(modes):
        half = nt_dot(take, val_ref[0, m])
        full = nt_dot(half.astype(jnp.bfloat16), take)
        keep = (row // bands_v == col // bands_v) & (row % bands_v >= first_ref[m, 1])
        wh_ref[m * rows_h:(m + 1) * rows_h, :] = jnp.where(keep, full, 0.0).astype(jnp.bfloat16)


def products_kernel(first_ref, coeffs_ref, cond_ref, val_ref, out_ref, we_ref, wh_ref):
    _, bands_c, bands_v, tile = coeffs_ref.shape
    modes = cond_ref.shape[1]
    rows_e, rows_h = bands_c * PART_V, PART_C * bands_v

    @pl.when(pl.program_id(1) == 0)
    def _():
        fill_weights(first_ref, cond_ref, val_ref, we_ref, wh_ref)

    electron = []
    for h in range(bands_v // PART_V):
        x = coeffs_ref[0, :, h * PART_V:(h + 1) * PART_V, :].reshape(rows_e, tile)
        e = jnp.dot(we_ref[...], x, preferred_element_type=jnp.float32)
        electron.append(e.reshape(modes, bands_c, PART_V, tile))
    for q in range(bands_c // PART_C):
        own = slice(q * PART_C, (q + 1) * PART_C)
        y = coeffs_ref[0, own].reshape(rows_h, tile)
        hole = jnp.dot(wh_ref[...], y, preferred_element_type=jnp.float32)
        hole = hole.reshape(modes, PART_C, bands_v, tile)
        for m in range(modes):
            for h in range(bands_v // PART_V):
                cols = slice(h * PART_V, (h + 1) * PART_V)
                value = electron[h][m, own] - hole[m, :, cols]
                out_ref[0, m, 0, own, cols, :] = value.astype(jnp.bfloat16)


def products_of(coeffs, g_cond, g_val, band_first):
    k_local, bands_c, bands_v, excitons = coeffs.shape
    modes = g_cond.shape[1]
    tile = 256
    rows_e, rows_h = bands_c * PART_V, PART_C * bands_v
    depth = bands_c * bands_v
    return pl.pallas_call(
        products_kernel,
        out_shape=jax.ShapeDtypeStruct(
            (k_local, modes, excitons // tile, bands_c, bands_v, tile), jnp.bfloat16
        ),
        grid=(k_local, excitons // tile),
        in_specs=[
            pl.BlockSpec(memory_space=pltpu.SMEM),
            pl.BlockSpec((1, bands_c, bands_v, tile), lambda k, s: (k, 0, 0, s)),
            pl.BlockSpec((1, modes, bands_c, bands_c), lambda k, s: (k, 0, 0, 0)),
            pl.BlockSpec((1, modes, bands_v, bands_v), lambda k, s: (k, 0, 0, 0)),
        ],
        out_specs=pl.BlockSpec(
            (1, modes, 1, bands_c, bands_v, tile), lambda k, s: (k, 0, s, 0, 0, 0)
        ),
        scratch_shapes=[
            pltpu.VMEM((modes * rows_e, rows_e), jnp.bfloat16),
            pltpu.VMEM((modes * rows_h, rows_h), jnp.bfloat16),
        ],
        compiler_params=pltpu.CompilerParams(vmem_limit_bytes=60 * MIB),
        cost_estimate=pl.CostEstimate(
            flops=2 * k_local * modes * excitons * depth * (rows_e + rows_h),
            bytes_accessed=2 * coeffs.size * (1 + modes),
            transcendentals=0,
        ),
    )(band_first, coeffs, g_cond, g_val)


def turn_kernel(first, order_ref, coeffs_ref, *refs):
    *out_refs, held, sems = refs
    pieces, k_local, parts, rows, width = held.shape

    def copy(i, k, p):
        columns = pl.ds(pl.multiple_of(order_ref[first + i] * width, width), width)
        source = coeffs_ref.at[k, pl.ds(p * rows, rows), columns]
        return pltpu.make_async_copy(source, held.at[i, k, p], sems.at[i, k, p])

    steps = [(i, k, p) for i in range(pieces) for k in range(k_local) for p in range(parts)]
    for step in steps:
        copy(*step).start()
    for step in steps:
        i, k, p = step
        copy(*step).wait()
        out_refs[i][k, :, p * rows:(p + 1) * rows] = held[i, k, p].T


def turned_pieces(flat, order, first, pieces, width):
    k_local, depth, _ = flat.shape
    parts = 2
    return pl.pallas_call(
        functools.partial(turn_kernel, first),
        out_shape=[jax.ShapeDtypeStruct((k_local, width, depth), jnp.bfloat16)] * pieces,
        in_specs=[
            pl.BlockSpec(memory_space=pltpu.SMEM),
            pl.BlockSpec(memory_space=pl.ANY),
        ],
        out_specs=[pl.BlockSpec(memory_space=pltpu.VMEM)] * pieces,
        scratch_shapes=[
            pltpu.VMEM((pieces, k_local, parts, depth // parts, width), jnp.bfloat16),
            pltpu.SemaphoreType.DMA((pieces, k_local, parts)),
        ],
        compiler_params=pltpu.CompilerParams(vmem_limit_bytes=60 * MIB),
        cost_estimate=pl.CostEstimate(
            flops=0, bytes_accessed=4 * pieces * k_local * depth * width, transcendentals=0
        ),
    )(order, flat)


def rows_kernel(pick_ref, own_ref, next_ref, right_ref, mine_ref, other_ref, send_ref, *refs):
    own_held, next_held, held, left, own_sems, next_sems, sems = refs
    k_local, depth, width = own_held.shape
    tiles, _, _, tile = held.shape
    core, x = pick_ref[k_local + 1], pick_ref[k_local + 2]
    columns = pl.ds(pl.multiple_of(pick_ref[k_local] * width, width), width)
    near = [pick_ref[k] < k_local for k in range(k_local)]

    def copy_own(k):
        source = own_ref.at[jnp.minimum(pick_ref[k], k_local - 1), :, columns]
        return pltpu.make_async_copy(source, own_held.at[k], own_sems.at[k])

    def copy_next(k):
        source = next_ref.at[jnp.maximum(pick_ref[k] - k_local, 0)]
        return pltpu.make_async_copy(source, next_held.at[k], next_sems.at[k])

    def copy_right(t, k):
        return pltpu.make_async_copy(right_ref.at[k, t], held.at[t, k], sems.at[t, k])

    for k in range(k_local):
        copy_own(k).start()
        copy_next(k).start()
    for t in range(tiles):
        for k in range(k_local):
            copy_right(t, k).start()
    for k in range(k_local):
        copy_own(k).wait()
        copy_next(k).wait()

        @pl.when(near[k])
        def _():
            left[:, k * depth:(k + 1) * depth] = own_held[k].T

        @pl.when(jnp.logical_not(near[k]))
        def _():
            left[:, k * depth:(k + 1) * depth] = next_held[k]

    for t in range(tiles):
        for k in range(k_local):
            copy_right(t, k).wait()
        right = held[t].reshape(k_local * depth, tile)
        total = jnp.dot(left[...], right, preferred_element_type=jnp.float32)
        parts = total.reshape(2, 2, width // 4, tile)
        mine = jnp.where(x == 0, parts[0], parts[1])
        other = jnp.where(x == 0, parts[1], parts[0])
        place = slice(t * tile, (t + 1) * tile)
        mine_ref[:, place] = jnp.where(core == 0, mine[0], mine[1])
        other_ref[:, place] = jnp.where(core == 0, other[0], other[1])
        send_ref[:width // 4, place] = jnp.where(core == 0, mine[1], mine[0]).astype(jnp.bfloat16)
        send_ref[width // 4:, place] = jnp.where(core == 0, other[1], other[0]).astype(jnp.bfloat16)


def rows_of(pick, own, following, products):
    k_local, width, depth = following.shape
    _, tiles, _, tile = products.shape
    columns = tiles * tile
    return pl.pallas_call(
        rows_kernel,
        out_shape=[
            jax.ShapeDtypeStruct((width // 4, columns), jnp.float32),
            jax.ShapeDtypeStruct((width // 4, columns), jnp.float32),
            jax.ShapeDtypeStruct((width // 2, columns), jnp.bfloat16),
        ],
        in_specs=[pl.BlockSpec(memory_space=pltpu.SMEM)]
        + [pl.BlockSpec(memory_space=pl.ANY)] * 3,
        out_specs=[pl.BlockSpec(memory_space=pltpu.VMEM)] * 3,
        scratch_shapes=[
            pltpu.VMEM((k_local, depth, width), jnp.bfloat16),
            pltpu.VMEM((k_local, width, depth), jnp.bfloat16),
            pltpu.VMEM((tiles, k_local, depth, tile), jnp.bfloat16),
            pltpu.VMEM((width, k_local * depth), jnp.bfloat16),
            pltpu.SemaphoreType.DMA((k_local,)),
            pltpu.SemaphoreType.DMA((k_local,)),
            pltpu.SemaphoreType.DMA((tiles, k_local)),
        ],
        compiler_params=pltpu.CompilerParams(vmem_limit_bytes=50 * MIB),
        cost_estimate=pl.CostEstimate(
            flops=2 * k_local * depth * width * columns,
            bytes_accessed=2 * k_local * depth * columns,
            transcendentals=0,
        ),
    )(pick, own, following, products)


def on_two_by_four(coeffs, g_cond, g_val, k_plus_q, band_first, norm_factor):
    k_local, bands_c, bands_v, excitons = coeffs.shape
    modes = g_cond.shape[1]
    size = lax.axis_size("ka")
    width = excitons // 4
    me = lax.axis_index("ka")
    core, x, z = me & 1, me >> 1 & 1, me >> 2
    flat = coeffs.reshape(k_local, bands_c * bands_v, excitons)

    behind_z = (me + size - 1) % size >> 2
    order = behind_z ^ jnp.arange(3, -1, -1, dtype=jnp.int32)
    pieces = turned_pieces(flat, order, 0, 1, width)
    order, _ = lax.optimization_barrier((order, pieces))
    pieces += turned_pieces(flat, order, 1, 3, width)
    following = [permute(piece, lambda i: i - 1) for piece in pieces]
    products = products_of(coeffs, g_cond, g_val, band_first)
    products = products.reshape(k_local, -1, bands_c * bands_v, products.shape[-1])
    places = jnp.mod(k_plus_q - me * k_local, k_local * size)

    def rows(step, after):
        pick = jnp.concatenate((places, jnp.stack((z ^ (3 - step), core, x))))
        pick, _ = lax.optimization_barrier((pick, after))
        mine, other, send = rows_of(pick, flat, following[step], products)
        return mine, other, permute(send, lambda i: i ^ 1)

    def for_x(step, from_core):
        return (step[1] + from_core[width // 4:].astype(jnp.float32)).astype(jnp.bfloat16)

    def from_x(send):
        return permute(send, lambda i: i ^ 2).astype(jnp.float32)

    def own_sum(step, from_core, across):
        return step[0] + from_core[:width // 4].astype(jnp.float32) + across

    def over(value, bit):
        return permute(value, lambda i: i ^ bit).astype(jnp.float32)

    step_0 = rows(0, products)
    step_1 = rows(1, step_0[0])
    step_2 = rows(2, step_1[0])
    core_0, core_1, core_2, following[3] = lax.optimization_barrier(
        (step_0[2], step_1[2], step_2[2], following[3])
    )
    send_0, send_1 = for_x(step_0, core_0), for_x(step_1, core_1)
    across_0, across_1 = from_x(send_0), from_x(send_1)
    across_0, _ = lax.optimization_barrier((across_0, send_1))
    far = own_sum(step_0, core_0, across_0).astype(jnp.bfloat16)
    step_3 = rows(3, far)
    far = over(far, 4)
    send_2, _ = lax.optimization_barrier((for_x(step_2, core_2), step_3[0]))
    across_2 = from_x(send_2)
    pair = (own_sum(step_1, core_1, across_1) + far).astype(jnp.bfloat16)
    send_3 = for_x(step_3, step_3[2])
    across_2, _ = lax.optimization_barrier((across_2, (pair, send_3)))
    pair = over(pair, 8)
    near = over(own_sum(step_2, core_2, across_2).astype(jnp.bfloat16), 4)
    across_3 = from_x(send_3)
    total = own_sum(step_3, step_3[2], across_3) + near + pair
    return (total * norm_factor).reshape(width // 4, modes, excitons)


def on_any(coeffs, g_cond, g_val, k_plus_q, band_first, norm_factor):
    k_local, bands_c, bands_v, excitons = coeffs.shape
    modes = g_cond.shape[1]
    size = lax.axis_size("ka")
    depth = bands_c * bands_v
    flat = coeffs.reshape(k_local, depth, excitons)
    blocks = jnp.concatenate((flat, permute(flat, lambda i: i - 1)), 0)
    offsets = jnp.mod(k_plus_q - lax.axis_index("ka") * k_local, k_local * size)
    products = products_of(coeffs, g_cond, g_val, band_first)
    products = products.reshape(k_local, modes, -1, depth, products.shape[-1])
    products = jnp.moveaxis(products, 2, 3).reshape(k_local, modes, depth, excitons)
    partners = [
        lax.dynamic_index_in_dim(blocks, offsets[k], 0, keepdims=False) for k in range(k_local)
    ]
    running = jnp.einsum(
        "kds,kmdt->smt", jnp.stack(partners), products, preferred_element_type=jnp.float32
    )
    return lax.psum_scatter(running * norm_factor, "ka", scatter_dimension=0, tiled=True)


def shards(coeffs, g_cond, g_val, k_plus_q, band_first):
    k_local, bands_c, bands_v, excitons = coeffs.shape
    size = lax.axis_size("ka")
    norm_factor = 1.0 / math.sqrt(bands_c * bands_v * k_local * size)
    whole_tiles = excitons % (4 * 128) == 0
    plan = on_two_by_four if size == 16 and whole_tiles else on_any
    return plan(coeffs, g_cond, g_val, k_plus_q, band_first, norm_factor)


def solution(mesh):
    in_specs = (
        P(("groups", "ka"), None, None, None),
        P(("groups", "ka"), None, None, None),
        P(("groups", "ka"), None, None, None),
        P(("groups", "ka")),
        P("groups", None),
    )
    out_specs = P(("groups", "ka"), None, None)
    return jax.shard_map(shards, mesh=mesh, in_specs=in_specs, out_specs=out_specs, check_vma=False)
```

```python
import functools
import math

import jax
import jax.numpy as jnp
from jax import lax
from jax.experimental import pallas as pl
from jax.experimental.pallas import tpu as pltpu
from jax.sharding import PartitionSpec as P

MIB = 1024 * 1024


def permute(x, target):
    size = lax.axis_size("ka")
    pairs = [(i, target(i)) for i in range(size)]
    return lax.ppermute(x, "ka", [(i, j % size) for i, j in pairs if j is not None])


def nt_dot(a, b):
    return lax.dot_general(a, b, (((1,), (1,)), ((), ())), preferred_element_type=jnp.float32)


def iotas(rows, cols):
    shape = (rows, cols)
    return lax.broadcasted_iota(jnp.int32, shape, 0), lax.broadcasted_iota(jnp.int32, shape, 1)


def ones_where(condition):
    return jnp.where(condition, 1.0, 0.0).astype(jnp.bfloat16)


PART_C, PART_V = 8, 16


def fill_weights(first_ref, cond_ref, val_ref, we_ref, wh_ref):
    _, modes, bands_c, _ = cond_ref.shape
    bands_v = val_ref.shape[2]
    rows_e, rows_h = bands_c * PART_V, PART_C * bands_v
    row, col = iotas(rows_e, bands_c)
    take = ones_where(row // PART_V == col)
    row, col = iotas(rows_e, rows_e)
    for m in range(modes):
        half = jnp.dot(take, cond_ref[0, m], preferred_element_type=jnp.float32)
        full = nt_dot(half.astype(jnp.bfloat16), take)
        keep = (row % PART_V == col % PART_V) & (row // PART_V >= first_ref[m, 0])
        we_ref[m * rows_e:(m + 1) * rows_e, :] = jnp.where(keep, full, 0.0).astype(jnp.bfloat16)
    row, col = iotas(rows_h, bands_v)
    take = ones_where(row % bands_v == col)
    row, col = iotas(rows_h, rows_h)
    for m in range(modes):
        half = nt_dot(take, val_ref[0, m])
        full = nt_dot(half.astype(jnp.bfloat16), take)
        keep = (row // bands_v == col // bands_v) & (row % bands_v >= first_ref[m, 1])
        wh_ref[m * rows_h:(m + 1) * rows_h, :] = jnp.where(keep, full, 0.0).astype(jnp.bfloat16)


def products_kernel(first_ref, coeffs_ref, cond_ref, val_ref, out_ref, we_ref, wh_ref):
    _, bands_c, bands_v, tile = coeffs_ref.shape
    modes = cond_ref.shape[1]
    rows_e, rows_h = bands_c * PART_V, PART_C * bands_v

    @pl.when(pl.program_id(1) == 0)
    def _():
        fill_weights(first_ref, cond_ref, val_ref, we_ref, wh_ref)

    electron = []
    for h in range(bands_v // PART_V):
        x = coeffs_ref[0, :, h * PART_V:(h + 1) * PART_V, :].reshape(rows_e, tile)
        e = jnp.dot(we_ref[...], x, preferred_element_type=jnp.float32)
        electron.append(e.reshape(modes, bands_c, PART_V, tile))
    for q in range(bands_c // PART_C):
        own = slice(q * PART_C, (q + 1) * PART_C)
        y = coeffs_ref[0, own].reshape(rows_h, tile)
        hole = jnp.dot(wh_ref[...], y, preferred_element_type=jnp.float32)
        hole = hole.reshape(modes, PART_C, bands_v, tile)
        for m in range(modes):
            for h in range(bands_v // PART_V):
                cols = slice(h * PART_V, (h + 1) * PART_V)
                value = electron[h][m, own] - hole[m, :, cols]
                out_ref[0, m, own, cols, :] = value.astype(jnp.bfloat16)


def products_of(coeffs, g_cond, g_val, band_first):
    k_local, bands_c, bands_v, excitons = coeffs.shape
    modes = g_cond.shape[1]
    tile = 256
    rows_e, rows_h = bands_c * PART_V, PART_C * bands_v
    depth = bands_c * bands_v
    return pl.pallas_call(
        products_kernel,
        out_shape=jax.ShapeDtypeStruct((k_local, modes, bands_c, bands_v, excitons), jnp.bfloat16),
        grid=(k_local, excitons // tile),
        in_specs=[
            pl.BlockSpec(memory_space=pltpu.SMEM),
            pl.BlockSpec((1, bands_c, bands_v, tile), lambda k, s: (k, 0, 0, s)),
            pl.BlockSpec((1, modes, bands_c, bands_c), lambda k, s: (k, 0, 0, 0)),
            pl.BlockSpec((1, modes, bands_v, bands_v), lambda k, s: (k, 0, 0, 0)),
        ],
        out_specs=pl.BlockSpec((1, modes, bands_c, bands_v, tile), lambda k, s: (k, 0, 0, 0, s)),
        scratch_shapes=[
            pltpu.VMEM((modes * rows_e, rows_e), jnp.bfloat16),
            pltpu.VMEM((modes * rows_h, rows_h), jnp.bfloat16),
        ],
        compiler_params=pltpu.CompilerParams(vmem_limit_bytes=60 * MIB),
        cost_estimate=pl.CostEstimate(
            flops=2 * k_local * modes * excitons * depth * (rows_e + rows_h),
            bytes_accessed=2 * coeffs.size * (1 + modes),
            transcendentals=0,
        ),
    )(band_first, coeffs, g_cond, g_val)


def turn_kernel(first, order_ref, coeffs_ref, *refs):
    *out_refs, held, sems = refs
    pieces, k_local, parts, rows, width = held.shape

    def copy(i, k, p):
        columns = pl.ds(pl.multiple_of(order_ref[first + i] * width, width), width)
        source = coeffs_ref.at[k, pl.ds(p * rows, rows), columns]
        return pltpu.make_async_copy(source, held.at[i, k, p], sems.at[i, k, p])

    steps = [(i, k, p) for i in range(pieces) for k in range(k_local) for p in range(parts)]
    for step in steps:
        copy(*step).start()
    for step in steps:
        i, k, p = step
        copy(*step).wait()
        out_refs[i][k, :, p * rows:(p + 1) * rows] = held[i, k, p].T


def turned_pieces(flat, order, first, pieces, width):
    k_local, depth, _ = flat.shape
    parts = 2
    return pl.pallas_call(
        functools.partial(turn_kernel, first),
        out_shape=[jax.ShapeDtypeStruct((k_local, width, depth), jnp.bfloat16)] * pieces,
        in_specs=[
            pl.BlockSpec(memory_space=pltpu.SMEM),
            pl.BlockSpec(memory_space=pl.ANY),
        ],
        out_specs=[pl.BlockSpec(memory_space=pltpu.VMEM)] * pieces,
        scratch_shapes=[
            pltpu.VMEM((pieces, k_local, parts, depth // parts, width), jnp.bfloat16),
            pltpu.SemaphoreType.DMA((pieces, k_local, parts)),
        ],
        compiler_params=pltpu.CompilerParams(vmem_limit_bytes=60 * MIB),
        cost_estimate=pl.CostEstimate(
            flops=0, bytes_accessed=4 * pieces * k_local * depth * width, transcendentals=0
        ),
    )(order, flat)


def rows_kernel(pick_ref, own_ref, next_ref, right_ref, mine_ref, other_ref, send_ref, *refs):
    own_held, next_held, held, left, own_sems, next_sems, sems = refs
    k_local, depth, width = own_held.shape
    tiles, _, _, tile = held.shape
    per_mode = right_ref.shape[3] // tile
    core, x = pick_ref[k_local + 1], pick_ref[k_local + 2]
    columns = pl.ds(pl.multiple_of(pick_ref[k_local] * width, width), width)
    near = [pick_ref[k] < k_local for k in range(k_local)]

    def copy_own(k):
        source = own_ref.at[jnp.minimum(pick_ref[k], k_local - 1), :, columns]
        return pltpu.make_async_copy(source, own_held.at[k], own_sems.at[k])

    def copy_next(k):
        source = next_ref.at[jnp.maximum(pick_ref[k] - k_local, 0)]
        return pltpu.make_async_copy(source, next_held.at[k], next_sems.at[k])

    def copy_right(t, k):
        source = right_ref.at[k, t // per_mode, :, pl.ds(t % per_mode * tile, tile)]
        return pltpu.make_async_copy(source, held.at[t, k], sems.at[t, k])

    for k in range(k_local):
        copy_own(k).start()
        copy_next(k).start()
    ahead = 2
    for t in range(ahead):
        for k in range(k_local):
            copy_right(t, k).start()
    for k in range(k_local):
        copy_own(k).wait()
        copy_next(k).wait()

        @pl.when(near[k])
        def _():
            left[:, k * depth:(k + 1) * depth] = own_held[k].T

        @pl.when(jnp.logical_not(near[k]))
        def _():
            left[:, k * depth:(k + 1) * depth] = next_held[k]

    for t in range(tiles):
        for k in range(k_local):
            copy_right(t, k).wait()
        if t + ahead < tiles:
            for k in range(k_local):
                copy_right(t + ahead, k).start()
        right = held[t].reshape(k_local * depth, tile)
        total = jnp.dot(left[...], right, preferred_element_type=jnp.float32)
        parts = total.reshape(2, 2, width // 4, tile)
        mine = jnp.where(x == 0, parts[0], parts[1])
        other = jnp.where(x == 0, parts[1], parts[0])
        place = slice(t * tile, (t + 1) * tile)
        mine_ref[:, place] = jnp.where(core == 0, mine[0], mine[1])
        other_ref[:, place] = jnp.where(core == 0, other[0], other[1])
        send_ref[:width // 4, place] = jnp.where(core == 0, mine[1], mine[0]).astype(jnp.bfloat16)
        send_ref[width // 4:, place] = jnp.where(core == 0, other[1], other[0]).astype(jnp.bfloat16)


def rows_of(pick, own, following, products):
    k_local, width, depth = following.shape
    modes, excitons = products.shape[1], products.shape[3]
    columns, tile = modes * excitons, 512
    tiles = columns // tile
    return pl.pallas_call(
        rows_kernel,
        out_shape=[
            jax.ShapeDtypeStruct((width // 4, columns), jnp.float32),
            jax.ShapeDtypeStruct((width // 4, columns), jnp.float32),
            jax.ShapeDtypeStruct((width // 2, columns), jnp.bfloat16),
        ],
        in_specs=[pl.BlockSpec(memory_space=pltpu.SMEM)]
        + [pl.BlockSpec(memory_space=pl.ANY)] * 3,
        out_specs=[pl.BlockSpec(memory_space=pltpu.VMEM)] * 3,
        scratch_shapes=[
            pltpu.VMEM((k_local, depth, width), jnp.bfloat16),
            pltpu.VMEM((k_local, width, depth), jnp.bfloat16),
            pltpu.VMEM((tiles, k_local, depth, tile), jnp.bfloat16),
            pltpu.VMEM((width, k_local * depth), jnp.bfloat16),
            pltpu.SemaphoreType.DMA((k_local,)),
            pltpu.SemaphoreType.DMA((k_local,)),
            pltpu.SemaphoreType.DMA((tiles, k_local)),
        ],
        compiler_params=pltpu.CompilerParams(vmem_limit_bytes=50 * MIB),
        cost_estimate=pl.CostEstimate(
            flops=2 * k_local * depth * width * columns,
            bytes_accessed=2 * k_local * depth * columns,
            transcendentals=0,
        ),
    )(pick, own, following, products)


def on_two_by_four(coeffs, g_cond, g_val, k_plus_q, band_first, norm_factor):
    k_local, bands_c, bands_v, excitons = coeffs.shape
    modes = g_cond.shape[1]
    size = lax.axis_size("ka")
    width = excitons // 4
    me = lax.axis_index("ka")
    core, x, z = me & 1, me >> 1 & 1, me >> 2
    flat = coeffs.reshape(k_local, bands_c * bands_v, excitons)

    behind_z = (me + size - 1) % size >> 2
    order = behind_z ^ jnp.arange(3, -1, -1, dtype=jnp.int32)
    pieces = turned_pieces(flat, order, 0, 1, width)
    order, _ = lax.optimization_barrier((order, pieces))
    pieces += turned_pieces(flat, order, 1, 3, width)
    following = [permute(piece, lambda i: i - 1) for piece in pieces]
    products = products_of(coeffs, g_cond, g_val, band_first)
    products = products.reshape(k_local, modes, bands_c * bands_v, excitons)
    places = jnp.mod(k_plus_q - me * k_local, k_local * size)

    def rows(step, after):
        pick = jnp.concatenate((places, jnp.stack((z ^ (3 - step), core, x))))
        pick, _ = lax.optimization_barrier((pick, after))
        mine, other, send = rows_of(pick, flat, following[step], products)
        return mine, other, permute(send, lambda i: i ^ 1)

    def for_x(step, from_core):
        return (step[1] + from_core[width // 4:].astype(jnp.float32)).astype(jnp.bfloat16)

    def from_x(send):
        return permute(send, lambda i: i ^ 2).astype(jnp.float32)

    def own_sum(step, from_core, across):
        return step[0] + from_core[:width // 4].astype(jnp.float32) + across

    def over(value, bit):
        return permute(value, lambda i: i ^ bit).astype(jnp.float32)

    step_0 = rows(0, products)
    step_1 = rows(1, step_0[0])
    step_2 = rows(2, step_1[0])
    core_0, core_1, core_2, following[3] = lax.optimization_barrier(
        (step_0[2], step_1[2], step_2[2], following[3])
    )
    send_0, send_1 = for_x(step_0, core_0), for_x(step_1, core_1)
    across_0, across_1 = from_x(send_0), from_x(send_1)
    across_0, _ = lax.optimization_barrier((across_0, send_1))
    far = own_sum(step_0, core_0, across_0).astype(jnp.bfloat16)
    step_3 = rows(3, far)
    far = over(far, 4)
    send_2, _ = lax.optimization_barrier((for_x(step_2, core_2), step_3[0]))
    across_2 = from_x(send_2)
    pair = (own_sum(step_1, core_1, across_1) + far).astype(jnp.bfloat16)
    send_3 = for_x(step_3, step_3[2])
    across_2, _ = lax.optimization_barrier((across_2, (pair, send_3)))
    pair = over(pair, 8)
    near = over(own_sum(step_2, core_2, across_2).astype(jnp.bfloat16), 4)
    across_3 = from_x(send_3)
    total = own_sum(step_3, step_3[2], across_3) + near + pair
    return (total * norm_factor).reshape(width // 4, modes, excitons)


def on_any(coeffs, g_cond, g_val, k_plus_q, band_first, norm_factor):
    k_local, bands_c, bands_v, excitons = coeffs.shape
    modes = g_cond.shape[1]
    size = lax.axis_size("ka")
    depth = bands_c * bands_v
    flat = coeffs.reshape(k_local, depth, excitons)
    blocks = jnp.concatenate((flat, permute(flat, lambda i: i - 1)), 0)
    offsets = jnp.mod(k_plus_q - lax.axis_index("ka") * k_local, k_local * size)
    products = products_of(coeffs, g_cond, g_val, band_first)
    products = products.reshape(k_local, modes, depth, excitons)
    partners = [
        lax.dynamic_index_in_dim(blocks, offsets[k], 0, keepdims=False) for k in range(k_local)
    ]
    running = jnp.einsum(
        "kds,kmdt->smt", jnp.stack(partners), products, preferred_element_type=jnp.float32
    )
    return lax.psum_scatter(running * norm_factor, "ka", scatter_dimension=0, tiled=True)


def shards(coeffs, g_cond, g_val, k_plus_q, band_first):
    k_local, bands_c, bands_v, excitons = coeffs.shape
    size = lax.axis_size("ka")
    norm_factor = 1.0 / math.sqrt(bands_c * bands_v * k_local * size)
    whole_tiles = excitons % (4 * 128) == 0
    plan = on_two_by_four if size == 16 and whole_tiles else on_any
    return plan(coeffs, g_cond, g_val, k_plus_q, band_first, norm_factor)


def solution(mesh):
    in_specs = (
        P(("groups", "ka"), None, None, None),
        P(("groups", "ka"), None, None, None),
        P(("groups", "ka"), None, None, None),
        P(("groups", "ka")),
        P("groups", None),
    )
    out_specs = P(("groups", "ka"), None, None)
    return jax.shard_map(shards, mesh=mesh, in_specs=in_specs, out_specs=out_specs, check_vma=False)
```

```python
import functools
import math

import jax
import jax.numpy as jnp
from jax import lax
from jax.experimental import pallas as pl
from jax.experimental.pallas import tpu as pltpu
from jax.sharding import PartitionSpec as P

MIB = 1024 * 1024


def permute(x, target):
    size = lax.axis_size("ka")
    pairs = [(i, target(i)) for i in range(size)]
    return lax.ppermute(x, "ka", [(i, j % size) for i, j in pairs if j is not None])


def nt_dot(a, b):
    return lax.dot_general(a, b, (((1,), (1,)), ((), ())), preferred_element_type=jnp.float32)


def iotas(rows, cols):
    shape = (rows, cols)
    return lax.broadcasted_iota(jnp.int32, shape, 0), lax.broadcasted_iota(jnp.int32, shape, 1)


def ones_where(condition):
    return jnp.where(condition, 1.0, 0.0).astype(jnp.bfloat16)


PART_C, PART_V = 8, 16


def fill_weights(first_ref, cond_ref, val_ref, we_ref, wh_ref):
    _, modes, bands_c, _ = cond_ref.shape
    bands_v = val_ref.shape[2]
    rows_e, rows_h = bands_c * PART_V, PART_C * bands_v
    row, col = iotas(rows_e, bands_c)
    take = ones_where(row // PART_V == col)
    row, col = iotas(rows_e, rows_e)
    for m in range(modes):
        half = jnp.dot(take, cond_ref[0, m], preferred_element_type=jnp.float32)
        full = nt_dot(half.astype(jnp.bfloat16), take)
        keep = (row % PART_V == col % PART_V) & (row // PART_V >= first_ref[m, 0])
        we_ref[m * rows_e:(m + 1) * rows_e, :] = jnp.where(keep, full, 0.0).astype(jnp.bfloat16)
    row, col = iotas(rows_h, bands_v)
    take = ones_where(row % bands_v == col)
    row, col = iotas(rows_h, rows_h)
    for m in range(modes):
        half = nt_dot(take, val_ref[0, m])
        full = nt_dot(half.astype(jnp.bfloat16), take)
        keep = (row // bands_v == col // bands_v) & (row % bands_v >= first_ref[m, 1])
        wh_ref[m * rows_h:(m + 1) * rows_h, :] = jnp.where(keep, full, 0.0).astype(jnp.bfloat16)


def products_kernel(first_ref, coeffs_ref, cond_ref, val_ref, out_ref, we_ref, wh_ref):
    _, bands_c, bands_v, tile = coeffs_ref.shape
    modes = cond_ref.shape[1]
    rows_e, rows_h = bands_c * PART_V, PART_C * bands_v

    @pl.when(pl.program_id(1) == 0)
    def _():
        fill_weights(first_ref, cond_ref, val_ref, we_ref, wh_ref)

    electron = []
    for h in range(bands_v // PART_V):
        x = coeffs_ref[0, :, h * PART_V:(h + 1) * PART_V, :].reshape(rows_e, tile)
        e = jnp.dot(we_ref[...], x, preferred_element_type=jnp.float32)
        electron.append(e.reshape(modes, bands_c, PART_V, tile))
    for q in range(bands_c // PART_C):
        own = slice(q * PART_C, (q + 1) * PART_C)
        y = coeffs_ref[0, own].reshape(rows_h, tile)
        hole = jnp.dot(wh_ref[...], y, preferred_element_type=jnp.float32)
        hole = hole.reshape(modes, PART_C, bands_v, tile)
        for m in range(modes):
            for h in range(bands_v // PART_V):
                cols = slice(h * PART_V, (h + 1) * PART_V)
                value = electron[h][m, own] - hole[m, :, cols]
                out_ref[0, m, own, cols, :] = value.astype(jnp.bfloat16)


def products_of(coeffs, g_cond, g_val, band_first):
    k_local, bands_c, bands_v, excitons = coeffs.shape
    modes = g_cond.shape[1]
    tile = 256
    rows_e, rows_h = bands_c * PART_V, PART_C * bands_v
    depth = bands_c * bands_v
    return pl.pallas_call(
        products_kernel,
        out_shape=jax.ShapeDtypeStruct((k_local, modes, bands_c, bands_v, excitons), jnp.bfloat16),
        grid=(k_local, excitons // tile),
        in_specs=[
            pl.BlockSpec(memory_space=pltpu.SMEM),
            pl.BlockSpec((1, bands_c, bands_v, tile), lambda k, s: (k, 0, 0, s)),
            pl.BlockSpec((1, modes, bands_c, bands_c), lambda k, s: (k, 0, 0, 0)),
            pl.BlockSpec((1, modes, bands_v, bands_v), lambda k, s: (k, 0, 0, 0)),
        ],
        out_specs=pl.BlockSpec((1, modes, bands_c, bands_v, tile), lambda k, s: (k, 0, 0, 0, s)),
        scratch_shapes=[
            pltpu.VMEM((modes * rows_e, rows_e), jnp.bfloat16),
            pltpu.VMEM((modes * rows_h, rows_h), jnp.bfloat16),
        ],
        compiler_params=pltpu.CompilerParams(vmem_limit_bytes=60 * MIB),
        cost_estimate=pl.CostEstimate(
            flops=2 * k_local * modes * excitons * depth * (rows_e + rows_h),
            bytes_accessed=2 * coeffs.size * (1 + modes),
            transcendentals=0,
        ),
    )(band_first, coeffs, g_cond, g_val)


def turn_kernel(first, coeffs_ref, *refs):
    *out_refs, held, sems = refs
    pieces, k_local, parts, rows, width = held.shape
    size = lax.axis_size("ka")
    behind_z = lax.shift_right_logical(lax.rem(lax.axis_index("ka") + size - 1, size), 2)

    def copy(i, k, p):
        columns = pl.ds(pl.multiple_of((behind_z ^ (3 - first - i)) * width, width), width)
        source = coeffs_ref.at[k, pl.ds(p * rows, rows), columns]
        return pltpu.make_async_copy(source, held.at[i, k, p], sems.at[i, k, p])

    steps = [(i, k, p) for i in range(pieces) for k in range(k_local) for p in range(parts)]
    for step in steps:
        copy(*step).start()
    for step in steps:
        i, k, p = step
        copy(*step).wait()
        out_refs[i][k, :, p * rows:(p + 1) * rows] = held[i, k, p].T


def turned_pieces(flat, first, pieces, width):
    k_local, depth, _ = flat.shape
    parts = 2
    return pl.pallas_call(
        functools.partial(turn_kernel, first),
        out_shape=[jax.ShapeDtypeStruct((k_local, width, depth), jnp.bfloat16)] * pieces,
        in_specs=[pl.BlockSpec(memory_space=pl.ANY)],
        out_specs=[pl.BlockSpec(memory_space=pltpu.VMEM)] * pieces,
        scratch_shapes=[
            pltpu.VMEM((pieces, k_local, parts, depth // parts, width), jnp.bfloat16),
            pltpu.SemaphoreType.DMA((pieces, k_local, parts)),
        ],
        compiler_params=pltpu.CompilerParams(vmem_limit_bytes=60 * MIB),
        cost_estimate=pl.CostEstimate(
            flops=0, bytes_accessed=4 * pieces * k_local * depth * width, transcendentals=0
        ),
    )(flat)


def rows_kernel(pick_ref, own_ref, next_ref, right_ref, mine_ref, other_ref, send_ref, *refs):
    own_held, next_held, held, left, own_sems, next_sems, sems = refs
    k_local, depth, width = own_held.shape
    tiles, _, _, tile = held.shape
    per_mode = right_ref.shape[3] // tile
    core, x = pick_ref[k_local + 1], pick_ref[k_local + 2]
    columns = pl.ds(pl.multiple_of(pick_ref[k_local] * width, width), width)
    near = [pick_ref[k] < k_local for k in range(k_local)]

    def copy_own(k):
        source = own_ref.at[jnp.minimum(pick_ref[k], k_local - 1), :, columns]
        return pltpu.make_async_copy(source, own_held.at[k], own_sems.at[k])

    def copy_next(k):
        source = next_ref.at[jnp.maximum(pick_ref[k] - k_local, 0)]
        return pltpu.make_async_copy(source, next_held.at[k], next_sems.at[k])

    def copy_right(t, k):
        source = right_ref.at[k, t // per_mode, :, pl.ds(t % per_mode * tile, tile)]
        return pltpu.make_async_copy(source, held.at[t, k], sems.at[t, k])

    for k in range(k_local):
        copy_own(k).start()
        copy_next(k).start()
    for t in range(tiles):
        for k in range(k_local):
            copy_right(t, k).start()
    for k in range(k_local):
        copy_own(k).wait()
        copy_next(k).wait()

        @pl.when(near[k])
        def _():
            left[:, k * depth:(k + 1) * depth] = own_held[k].T

        @pl.when(jnp.logical_not(near[k]))
        def _():
            left[:, k * depth:(k + 1) * depth] = next_held[k]

    for t in range(tiles):
        for k in range(k_local):
            copy_right(t, k).wait()
        right = held[t].reshape(k_local * depth, tile)
        total = jnp.dot(left[...], right, preferred_element_type=jnp.float32)
        parts = total.reshape(2, 2, width // 4, tile)
        mine = jnp.where(x == 0, parts[0], parts[1])
        other = jnp.where(x == 0, parts[1], parts[0])
        place = slice(t * tile, (t + 1) * tile)
        mine_ref[:, place] = jnp.where(core == 0, mine[0], mine[1])
        other_ref[:, place] = jnp.where(core == 0, other[0], other[1])
        send_ref[:width // 4, place] = jnp.where(core == 0, mine[1], mine[0]).astype(jnp.bfloat16)
        send_ref[width // 4:, place] = jnp.where(core == 0, other[1], other[0]).astype(jnp.bfloat16)


def rows_of(pick, own, following, products):
    k_local, width, depth = following.shape
    modes, excitons = products.shape[1], products.shape[3]
    columns, tile = modes * excitons, 512
    tiles = columns // tile
    return pl.pallas_call(
        rows_kernel,
        out_shape=[
            jax.ShapeDtypeStruct((width // 4, columns), jnp.float32),
            jax.ShapeDtypeStruct((width // 4, columns), jnp.float32),
            jax.ShapeDtypeStruct((width // 2, columns), jnp.bfloat16),
        ],
        in_specs=[pl.BlockSpec(memory_space=pltpu.SMEM)]
        + [pl.BlockSpec(memory_space=pl.ANY)] * 3,
        out_specs=[pl.BlockSpec(memory_space=pltpu.VMEM)] * 3,
        scratch_shapes=[
            pltpu.VMEM((k_local, depth, width), jnp.bfloat16),
            pltpu.VMEM((k_local, width, depth), jnp.bfloat16),
            pltpu.VMEM((tiles, k_local, depth, tile), jnp.bfloat16),
            pltpu.VMEM((width, k_local * depth), jnp.bfloat16),
            pltpu.SemaphoreType.DMA((k_local,)),
            pltpu.SemaphoreType.DMA((k_local,)),
            pltpu.SemaphoreType.DMA((tiles, k_local)),
        ],
        compiler_params=pltpu.CompilerParams(vmem_limit_bytes=50 * MIB),
        cost_estimate=pl.CostEstimate(
            flops=2 * k_local * depth * width * columns,
            bytes_accessed=2 * k_local * depth * columns,
            transcendentals=0,
        ),
    )(pick, own, following, products)


def close_kernel(factor, mine_ref, core_ref, across_ref, near_ref, pair_ref, out_ref):
    _, modes, excitons = out_ref.shape
    total = mine_ref[...]
    for ref in (core_ref, across_ref, near_ref, pair_ref):
        total = total + ref[...].astype(jnp.float32)
    total = total * factor
    for m in range(modes):
        out_ref[:, m, :] = total[:, m * excitons:(m + 1) * excitons]


def closed(mine, from_core, across, near, pair, modes, factor):
    rows, columns = mine.shape
    step = 16
    part = pl.BlockSpec((step, columns), lambda i: (i, 0))
    return pl.pallas_call(
        functools.partial(close_kernel, factor),
        out_shape=jax.ShapeDtypeStruct((rows, modes, columns // modes), jnp.float32),
        grid=(rows // step,),
        in_specs=[part] * 5,
        out_specs=pl.BlockSpec((step, modes, columns // modes), lambda i: (i, 0, 0)),
        cost_estimate=pl.CostEstimate(
            flops=5 * mine.size, bytes_accessed=16 * mine.size, transcendentals=0
        ),
    )(mine, from_core, across, near, pair)


def on_two_by_four(coeffs, g_cond, g_val, k_plus_q, band_first, norm_factor):
    k_local, bands_c, bands_v, excitons = coeffs.shape
    modes = g_cond.shape[1]
    size = lax.axis_size("ka")
    width = excitons // 4
    me = lax.axis_index("ka")
    core, x, z = me & 1, me >> 1 & 1, me >> 2
    flat = coeffs.reshape(k_local, bands_c * bands_v, excitons)

    pieces = turned_pieces(flat, 0, 1, width)
    rest, _ = lax.optimization_barrier((flat, pieces))
    pieces += turned_pieces(rest, 1, 3, width)
    following = [permute(piece, lambda i: i - 1) for piece in pieces]
    products = products_of(coeffs, g_cond, g_val, band_first)
    products = products.reshape(k_local, modes, bands_c * bands_v, excitons)
    places = jnp.mod(k_plus_q - me * k_local, k_local * size)

    def rows(step, after):
        pick = jnp.concatenate((places, jnp.stack((z ^ (3 - step), core, x))))
        pick, _ = lax.optimization_barrier((pick, after))
        mine, other, send = rows_of(pick, flat, following[step], products)
        return mine, other, permute(send, lambda i: i ^ 1)

    def for_x(step, from_core):
        return (step[1] + from_core[width // 4:].astype(jnp.float32)).astype(jnp.bfloat16)

    def from_x(send):
        return permute(send, lambda i: i ^ 2)

    def own_sum(mine, from_core, across):
        return mine + from_core[:width // 4].astype(jnp.float32) + across.astype(jnp.float32)

    def over(value, bit):
        return permute(value.astype(jnp.bfloat16), lambda i: i ^ bit)

    step_0 = rows(0, products)
    step_1 = rows(1, step_0[0])
    step_2 = rows(2, step_1[0])
    core_0, core_1, core_2, following[3] = lax.optimization_barrier(
        (step_0[2], step_1[2], step_2[2], following[3])
    )
    send_0, send_1, send_2 = for_x(step_0, core_0), for_x(step_1, core_1), for_x(step_2, core_2)
    across_0, across_1, across_2 = from_x(send_0), from_x(send_1), from_x(send_2)
    mine_3, other_3, core_3 = rows(3, (send_0, send_1, send_2))
    far = own_sum(step_0[0], core_0, across_0)
    far = over(far, 4)
    send_3 = for_x((mine_3, other_3), core_3)
    across_3 = from_x(send_3)
    pair = own_sum(step_1[0], core_1, across_1) + far.astype(jnp.float32)
    mine_2, _ = lax.optimization_barrier((step_2[0], pair))
    pair = over(pair, 8)
    near = over(own_sum(mine_2, core_2, across_2), 4)
    return closed(mine_3, core_3, across_3, near, pair, modes, norm_factor)


def on_any(coeffs, g_cond, g_val, k_plus_q, band_first, norm_factor):
    k_local, bands_c, bands_v, excitons = coeffs.shape
    modes = g_cond.shape[1]
    size = lax.axis_size("ka")
    depth = bands_c * bands_v
    flat = coeffs.reshape(k_local, depth, excitons)
    blocks = jnp.concatenate((flat, permute(flat, lambda i: i - 1)), 0)
    offsets = jnp.mod(k_plus_q - lax.axis_index("ka") * k_local, k_local * size)
    products = products_of(coeffs, g_cond, g_val, band_first)
    products = products.reshape(k_local, modes, depth, excitons)
    partners = [
        lax.dynamic_index_in_dim(blocks, offsets[k], 0, keepdims=False) for k in range(k_local)
    ]
    running = jnp.einsum(
        "kds,kmdt->smt", jnp.stack(partners), products, preferred_element_type=jnp.float32
    )
    return lax.psum_scatter(running * norm_factor, "ka", scatter_dimension=0, tiled=True)


def shards(coeffs, g_cond, g_val, k_plus_q, band_first):
    k_local, bands_c, bands_v, excitons = coeffs.shape
    size = lax.axis_size("ka")
    norm_factor = 1.0 / math.sqrt(bands_c * bands_v * k_local * size)
    whole_tiles = excitons % (4 * 128) == 0
    plan = on_two_by_four if size == 16 and whole_tiles else on_any
    return plan(coeffs, g_cond, g_val, k_plus_q, band_first, norm_factor)


def solution(mesh):
    in_specs = (
        P(("groups", "ka"), None, None, None),
        P(("groups", "ka"), None, None, None),
        P(("groups", "ka"), None, None, None),
        P(("groups", "ka")),
        P("groups", None),
    )
    out_specs = P(("groups", "ka"), None, None)
    return jax.shard_map(shards, mesh=mesh, in_specs=in_specs, out_specs=out_specs, check_vma=False)
```

```python
import functools
import math

import jax
import jax.numpy as jnp
from jax import lax
from jax.experimental import pallas as pl
from jax.experimental.pallas import tpu as pltpu
from jax.sharding import PartitionSpec as P

MIB = 1024 * 1024


def permute(x, target):
    size = lax.axis_size("ka")
    pairs = [(i, target(i)) for i in range(size)]
    return lax.ppermute(x, "ka", [(i, j % size) for i, j in pairs if j is not None])


def nt_dot(a, b):
    return lax.dot_general(a, b, (((1,), (1,)), ((), ())), preferred_element_type=jnp.float32)


def iotas(rows, cols):
    shape = (rows, cols)
    return lax.broadcasted_iota(jnp.int32, shape, 0), lax.broadcasted_iota(jnp.int32, shape, 1)


def ones_where(condition):
    return jnp.where(condition, 1.0, 0.0).astype(jnp.bfloat16)


PART_C, PART_V = 8, 16


def fill_weights(first_ref, cond_ref, val_ref, we_ref, wh_ref):
    _, modes, bands_c, _ = cond_ref.shape
    bands_v = val_ref.shape[2]
    rows_e, rows_h = bands_c * PART_V, PART_C * bands_v
    row, col = iotas(rows_e, bands_c)
    take = ones_where(row // PART_V == col)
    row, col = iotas(rows_e, rows_e)
    for m in range(modes):
        half = jnp.dot(take, cond_ref[0, m], preferred_element_type=jnp.float32)
        full = nt_dot(half.astype(jnp.bfloat16), take)
        keep = (row % PART_V == col % PART_V) & (row // PART_V >= first_ref[m, 0])
        we_ref[m * rows_e:(m + 1) * rows_e, :] = jnp.where(keep, full, 0.0).astype(jnp.bfloat16)
    row, col = iotas(rows_h, bands_v)
    take = ones_where(row % bands_v == col)
    row, col = iotas(rows_h, rows_h)
    for m in range(modes):
        half = nt_dot(take, val_ref[0, m])
        full = nt_dot(half.astype(jnp.bfloat16), take)
        keep = (row // bands_v == col // bands_v) & (row % bands_v >= first_ref[m, 1])
        wh_ref[m * rows_h:(m + 1) * rows_h, :] = jnp.where(keep, full, 0.0).astype(jnp.bfloat16)


def products_kernel(first_ref, coeffs_ref, cond_ref, val_ref, out_ref, we_ref, wh_ref):
    _, bands_c, bands_v, tile = coeffs_ref.shape
    modes = cond_ref.shape[1]
    rows_e, rows_h = bands_c * PART_V, PART_C * bands_v

    @pl.when(pl.program_id(1) == 0)
    def _():
        fill_weights(first_ref, cond_ref, val_ref, we_ref, wh_ref)

    electron = []
    for h in range(bands_v // PART_V):
        x = coeffs_ref[0, :, h * PART_V:(h + 1) * PART_V, :].reshape(rows_e, tile)
        e = jnp.dot(we_ref[...], x, preferred_element_type=jnp.float32)
        electron.append(e.reshape(modes, bands_c, PART_V, tile))
    for q in range(bands_c // PART_C):
        own = slice(q * PART_C, (q + 1) * PART_C)
        y = coeffs_ref[0, own].reshape(rows_h, tile)
        hole = jnp.dot(wh_ref[...], y, preferred_element_type=jnp.float32)
        hole = hole.reshape(modes, PART_C, bands_v, tile)
        for m in range(modes):
            for h in range(bands_v // PART_V):
                cols = slice(h * PART_V, (h + 1) * PART_V)
                value = electron[h][m, own] - hole[m, :, cols]
                out_ref[0, m, own, cols, :] = value.astype(jnp.bfloat16)


def products_of(coeffs, g_cond, g_val, band_first):
    k_local, bands_c, bands_v, excitons = coeffs.shape
    modes = g_cond.shape[1]
    tile = 256
    rows_e, rows_h = bands_c * PART_V, PART_C * bands_v
    depth = bands_c * bands_v
    return pl.pallas_call(
        products_kernel,
        out_shape=jax.ShapeDtypeStruct((k_local, modes, bands_c, bands_v, excitons), jnp.bfloat16),
        grid=(k_local, excitons // tile),
        in_specs=[
            pl.BlockSpec(memory_space=pltpu.SMEM),
            pl.BlockSpec((1, bands_c, bands_v, tile), lambda k, s: (k, 0, 0, s)),
            pl.BlockSpec((1, modes, bands_c, bands_c), lambda k, s: (k, 0, 0, 0)),
            pl.BlockSpec((1, modes, bands_v, bands_v), lambda k, s: (k, 0, 0, 0)),
        ],
        out_specs=pl.BlockSpec((1, modes, bands_c, bands_v, tile), lambda k, s: (k, 0, 0, 0, s)),
        scratch_shapes=[
            pltpu.VMEM((modes * rows_e, rows_e), jnp.bfloat16),
            pltpu.VMEM((modes * rows_h, rows_h), jnp.bfloat16),
        ],
        compiler_params=pltpu.CompilerParams(vmem_limit_bytes=60 * MIB),
        cost_estimate=pl.CostEstimate(
            flops=2 * k_local * modes * excitons * depth * (rows_e + rows_h),
            bytes_accessed=2 * coeffs.size * (1 + modes),
            transcendentals=0,
        ),
    )(band_first, coeffs, g_cond, g_val)


def turn_kernel(first, coeffs_ref, *refs):
    *out_refs, held, sems = refs
    pieces, k_local, parts, rows, width = held.shape
    size = lax.axis_size("ka")
    behind_z = lax.shift_right_logical(lax.rem(lax.axis_index("ka") + size - 1, size), 2)

    def copy(i, k, p):
        columns = pl.ds(pl.multiple_of((behind_z ^ (3 - first - i)) * width, width), width)
        source = coeffs_ref.at[k, pl.ds(p * rows, rows), columns]
        return pltpu.make_async_copy(source, held.at[i, k, p], sems.at[i, k, p])

    steps = [(i, k, p) for i in range(pieces) for k in range(k_local) for p in range(parts)]
    for step in steps:
        copy(*step).start()
    for step in steps:
        i, k, p = step
        copy(*step).wait()
        out_refs[i][k, :, p * rows:(p + 1) * rows] = held[i, k, p].T


def turned_pieces(flat, first, pieces, width):
    k_local, depth, _ = flat.shape
    parts = 2
    return pl.pallas_call(
        functools.partial(turn_kernel, first),
        out_shape=[jax.ShapeDtypeStruct((k_local, width, depth), jnp.bfloat16)] * pieces,
        in_specs=[pl.BlockSpec(memory_space=pl.ANY)],
        out_specs=[pl.BlockSpec(memory_space=pltpu.VMEM)] * pieces,
        scratch_shapes=[
            pltpu.VMEM((pieces, k_local, parts, depth // parts, width), jnp.bfloat16),
            pltpu.SemaphoreType.DMA((pieces, k_local, parts)),
        ],
        compiler_params=pltpu.CompilerParams(vmem_limit_bytes=60 * MIB),
        cost_estimate=pl.CostEstimate(
            flops=0, bytes_accessed=4 * pieces * k_local * depth * width, transcendentals=0
        ),
    )(flat)


def rows_kernel(pick_ref, own_ref, next_ref, right_ref, mine_ref, other_ref, send_ref, *refs):
    own_held, next_held, held, left, own_sems, next_sems, sems = refs
    k_local, depth, width = own_held.shape
    tiles, _, _, tile = held.shape
    per_mode = right_ref.shape[3] // tile
    core, x = pick_ref[k_local + 1], pick_ref[k_local + 2]
    columns = pl.ds(pl.multiple_of(pick_ref[k_local] * width, width), width)
    near = [pick_ref[k] < k_local for k in range(k_local)]

    def copy_own(k):
        source = own_ref.at[jnp.minimum(pick_ref[k], k_local - 1), :, columns]
        return pltpu.make_async_copy(source, own_held.at[k], own_sems.at[k])

    def copy_next(k):
        source = next_ref.at[jnp.maximum(pick_ref[k] - k_local, 0)]
        return pltpu.make_async_copy(source, next_held.at[k], next_sems.at[k])

    def copy_right(t, k):
        source = right_ref.at[k, t // per_mode, :, pl.ds(t % per_mode * tile, tile)]
        return pltpu.make_async_copy(source, held.at[t, k], sems.at[t, k])

    for k in range(k_local):
        copy_own(k).start()
        copy_next(k).start()
    for t in range(tiles):
        for k in range(k_local):
            copy_right(t, k).start()
    for k in range(k_local):
        copy_own(k).wait()
        copy_next(k).wait()

        @pl.when(near[k])
        def _():
            left[:, k * depth:(k + 1) * depth] = own_held[k].T

        @pl.when(jnp.logical_not(near[k]))
        def _():
            left[:, k * depth:(k + 1) * depth] = next_held[k]

    for t in range(tiles):
        for k in range(k_local):
            copy_right(t, k).wait()
        right = held[t].reshape(k_local * depth, tile)
        total = jnp.dot(left[...], right, preferred_element_type=jnp.float32)
        parts = total.reshape(2, 2, width // 4, tile)
        mine = jnp.where(x == 0, parts[0], parts[1])
        other = jnp.where(x == 0, parts[1], parts[0])
        place = slice(t * tile, (t + 1) * tile)
        mine_ref[:, place] = jnp.where(core == 0, mine[0], mine[1])
        other_ref[:, place] = jnp.where(core == 0, other[0], other[1])
        send_ref[:width // 4, place] = jnp.where(core == 0, mine[1], mine[0]).astype(jnp.bfloat16)
        send_ref[width // 4:, place] = jnp.where(core == 0, other[1], other[0]).astype(jnp.bfloat16)


def rows_of(pick, own, following, products):
    k_local, width, depth = following.shape
    modes, excitons = products.shape[1], products.shape[3]
    columns, tile = modes * excitons, 512
    tiles = columns // tile
    return pl.pallas_call(
        rows_kernel,
        out_shape=[
            jax.ShapeDtypeStruct((width // 4, columns), jnp.float32),
            jax.ShapeDtypeStruct((width // 4, columns), jnp.float32),
            jax.ShapeDtypeStruct((width // 2, columns), jnp.bfloat16),
        ],
        in_specs=[pl.BlockSpec(memory_space=pltpu.SMEM)]
        + [pl.BlockSpec(memory_space=pl.ANY)] * 3,
        out_specs=[pl.BlockSpec(memory_space=pltpu.VMEM)] * 3,
        scratch_shapes=[
            pltpu.VMEM((k_local, depth, width), jnp.bfloat16),
            pltpu.VMEM((k_local, width, depth), jnp.bfloat16),
            pltpu.VMEM((tiles, k_local, depth, tile), jnp.bfloat16),
            pltpu.VMEM((width, k_local * depth), jnp.bfloat16),
            pltpu.SemaphoreType.DMA((k_local,)),
            pltpu.SemaphoreType.DMA((k_local,)),
            pltpu.SemaphoreType.DMA((tiles, k_local)),
        ],
        compiler_params=pltpu.CompilerParams(vmem_limit_bytes=50 * MIB),
        cost_estimate=pl.CostEstimate(
            flops=2 * k_local * depth * width * columns,
            bytes_accessed=2 * k_local * depth * columns,
            transcendentals=0,
        ),
    )(pick, own, following, products)


def on_two_by_four(coeffs, g_cond, g_val, k_plus_q, band_first, norm_factor):
    k_local, bands_c, bands_v, excitons = coeffs.shape
    modes = g_cond.shape[1]
    size = lax.axis_size("ka")
    width = excitons // 4
    me = lax.axis_index("ka")
    core, x, z = me & 1, me >> 1 & 1, me >> 2
    flat = coeffs.reshape(k_local, bands_c * bands_v, excitons)

    pieces = turned_pieces(flat, 0, 1, width)
    rest, _ = lax.optimization_barrier((flat, pieces))
    pieces += turned_pieces(rest, 1, 3, width)
    following = [permute(piece, lambda i: i - 1) for piece in pieces]
    products = products_of(coeffs, g_cond, g_val, band_first)
    products = products.reshape(k_local, modes, bands_c * bands_v, excitons)
    places = jnp.mod(k_plus_q - me * k_local, k_local * size)

    def rows(step, after):
        pick = jnp.concatenate((places, jnp.stack((z ^ (3 - step), core, x))))
        pick, _ = lax.optimization_barrier((pick, after))
        mine, other, send = rows_of(pick, flat, following[step], products)
        return mine, other, permute(send, lambda i: i ^ 1)

    def for_x(step, from_core):
        return (step[1] + from_core[width // 4:].astype(jnp.float32)).astype(jnp.bfloat16)

    def from_x(send):
        return permute(send, lambda i: i ^ 2)

    def own_sum(mine, from_core, across):
        return mine + from_core[:width // 4].astype(jnp.float32) + across.astype(jnp.float32)

    def over(value, bit):
        return permute(value.astype(jnp.bfloat16), lambda i: i ^ bit)

    step_0 = rows(0, products)
    step_1 = rows(1, step_0[0])
    step_2 = rows(2, step_1[0])
    core_0, core_1, core_2, following[3] = lax.optimization_barrier(
        (step_0[2], step_1[2], step_2[2], following[3])
    )
    send_0, send_1, send_2 = for_x(step_0, core_0), for_x(step_1, core_1), for_x(step_2, core_2)
    across_0, across_1, across_2 = from_x(send_0), from_x(send_1), from_x(send_2)
    mine_3, other_3, core_3 = rows(3, (send_0, send_1, send_2))
    mine_0, _ = lax.optimization_barrier((step_0[0], mine_3))
    far = own_sum(mine_0, core_0, across_0)
    far = over(far, 4)
    send_3 = for_x((mine_3, other_3), core_3)
    across_3 = from_x(send_3)
    pair = own_sum(step_1[0], core_1, across_1) + far.astype(jnp.float32)
    mine_2, _ = lax.optimization_barrier((step_2[0], pair))
    pair = over(pair, 8)
    near = over(own_sum(mine_2, core_2, across_2), 4)
    total = own_sum(mine_3, core_3, across_3) + near.astype(jnp.float32) + pair.astype(jnp.float32)
    return (total * norm_factor).reshape(width // 4, modes, excitons)


def on_any(coeffs, g_cond, g_val, k_plus_q, band_first, norm_factor):
    k_local, bands_c, bands_v, excitons = coeffs.shape
    modes = g_cond.shape[1]
    size = lax.axis_size("ka")
    depth = bands_c * bands_v
    flat = coeffs.reshape(k_local, depth, excitons)
    blocks = jnp.concatenate((flat, permute(flat, lambda i: i - 1)), 0)
    offsets = jnp.mod(k_plus_q - lax.axis_index("ka") * k_local, k_local * size)
    products = products_of(coeffs, g_cond, g_val, band_first)
    products = products.reshape(k_local, modes, depth, excitons)
    partners = [
        lax.dynamic_index_in_dim(blocks, offsets[k], 0, keepdims=False) for k in range(k_local)
    ]
    running = jnp.einsum(
        "kds,kmdt->smt", jnp.stack(partners), products, preferred_element_type=jnp.float32
    )
    return lax.psum_scatter(running * norm_factor, "ka", scatter_dimension=0, tiled=True)


def shards(coeffs, g_cond, g_val, k_plus_q, band_first):
    k_local, bands_c, bands_v, excitons = coeffs.shape
    size = lax.axis_size("ka")
    norm_factor = 1.0 / math.sqrt(bands_c * bands_v * k_local * size)
    whole_tiles = excitons % (4 * 128) == 0
    plan = on_two_by_four if size == 16 and whole_tiles else on_any
    return plan(coeffs, g_cond, g_val, k_plus_q, band_first, norm_factor)


def solution(mesh):
    in_specs = (
        P(("groups", "ka"), None, None, None),
        P(("groups", "ka"), None, None, None),
        P(("groups", "ka"), None, None, None),
        P(("groups", "ka")),
        P("groups", None),
    )
    out_specs = P(("groups", "ka"), None, None)
    return jax.shard_map(shards, mesh=mesh, in_specs=in_specs, out_specs=out_specs, check_vma=False)
```

```python
import functools
import math

import jax
import jax.numpy as jnp
from jax import lax
from jax.experimental import pallas as pl
from jax.experimental.pallas import tpu as pltpu
from jax.sharding import PartitionSpec as P

MIB = 1024 * 1024


def permute(x, target):
    size = lax.axis_size("ka")
    pairs = [(i, target(i)) for i in range(size)]
    return lax.ppermute(x, "ka", [(i, j % size) for i, j in pairs if j is not None])


def nt_dot(a, b):
    return lax.dot_general(a, b, (((1,), (1,)), ((), ())), preferred_element_type=jnp.float32)


def iotas(rows, cols):
    shape = (rows, cols)
    return lax.broadcasted_iota(jnp.int32, shape, 0), lax.broadcasted_iota(jnp.int32, shape, 1)


def ones_where(condition):
    return jnp.where(condition, 1.0, 0.0).astype(jnp.bfloat16)


PART_C, PART_V = 8, 16


def fill_weights(first_ref, cond_ref, val_ref, we_ref, wh_ref):
    _, modes, bands_c, _ = cond_ref.shape
    bands_v = val_ref.shape[2]
    rows_e, rows_h = bands_c * PART_V, PART_C * bands_v
    row, col = iotas(rows_e, bands_c)
    take = ones_where(row // PART_V == col)
    row, col = iotas(rows_e, rows_e)
    for m in range(modes):
        half = jnp.dot(take, cond_ref[0, m], preferred_element_type=jnp.float32)
        full = nt_dot(half.astype(jnp.bfloat16), take)
        keep = (row % PART_V == col % PART_V) & (row // PART_V >= first_ref[m, 0])
        we_ref[m * rows_e:(m + 1) * rows_e, :] = jnp.where(keep, full, 0.0).astype(jnp.bfloat16)
    row, col = iotas(rows_h, bands_v)
    take = ones_where(row % bands_v == col)
    row, col = iotas(rows_h, rows_h)
    for m in range(modes):
        half = nt_dot(take, val_ref[0, m])
        full = nt_dot(half.astype(jnp.bfloat16), take)
        keep = (row // bands_v == col // bands_v) & (row % bands_v >= first_ref[m, 1])
        wh_ref[m * rows_h:(m + 1) * rows_h, :] = jnp.where(keep, full, 0.0).astype(jnp.bfloat16)


def products_kernel(first_ref, coeffs_ref, cond_ref, val_ref, out_ref, we_ref, wh_ref):
    _, bands_c, bands_v, tile = coeffs_ref.shape
    modes = cond_ref.shape[1]
    rows_e, rows_h = bands_c * PART_V, PART_C * bands_v

    @pl.when(pl.program_id(1) == 0)
    def _():
        fill_weights(first_ref, cond_ref, val_ref, we_ref, wh_ref)

    electron = []
    for h in range(bands_v // PART_V):
        x = coeffs_ref[0, :, h * PART_V:(h + 1) * PART_V, :].reshape(rows_e, tile)
        e = jnp.dot(we_ref[...], x, preferred_element_type=jnp.float32)
        electron.append(e.reshape(modes, bands_c, PART_V, tile))
    for q in range(bands_c // PART_C):
        own = slice(q * PART_C, (q + 1) * PART_C)
        y = coeffs_ref[0, own].reshape(rows_h, tile)
        hole = jnp.dot(wh_ref[...], y, preferred_element_type=jnp.float32)
        hole = hole.reshape(modes, PART_C, bands_v, tile)
        for m in range(modes):
            for h in range(bands_v // PART_V):
                cols = slice(h * PART_V, (h + 1) * PART_V)
                value = electron[h][m, own] - hole[m, :, cols]
                out_ref[0, m, own, cols, :] = value.astype(jnp.bfloat16)


def products_of(coeffs, g_cond, g_val, band_first):
    k_local, bands_c, bands_v, excitons = coeffs.shape
    modes = g_cond.shape[1]
    tile = 256
    rows_e, rows_h = bands_c * PART_V, PART_C * bands_v
    depth = bands_c * bands_v
    return pl.pallas_call(
        products_kernel,
        out_shape=jax.ShapeDtypeStruct((k_local, modes, bands_c, bands_v, excitons), jnp.bfloat16),
        grid=(k_local, excitons // tile),
        in_specs=[
            pl.BlockSpec(memory_space=pltpu.SMEM),
            pl.BlockSpec((1, bands_c, bands_v, tile), lambda k, s: (k, 0, 0, s)),
            pl.BlockSpec((1, modes, bands_c, bands_c), lambda k, s: (k, 0, 0, 0)),
            pl.BlockSpec((1, modes, bands_v, bands_v), lambda k, s: (k, 0, 0, 0)),
        ],
        out_specs=pl.BlockSpec((1, modes, bands_c, bands_v, tile), lambda k, s: (k, 0, 0, 0, s)),
        scratch_shapes=[
            pltpu.VMEM((modes * rows_e, rows_e), jnp.bfloat16),
            pltpu.VMEM((modes * rows_h, rows_h), jnp.bfloat16),
        ],
        compiler_params=pltpu.CompilerParams(vmem_limit_bytes=60 * MIB),
        cost_estimate=pl.CostEstimate(
            flops=2 * k_local * modes * excitons * depth * (rows_e + rows_h),
            bytes_accessed=2 * coeffs.size * (1 + modes),
            transcendentals=0,
        ),
    )(band_first, coeffs, g_cond, g_val)


def turn_kernel(first, coeffs_ref, *refs):
    *out_refs, held, sems = refs
    pieces, k_local, parts, rows, width = held.shape
    size = lax.axis_size("ka")
    behind_z = lax.shift_right_logical(lax.rem(lax.axis_index("ka") + size - 1, size), 2)

    def copy(i, k, p):
        columns = pl.ds(pl.multiple_of((behind_z ^ (3 - first - i)) * width, width), width)
        source = coeffs_ref.at[k, pl.ds(p * rows, rows), columns]
        return pltpu.make_async_copy(source, held.at[i, k, p], sems.at[i, k, p])

    steps = [(i, k, p) for i in range(pieces) for k in range(k_local) for p in range(parts)]
    for step in steps:
        copy(*step).start()
    for step in steps:
        i, k, p = step
        copy(*step).wait()
        out_refs[i][k, :, p * rows:(p + 1) * rows] = held[i, k, p].T


def turned_pieces(flat, first, pieces, width):
    k_local, depth, _ = flat.shape
    parts = 2
    return pl.pallas_call(
        functools.partial(turn_kernel, first),
        out_shape=[jax.ShapeDtypeStruct((k_local, width, depth), jnp.bfloat16)] * pieces,
        in_specs=[pl.BlockSpec(memory_space=pl.ANY)],
        out_specs=[pl.BlockSpec(memory_space=pltpu.VMEM)] * pieces,
        scratch_shapes=[
            pltpu.VMEM((pieces, k_local, parts, depth // parts, width), jnp.bfloat16),
            pltpu.SemaphoreType.DMA((pieces, k_local, parts)),
        ],
        compiler_params=pltpu.CompilerParams(vmem_limit_bytes=60 * MIB),
        cost_estimate=pl.CostEstimate(
            flops=0, bytes_accessed=4 * pieces * k_local * depth * width, transcendentals=0
        ),
    )(flat)


def rows_kernel(pick_ref, own_ref, next_ref, right_ref, mine_ref, other_ref, send_ref, *refs):
    own_held, next_held, held, left, own_sems, next_sems, sems = refs
    k_local, depth, width = own_held.shape
    tiles, _, _, tile = held.shape
    per_mode = right_ref.shape[3] // tile
    core, x = pick_ref[k_local + 1], pick_ref[k_local + 2]
    columns = pl.ds(pl.multiple_of(pick_ref[k_local] * width, width), width)
    near = [pick_ref[k] < k_local for k in range(k_local)]

    def copy_own(k):
        source = own_ref.at[jnp.minimum(pick_ref[k], k_local - 1), :, columns]
        return pltpu.make_async_copy(source, own_held.at[k], own_sems.at[k])

    def copy_next(k):
        source = next_ref.at[jnp.maximum(pick_ref[k] - k_local, 0)]
        return pltpu.make_async_copy(source, next_held.at[k], next_sems.at[k])

    def copy_right(t, k):
        source = right_ref.at[k, t // per_mode, :, pl.ds(t % per_mode * tile, tile)]
        return pltpu.make_async_copy(source, held.at[t, k], sems.at[t, k])

    for k in range(k_local):
        copy_own(k).start()
        copy_next(k).start()
    for t in range(tiles):
        for k in range(k_local):
            copy_right(t, k).start()
    for k in range(k_local):
        copy_own(k).wait()
        copy_next(k).wait()

        @pl.when(near[k])
        def _():
            left[:, k * depth:(k + 1) * depth] = own_held[k].T

        @pl.when(jnp.logical_not(near[k]))
        def _():
            left[:, k * depth:(k + 1) * depth] = next_held[k]

    for t in range(tiles):
        for k in range(k_local):
            copy_right(t, k).wait()
        right = held[t].reshape(k_local * depth, tile)
        total = jnp.dot(left[...], right, preferred_element_type=jnp.float32)
        parts = total.reshape(2, 2, width // 4, tile)
        mine = jnp.where(x == 0, parts[0], parts[1])
        other = jnp.where(x == 0, parts[1], parts[0])
        place = slice(t * tile, (t + 1) * tile)
        mine_ref[:, place] = jnp.where(core == 0, mine[0], mine[1])
        other_ref[:, place] = jnp.where(core == 0, other[0], other[1])
        send_ref[:width // 4, place] = jnp.where(core == 0, mine[1], mine[0]).astype(jnp.bfloat16)
        send_ref[width // 4:, place] = jnp.where(core == 0, other[1], other[0]).astype(jnp.bfloat16)


def rows_of(pick, own, following, products):
    k_local, width, depth = following.shape
    modes, excitons = products.shape[1], products.shape[3]
    columns, tile = modes * excitons, 512
    tiles = columns // tile
    return pl.pallas_call(
        rows_kernel,
        out_shape=[
            jax.ShapeDtypeStruct((width // 4, columns), jnp.float32),
            jax.ShapeDtypeStruct((width // 4, columns), jnp.float32),
            jax.ShapeDtypeStruct((width // 2, columns), jnp.bfloat16),
        ],
        in_specs=[pl.BlockSpec(memory_space=pltpu.SMEM)]
        + [pl.BlockSpec(memory_space=pl.ANY)] * 3,
        out_specs=[pl.BlockSpec(memory_space=pltpu.VMEM)] * 3,
        scratch_shapes=[
            pltpu.VMEM((k_local, depth, width), jnp.bfloat16),
            pltpu.VMEM((k_local, width, depth), jnp.bfloat16),
            pltpu.VMEM((tiles, k_local, depth, tile), jnp.bfloat16),
            pltpu.VMEM((width, k_local * depth), jnp.bfloat16),
            pltpu.SemaphoreType.DMA((k_local,)),
            pltpu.SemaphoreType.DMA((k_local,)),
            pltpu.SemaphoreType.DMA((tiles, k_local)),
        ],
        compiler_params=pltpu.CompilerParams(vmem_limit_bytes=50 * MIB),
        cost_estimate=pl.CostEstimate(
            flops=2 * k_local * depth * width * columns,
            bytes_accessed=2 * k_local * depth * columns,
            transcendentals=0,
        ),
    )(pick, own, following, products)


def on_two_by_four(coeffs, g_cond, g_val, k_plus_q, band_first, norm_factor):
    k_local, bands_c, bands_v, excitons = coeffs.shape
    modes = g_cond.shape[1]
    size = lax.axis_size("ka")
    width = excitons // 4
    me = lax.axis_index("ka")
    core, x, z = me & 1, me >> 1 & 1, me >> 2
    flat = coeffs.reshape(k_local, bands_c * bands_v, excitons)

    pieces = turned_pieces(flat, 0, 1, width)
    rest, _ = lax.optimization_barrier((flat, pieces))
    pieces += turned_pieces(rest, 1, 3, width)
    following = [permute(piece, lambda i: i - 1) for piece in pieces]
    products = products_of(coeffs, g_cond, g_val, band_first)
    products = products.reshape(k_local, modes, bands_c * bands_v, excitons)
    places = jnp.mod(k_plus_q - me * k_local, k_local * size)

    def rows(step, after):
        pick = jnp.concatenate((places, jnp.stack((z ^ (3 - step), core, x))))
        pick, _ = lax.optimization_barrier((pick, after))
        mine, other, send = rows_of(pick, flat, following[step], products)
        return mine, other, permute(send, lambda i: i ^ 1)

    def for_x(step, from_core):
        return (step[1] + from_core[width // 4:].astype(jnp.float32)).astype(jnp.bfloat16)

    def from_x(send):
        return permute(send, lambda i: i ^ 2)

    def own_sum(mine, from_core, across):
        return mine + from_core[:width // 4].astype(jnp.float32) + across.astype(jnp.float32)

    def over(value, bit):
        return permute(value.astype(jnp.bfloat16), lambda i: i ^ bit)

    step_0 = rows(0, products)
    step_1 = rows(1, step_0[0])
    step_2 = rows(2, step_1[0])
    core_0, core_1, core_2, following[3] = lax.optimization_barrier(
        (step_0[2], step_1[2], step_2[2], following[3])
    )
    send_0, send_1, send_2 = for_x(step_0, core_0), for_x(step_1, core_1), for_x(step_2, core_2)
    mine_3, other_3, core_3 = rows(3, send_0)
    send_1, _ = lax.optimization_barrier((send_1, mine_3))
    across_0, across_1, across_2 = from_x(send_0), from_x(send_1), from_x(send_2)
    mine_0, _ = lax.optimization_barrier((step_0[0], send_1))
    far = own_sum(mine_0, core_0, across_0)
    far = over(far, 4)
    send_3 = for_x((mine_3, other_3), core_3)
    across_3 = from_x(send_3)
    pair = own_sum(step_1[0], core_1, across_1) + far.astype(jnp.float32)
    mine_2, _ = lax.optimization_barrier((step_2[0], pair))
    pair = over(pair, 8)
    near = over(own_sum(mine_2, core_2, across_2), 4)
    total = own_sum(mine_3, core_3, across_3) + near.astype(jnp.float32) + pair.astype(jnp.float32)
    return (total * norm_factor).reshape(width // 4, modes, excitons)


def on_any(coeffs, g_cond, g_val, k_plus_q, band_first, norm_factor):
    k_local, bands_c, bands_v, excitons = coeffs.shape
    modes = g_cond.shape[1]
    size = lax.axis_size("ka")
    depth = bands_c * bands_v
    flat = coeffs.reshape(k_local, depth, excitons)
    blocks = jnp.concatenate((flat, permute(flat, lambda i: i - 1)), 0)
    offsets = jnp.mod(k_plus_q - lax.axis_index("ka") * k_local, k_local * size)
    products = products_of(coeffs, g_cond, g_val, band_first)
    products = products.reshape(k_local, modes, depth, excitons)
    partners = [
        lax.dynamic_index_in_dim(blocks, offsets[k], 0, keepdims=False) for k in range(k_local)
    ]
    running = jnp.einsum(
        "kds,kmdt->smt", jnp.stack(partners), products, preferred_element_type=jnp.float32
    )
    return lax.psum_scatter(running * norm_factor, "ka", scatter_dimension=0, tiled=True)


def shards(coeffs, g_cond, g_val, k_plus_q, band_first):
    k_local, bands_c, bands_v, excitons = coeffs.shape
    size = lax.axis_size("ka")
    norm_factor = 1.0 / math.sqrt(bands_c * bands_v * k_local * size)
    whole_tiles = excitons % (4 * 128) == 0
    plan = on_two_by_four if size == 16 and whole_tiles else on_any
    return plan(coeffs, g_cond, g_val, k_plus_q, band_first, norm_factor)


def solution(mesh):
    in_specs = (
        P(("groups", "ka"), None, None, None),
        P(("groups", "ka"), None, None, None),
        P(("groups", "ka"), None, None, None),
        P(("groups", "ka")),
        P("groups", None),
    )
    out_specs = P(("groups", "ka"), None, None)
    return jax.shard_map(shards, mesh=mesh, in_specs=in_specs, out_specs=out_specs, check_vma=False)
```

```python
import functools
import math

import jax
import jax.numpy as jnp
from jax import lax
from jax.experimental import pallas as pl
from jax.experimental.pallas import tpu as pltpu
from jax.sharding import PartitionSpec as P

MIB = 1024 * 1024


def permute(x, target):
    size = lax.axis_size("ka")
    pairs = [(i, target(i)) for i in range(size)]
    return lax.ppermute(x, "ka", [(i, j % size) for i, j in pairs if j is not None])


def nt_dot(a, b):
    return lax.dot_general(a, b, (((1,), (1,)), ((), ())), preferred_element_type=jnp.float32)


def iotas(rows, cols):
    shape = (rows, cols)
    return lax.broadcasted_iota(jnp.int32, shape, 0), lax.broadcasted_iota(jnp.int32, shape, 1)


def ones_where(condition):
    return jnp.where(condition, 1.0, 0.0).astype(jnp.bfloat16)


PART_C, PART_V = 8, 16


def fill_weights(first_ref, cond_ref, val_ref, we_ref, wh_ref):
    _, modes, bands_c, _ = cond_ref.shape
    bands_v = val_ref.shape[2]
    rows_e, rows_h = bands_c * PART_V, PART_C * bands_v
    row, col = iotas(rows_e, bands_c)
    take = ones_where(row // PART_V == col)
    row, col = iotas(rows_e, rows_e)
    for m in range(modes):
        half = jnp.dot(take, cond_ref[0, m], preferred_element_type=jnp.float32)
        full = nt_dot(half.astype(jnp.bfloat16), take)
        keep = (row % PART_V == col % PART_V) & (row // PART_V >= first_ref[m, 0])
        we_ref[m * rows_e:(m + 1) * rows_e, :] = jnp.where(keep, full, 0.0).astype(jnp.bfloat16)
    row, col = iotas(rows_h, bands_v)
    take = ones_where(row % bands_v == col)
    row, col = iotas(rows_h, rows_h)
    for m in range(modes):
        half = nt_dot(take, val_ref[0, m])
        full = nt_dot(half.astype(jnp.bfloat16), take)
        keep = (row // bands_v == col // bands_v) & (row % bands_v >= first_ref[m, 1])
        wh_ref[m * rows_h:(m + 1) * rows_h, :] = jnp.where(keep, full, 0.0).astype(jnp.bfloat16)


def products_kernel(first_ref, coeffs_ref, cond_ref, val_ref, out_ref, we_ref, wh_ref):
    _, bands_c, bands_v, tile = coeffs_ref.shape
    modes = cond_ref.shape[1]
    rows_e, rows_h = bands_c * PART_V, PART_C * bands_v

    @pl.when(pl.program_id(1) == 0)
    def _():
        fill_weights(first_ref, cond_ref, val_ref, we_ref, wh_ref)

    electron = []
    for h in range(bands_v // PART_V):
        x = coeffs_ref[0, :, h * PART_V:(h + 1) * PART_V, :].reshape(rows_e, tile)
        e = jnp.dot(we_ref[...], x, preferred_element_type=jnp.float32)
        electron.append(e.reshape(modes, bands_c, PART_V, tile))
    for q in range(bands_c // PART_C):
        own = slice(q * PART_C, (q + 1) * PART_C)
        y = coeffs_ref[0, own].reshape(rows_h, tile)
        hole = jnp.dot(wh_ref[...], y, preferred_element_type=jnp.float32)
        hole = hole.reshape(modes, PART_C, bands_v, tile)
        for m in range(modes):
            for h in range(bands_v // PART_V):
                cols = slice(h * PART_V, (h + 1) * PART_V)
                value = electron[h][m, own] - hole[m, :, cols]
                out_ref[0, m, own, cols, :] = value.astype(jnp.bfloat16)


def products_of(coeffs, g_cond, g_val, band_first):
    k_local, bands_c, bands_v, excitons = coeffs.shape
    modes = g_cond.shape[1]
    tile = 256
    rows_e, rows_h = bands_c * PART_V, PART_C * bands_v
    depth = bands_c * bands_v
    return pl.pallas_call(
        products_kernel,
        out_shape=jax.ShapeDtypeStruct((k_local, modes, bands_c, bands_v, excitons), jnp.bfloat16),
        grid=(k_local, excitons // tile),
        in_specs=[
            pl.BlockSpec(memory_space=pltpu.SMEM),
            pl.BlockSpec((1, bands_c, bands_v, tile), lambda k, s: (k, 0, 0, s)),
            pl.BlockSpec((1, modes, bands_c, bands_c), lambda k, s: (k, 0, 0, 0)),
            pl.BlockSpec((1, modes, bands_v, bands_v), lambda k, s: (k, 0, 0, 0)),
        ],
        out_specs=pl.BlockSpec((1, modes, bands_c, bands_v, tile), lambda k, s: (k, 0, 0, 0, s)),
        scratch_shapes=[
            pltpu.VMEM((modes * rows_e, rows_e), jnp.bfloat16),
            pltpu.VMEM((modes * rows_h, rows_h), jnp.bfloat16),
        ],
        compiler_params=pltpu.CompilerParams(vmem_limit_bytes=60 * MIB),
        cost_estimate=pl.CostEstimate(
            flops=2 * k_local * modes * excitons * depth * (rows_e + rows_h),
            bytes_accessed=2 * coeffs.size * (1 + modes),
            transcendentals=0,
        ),
    )(band_first, coeffs, g_cond, g_val)


def turn_kernel(first, coeffs_ref, *refs):
    *out_refs, held, sems = refs
    pieces, k_local, parts, rows, width = held.shape
    size = lax.axis_size("ka")
    behind_z = lax.shift_right_logical(lax.rem(lax.axis_index("ka") + size - 1, size), 2)

    def copy(i, k, p):
        columns = pl.ds(pl.multiple_of((behind_z ^ (3 - first - i)) * width, width), width)
        source = coeffs_ref.at[k, pl.ds(p * rows, rows), columns]
        return pltpu.make_async_copy(source, held.at[i, k, p], sems.at[i, k, p])

    steps = [(i, k, p) for i in range(pieces) for k in range(k_local) for p in range(parts)]
    for step in steps:
        copy(*step).start()
    for step in steps:
        i, k, p = step
        copy(*step).wait()
        out_refs[i][k, :, p * rows:(p + 1) * rows] = held[i, k, p].T


def turned_pieces(flat, first, pieces, width):
    k_local, depth, _ = flat.shape
    parts = 2
    return pl.pallas_call(
        functools.partial(turn_kernel, first),
        out_shape=[jax.ShapeDtypeStruct((k_local, width, depth), jnp.bfloat16)] * pieces,
        in_specs=[pl.BlockSpec(memory_space=pl.ANY)],
        out_specs=[pl.BlockSpec(memory_space=pltpu.VMEM)] * pieces,
        scratch_shapes=[
            pltpu.VMEM((pieces, k_local, parts, depth // parts, width), jnp.bfloat16),
            pltpu.SemaphoreType.DMA((pieces, k_local, parts)),
        ],
        compiler_params=pltpu.CompilerParams(vmem_limit_bytes=60 * MIB),
        cost_estimate=pl.CostEstimate(
            flops=0, bytes_accessed=4 * pieces * k_local * depth * width, transcendentals=0
        ),
    )(flat)


def rows_kernel(pick_ref, own_ref, next_ref, right_ref, mine_ref, other_ref, send_ref, *refs):
    own_held, next_held, held, left, own_sems, next_sems, sems = refs
    k_local, depth, width = own_held.shape
    tiles, _, _, tile = held.shape
    per_mode = right_ref.shape[3] // tile
    core, x = pick_ref[k_local + 1], pick_ref[k_local + 2]
    columns = pl.ds(pl.multiple_of(pick_ref[k_local] * width, width), width)
    near = [pick_ref[k] < k_local for k in range(k_local)]

    def copy_own(k):
        source = own_ref.at[jnp.minimum(pick_ref[k], k_local - 1), :, columns]
        return pltpu.make_async_copy(source, own_held.at[k], own_sems.at[k])

    def copy_next(k):
        source = next_ref.at[jnp.maximum(pick_ref[k] - k_local, 0)]
        return pltpu.make_async_copy(source, next_held.at[k], next_sems.at[k])

    def copy_right(t, k):
        source = right_ref.at[k, t // per_mode, :, pl.ds(t % per_mode * tile, tile)]
        return pltpu.make_async_copy(source, held.at[t, k], sems.at[t, k])

    for k in range(k_local):
        copy_own(k).start()
        copy_next(k).start()
    for t in range(tiles):
        for k in range(k_local):
            copy_right(t, k).start()
    for k in range(k_local):
        copy_own(k).wait()
        copy_next(k).wait()

        @pl.when(near[k])
        def _():
            left[:, k * depth:(k + 1) * depth] = own_held[k].T

        @pl.when(jnp.logical_not(near[k]))
        def _():
            left[:, k * depth:(k + 1) * depth] = next_held[k]

    for t in range(tiles):
        for k in range(k_local):
            copy_right(t, k).wait()
        right = held[t].reshape(k_local * depth, tile)
        total = jnp.dot(left[...], right, preferred_element_type=jnp.float32)
        parts = total.reshape(2, 2, width // 4, tile)
        mine = jnp.where(x == 0, parts[0], parts[1])
        other = jnp.where(x == 0, parts[1], parts[0])
        place = slice(t * tile, (t + 1) * tile)
        mine_ref[:, place] = jnp.where(core == 0, mine[0], mine[1])
        other_ref[:, place] = jnp.where(core == 0, other[0], other[1])
        send_ref[:width // 4, place] = jnp.where(core == 0, mine[1], mine[0]).astype(jnp.bfloat16)
        send_ref[width // 4:, place] = jnp.where(core == 0, other[1], other[0]).astype(jnp.bfloat16)


def rows_of(pick, own, following, products):
    k_local, width, depth = following.shape
    modes, excitons = products.shape[1], products.shape[3]
    columns, tile = modes * excitons, 512
    tiles = columns // tile
    return pl.pallas_call(
        rows_kernel,
        out_shape=[
            jax.ShapeDtypeStruct((width // 4, columns), jnp.float32),
            jax.ShapeDtypeStruct((width // 4, columns), jnp.float32),
            jax.ShapeDtypeStruct((width // 2, columns), jnp.bfloat16),
        ],
        in_specs=[pl.BlockSpec(memory_space=pltpu.SMEM)]
        + [pl.BlockSpec(memory_space=pl.ANY)] * 3,
        out_specs=[pl.BlockSpec(memory_space=pltpu.VMEM)] * 3,
        scratch_shapes=[
            pltpu.VMEM((k_local, depth, width), jnp.bfloat16),
            pltpu.VMEM((k_local, width, depth), jnp.bfloat16),
            pltpu.VMEM((tiles, k_local, depth, tile), jnp.bfloat16),
            pltpu.VMEM((width, k_local * depth), jnp.bfloat16),
            pltpu.SemaphoreType.DMA((k_local,)),
            pltpu.SemaphoreType.DMA((k_local,)),
            pltpu.SemaphoreType.DMA((tiles, k_local)),
        ],
        compiler_params=pltpu.CompilerParams(vmem_limit_bytes=50 * MIB),
        cost_estimate=pl.CostEstimate(
            flops=2 * k_local * depth * width * columns,
            bytes_accessed=2 * k_local * depth * columns,
            transcendentals=0,
        ),
    )(pick, own, following, products)


def on_two_by_four(coeffs, g_cond, g_val, k_plus_q, band_first, norm_factor):
    k_local, bands_c, bands_v, excitons = coeffs.shape
    modes = g_cond.shape[1]
    size = lax.axis_size("ka")
    width = excitons // 4
    me = lax.axis_index("ka")
    core, x, z = me & 1, me >> 1 & 1, me >> 2
    flat = coeffs.reshape(k_local, bands_c * bands_v, excitons)

    pieces = turned_pieces(flat, 0, 1, width)
    rest, _ = lax.optimization_barrier((flat, pieces))
    pieces += turned_pieces(rest, 1, 3, width)
    following = [permute(piece, lambda i: i - 1) for piece in pieces[:3]]
    products = products_of(coeffs, g_cond, g_val, band_first)
    products = products.reshape(k_local, modes, bands_c * bands_v, excitons)
    places = jnp.mod(k_plus_q - me * k_local, k_local * size)

    def rows(step, after):
        pick = jnp.concatenate((places, jnp.stack((z ^ (3 - step), core, x))))
        pick, _ = lax.optimization_barrier((pick, after))
        mine, other, send = rows_of(pick, flat, following[step], products)
        return mine, other, permute(send, lambda i: i ^ 1)

    def for_x(step, from_core):
        return (step[1] + from_core[width // 4:].astype(jnp.float32)).astype(jnp.bfloat16)

    def from_x(send):
        return permute(send, lambda i: i ^ 2)

    def own_sum(mine, from_core, across):
        return mine + from_core[:width // 4].astype(jnp.float32) + across.astype(jnp.float32)

    def over(value, bit):
        return permute(value.astype(jnp.bfloat16), lambda i: i ^ bit)

    step_0 = rows(0, products)
    step_1 = rows(1, step_0[0])
    core_0, following[2], _ = lax.optimization_barrier((step_0[2], following[2], step_1[0]))
    send_0 = for_x(step_0, core_0)
    across_0 = from_x(send_0)
    step_2 = rows(2, (step_1[0], send_0))
    last_piece, _ = lax.optimization_barrier((pieces[3], (across_0, step_2[0])))
    following.append(permute(last_piece, lambda i: i - 1))
    far = own_sum(step_0[0], core_0, across_0)
    core_1, core_2, following[3] = lax.optimization_barrier((step_1[2], step_2[2], following[3]))
    send_1, send_2 = for_x(step_1, core_1), for_x(step_2, core_2)
    across_1 = from_x(send_1)
    mine_3, other_3, core_3 = rows(3, (far, send_1))
    send_2, _ = lax.optimization_barrier((send_2, mine_3))
    across_2 = from_x(send_2)
    far = over(far, 4)
    send_3 = for_x((mine_3, other_3), core_3)
    across_3 = from_x(send_3)
    pair = own_sum(step_1[0], core_1, across_1) + far.astype(jnp.float32)
    mine_2, _ = lax.optimization_barrier((step_2[0], pair))
    pair = over(pair, 8)
    near = over(own_sum(mine_2, core_2, across_2), 4)
    total = own_sum(mine_3, core_3, across_3) + near.astype(jnp.float32) + pair.astype(jnp.float32)
    return (total * norm_factor).reshape(width // 4, modes, excitons)


def on_any(coeffs, g_cond, g_val, k_plus_q, band_first, norm_factor):
    k_local, bands_c, bands_v, excitons = coeffs.shape
    modes = g_cond.shape[1]
    size = lax.axis_size("ka")
    depth = bands_c * bands_v
    flat = coeffs.reshape(k_local, depth, excitons)
    blocks = jnp.concatenate((flat, permute(flat, lambda i: i - 1)), 0)
    offsets = jnp.mod(k_plus_q - lax.axis_index("ka") * k_local, k_local * size)
    products = products_of(coeffs, g_cond, g_val, band_first)
    products = products.reshape(k_local, modes, depth, excitons)
    partners = [
        lax.dynamic_index_in_dim(blocks, offsets[k], 0, keepdims=False) for k in range(k_local)
    ]
    running = jnp.einsum(
        "kds,kmdt->smt", jnp.stack(partners), products, preferred_element_type=jnp.float32
    )
    return lax.psum_scatter(running * norm_factor, "ka", scatter_dimension=0, tiled=True)


def shards(coeffs, g_cond, g_val, k_plus_q, band_first):
    k_local, bands_c, bands_v, excitons = coeffs.shape
    size = lax.axis_size("ka")
    norm_factor = 1.0 / math.sqrt(bands_c * bands_v * k_local * size)
    whole_tiles = excitons % (4 * 128) == 0
    plan = on_two_by_four if size == 16 and whole_tiles else on_any
    return plan(coeffs, g_cond, g_val, k_plus_q, band_first, norm_factor)


def solution(mesh):
    in_specs = (
        P(("groups", "ka"), None, None, None),
        P(("groups", "ka"), None, None, None),
        P(("groups", "ka"), None, None, None),
        P(("groups", "ka")),
        P("groups", None),
    )
    out_specs = P(("groups", "ka"), None, None)
    return jax.shard_map(shards, mesh=mesh, in_specs=in_specs, out_specs=out_specs, check_vma=False)
```

```python
import functools
import math

import jax
import jax.numpy as jnp
from jax import lax
from jax.experimental import pallas as pl
from jax.experimental.pallas import tpu as pltpu
from jax.sharding import PartitionSpec as P

MIB = 1024 * 1024


def permute(x, target):
    size = lax.axis_size("ka")
    pairs = [(i, target(i)) for i in range(size)]
    return lax.ppermute(x, "ka", [(i, j % size) for i, j in pairs if j is not None])


def nt_dot(a, b):
    return lax.dot_general(a, b, (((1,), (1,)), ((), ())), preferred_element_type=jnp.float32)


def iotas(rows, cols):
    shape = (rows, cols)
    return lax.broadcasted_iota(jnp.int32, shape, 0), lax.broadcasted_iota(jnp.int32, shape, 1)


def ones_where(condition):
    return jnp.where(condition, 1.0, 0.0).astype(jnp.bfloat16)


PART_C, PART_V = 8, 16


def fill_weights(first_ref, cond_ref, val_ref, we_ref, wh_ref):
    _, modes, bands_c, _ = cond_ref.shape
    bands_v = val_ref.shape[2]
    rows_e, rows_h = bands_c * PART_V, PART_C * bands_v
    row, col = iotas(rows_e, bands_c)
    take = ones_where(row // PART_V == col)
    row, col = iotas(rows_e, rows_e)
    for m in range(modes):
        half = jnp.dot(take, cond_ref[0, m], preferred_element_type=jnp.float32)
        full = nt_dot(half.astype(jnp.bfloat16), take)
        keep = (row % PART_V == col % PART_V) & (row // PART_V >= first_ref[m, 0])
        we_ref[m * rows_e:(m + 1) * rows_e, :] = jnp.where(keep, full, 0.0).astype(jnp.bfloat16)
    row, col = iotas(rows_h, bands_v)
    take = ones_where(row % bands_v == col)
    row, col = iotas(rows_h, rows_h)
    for m in range(modes):
        half = nt_dot(take, val_ref[0, m])
        full = nt_dot(half.astype(jnp.bfloat16), take)
        keep = (row // bands_v == col // bands_v) & (row % bands_v >= first_ref[m, 1])
        wh_ref[m * rows_h:(m + 1) * rows_h, :] = jnp.where(keep, full, 0.0).astype(jnp.bfloat16)


def products_kernel(first_ref, coeffs_ref, cond_ref, val_ref, out_ref, we_ref, wh_ref):
    _, bands_c, bands_v, tile = coeffs_ref.shape
    modes = cond_ref.shape[1]
    rows_e, rows_h = bands_c * PART_V, PART_C * bands_v

    @pl.when(pl.program_id(1) == 0)
    def _():
        fill_weights(first_ref, cond_ref, val_ref, we_ref, wh_ref)

    electron = []
    for h in range(bands_v // PART_V):
        x = coeffs_ref[0, :, h * PART_V:(h + 1) * PART_V, :].reshape(rows_e, tile)
        e = jnp.dot(we_ref[...], x, preferred_element_type=jnp.float32)
        electron.append(e.reshape(modes, bands_c, PART_V, tile))
    for q in range(bands_c // PART_C):
        own = slice(q * PART_C, (q + 1) * PART_C)
        y = coeffs_ref[0, own].reshape(rows_h, tile)
        hole = jnp.dot(wh_ref[...], y, preferred_element_type=jnp.float32)
        hole = hole.reshape(modes, PART_C, bands_v, tile)
        for m in range(modes):
            for h in range(bands_v // PART_V):
                cols = slice(h * PART_V, (h + 1) * PART_V)
                value = electron[h][m, own] - hole[m, :, cols]
                out_ref[0, m, own, cols, :] = value.astype(jnp.bfloat16)


def products_of(coeffs, g_cond, g_val, band_first):
    k_local, bands_c, bands_v, excitons = coeffs.shape
    modes = g_cond.shape[1]
    tile = 256
    rows_e, rows_h = bands_c * PART_V, PART_C * bands_v
    depth = bands_c * bands_v
    return pl.pallas_call(
        products_kernel,
        out_shape=jax.ShapeDtypeStruct((k_local, modes, bands_c, bands_v, excitons), jnp.bfloat16),
        grid=(k_local, excitons // tile),
        in_specs=[
            pl.BlockSpec(memory_space=pltpu.SMEM),
            pl.BlockSpec((1, bands_c, bands_v, tile), lambda k, s: (k, 0, 0, s)),
            pl.BlockSpec((1, modes, bands_c, bands_c), lambda k, s: (k, 0, 0, 0)),
            pl.BlockSpec((1, modes, bands_v, bands_v), lambda k, s: (k, 0, 0, 0)),
        ],
        out_specs=pl.BlockSpec((1, modes, bands_c, bands_v, tile), lambda k, s: (k, 0, 0, 0, s)),
        scratch_shapes=[
            pltpu.VMEM((modes * rows_e, rows_e), jnp.bfloat16),
            pltpu.VMEM((modes * rows_h, rows_h), jnp.bfloat16),
        ],
        compiler_params=pltpu.CompilerParams(vmem_limit_bytes=60 * MIB),
        cost_estimate=pl.CostEstimate(
            flops=2 * k_local * modes * excitons * depth * (rows_e + rows_h),
            bytes_accessed=2 * coeffs.size * (1 + modes),
            transcendentals=0,
        ),
    )(band_first, coeffs, g_cond, g_val)


def turn_kernel(first, coeffs_ref, *refs):
    *out_refs, held, sems = refs
    pieces, k_local, parts, rows, width = held.shape
    size = lax.axis_size("ka")
    behind_z = lax.shift_right_logical(lax.rem(lax.axis_index("ka") + size - 1, size), 2)

    def copy(i, k, p):
        columns = pl.ds(pl.multiple_of((behind_z ^ (3 - first - i)) * width, width), width)
        source = coeffs_ref.at[k, pl.ds(p * rows, rows), columns]
        return pltpu.make_async_copy(source, held.at[i, k, p], sems.at[i, k, p])

    steps = [(i, k, p) for i in range(pieces) for k in range(k_local) for p in range(parts)]
    for step in steps:
        copy(*step).start()
    for step in steps:
        i, k, p = step
        copy(*step).wait()
        out_refs[i][k, :, p * rows:(p + 1) * rows] = held[i, k, p].T


def turned_pieces(flat, first, pieces, width):
    k_local, depth, _ = flat.shape
    parts = 2
    return pl.pallas_call(
        functools.partial(turn_kernel, first),
        out_shape=[jax.ShapeDtypeStruct((k_local, width, depth), jnp.bfloat16)] * pieces,
        in_specs=[pl.BlockSpec(memory_space=pl.ANY)],
        out_specs=[pl.BlockSpec(memory_space=pltpu.VMEM)] * pieces,
        scratch_shapes=[
            pltpu.VMEM((pieces, k_local, parts, depth // parts, width), jnp.bfloat16),
            pltpu.SemaphoreType.DMA((pieces, k_local, parts)),
        ],
        compiler_params=pltpu.CompilerParams(vmem_limit_bytes=60 * MIB),
        cost_estimate=pl.CostEstimate(
            flops=0, bytes_accessed=4 * pieces * k_local * depth * width, transcendentals=0
        ),
    )(flat)


def rows_kernel(pick_ref, own_ref, next_ref, right_ref, mine_ref, other_ref, send_ref, *refs):
    own_held, next_held, held, left, own_sems, next_sems, sems = refs
    k_local, depth, width = own_held.shape
    tiles, _, _, tile = held.shape
    per_mode = right_ref.shape[3] // tile
    core, x = pick_ref[k_local + 1], pick_ref[k_local + 2]
    columns = pl.ds(pl.multiple_of(pick_ref[k_local] * width, width), width)
    near = [pick_ref[k] < k_local for k in range(k_local)]

    def copy_own(k):
        source = own_ref.at[jnp.minimum(pick_ref[k], k_local - 1), :, columns]
        return pltpu.make_async_copy(source, own_held.at[k], own_sems.at[k])

    def copy_next(k):
        source = next_ref.at[jnp.maximum(pick_ref[k] - k_local, 0)]
        return pltpu.make_async_copy(source, next_held.at[k], next_sems.at[k])

    def copy_right(t, k):
        source = right_ref.at[k, t // per_mode, :, pl.ds(t % per_mode * tile, tile)]
        return pltpu.make_async_copy(source, held.at[t, k], sems.at[t, k])

    for k in range(k_local):
        copy_own(k).start()
        copy_next(k).start()
    for t in range(tiles):
        for k in range(k_local):
            copy_right(t, k).start()
    for k in range(k_local):
        copy_own(k).wait()
        copy_next(k).wait()

        @pl.when(near[k])
        def _():
            left[:, k * depth:(k + 1) * depth] = own_held[k].T

        @pl.when(jnp.logical_not(near[k]))
        def _():
            left[:, k * depth:(k + 1) * depth] = next_held[k]

    for t in range(tiles):
        for k in range(k_local):
            copy_right(t, k).wait()
        right = held[t].reshape(k_local * depth, tile)
        total = jnp.dot(left[...], right, preferred_element_type=jnp.float32)
        parts = total.reshape(2, 2, width // 4, tile)
        mine = jnp.where(x == 0, parts[0], parts[1])
        other = jnp.where(x == 0, parts[1], parts[0])
        place = slice(t * tile, (t + 1) * tile)
        mine_ref[:, place] = jnp.where(core == 0, mine[0], mine[1])
        other_ref[:, place] = jnp.where(core == 0, other[0], other[1])
        send_ref[:width // 4, place] = jnp.where(core == 0, mine[1], mine[0]).astype(jnp.bfloat16)
        send_ref[width // 4:, place] = jnp.where(core == 0, other[1], other[0]).astype(jnp.bfloat16)


def rows_of(pick, own, following, products):
    k_local, width, depth = following.shape
    modes, excitons = products.shape[1], products.shape[3]
    columns, tile = modes * excitons, 512
    tiles = columns // tile
    return pl.pallas_call(
        rows_kernel,
        out_shape=[
            jax.ShapeDtypeStruct((width // 4, columns), jnp.float32),
            jax.ShapeDtypeStruct((width // 4, columns), jnp.float32),
            jax.ShapeDtypeStruct((width // 2, columns), jnp.bfloat16),
        ],
        in_specs=[pl.BlockSpec(memory_space=pltpu.SMEM)]
        + [pl.BlockSpec(memory_space=pl.ANY)] * 3,
        out_specs=[pl.BlockSpec(memory_space=pltpu.VMEM)] * 3,
        scratch_shapes=[
            pltpu.VMEM((k_local, depth, width), jnp.bfloat16),
            pltpu.VMEM((k_local, width, depth), jnp.bfloat16),
            pltpu.VMEM((tiles, k_local, depth, tile), jnp.bfloat16),
            pltpu.VMEM((width, k_local * depth), jnp.bfloat16),
            pltpu.SemaphoreType.DMA((k_local,)),
            pltpu.SemaphoreType.DMA((k_local,)),
            pltpu.SemaphoreType.DMA((tiles, k_local)),
        ],
        compiler_params=pltpu.CompilerParams(vmem_limit_bytes=50 * MIB),
        cost_estimate=pl.CostEstimate(
            flops=2 * k_local * depth * width * columns,
            bytes_accessed=2 * k_local * depth * columns,
            transcendentals=0,
        ),
    )(pick, own, following, products)


def on_two_by_four(coeffs, g_cond, g_val, k_plus_q, band_first, norm_factor):
    k_local, bands_c, bands_v, excitons = coeffs.shape
    modes = g_cond.shape[1]
    size = lax.axis_size("ka")
    width = excitons // 4
    me = lax.axis_index("ka")
    core, x, z = me & 1, me >> 1 & 1, me >> 2
    flat = coeffs.reshape(k_local, bands_c * bands_v, excitons)

    pieces = turned_pieces(flat, 0, 1, width)
    rest, _ = lax.optimization_barrier((flat, pieces))
    pieces += turned_pieces(rest, 1, 3, width)
    following = [permute(piece, lambda i: i - 1) for piece in pieces]
    products = products_of(coeffs, g_cond, g_val, band_first)
    products = products.reshape(k_local, modes, bands_c * bands_v, excitons)
    places = jnp.mod(k_plus_q - me * k_local, k_local * size)

    def rows(step, after):
        pick = jnp.concatenate((places, jnp.stack((z ^ (3 - step), core, x))))
        pick, _ = lax.optimization_barrier((pick, after))
        mine, other, send = rows_of(pick, flat, following[step], products)
        return mine, other, permute(send, lambda i: i ^ 1)

    half = width // 4

    def summed(step, from_core):
        from_core = from_core.astype(jnp.float32)
        return step[0] + from_core[:half], step[1] + from_core[half:]

    def over(value, bits):
        return permute(value.astype(jnp.bfloat16), lambda i: i ^ bits)

    def total_of(value, *arrived):
        for array in arrived:
            value = value + array.astype(jnp.float32)
        return value

    step_0 = rows(0, products)
    step_1 = rows(1, step_0[0])
    step_2 = rows(2, step_1[0])
    core_0, core_1, core_2, following[3] = lax.optimization_barrier(
        (step_0[2], step_1[2], step_2[2], following[3])
    )
    mine_0, other_0 = summed(step_0, core_0)
    mine_1, other_1 = summed(step_1, core_1)
    mine_2, other_2 = summed(step_2, core_2)
    sends = [value.astype(jnp.bfloat16) for value in (mine_0, other_0, other_1, mine_2, other_2)]
    step_3 = rows(3, sends)
    far = over(sends[0], 4), over(sends[1], 6)
    across_1 = over(sends[2], 2)
    near = over(sends[3], 4), over(sends[4], 6)
    mine_1, _ = lax.optimization_barrier((mine_1, step_3[0]))
    pair = over(total_of(mine_1, across_1, *far), 8)
    mine_3, other_3 = summed(step_3, step_3[2])
    total = total_of(mine_3, over(other_3, 2), pair, *near)
    return (total * norm_factor).reshape(width // 4, modes, excitons)


def on_any(coeffs, g_cond, g_val, k_plus_q, band_first, norm_factor):
    k_local, bands_c, bands_v, excitons = coeffs.shape
    modes = g_cond.shape[1]
    size = lax.axis_size("ka")
    depth = bands_c * bands_v
    flat = coeffs.reshape(k_local, depth, excitons)
    blocks = jnp.concatenate((flat, permute(flat, lambda i: i - 1)), 0)
    offsets = jnp.mod(k_plus_q - lax.axis_index("ka") * k_local, k_local * size)
    products = products_of(coeffs, g_cond, g_val, band_first)
    products = products.reshape(k_local, modes, depth, excitons)
    partners = [
        lax.dynamic_index_in_dim(blocks, offsets[k], 0, keepdims=False) for k in range(k_local)
    ]
    running = jnp.einsum(
        "kds,kmdt->smt", jnp.stack(partners), products, preferred_element_type=jnp.float32
    )
    return lax.psum_scatter(running * norm_factor, "ka", scatter_dimension=0, tiled=True)


def shards(coeffs, g_cond, g_val, k_plus_q, band_first):
    k_local, bands_c, bands_v, excitons = coeffs.shape
    size = lax.axis_size("ka")
    norm_factor = 1.0 / math.sqrt(bands_c * bands_v * k_local * size)
    whole_tiles = excitons % (4 * 128) == 0
    plan = on_two_by_four if size == 16 and whole_tiles else on_any
    return plan(coeffs, g_cond, g_val, k_plus_q, band_first, norm_factor)


def solution(mesh):
    in_specs = (
        P(("groups", "ka"), None, None, None),
        P(("groups", "ka"), None, None, None),
        P(("groups", "ka"), None, None, None),
        P(("groups", "ka")),
        P("groups", None),
    )
    out_specs = P(("groups", "ka"), None, None)
    return jax.shard_map(shards, mesh=mesh, in_specs=in_specs, out_specs=out_specs, check_vma=False)
```

```python
import functools
import math

import jax
import jax.numpy as jnp
from jax import lax
from jax.experimental import pallas as pl
from jax.experimental.pallas import tpu as pltpu
from jax.sharding import PartitionSpec as P

MIB = 1024 * 1024


def permute(x, target):
    size = lax.axis_size("ka")
    pairs = [(i, target(i)) for i in range(size)]
    return lax.ppermute(x, "ka", [(i, j % size) for i, j in pairs if j is not None])


def nt_dot(a, b):
    return lax.dot_general(a, b, (((1,), (1,)), ((), ())), preferred_element_type=jnp.float32)


def iotas(rows, cols):
    shape = (rows, cols)
    return lax.broadcasted_iota(jnp.int32, shape, 0), lax.broadcasted_iota(jnp.int32, shape, 1)


def ones_where(condition):
    return jnp.where(condition, 1.0, 0.0).astype(jnp.bfloat16)


PART_C, PART_V = 8, 16


def fill_weights(first_ref, cond_ref, val_ref, we_ref, wh_ref):
    _, modes, bands_c, _ = cond_ref.shape
    bands_v = val_ref.shape[2]
    rows_e, rows_h = bands_c * PART_V, PART_C * bands_v
    row, col = iotas(rows_e, bands_c)
    take = ones_where(row // PART_V == col)
    row, col = iotas(rows_e, rows_e)
    for m in range(modes):
        half = jnp.dot(take, cond_ref[0, m], preferred_element_type=jnp.float32)
        full = nt_dot(half.astype(jnp.bfloat16), take)
        keep = (row % PART_V == col % PART_V) & (row // PART_V >= first_ref[m, 0])
        we_ref[m * rows_e:(m + 1) * rows_e, :] = jnp.where(keep, full, 0.0).astype(jnp.bfloat16)
    row, col = iotas(rows_h, bands_v)
    take = ones_where(row % bands_v == col)
    row, col = iotas(rows_h, rows_h)
    for m in range(modes):
        half = nt_dot(take, val_ref[0, m])
        full = nt_dot(half.astype(jnp.bfloat16), take)
        keep = (row // bands_v == col // bands_v) & (row % bands_v >= first_ref[m, 1])
        wh_ref[m * rows_h:(m + 1) * rows_h, :] = jnp.where(keep, full, 0.0).astype(jnp.bfloat16)


def products_kernel(first_ref, coeffs_ref, cond_ref, val_ref, out_ref, we_ref, wh_ref):
    _, bands_c, bands_v, tile = coeffs_ref.shape
    modes = cond_ref.shape[1]
    rows_e, rows_h = bands_c * PART_V, PART_C * bands_v

    @pl.when(pl.program_id(1) == 0)
    def _():
        fill_weights(first_ref, cond_ref, val_ref, we_ref, wh_ref)

    electron = []
    for h in range(bands_v // PART_V):
        x = coeffs_ref[0, :, h * PART_V:(h + 1) * PART_V, :].reshape(rows_e, tile)
        e = jnp.dot(we_ref[...], x, preferred_element_type=jnp.float32)
        electron.append(e.reshape(modes, bands_c, PART_V, tile))
    for q in range(bands_c // PART_C):
        own = slice(q * PART_C, (q + 1) * PART_C)
        y = coeffs_ref[0, own].reshape(rows_h, tile)
        hole = jnp.dot(wh_ref[...], y, preferred_element_type=jnp.float32)
        hole = hole.reshape(modes, PART_C, bands_v, tile)
        for m in range(modes):
            for h in range(bands_v // PART_V):
                cols = slice(h * PART_V, (h + 1) * PART_V)
                value = electron[h][m, own] - hole[m, :, cols]
                out_ref[0, m, own, cols, :] = value.astype(jnp.bfloat16)


def products_of(coeffs, g_cond, g_val, band_first):
    k_local, bands_c, bands_v, excitons = coeffs.shape
    modes = g_cond.shape[1]
    tile = 256
    rows_e, rows_h = bands_c * PART_V, PART_C * bands_v
    depth = bands_c * bands_v
    return pl.pallas_call(
        products_kernel,
        out_shape=jax.ShapeDtypeStruct((k_local, modes, bands_c, bands_v, excitons), jnp.bfloat16),
        grid=(k_local, excitons // tile),
        in_specs=[
            pl.BlockSpec(memory_space=pltpu.SMEM),
            pl.BlockSpec((1, bands_c, bands_v, tile), lambda k, s: (k, 0, 0, s)),
            pl.BlockSpec((1, modes, bands_c, bands_c), lambda k, s: (k, 0, 0, 0)),
            pl.BlockSpec((1, modes, bands_v, bands_v), lambda k, s: (k, 0, 0, 0)),
        ],
        out_specs=pl.BlockSpec((1, modes, bands_c, bands_v, tile), lambda k, s: (k, 0, 0, 0, s)),
        scratch_shapes=[
            pltpu.VMEM((modes * rows_e, rows_e), jnp.bfloat16),
            pltpu.VMEM((modes * rows_h, rows_h), jnp.bfloat16),
        ],
        compiler_params=pltpu.CompilerParams(vmem_limit_bytes=60 * MIB),
        cost_estimate=pl.CostEstimate(
            flops=2 * k_local * modes * excitons * depth * (rows_e + rows_h),
            bytes_accessed=2 * coeffs.size * (1 + modes),
            transcendentals=0,
        ),
    )(band_first, coeffs, g_cond, g_val)


def turn_kernel(first, coeffs_ref, *refs):
    *out_refs, held, sems = refs
    pieces, k_local, parts, rows, width = held.shape
    size = lax.axis_size("ka")
    behind_z = lax.shift_right_logical(lax.rem(lax.axis_index("ka") + size - 1, size), 2)

    def copy(i, k, p):
        columns = pl.ds(pl.multiple_of((behind_z ^ (3 - first - i)) * width, width), width)
        source = coeffs_ref.at[k, pl.ds(p * rows, rows), columns]
        return pltpu.make_async_copy(source, held.at[i, k, p], sems.at[i, k, p])

    steps = [(i, k, p) for i in range(pieces) for k in range(k_local) for p in range(parts)]
    for step in steps:
        copy(*step).start()
    for step in steps:
        i, k, p = step
        copy(*step).wait()
        out_refs[i][k, :, p * rows:(p + 1) * rows] = held[i, k, p].T


def turned_pieces(flat, first, pieces, width):
    k_local, depth, _ = flat.shape
    parts = 2
    return pl.pallas_call(
        functools.partial(turn_kernel, first),
        out_shape=[jax.ShapeDtypeStruct((k_local, width, depth), jnp.bfloat16)] * pieces,
        in_specs=[pl.BlockSpec(memory_space=pl.ANY)],
        out_specs=[pl.BlockSpec(memory_space=pltpu.VMEM)] * pieces,
        scratch_shapes=[
            pltpu.VMEM((pieces, k_local, parts, depth // parts, width), jnp.bfloat16),
            pltpu.SemaphoreType.DMA((pieces, k_local, parts)),
        ],
        compiler_params=pltpu.CompilerParams(vmem_limit_bytes=60 * MIB),
        cost_estimate=pl.CostEstimate(
            flops=0, bytes_accessed=4 * pieces * k_local * depth * width, transcendentals=0
        ),
    )(flat)


def rows_kernel(pick_ref, own_ref, next_ref, right_ref, mine_ref, other_ref, send_ref, *refs):
    own_held, next_held, held, left, own_sems, next_sems, sems = refs
    k_local, depth, width = own_held.shape
    tiles, _, _, tile = held.shape
    per_mode = right_ref.shape[3] // tile
    core, x = pick_ref[k_local + 1], pick_ref[k_local + 2]
    columns = pl.ds(pl.multiple_of(pick_ref[k_local] * width, width), width)
    near = [pick_ref[k] < k_local for k in range(k_local)]

    def copy_own(k):
        source = own_ref.at[jnp.minimum(pick_ref[k], k_local - 1), :, columns]
        return pltpu.make_async_copy(source, own_held.at[k], own_sems.at[k])

    def copy_next(k):
        source = next_ref.at[jnp.maximum(pick_ref[k] - k_local, 0)]
        return pltpu.make_async_copy(source, next_held.at[k], next_sems.at[k])

    def copy_right(t, k):
        source = right_ref.at[k, t // per_mode, :, pl.ds(t % per_mode * tile, tile)]
        return pltpu.make_async_copy(source, held.at[t, k], sems.at[t, k])

    for k in range(k_local):
        copy_own(k).start()
        copy_next(k).start()
    for t in range(tiles):
        for k in range(k_local):
            copy_right(t, k).start()
    for k in range(k_local):
        copy_own(k).wait()
        copy_next(k).wait()

        @pl.when(near[k])
        def _():
            left[:, k * depth:(k + 1) * depth] = own_held[k].T

        @pl.when(jnp.logical_not(near[k]))
        def _():
            left[:, k * depth:(k + 1) * depth] = next_held[k]

    for t in range(tiles):
        for k in range(k_local):
            copy_right(t, k).wait()
        right = held[t].reshape(k_local * depth, tile)
        total = jnp.dot(left[...], right, preferred_element_type=jnp.float32)
        parts = total.reshape(2, 2, width // 4, tile)
        mine = jnp.where(x == 0, parts[0], parts[1])
        other = jnp.where(x == 0, parts[1], parts[0])
        place = slice(t * tile, (t + 1) * tile)
        mine_ref[:, place] = jnp.where(core == 0, mine[0], mine[1])
        other_ref[:, place] = jnp.where(core == 0, other[0], other[1])
        send_ref[:width // 4, place] = jnp.where(core == 0, mine[1], mine[0]).astype(jnp.bfloat16)
        send_ref[width // 4:, place] = jnp.where(core == 0, other[1], other[0]).astype(jnp.bfloat16)


def rows_of(pick, own, following, products):
    k_local, width, depth = following.shape
    modes, excitons = products.shape[1], products.shape[3]
    columns, tile = modes * excitons, 512
    tiles = columns // tile
    return pl.pallas_call(
        rows_kernel,
        out_shape=[
            jax.ShapeDtypeStruct((width // 4, columns), jnp.float32),
            jax.ShapeDtypeStruct((width // 4, columns), jnp.float32),
            jax.ShapeDtypeStruct((width // 2, columns), jnp.bfloat16),
        ],
        in_specs=[pl.BlockSpec(memory_space=pltpu.SMEM)]
        + [pl.BlockSpec(memory_space=pl.ANY)] * 3,
        out_specs=[pl.BlockSpec(memory_space=pltpu.VMEM)] * 3,
        scratch_shapes=[
            pltpu.VMEM((k_local, depth, width), jnp.bfloat16),
            pltpu.VMEM((k_local, width, depth), jnp.bfloat16),
            pltpu.VMEM((tiles, k_local, depth, tile), jnp.bfloat16),
            pltpu.VMEM((width, k_local * depth), jnp.bfloat16),
            pltpu.SemaphoreType.DMA((k_local,)),
            pltpu.SemaphoreType.DMA((k_local,)),
            pltpu.SemaphoreType.DMA((tiles, k_local)),
        ],
        compiler_params=pltpu.CompilerParams(vmem_limit_bytes=50 * MIB),
        cost_estimate=pl.CostEstimate(
            flops=2 * k_local * depth * width * columns,
            bytes_accessed=2 * k_local * depth * columns,
            transcendentals=0,
        ),
    )(pick, own, following, products)


def on_two_by_four(coeffs, g_cond, g_val, k_plus_q, band_first, norm_factor):
    k_local, bands_c, bands_v, excitons = coeffs.shape
    modes = g_cond.shape[1]
    size = lax.axis_size("ka")
    width = excitons // 4
    me = lax.axis_index("ka")
    core, x, z = me & 1, me >> 1 & 1, me >> 2
    flat = coeffs.reshape(k_local, bands_c * bands_v, excitons)

    pieces = turned_pieces(flat, 0, 1, width)
    rest, _ = lax.optimization_barrier((flat, pieces))
    pieces += turned_pieces(rest, 1, 3, width)
    following = [permute(piece, lambda i: i - 1) for piece in pieces]
    products = products_of(coeffs, g_cond, g_val, band_first)
    products = products.reshape(k_local, modes, bands_c * bands_v, excitons)
    places = jnp.mod(k_plus_q - me * k_local, k_local * size)

    def rows(step, after):
        pick = jnp.concatenate((places, jnp.stack((z ^ (3 - step), core, x))))
        pick, _ = lax.optimization_barrier((pick, after))
        mine, other, send = rows_of(pick, flat, following[step], products)
        return mine, other, permute(send, lambda i: i ^ 1)

    half = width // 4

    def summed(step, from_core):
        from_core = from_core.astype(jnp.float32)
        return step[0] + from_core[:half], step[1] + from_core[half:]

    def over(value, bits):
        return permute(value.astype(jnp.bfloat16), lambda i: i ^ bits)

    def total_of(value, *arrived):
        for array in arrived:
            value = value + array.astype(jnp.float32)
        return value

    step_0 = rows(0, products)
    step_1 = rows(1, step_0[0])
    step_2 = rows(2, step_1[0])
    core_0, core_1, core_2, following[3] = lax.optimization_barrier(
        (step_0[2], step_1[2], step_2[2], following[3])
    )
    mine_0, other_0 = summed(step_0, core_0)
    mine_1, other_1 = summed(step_1, core_1)
    mine_2, other_2 = summed(step_2, core_2)
    sends = [value.astype(jnp.bfloat16) for value in (mine_0, other_0, other_1, other_2)]
    step_3 = rows(3, sends)
    far = over(sends[0], 4), over(sends[1], 6)
    across_1 = over(sends[2], 2)
    send_2, _ = lax.optimization_barrier((sends[3], step_3[0]))
    across_2 = over(send_2, 2)
    mine_1, _ = lax.optimization_barrier((mine_1, step_3[0]))
    pair = total_of(mine_1, across_1, *far)
    mine_3, other_3 = summed(step_3, step_3[2])
    mine_2, _ = lax.optimization_barrier((mine_2, (pair, other_3)))
    pair = over(pair, 8)
    near = over(total_of(mine_2, across_2), 4)
    total = total_of(mine_3, over(other_3, 2), pair, near)
    return (total * norm_factor).reshape(width // 4, modes, excitons)


def on_any(coeffs, g_cond, g_val, k_plus_q, band_first, norm_factor):
    k_local, bands_c, bands_v, excitons = coeffs.shape
    modes = g_cond.shape[1]
    size = lax.axis_size("ka")
    depth = bands_c * bands_v
    flat = coeffs.reshape(k_local, depth, excitons)
    blocks = jnp.concatenate((flat, permute(flat, lambda i: i - 1)), 0)
    offsets = jnp.mod(k_plus_q - lax.axis_index("ka") * k_local, k_local * size)
    products = products_of(coeffs, g_cond, g_val, band_first)
    products = products.reshape(k_local, modes, depth, excitons)
    partners = [
        lax.dynamic_index_in_dim(blocks, offsets[k], 0, keepdims=False) for k in range(k_local)
    ]
    running = jnp.einsum(
        "kds,kmdt->smt", jnp.stack(partners), products, preferred_element_type=jnp.float32
    )
    return lax.psum_scatter(running * norm_factor, "ka", scatter_dimension=0, tiled=True)


def shards(coeffs, g_cond, g_val, k_plus_q, band_first):
    k_local, bands_c, bands_v, excitons = coeffs.shape
    size = lax.axis_size("ka")
    norm_factor = 1.0 / math.sqrt(bands_c * bands_v * k_local * size)
    whole_tiles = excitons % (4 * 128) == 0
    plan = on_two_by_four if size == 16 and whole_tiles else on_any
    return plan(coeffs, g_cond, g_val, k_plus_q, band_first, norm_factor)


def solution(mesh):
    in_specs = (
        P(("groups", "ka"), None, None, None),
        P(("groups", "ka"), None, None, None),
        P(("groups", "ka"), None, None, None),
        P(("groups", "ka")),
        P("groups", None),
    )
    out_specs = P(("groups", "ka"), None, None)
    return jax.shard_map(shards, mesh=mesh, in_specs=in_specs, out_specs=out_specs, check_vma=False)
```

```python
import functools
import math

import jax
import jax.numpy as jnp
from jax import lax
from jax.experimental import pallas as pl
from jax.experimental.pallas import tpu as pltpu
from jax.sharding import PartitionSpec as P

MIB = 1024 * 1024


def permute(x, target):
    size = lax.axis_size("ka")
    pairs = [(i, target(i)) for i in range(size)]
    return lax.ppermute(x, "ka", [(i, j % size) for i, j in pairs if j is not None])


def nt_dot(a, b):
    return lax.dot_general(a, b, (((1,), (1,)), ((), ())), preferred_element_type=jnp.float32)


def iotas(rows, cols):
    shape = (rows, cols)
    return lax.broadcasted_iota(jnp.int32, shape, 0), lax.broadcasted_iota(jnp.int32, shape, 1)


def ones_where(condition):
    return jnp.where(condition, 1.0, 0.0).astype(jnp.bfloat16)


PART_C, PART_V = 8, 16


def fill_weights(first_ref, cond_ref, val_ref, we_ref, wh_ref):
    _, modes, bands_c, _ = cond_ref.shape
    bands_v = val_ref.shape[2]
    rows_e, rows_h = bands_c * PART_V, PART_C * bands_v
    row, col = iotas(rows_e, bands_c)
    take = ones_where(row // PART_V == col)
    row, col = iotas(rows_e, rows_e)
    for m in range(modes):
        half = jnp.dot(take, cond_ref[0, m], preferred_element_type=jnp.float32)
        full = nt_dot(half.astype(jnp.bfloat16), take)
        keep = (row % PART_V == col % PART_V) & (row // PART_V >= first_ref[m, 0])
        we_ref[m * rows_e:(m + 1) * rows_e, :] = jnp.where(keep, full, 0.0).astype(jnp.bfloat16)
    row, col = iotas(rows_h, bands_v)
    take = ones_where(row % bands_v == col)
    row, col = iotas(rows_h, rows_h)
    for m in range(modes):
        half = nt_dot(take, val_ref[0, m])
        full = nt_dot(half.astype(jnp.bfloat16), take)
        keep = (row // bands_v == col // bands_v) & (row % bands_v >= first_ref[m, 1])
        wh_ref[m * rows_h:(m + 1) * rows_h, :] = jnp.where(keep, full, 0.0).astype(jnp.bfloat16)


def products_kernel(first_ref, coeffs_ref, cond_ref, val_ref, out_ref, we_ref, wh_ref):
    _, bands_c, bands_v, tile = coeffs_ref.shape
    modes = cond_ref.shape[1]
    rows_e, rows_h = bands_c * PART_V, PART_C * bands_v

    @pl.when(pl.program_id(1) == 0)
    def _():
        fill_weights(first_ref, cond_ref, val_ref, we_ref, wh_ref)

    electron = []
    for h in range(bands_v // PART_V):
        x = coeffs_ref[0, :, h * PART_V:(h + 1) * PART_V, :].reshape(rows_e, tile)
        e = jnp.dot(we_ref[...], x, preferred_element_type=jnp.float32)
        electron.append(e.reshape(modes, bands_c, PART_V, tile))
    for q in range(bands_c // PART_C):
        own = slice(q * PART_C, (q + 1) * PART_C)
        y = coeffs_ref[0, own].reshape(rows_h, tile)
        hole = jnp.dot(wh_ref[...], y, preferred_element_type=jnp.float32)
        hole = hole.reshape(modes, PART_C, bands_v, tile)
        for m in range(modes):
            for h in range(bands_v // PART_V):
                cols = slice(h * PART_V, (h + 1) * PART_V)
                value = electron[h][m, own] - hole[m, :, cols]
                out_ref[0, m, own, cols, :] = value.astype(jnp.bfloat16)


def products_of(coeffs, g_cond, g_val, band_first):
    k_local, bands_c, bands_v, excitons = coeffs.shape
    modes = g_cond.shape[1]
    tile = 256
    rows_e, rows_h = bands_c * PART_V, PART_C * bands_v
    depth = bands_c * bands_v
    return pl.pallas_call(
        products_kernel,
        out_shape=jax.ShapeDtypeStruct((k_local, modes, bands_c, bands_v, excitons), jnp.bfloat16),
        grid=(k_local, excitons // tile),
        in_specs=[
            pl.BlockSpec(memory_space=pltpu.SMEM),
            pl.BlockSpec((1, bands_c, bands_v, tile), lambda k, s: (k, 0, 0, s)),
            pl.BlockSpec((1, modes, bands_c, bands_c), lambda k, s: (k, 0, 0, 0)),
            pl.BlockSpec((1, modes, bands_v, bands_v), lambda k, s: (k, 0, 0, 0)),
        ],
        out_specs=pl.BlockSpec((1, modes, bands_c, bands_v, tile), lambda k, s: (k, 0, 0, 0, s)),
        scratch_shapes=[
            pltpu.VMEM((modes * rows_e, rows_e), jnp.bfloat16),
            pltpu.VMEM((modes * rows_h, rows_h), jnp.bfloat16),
        ],
        compiler_params=pltpu.CompilerParams(vmem_limit_bytes=60 * MIB),
        cost_estimate=pl.CostEstimate(
            flops=2 * k_local * modes * excitons * depth * (rows_e + rows_h),
            bytes_accessed=2 * coeffs.size * (1 + modes),
            transcendentals=0,
        ),
    )(band_first, coeffs, g_cond, g_val)


def turn_kernel(first, coeffs_ref, *refs):
    *out_refs, held, sems = refs
    pieces, k_local, parts, rows, width = held.shape
    size = lax.axis_size("ka")
    behind_z = lax.shift_right_logical(lax.rem(lax.axis_index("ka") + size - 1, size), 2)

    def copy(i, k, p):
        columns = pl.ds(pl.multiple_of((behind_z ^ (3 - first - i)) * width, width), width)
        source = coeffs_ref.at[k, pl.ds(p * rows, rows), columns]
        return pltpu.make_async_copy(source, held.at[i, k, p], sems.at[i, k, p])

    steps = [(i, k, p) for i in range(pieces) for k in range(k_local) for p in range(parts)]
    for step in steps:
        copy(*step).start()
    for step in steps:
        i, k, p = step
        copy(*step).wait()
        out_refs[i][k, :, p * rows:(p + 1) * rows] = held[i, k, p].T


def turned_pieces(flat, first, pieces, width):
    k_local, depth, _ = flat.shape
    parts = 2
    return pl.pallas_call(
        functools.partial(turn_kernel, first),
        out_shape=[jax.ShapeDtypeStruct((k_local, width, depth), jnp.bfloat16)] * pieces,
        in_specs=[pl.BlockSpec(memory_space=pl.ANY)],
        out_specs=[pl.BlockSpec(memory_space=pltpu.VMEM)] * pieces,
        scratch_shapes=[
            pltpu.VMEM((pieces, k_local, parts, depth // parts, width), jnp.bfloat16),
            pltpu.SemaphoreType.DMA((pieces, k_local, parts)),
        ],
        compiler_params=pltpu.CompilerParams(vmem_limit_bytes=60 * MIB),
        cost_estimate=pl.CostEstimate(
            flops=0, bytes_accessed=4 * pieces * k_local * depth * width, transcendentals=0
        ),
    )(flat)


def rows_kernel(pick_ref, own_ref, next_ref, right_ref, mine_ref, other_ref, send_ref, *refs):
    own_held, next_held, held, left, own_sems, next_sems, sems = refs
    k_local, depth, width = own_held.shape
    tiles, _, _, tile = held.shape
    per_mode = right_ref.shape[3] // tile
    core, x = pick_ref[k_local + 1], pick_ref[k_local + 2]
    columns = pl.ds(pl.multiple_of(pick_ref[k_local] * width, width), width)
    near = [pick_ref[k] < k_local for k in range(k_local)]

    def copy_own(k):
        source = own_ref.at[jnp.minimum(pick_ref[k], k_local - 1), :, columns]
        return pltpu.make_async_copy(source, own_held.at[k], own_sems.at[k])

    def copy_next(k):
        source = next_ref.at[jnp.maximum(pick_ref[k] - k_local, 0)]
        return pltpu.make_async_copy(source, next_held.at[k], next_sems.at[k])

    def copy_right(t, k):
        source = right_ref.at[k, t // per_mode, :, pl.ds(t % per_mode * tile, tile)]
        return pltpu.make_async_copy(source, held.at[t, k], sems.at[t, k])

    for k in range(k_local):
        copy_own(k).start()
        copy_next(k).start()
    for t in range(tiles):
        for k in range(k_local):
            copy_right(t, k).start()
    for k in range(k_local):
        copy_own(k).wait()
        copy_next(k).wait()

        @pl.when(near[k])
        def _():
            left[:, k * depth:(k + 1) * depth] = own_held[k].T

        @pl.when(jnp.logical_not(near[k]))
        def _():
            left[:, k * depth:(k + 1) * depth] = next_held[k]

    for t in range(tiles):
        for k in range(k_local):
            copy_right(t, k).wait()
        right = held[t].reshape(k_local * depth, tile)
        total = jnp.dot(left[...], right, preferred_element_type=jnp.float32)
        parts = total.reshape(2, 2, width // 4, tile)
        mine = jnp.where(x == 0, parts[0], parts[1])
        other = jnp.where(x == 0, parts[1], parts[0])
        place = slice(t * tile, (t + 1) * tile)
        mine_ref[:, place] = jnp.where(core == 0, mine[0], mine[1])
        other_ref[:, place] = jnp.where(core == 0, other[0], other[1])
        send_ref[:width // 4, place] = jnp.where(core == 0, mine[1], mine[0]).astype(jnp.bfloat16)
        send_ref[width // 4:, place] = jnp.where(core == 0, other[1], other[0]).astype(jnp.bfloat16)


def rows_of(pick, own, following, products):
    k_local, width, depth = following.shape
    modes, excitons = products.shape[1], products.shape[3]
    columns, tile = modes * excitons, 512
    tiles = columns // tile
    return pl.pallas_call(
        rows_kernel,
        out_shape=[
            jax.ShapeDtypeStruct((width // 4, columns), jnp.float32),
            jax.ShapeDtypeStruct((width // 4, columns), jnp.float32),
            jax.ShapeDtypeStruct((width // 2, columns), jnp.bfloat16),
        ],
        in_specs=[pl.BlockSpec(memory_space=pltpu.SMEM)]
        + [pl.BlockSpec(memory_space=pl.ANY)] * 3,
        out_specs=[pl.BlockSpec(memory_space=pltpu.VMEM)] * 3,
        scratch_shapes=[
            pltpu.VMEM((k_local, depth, width), jnp.bfloat16),
            pltpu.VMEM((k_local, width, depth), jnp.bfloat16),
            pltpu.VMEM((tiles, k_local, depth, tile), jnp.bfloat16),
            pltpu.VMEM((width, k_local * depth), jnp.bfloat16),
            pltpu.SemaphoreType.DMA((k_local,)),
            pltpu.SemaphoreType.DMA((k_local,)),
            pltpu.SemaphoreType.DMA((tiles, k_local)),
        ],
        compiler_params=pltpu.CompilerParams(vmem_limit_bytes=50 * MIB),
        cost_estimate=pl.CostEstimate(
            flops=2 * k_local * depth * width * columns,
            bytes_accessed=2 * k_local * depth * columns,
            transcendentals=0,
        ),
    )(pick, own, following, products)


def on_two_by_four(coeffs, g_cond, g_val, k_plus_q, band_first, norm_factor):
    k_local, bands_c, bands_v, excitons = coeffs.shape
    modes = g_cond.shape[1]
    size = lax.axis_size("ka")
    width = excitons // 4
    me = lax.axis_index("ka")
    core, x, z = me & 1, me >> 1 & 1, me >> 2
    flat = coeffs.reshape(k_local, bands_c * bands_v, excitons)

    pieces = turned_pieces(flat, 0, 1, width)
    rest, _ = lax.optimization_barrier((flat, pieces))
    pieces += turned_pieces(rest, 1, 3, width)
    following = [permute(piece, lambda i: i - 1) for piece in pieces]
    products = products_of(coeffs, g_cond, g_val, band_first)
    products = products.reshape(k_local, modes, bands_c * bands_v, excitons)
    places = jnp.mod(k_plus_q - me * k_local, k_local * size)

    def rows(step, after):
        pick = jnp.concatenate((places, jnp.stack((z ^ (3 - step), core, x))))
        pick, _ = lax.optimization_barrier((pick, after))
        mine, other, send = rows_of(pick, flat, following[step], products)
        return mine, other, permute(send, lambda i: i ^ 1)

    half = width // 4

    def summed(step, from_core):
        from_core = from_core.astype(jnp.float32)
        return step[0] + from_core[:half], step[1] + from_core[half:]

    def over(value, bits):
        return permute(value.astype(jnp.bfloat16), lambda i: i ^ bits)

    def total_of(value, *arrived):
        for array in arrived:
            value = value + array.astype(jnp.float32)
        return value

    step_0 = rows(0, products)
    step_1 = rows(1, step_0[0])
    step_2 = rows(2, step_1[0])
    core_0, core_1, core_2, following[3] = lax.optimization_barrier(
        (step_0[2], step_1[2], step_2[2], following[3])
    )
    mine_0, other_0 = summed(step_0, core_0)
    mine_1, other_1 = summed(step_1, core_1)
    mine_2, other_2 = summed(step_2, core_2)
    both = jnp.concatenate((other_1.astype(jnp.bfloat16), other_2.astype(jnp.bfloat16)))
    sends = mine_0.astype(jnp.bfloat16), other_0.astype(jnp.bfloat16)
    step_3 = rows(3, (both, sends))
    across = over(both, 2)
    far = over(sends[0], 4), over(sends[1], 6)
    mine_1, _ = lax.optimization_barrier((mine_1, step_3[0]))
    pair = total_of(mine_1, across[:half], *far)
    mine_2, _ = lax.optimization_barrier((mine_2, pair))
    pair = over(pair, 8)
    near = over(total_of(mine_2, across[half:]), 4)
    core_3, _ = lax.optimization_barrier((step_3[2], mine_2))
    mine_3, other_3 = summed(step_3, core_3)
    mine_3, other_3 = lax.optimization_barrier((mine_3, other_3.astype(jnp.bfloat16)))
    total = lax.optimization_barrier(total_of(mine_3, pair))
    total = total_of(total, over(other_3, 2), near)
    return (total * norm_factor).reshape(width // 4, modes, excitons)


def on_any(coeffs, g_cond, g_val, k_plus_q, band_first, norm_factor):
    k_local, bands_c, bands_v, excitons = coeffs.shape
    modes = g_cond.shape[1]
    size = lax.axis_size("ka")
    depth = bands_c * bands_v
    flat = coeffs.reshape(k_local, depth, excitons)
    blocks = jnp.concatenate((flat, permute(flat, lambda i: i - 1)), 0)
    offsets = jnp.mod(k_plus_q - lax.axis_index("ka") * k_local, k_local * size)
    products = products_of(coeffs, g_cond, g_val, band_first)
    products = products.reshape(k_local, modes, depth, excitons)
    partners = [
        lax.dynamic_index_in_dim(blocks, offsets[k], 0, keepdims=False) for k in range(k_local)
    ]
    running = jnp.einsum(
        "kds,kmdt->smt", jnp.stack(partners), products, preferred_element_type=jnp.float32
    )
    return lax.psum_scatter(running * norm_factor, "ka", scatter_dimension=0, tiled=True)


def shards(coeffs, g_cond, g_val, k_plus_q, band_first):
    k_local, bands_c, bands_v, excitons = coeffs.shape
    size = lax.axis_size("ka")
    norm_factor = 1.0 / math.sqrt(bands_c * bands_v * k_local * size)
    whole_tiles = excitons % (4 * 128) == 0
    plan = on_two_by_four if size == 16 and whole_tiles else on_any
    return plan(coeffs, g_cond, g_val, k_plus_q, band_first, norm_factor)


def solution(mesh):
    in_specs = (
        P(("groups", "ka"), None, None, None),
        P(("groups", "ka"), None, None, None),
        P(("groups", "ka"), None, None, None),
        P(("groups", "ka")),
        P("groups", None),
    )
    out_specs = P(("groups", "ka"), None, None)
    return jax.shard_map(shards, mesh=mesh, in_specs=in_specs, out_specs=out_specs, check_vma=False)
```

```python
import functools
import math

import jax
import jax.numpy as jnp
from jax import lax
from jax.experimental import pallas as pl
from jax.experimental.pallas import tpu as pltpu
from jax.sharding import PartitionSpec as P

MIB = 1024 * 1024


def permute(x, target):
    size = lax.axis_size("ka")
    pairs = [(i, target(i)) for i in range(size)]
    return lax.ppermute(x, "ka", [(i, j % size) for i, j in pairs if j is not None])


def nt_dot(a, b):
    return lax.dot_general(a, b, (((1,), (1,)), ((), ())), preferred_element_type=jnp.float32)


def iotas(rows, cols):
    shape = (rows, cols)
    return lax.broadcasted_iota(jnp.int32, shape, 0), lax.broadcasted_iota(jnp.int32, shape, 1)


def ones_where(condition):
    return jnp.where(condition, 1.0, 0.0).astype(jnp.bfloat16)


PART_C, PART_V = 8, 16


def fill_weights(first_ref, cond_ref, val_ref, we_ref, wh_ref):
    _, modes, bands_c, _ = cond_ref.shape
    bands_v = val_ref.shape[2]
    rows_e, rows_h = bands_c * PART_V, PART_C * bands_v
    row, col = iotas(rows_e, bands_c)
    take = ones_where(row // PART_V == col)
    row, col = iotas(rows_e, rows_e)
    for m in range(modes):
        half = jnp.dot(take, cond_ref[0, m], preferred_element_type=jnp.float32)
        full = nt_dot(half.astype(jnp.bfloat16), take)
        keep = (row % PART_V == col % PART_V) & (row // PART_V >= first_ref[m, 0])
        we_ref[m * rows_e:(m + 1) * rows_e, :] = jnp.where(keep, full, 0.0).astype(jnp.bfloat16)
    row, col = iotas(rows_h, bands_v)
    take = ones_where(row % bands_v == col)
    row, col = iotas(rows_h, rows_h)
    for m in range(modes):
        half = nt_dot(take, val_ref[0, m])
        full = nt_dot(half.astype(jnp.bfloat16), take)
        keep = (row // bands_v == col // bands_v) & (row % bands_v >= first_ref[m, 1])
        wh_ref[m * rows_h:(m + 1) * rows_h, :] = jnp.where(keep, full, 0.0).astype(jnp.bfloat16)


def products_kernel(first_ref, coeffs_ref, cond_ref, val_ref, out_ref, we_ref, wh_ref):
    _, bands_c, bands_v, tile = coeffs_ref.shape
    modes = cond_ref.shape[1]
    rows_e, rows_h = bands_c * PART_V, PART_C * bands_v

    @pl.when(pl.program_id(1) == 0)
    def _():
        fill_weights(first_ref, cond_ref, val_ref, we_ref, wh_ref)

    electron = []
    for h in range(bands_v // PART_V):
        x = coeffs_ref[0, :, h * PART_V:(h + 1) * PART_V, :].reshape(rows_e, tile)
        e = jnp.dot(we_ref[...], x, preferred_element_type=jnp.float32)
        electron.append(e.reshape(modes, bands_c, PART_V, tile))
    for q in range(bands_c // PART_C):
        own = slice(q * PART_C, (q + 1) * PART_C)
        y = coeffs_ref[0, own].reshape(rows_h, tile)
        hole = jnp.dot(wh_ref[...], y, preferred_element_type=jnp.float32)
        hole = hole.reshape(modes, PART_C, bands_v, tile)
        for m in range(modes):
            for h in range(bands_v // PART_V):
                cols = slice(h * PART_V, (h + 1) * PART_V)
                value = electron[h][m, own] - hole[m, :, cols]
                out_ref[0, m, own, cols, :] = value.astype(jnp.bfloat16)


def products_of(coeffs, g_cond, g_val, band_first):
    k_local, bands_c, bands_v, excitons = coeffs.shape
    modes = g_cond.shape[1]
    tile = 256
    rows_e, rows_h = bands_c * PART_V, PART_C * bands_v
    depth = bands_c * bands_v
    return pl.pallas_call(
        products_kernel,
        out_shape=jax.ShapeDtypeStruct((k_local, modes, bands_c, bands_v, excitons), jnp.bfloat16),
        grid=(k_local, excitons // tile),
        in_specs=[
            pl.BlockSpec(memory_space=pltpu.SMEM),
            pl.BlockSpec((1, bands_c, bands_v, tile), lambda k, s: (k, 0, 0, s)),
            pl.BlockSpec((1, modes, bands_c, bands_c), lambda k, s: (k, 0, 0, 0)),
            pl.BlockSpec((1, modes, bands_v, bands_v), lambda k, s: (k, 0, 0, 0)),
        ],
        out_specs=pl.BlockSpec((1, modes, bands_c, bands_v, tile), lambda k, s: (k, 0, 0, 0, s)),
        scratch_shapes=[
            pltpu.VMEM((modes * rows_e, rows_e), jnp.bfloat16),
            pltpu.VMEM((modes * rows_h, rows_h), jnp.bfloat16),
        ],
        compiler_params=pltpu.CompilerParams(vmem_limit_bytes=60 * MIB),
        cost_estimate=pl.CostEstimate(
            flops=2 * k_local * modes * excitons * depth * (rows_e + rows_h),
            bytes_accessed=2 * coeffs.size * (1 + modes),
            transcendentals=0,
        ),
    )(band_first, coeffs, g_cond, g_val)


def turn_kernel(first, coeffs_ref, *refs):
    *out_refs, held, sems = refs
    pieces, k_local, parts, rows, width = held.shape
    size = lax.axis_size("ka")
    behind_z = lax.shift_right_logical(lax.rem(lax.axis_index("ka") + size - 1, size), 2)

    def copy(i, k, p):
        columns = pl.ds(pl.multiple_of((behind_z ^ (3 - first - i)) * width, width), width)
        source = coeffs_ref.at[k, pl.ds(p * rows, rows), columns]
        return pltpu.make_async_copy(source, held.at[i, k, p], sems.at[i, k, p])

    steps = [(i, k, p) for i in range(pieces) for k in range(k_local) for p in range(parts)]
    for step in steps:
        copy(*step).start()
    for step in steps:
        i, k, p = step
        copy(*step).wait()
        out_refs[i][k, :, p * rows:(p + 1) * rows] = held[i, k, p].T


def turned_pieces(flat, first, pieces, width):
    k_local, depth, _ = flat.shape
    parts = 2
    return pl.pallas_call(
        functools.partial(turn_kernel, first),
        out_shape=[jax.ShapeDtypeStruct((k_local, width, depth), jnp.bfloat16)] * pieces,
        in_specs=[pl.BlockSpec(memory_space=pl.ANY)],
        out_specs=[pl.BlockSpec(memory_space=pltpu.VMEM)] * pieces,
        scratch_shapes=[
            pltpu.VMEM((pieces, k_local, parts, depth // parts, width), jnp.bfloat16),
            pltpu.SemaphoreType.DMA((pieces, k_local, parts)),
        ],
        compiler_params=pltpu.CompilerParams(vmem_limit_bytes=60 * MIB),
        cost_estimate=pl.CostEstimate(
            flops=0, bytes_accessed=4 * pieces * k_local * depth * width, transcendentals=0
        ),
    )(flat)


def rows_kernel(pick_ref, own_ref, next_ref, right_ref, mine_ref, other_ref, send_ref, *refs):
    own_held, next_held, held, left, own_sems, next_sems, sems = refs
    k_local, depth, width = own_held.shape
    tiles, _, _, tile = held.shape
    per_mode = right_ref.shape[3] // tile
    core, x = pick_ref[k_local + 1], pick_ref[k_local + 2]
    columns = pl.ds(pl.multiple_of(pick_ref[k_local] * width, width), width)
    near = [pick_ref[k] < k_local for k in range(k_local)]

    def copy_own(k):
        source = own_ref.at[jnp.minimum(pick_ref[k], k_local - 1), :, columns]
        return pltpu.make_async_copy(source, own_held.at[k], own_sems.at[k])

    def copy_next(k):
        source = next_ref.at[jnp.maximum(pick_ref[k] - k_local, 0)]
        return pltpu.make_async_copy(source, next_held.at[k], next_sems.at[k])

    def copy_right(t, k):
        source = right_ref.at[k, t // per_mode, :, pl.ds(t % per_mode * tile, tile)]
        return pltpu.make_async_copy(source, held.at[t, k], sems.at[t, k])

    for k in range(k_local):
        copy_own(k).start()
        copy_next(k).start()
    for t in range(tiles):
        for k in range(k_local):
            copy_right(t, k).start()
    for k in range(k_local):
        copy_own(k).wait()
        copy_next(k).wait()

        @pl.when(near[k])
        def _():
            left[:, k * depth:(k + 1) * depth] = own_held[k].T

        @pl.when(jnp.logical_not(near[k]))
        def _():
            left[:, k * depth:(k + 1) * depth] = next_held[k]

    for t in range(tiles):
        for k in range(k_local):
            copy_right(t, k).wait()
        right = held[t].reshape(k_local * depth, tile)
        total = jnp.dot(left[...], right, preferred_element_type=jnp.float32)
        parts = total.reshape(2, 2, width // 4, tile)
        mine = jnp.where(x == 0, parts[0], parts[1])
        other = jnp.where(x == 0, parts[1], parts[0])
        place = slice(t * tile, (t + 1) * tile)
        mine_ref[:, place] = jnp.where(core == 0, mine[0], mine[1])
        other_ref[:, place] = jnp.where(core == 0, other[0], other[1])
        send_ref[:width // 4, place] = jnp.where(core == 0, mine[1], mine[0]).astype(jnp.bfloat16)
        send_ref[width // 4:, place] = jnp.where(core == 0, other[1], other[0]).astype(jnp.bfloat16)


def rows_of(pick, own, following, products):
    k_local, width, depth = following.shape
    modes, excitons = products.shape[1], products.shape[3]
    columns, tile = modes * excitons, 512
    tiles = columns // tile
    return pl.pallas_call(
        rows_kernel,
        out_shape=[
            jax.ShapeDtypeStruct((width // 4, columns), jnp.float32),
            jax.ShapeDtypeStruct((width // 4, columns), jnp.float32),
            jax.ShapeDtypeStruct((width // 2, columns), jnp.bfloat16),
        ],
        in_specs=[pl.BlockSpec(memory_space=pltpu.SMEM)]
        + [pl.BlockSpec(memory_space=pl.ANY)] * 3,
        out_specs=[pl.BlockSpec(memory_space=pltpu.VMEM)] * 3,
        scratch_shapes=[
            pltpu.VMEM((k_local, depth, width), jnp.bfloat16),
            pltpu.VMEM((k_local, width, depth), jnp.bfloat16),
            pltpu.VMEM((tiles, k_local, depth, tile), jnp.bfloat16),
            pltpu.VMEM((width, k_local * depth), jnp.bfloat16),
            pltpu.SemaphoreType.DMA((k_local,)),
            pltpu.SemaphoreType.DMA((k_local,)),
            pltpu.SemaphoreType.DMA((tiles, k_local)),
        ],
        compiler_params=pltpu.CompilerParams(vmem_limit_bytes=50 * MIB),
        cost_estimate=pl.CostEstimate(
            flops=2 * k_local * depth * width * columns,
            bytes_accessed=2 * k_local * depth * columns,
            transcendentals=0,
        ),
    )(pick, own, following, products)


def on_two_by_four(coeffs, g_cond, g_val, k_plus_q, band_first, norm_factor):
    k_local, bands_c, bands_v, excitons = coeffs.shape
    modes = g_cond.shape[1]
    size = lax.axis_size("ka")
    width = excitons // 4
    me = lax.axis_index("ka")
    core, x, z = me & 1, me >> 1 & 1, me >> 2
    flat = coeffs.reshape(k_local, bands_c * bands_v, excitons)

    pieces = turned_pieces(flat, 0, 1, width)
    rest, _ = lax.optimization_barrier((flat, pieces))
    pieces += turned_pieces(rest, 1, 3, width)
    following = [permute(piece, lambda i: i - 1) for piece in pieces]
    products = products_of(coeffs, g_cond, g_val, band_first)
    products = products.reshape(k_local, modes, bands_c * bands_v, excitons)
    places = jnp.mod(k_plus_q - me * k_local, k_local * size)

    def rows(step, after):
        pick = jnp.concatenate((places, jnp.stack((z ^ (3 - step), core, x))))
        pick, _ = lax.optimization_barrier((pick, after))
        mine, other, send = rows_of(pick, flat, following[step], products)
        return mine, other, permute(send, lambda i: i ^ 1)

    half = width // 4

    def summed(step, from_core):
        from_core = from_core.astype(jnp.float32)
        return step[0] + from_core[:half], step[1] + from_core[half:]

    def over(value, bits):
        return permute(value.astype(jnp.bfloat16), lambda i: i ^ bits)

    def total_of(value, *arrived):
        for array in arrived:
            value = value + array.astype(jnp.float32)
        return value

    step_0 = rows(0, products)
    step_1 = rows(1, step_0[0])
    step_2 = rows(2, step_1[0])
    core_0, core_1, core_2, following[3] = lax.optimization_barrier(
        (step_0[2], step_1[2], step_2[2], following[3])
    )
    mine_0, other_0 = summed(step_0, core_0)
    mine_1, other_1 = summed(step_1, core_1)
    mine_2, other_2 = summed(step_2, core_2)
    sends = [value.astype(jnp.bfloat16) for value in (mine_0, other_0, other_1, other_2)]
    step_3 = rows(3, sends)
    across_1, across_2 = over(sends[2], 2), over(sends[3], 2)
    far = over(sends[0], 4), over(sends[1], 6)
    mine_1, _ = lax.optimization_barrier((mine_1, step_3[0]))
    mine_1 = total_of(mine_1, across_1)
    pair = total_of(lax.optimization_barrier(mine_1), *far)
    mine_2, _ = lax.optimization_barrier((mine_2, pair))
    pair = over(pair, 8)
    near = over(total_of(mine_2, across_2), 4)
    core_3, _ = lax.optimization_barrier((step_3[2], mine_2))
    mine_3, other_3 = summed(step_3, core_3)
    mine_3, other_3 = lax.optimization_barrier((mine_3, other_3.astype(jnp.bfloat16)))
    total = lax.optimization_barrier(total_of(mine_3, pair))
    total = total_of(total, over(other_3, 2), near)
    return (total * norm_factor).reshape(width // 4, modes, excitons)


def on_any(coeffs, g_cond, g_val, k_plus_q, band_first, norm_factor):
    k_local, bands_c, bands_v, excitons = coeffs.shape
    modes = g_cond.shape[1]
    size = lax.axis_size("ka")
    depth = bands_c * bands_v
    flat = coeffs.reshape(k_local, depth, excitons)
    blocks = jnp.concatenate((flat, permute(flat, lambda i: i - 1)), 0)
    offsets = jnp.mod(k_plus_q - lax.axis_index("ka") * k_local, k_local * size)
    products = products_of(coeffs, g_cond, g_val, band_first)
    products = products.reshape(k_local, modes, depth, excitons)
    partners = [
        lax.dynamic_index_in_dim(blocks, offsets[k], 0, keepdims=False) for k in range(k_local)
    ]
    running = jnp.einsum(
        "kds,kmdt->smt", jnp.stack(partners), products, preferred_element_type=jnp.float32
    )
    return lax.psum_scatter(running * norm_factor, "ka", scatter_dimension=0, tiled=True)


def shards(coeffs, g_cond, g_val, k_plus_q, band_first):
    k_local, bands_c, bands_v, excitons = coeffs.shape
    size = lax.axis_size("ka")
    norm_factor = 1.0 / math.sqrt(bands_c * bands_v * k_local * size)
    whole_tiles = excitons % (4 * 128) == 0
    plan = on_two_by_four if size == 16 and whole_tiles else on_any
    return plan(coeffs, g_cond, g_val, k_plus_q, band_first, norm_factor)


def solution(mesh):
    in_specs = (
        P(("groups", "ka"), None, None, None),
        P(("groups", "ka"), None, None, None),
        P(("groups", "ka"), None, None, None),
        P(("groups", "ka")),
        P("groups", None),
    )
    out_specs = P(("groups", "ka"), None, None)
    return jax.shard_map(shards, mesh=mesh, in_specs=in_specs, out_specs=out_specs, check_vma=False)
```

```python
import functools
import math

import jax
import jax.numpy as jnp
from jax import lax
from jax.experimental import pallas as pl
from jax.experimental.pallas import tpu as pltpu
from jax.sharding import PartitionSpec as P

MIB = 1024 * 1024


def permute(x, target):
    size = lax.axis_size("ka")
    pairs = [(i, target(i)) for i in range(size)]
    return lax.ppermute(x, "ka", [(i, j % size) for i, j in pairs if j is not None])


def nt_dot(a, b):
    return lax.dot_general(a, b, (((1,), (1,)), ((), ())), preferred_element_type=jnp.float32)


def iotas(rows, cols):
    shape = (rows, cols)
    return lax.broadcasted_iota(jnp.int32, shape, 0), lax.broadcasted_iota(jnp.int32, shape, 1)


def ones_where(condition):
    return jnp.where(condition, 1.0, 0.0).astype(jnp.bfloat16)


PART_C, PART_V = 8, 16


def fill_weights(first_ref, cond_ref, val_ref, we_ref, wh_ref):
    _, modes, bands_c, _ = cond_ref.shape
    bands_v = val_ref.shape[2]
    rows_e, rows_h = bands_c * PART_V, PART_C * bands_v
    row, col = iotas(rows_e, bands_c)
    take = ones_where(row // PART_V == col)
    row, col = iotas(rows_e, rows_e)
    for m in range(modes):
        half = jnp.dot(take, cond_ref[0, m], preferred_element_type=jnp.float32)
        full = nt_dot(half.astype(jnp.bfloat16), take)
        keep = (row % PART_V == col % PART_V) & (row // PART_V >= first_ref[m, 0])
        we_ref[m * rows_e:(m + 1) * rows_e, :] = jnp.where(keep, full, 0.0).astype(jnp.bfloat16)
    row, col = iotas(rows_h, bands_v)
    take = ones_where(row % bands_v == col)
    row, col = iotas(rows_h, rows_h)
    for m in range(modes):
        half = nt_dot(take, val_ref[0, m])
        full = nt_dot(half.astype(jnp.bfloat16), take)
        keep = (row // bands_v == col // bands_v) & (row % bands_v >= first_ref[m, 1])
        wh_ref[m * rows_h:(m + 1) * rows_h, :] = jnp.where(keep, full, 0.0).astype(jnp.bfloat16)


def products_kernel(first_ref, coeffs_ref, cond_ref, val_ref, out_ref, we_ref, wh_ref):
    _, bands_c, bands_v, tile = coeffs_ref.shape
    modes = cond_ref.shape[1]
    rows_e, rows_h = bands_c * PART_V, PART_C * bands_v

    @pl.when(pl.program_id(1) == 0)
    def _():
        fill_weights(first_ref, cond_ref, val_ref, we_ref, wh_ref)

    electron = []
    for h in range(bands_v // PART_V):
        x = coeffs_ref[0, :, h * PART_V:(h + 1) * PART_V, :].reshape(rows_e, tile)
        e = jnp.dot(we_ref[...], x, preferred_element_type=jnp.float32)
        electron.append(e.reshape(modes, bands_c, PART_V, tile))
    for q in range(bands_c // PART_C):
        own = slice(q * PART_C, (q + 1) * PART_C)
        y = coeffs_ref[0, own].reshape(rows_h, tile)
        hole = jnp.dot(wh_ref[...], y, preferred_element_type=jnp.float32)
        hole = hole.reshape(modes, PART_C, bands_v, tile)
        for m in range(modes):
            for h in range(bands_v // PART_V):
                cols = slice(h * PART_V, (h + 1) * PART_V)
                value = electron[h][m, own] - hole[m, :, cols]
                out_ref[0, m, own, cols, :] = value.astype(jnp.bfloat16)


def products_of(coeffs, g_cond, g_val, band_first):
    k_local, bands_c, bands_v, excitons = coeffs.shape
    modes = g_cond.shape[1]
    tile = 256
    rows_e, rows_h = bands_c * PART_V, PART_C * bands_v
    depth = bands_c * bands_v
    return pl.pallas_call(
        products_kernel,
        out_shape=jax.ShapeDtypeStruct((k_local, modes, bands_c, bands_v, excitons), jnp.bfloat16),
        grid=(k_local, excitons // tile),
        in_specs=[
            pl.BlockSpec(memory_space=pltpu.SMEM),
            pl.BlockSpec((1, bands_c, bands_v, tile), lambda k, s: (k, 0, 0, s)),
            pl.BlockSpec((1, modes, bands_c, bands_c), lambda k, s: (k, 0, 0, 0)),
            pl.BlockSpec((1, modes, bands_v, bands_v), lambda k, s: (k, 0, 0, 0)),
        ],
        out_specs=pl.BlockSpec((1, modes, bands_c, bands_v, tile), lambda k, s: (k, 0, 0, 0, s)),
        scratch_shapes=[
            pltpu.VMEM((modes * rows_e, rows_e), jnp.bfloat16),
            pltpu.VMEM((modes * rows_h, rows_h), jnp.bfloat16),
        ],
        compiler_params=pltpu.CompilerParams(vmem_limit_bytes=60 * MIB),
        cost_estimate=pl.CostEstimate(
            flops=2 * k_local * modes * excitons * depth * (rows_e + rows_h),
            bytes_accessed=2 * coeffs.size * (1 + modes),
            transcendentals=0,
        ),
    )(band_first, coeffs, g_cond, g_val)


def turn_kernel(first, coeffs_ref, *refs):
    *out_refs, held, sems = refs
    pieces, k_local, parts, rows, width = held.shape
    size = lax.axis_size("ka")
    behind_z = lax.shift_right_logical(lax.rem(lax.axis_index("ka") + size - 1, size), 2)

    def copy(i, k, p):
        columns = pl.ds(pl.multiple_of((behind_z ^ (3 - first - i)) * width, width), width)
        source = coeffs_ref.at[k, pl.ds(p * rows, rows), columns]
        return pltpu.make_async_copy(source, held.at[i, k, p], sems.at[i, k, p])

    steps = [(i, k, p) for i in range(pieces) for k in range(k_local) for p in range(parts)]
    for step in steps:
        copy(*step).start()
    for step in steps:
        i, k, p = step
        copy(*step).wait()
        out_refs[i][k, :, p * rows:(p + 1) * rows] = held[i, k, p].T


def turned_pieces(flat, first, pieces, width):
    k_local, depth, _ = flat.shape
    parts = 2
    return pl.pallas_call(
        functools.partial(turn_kernel, first),
        out_shape=[jax.ShapeDtypeStruct((k_local, width, depth), jnp.bfloat16)] * pieces,
        in_specs=[pl.BlockSpec(memory_space=pl.ANY)],
        out_specs=[pl.BlockSpec(memory_space=pltpu.VMEM)] * pieces,
        scratch_shapes=[
            pltpu.VMEM((pieces, k_local, parts, depth // parts, width), jnp.bfloat16),
            pltpu.SemaphoreType.DMA((pieces, k_local, parts)),
        ],
        compiler_params=pltpu.CompilerParams(vmem_limit_bytes=60 * MIB),
        cost_estimate=pl.CostEstimate(
            flops=0, bytes_accessed=4 * pieces * k_local * depth * width, transcendentals=0
        ),
    )(flat)


def rows_kernel(pick_ref, own_ref, next_ref, right_ref, mine_ref, other_ref, send_ref, *refs):
    own_held, next_held, held, left, own_sems, next_sems, sems = refs
    k_local, depth, width = own_held.shape
    tiles, _, _, tile = held.shape
    per_mode = right_ref.shape[3] // tile
    core, x = pick_ref[k_local + 1], pick_ref[k_local + 2]
    columns = pl.ds(pl.multiple_of(pick_ref[k_local] * width, width), width)
    near = [pick_ref[k] < k_local for k in range(k_local)]

    def copy_own(k):
        source = own_ref.at[jnp.minimum(pick_ref[k], k_local - 1), :, columns]
        return pltpu.make_async_copy(source, own_held.at[k], own_sems.at[k])

    def copy_next(k):
        source = next_ref.at[jnp.maximum(pick_ref[k] - k_local, 0)]
        return pltpu.make_async_copy(source, next_held.at[k], next_sems.at[k])

    def copy_right(t, k):
        source = right_ref.at[k, t // per_mode, :, pl.ds(t % per_mode * tile, tile)]
        return pltpu.make_async_copy(source, held.at[t, k], sems.at[t, k])

    for k in range(k_local):
        copy_own(k).start()
        copy_next(k).start()
    for t in range(tiles):
        for k in range(k_local):
            copy_right(t, k).start()
    for k in range(k_local):
        copy_own(k).wait()
        copy_next(k).wait()

        @pl.when(near[k])
        def _():
            left[:, k * depth:(k + 1) * depth] = own_held[k].T

        @pl.when(jnp.logical_not(near[k]))
        def _():
            left[:, k * depth:(k + 1) * depth] = next_held[k]

    for t in range(tiles):
        for k in range(k_local):
            copy_right(t, k).wait()
        right = held[t].reshape(k_local * depth, tile)
        total = jnp.dot(left[...], right, preferred_element_type=jnp.float32)
        parts = total.reshape(2, 2, width // 4, tile)
        mine = jnp.where(x == 0, parts[0], parts[1])
        other = jnp.where(x == 0, parts[1], parts[0])
        place = slice(t * tile, (t + 1) * tile)
        mine_ref[:, place] = jnp.where(core == 0, mine[0], mine[1])
        other_ref[:, place] = jnp.where(core == 0, other[0], other[1])
        send_ref[:width // 4, place] = jnp.where(core == 0, mine[1], mine[0]).astype(jnp.bfloat16)
        send_ref[width // 4:, place] = jnp.where(core == 0, other[1], other[0]).astype(jnp.bfloat16)


def rows_of(pick, own, following, products):
    k_local, width, depth = following.shape
    modes, excitons = products.shape[1], products.shape[3]
    columns, tile = modes * excitons, 512
    tiles = columns // tile
    return pl.pallas_call(
        rows_kernel,
        out_shape=[
            jax.ShapeDtypeStruct((width // 4, columns), jnp.float32),
            jax.ShapeDtypeStruct((width // 4, columns), jnp.float32),
            jax.ShapeDtypeStruct((width // 2, columns), jnp.bfloat16),
        ],
        in_specs=[pl.BlockSpec(memory_space=pltpu.SMEM)]
        + [pl.BlockSpec(memory_space=pl.ANY)] * 3,
        out_specs=[pl.BlockSpec(memory_space=pltpu.VMEM)] * 3,
        scratch_shapes=[
            pltpu.VMEM((k_local, depth, width), jnp.bfloat16),
            pltpu.VMEM((k_local, width, depth), jnp.bfloat16),
            pltpu.VMEM((tiles, k_local, depth, tile), jnp.bfloat16),
            pltpu.VMEM((width, k_local * depth), jnp.bfloat16),
            pltpu.SemaphoreType.DMA((k_local,)),
            pltpu.SemaphoreType.DMA((k_local,)),
            pltpu.SemaphoreType.DMA((tiles, k_local)),
        ],
        compiler_params=pltpu.CompilerParams(vmem_limit_bytes=50 * MIB),
        cost_estimate=pl.CostEstimate(
            flops=2 * k_local * depth * width * columns,
            bytes_accessed=2 * k_local * depth * columns,
            transcendentals=0,
        ),
    )(pick, own, following, products)


def on_two_by_four(coeffs, g_cond, g_val, k_plus_q, band_first, norm_factor):
    k_local, bands_c, bands_v, excitons = coeffs.shape
    modes = g_cond.shape[1]
    size = lax.axis_size("ka")
    width = excitons // 4
    me = lax.axis_index("ka")
    core, x, z = me & 1, me >> 1 & 1, me >> 2
    flat = coeffs.reshape(k_local, bands_c * bands_v, excitons)

    pieces = turned_pieces(flat, 0, 1, width)
    rest, _ = lax.optimization_barrier((flat, pieces))
    pieces += turned_pieces(rest, 1, 3, width)
    following = [permute(piece, lambda i: i - 1) for piece in pieces]
    products = products_of(coeffs, g_cond, g_val, band_first)
    products = products.reshape(k_local, modes, bands_c * bands_v, excitons)
    places = jnp.mod(k_plus_q - me * k_local, k_local * size)

    def rows(step, after, sent=True):
        pick = jnp.concatenate((places, jnp.stack((z ^ (3 - step), core, x))))
        pick, _ = lax.optimization_barrier((pick, after))
        mine, other, send = rows_of(pick, flat, following[step], products)
        return mine, other, permute(send, lambda i: i ^ 1) if sent else send

    half = width // 4

    def summed(step, from_core):
        from_core = from_core.astype(jnp.float32)
        return step[0] + from_core[:half], step[1] + from_core[half:]

    def over(value, bits):
        return permute(value.astype(jnp.bfloat16), lambda i: i ^ bits)

    def total_of(value, *arrived):
        for array in arrived:
            value = value + array.astype(jnp.float32)
        return value

    step_0 = rows(0, products)
    step_1 = rows(1, step_0[0])
    step_2 = rows(2, step_1[0])
    core_0, core_1, core_2, following[3] = lax.optimization_barrier(
        (step_0[2], step_1[2], step_2[2], following[3])
    )
    mine_0, other_0 = summed(step_0, core_0)
    mine_1, other_1 = summed(step_1, core_1)
    mine_2, other_2 = summed(step_2, core_2)
    sends = [value.astype(jnp.bfloat16) for value in (mine_0, other_0, other_1, other_2)]
    turns = [jnp.where(core == turn, sends[2], sends[0]) for turn in range(2)]
    arrived = [
        permute(turns[turn], lambda i: i ^ (2 if i % 2 == turn else 4)) for turn in range(2)
    ]
    arrived.append(over(sends[1], 6))
    across_2 = over(sends[3], 2)
    mine_3, other_3, send_3 = rows(3, (turns, sends), False)
    mine_1, _ = lax.optimization_barrier((mine_1, mine_3))
    pair = total_of(mine_1, *arrived)
    mine_2, _ = lax.optimization_barrier((mine_2, pair))
    send_3, _ = lax.optimization_barrier((send_3, pair))
    pair = over(pair, 8)
    near = over(total_of(mine_2, across_2), 4)
    core_3, _ = lax.optimization_barrier((over(send_3, 1), mine_2))
    mine_3, other_3 = summed((mine_3, other_3), core_3)
    mine_3, other_3 = lax.optimization_barrier((mine_3, other_3.astype(jnp.bfloat16)))
    total = lax.optimization_barrier(total_of(mine_3, pair))
    total = total_of(total, over(other_3, 2), near)
    return (total * norm_factor).reshape(width // 4, modes, excitons)


def on_any(coeffs, g_cond, g_val, k_plus_q, band_first, norm_factor):
    k_local, bands_c, bands_v, excitons = coeffs.shape
    modes = g_cond.shape[1]
    size = lax.axis_size("ka")
    depth = bands_c * bands_v
    flat = coeffs.reshape(k_local, depth, excitons)
    blocks = jnp.concatenate((flat, permute(flat, lambda i: i - 1)), 0)
    offsets = jnp.mod(k_plus_q - lax.axis_index("ka") * k_local, k_local * size)
    products = products_of(coeffs, g_cond, g_val, band_first)
    products = products.reshape(k_local, modes, depth, excitons)
    partners = [
        lax.dynamic_index_in_dim(blocks, offsets[k], 0, keepdims=False) for k in range(k_local)
    ]
    running = jnp.einsum(
        "kds,kmdt->smt", jnp.stack(partners), products, preferred_element_type=jnp.float32
    )
    return lax.psum_scatter(running * norm_factor, "ka", scatter_dimension=0, tiled=True)


def shards(coeffs, g_cond, g_val, k_plus_q, band_first):
    k_local, bands_c, bands_v, excitons = coeffs.shape
    size = lax.axis_size("ka")
    norm_factor = 1.0 / math.sqrt(bands_c * bands_v * k_local * size)
    whole_tiles = excitons % (4 * 128) == 0
    plan = on_two_by_four if size == 16 and whole_tiles else on_any
    return plan(coeffs, g_cond, g_val, k_plus_q, band_first, norm_factor)


def solution(mesh):
    in_specs = (
        P(("groups", "ka"), None, None, None),
        P(("groups", "ka"), None, None, None),
        P(("groups", "ka"), None, None, None),
        P(("groups", "ka")),
        P("groups", None),
    )
    out_specs = P(("groups", "ka"), None, None)
    return jax.shard_map(shards, mesh=mesh, in_specs=in_specs, out_specs=out_specs, check_vma=False)
```

```python
import functools
import math

import jax
import jax.numpy as jnp
from jax import lax
from jax.experimental import pallas as pl
from jax.experimental.pallas import tpu as pltpu
from jax.sharding import PartitionSpec as P

MIB = 1024 * 1024


def permute(x, target):
    size = lax.axis_size("ka")
    pairs = [(i, target(i)) for i in range(size)]
    return lax.ppermute(x, "ka", [(i, j % size) for i, j in pairs if j is not None])


def nt_dot(a, b):
    return lax.dot_general(a, b, (((1,), (1,)), ((), ())), preferred_element_type=jnp.float32)


def iotas(rows, cols):
    shape = (rows, cols)
    return lax.broadcasted_iota(jnp.int32, shape, 0), lax.broadcasted_iota(jnp.int32, shape, 1)


def ones_where(condition):
    return jnp.where(condition, 1.0, 0.0).astype(jnp.bfloat16)


PART_C, PART_V = 8, 16


def fill_weights(first_ref, cond_ref, val_ref, we_ref, wh_ref):
    _, modes, bands_c, _ = cond_ref.shape
    bands_v = val_ref.shape[2]
    rows_e, rows_h = bands_c * PART_V, PART_C * bands_v
    row, col = iotas(rows_e, bands_c)
    take = ones_where(row // PART_V == col)
    row, col = iotas(rows_e, rows_e)
    for m in range(modes):
        half = jnp.dot(take, cond_ref[0, m], preferred_element_type=jnp.float32)
        full = nt_dot(half.astype(jnp.bfloat16), take)
        keep = (row % PART_V == col % PART_V) & (row // PART_V >= first_ref[m, 0])
        we_ref[m * rows_e:(m + 1) * rows_e, :] = jnp.where(keep, full, 0.0).astype(jnp.bfloat16)
    row, col = iotas(rows_h, bands_v)
    take = ones_where(row % bands_v == col)
    row, col = iotas(rows_h, rows_h)
    for m in range(modes):
        half = nt_dot(take, val_ref[0, m])
        full = nt_dot(half.astype(jnp.bfloat16), take)
        keep = (row // bands_v == col // bands_v) & (row % bands_v >= first_ref[m, 1])
        wh_ref[m * rows_h:(m + 1) * rows_h, :] = jnp.where(keep, full, 0.0).astype(jnp.bfloat16)


def products_kernel(first_ref, coeffs_ref, cond_ref, val_ref, out_ref, we_ref, wh_ref):
    _, bands_c, bands_v, tile = coeffs_ref.shape
    modes = cond_ref.shape[1]
    rows_e, rows_h = bands_c * PART_V, PART_C * bands_v

    @pl.when(pl.program_id(1) == 0)
    def _():
        fill_weights(first_ref, cond_ref, val_ref, we_ref, wh_ref)

    electron = []
    for h in range(bands_v // PART_V):
        x = coeffs_ref[0, :, h * PART_V:(h + 1) * PART_V, :].reshape(rows_e, tile)
        e = jnp.dot(we_ref[...], x, preferred_element_type=jnp.float32)
        electron.append(e.reshape(modes, bands_c, PART_V, tile))
    for q in range(bands_c // PART_C):
        own = slice(q * PART_C, (q + 1) * PART_C)
        y = coeffs_ref[0, own].reshape(rows_h, tile)
        hole = jnp.dot(wh_ref[...], y, preferred_element_type=jnp.float32)
        hole = hole.reshape(modes, PART_C, bands_v, tile)
        for m in range(modes):
            for h in range(bands_v // PART_V):
                cols = slice(h * PART_V, (h + 1) * PART_V)
                value = electron[h][m, own] - hole[m, :, cols]
                out_ref[0, m, own, cols, :] = value.astype(jnp.bfloat16)


def products_of(coeffs, g_cond, g_val, band_first):
    k_local, bands_c, bands_v, excitons = coeffs.shape
    modes = g_cond.shape[1]
    tile = 256
    rows_e, rows_h = bands_c * PART_V, PART_C * bands_v
    depth = bands_c * bands_v
    return pl.pallas_call(
        products_kernel,
        out_shape=jax.ShapeDtypeStruct((k_local, modes, bands_c, bands_v, excitons), jnp.bfloat16),
        grid=(k_local, excitons // tile),
        in_specs=[
            pl.BlockSpec(memory_space=pltpu.SMEM),
            pl.BlockSpec((1, bands_c, bands_v, tile), lambda k, s: (k, 0, 0, s)),
            pl.BlockSpec((1, modes, bands_c, bands_c), lambda k, s: (k, 0, 0, 0)),
            pl.BlockSpec((1, modes, bands_v, bands_v), lambda k, s: (k, 0, 0, 0)),
        ],
        out_specs=pl.BlockSpec((1, modes, bands_c, bands_v, tile), lambda k, s: (k, 0, 0, 0, s)),
        scratch_shapes=[
            pltpu.VMEM((modes * rows_e, rows_e), jnp.bfloat16),
            pltpu.VMEM((modes * rows_h, rows_h), jnp.bfloat16),
        ],
        compiler_params=pltpu.CompilerParams(vmem_limit_bytes=60 * MIB),
        cost_estimate=pl.CostEstimate(
            flops=2 * k_local * modes * excitons * depth * (rows_e + rows_h),
            bytes_accessed=2 * coeffs.size * (1 + modes),
            transcendentals=0,
        ),
    )(band_first, coeffs, g_cond, g_val)


def turn_kernel(first, coeffs_ref, *refs):
    *out_refs, held, sems = refs
    pieces, k_local, parts, rows, width = held.shape
    size = lax.axis_size("ka")
    behind_z = lax.shift_right_logical(lax.rem(lax.axis_index("ka") + size - 1, size), 2)

    def copy(i, k, p):
        columns = pl.ds(pl.multiple_of((behind_z ^ (3 - first - i)) * width, width), width)
        source = coeffs_ref.at[k, pl.ds(p * rows, rows), columns]
        return pltpu.make_async_copy(source, held.at[i, k, p], sems.at[i, k, p])

    steps = [(i, k, p) for i in range(pieces) for k in range(k_local) for p in range(parts)]
    for step in steps:
        copy(*step).start()
    for step in steps:
        i, k, p = step
        copy(*step).wait()
        out_refs[i][k, :, p * rows:(p + 1) * rows] = held[i, k, p].T


def turned_pieces(flat, first, pieces, width):
    k_local, depth, _ = flat.shape
    parts = 2
    return pl.pallas_call(
        functools.partial(turn_kernel, first),
        out_shape=[jax.ShapeDtypeStruct((k_local, width, depth), jnp.bfloat16)] * pieces,
        in_specs=[pl.BlockSpec(memory_space=pl.ANY)],
        out_specs=[pl.BlockSpec(memory_space=pltpu.VMEM)] * pieces,
        scratch_shapes=[
            pltpu.VMEM((pieces, k_local, parts, depth // parts, width), jnp.bfloat16),
            pltpu.SemaphoreType.DMA((pieces, k_local, parts)),
        ],
        compiler_params=pltpu.CompilerParams(vmem_limit_bytes=60 * MIB),
        cost_estimate=pl.CostEstimate(
            flops=0, bytes_accessed=4 * pieces * k_local * depth * width, transcendentals=0
        ),
    )(flat)


def rows_kernel(pick_ref, own_ref, next_ref, right_ref, mine_ref, other_ref, send_ref, *refs):
    own_held, next_held, held, left, own_sems, next_sems, sems = refs
    k_local, depth, width = own_held.shape
    tiles, _, _, tile = held.shape
    per_mode = right_ref.shape[3] // tile
    core, x = pick_ref[k_local + 1], pick_ref[k_local + 2]
    columns = pl.ds(pl.multiple_of(pick_ref[k_local] * width, width), width)
    near = [pick_ref[k] < k_local for k in range(k_local)]

    def copy_own(k):
        source = own_ref.at[jnp.minimum(pick_ref[k], k_local - 1), :, columns]
        return pltpu.make_async_copy(source, own_held.at[k], own_sems.at[k])

    def copy_next(k):
        source = next_ref.at[jnp.maximum(pick_ref[k] - k_local, 0)]
        return pltpu.make_async_copy(source, next_held.at[k], next_sems.at[k])

    def copy_right(t, k):
        source = right_ref.at[k, t // per_mode, :, pl.ds(t % per_mode * tile, tile)]
        return pltpu.make_async_copy(source, held.at[t, k], sems.at[t, k])

    for k in range(k_local):
        copy_own(k).start()
        copy_next(k).start()
    for t in range(tiles):
        for k in range(k_local):
            copy_right(t, k).start()
    for k in range(k_local):
        copy_own(k).wait()
        copy_next(k).wait()

        @pl.when(near[k])
        def _():
            left[:, k * depth:(k + 1) * depth] = own_held[k].T

        @pl.when(jnp.logical_not(near[k]))
        def _():
            left[:, k * depth:(k + 1) * depth] = next_held[k]

    for t in range(tiles):
        for k in range(k_local):
            copy_right(t, k).wait()
        right = held[t].reshape(k_local * depth, tile)
        total = jnp.dot(left[...], right, preferred_element_type=jnp.float32)
        parts = total.reshape(2, 2, width // 4, tile)
        mine = jnp.where(x == 0, parts[0], parts[1])
        other = jnp.where(x == 0, parts[1], parts[0])
        place = slice(t * tile, (t + 1) * tile)
        mine_ref[:, place] = jnp.where(core == 0, mine[0], mine[1])
        other_ref[:, place] = jnp.where(core == 0, other[0], other[1])
        send_ref[:width // 4, place] = jnp.where(core == 0, mine[1], mine[0]).astype(jnp.bfloat16)
        send_ref[width // 4:, place] = jnp.where(core == 0, other[1], other[0]).astype(jnp.bfloat16)


def rows_of(pick, own, following, products):
    k_local, width, depth = following.shape
    modes, excitons = products.shape[1], products.shape[3]
    columns, tile = modes * excitons, 512
    tiles = columns // tile
    return pl.pallas_call(
        rows_kernel,
        out_shape=[
            jax.ShapeDtypeStruct((width // 4, columns), jnp.float32),
            jax.ShapeDtypeStruct((width // 4, columns), jnp.float32),
            jax.ShapeDtypeStruct((width // 2, columns), jnp.bfloat16),
        ],
        in_specs=[pl.BlockSpec(memory_space=pltpu.SMEM)]
        + [pl.BlockSpec(memory_space=pl.ANY)] * 3,
        out_specs=[pl.BlockSpec(memory_space=pltpu.VMEM)] * 3,
        scratch_shapes=[
            pltpu.VMEM((k_local, depth, width), jnp.bfloat16),
            pltpu.VMEM((k_local, width, depth), jnp.bfloat16),
            pltpu.VMEM((tiles, k_local, depth, tile), jnp.bfloat16),
            pltpu.VMEM((width, k_local * depth), jnp.bfloat16),
            pltpu.SemaphoreType.DMA((k_local,)),
            pltpu.SemaphoreType.DMA((k_local,)),
            pltpu.SemaphoreType.DMA((tiles, k_local)),
        ],
        compiler_params=pltpu.CompilerParams(vmem_limit_bytes=50 * MIB),
        cost_estimate=pl.CostEstimate(
            flops=2 * k_local * depth * width * columns,
            bytes_accessed=2 * k_local * depth * columns,
            transcendentals=0,
        ),
    )(pick, own, following, products)


def payloads_kernel(*refs):
    ins, (turn_0, turn_1, cross_0, cross_2, mine_1, mine_2) = refs[:9], refs[9:]
    half = turn_0.shape[0]

    def summed(block, own):
        rows = slice(0, half) if own else slice(half, 2 * half)
        mine, other, core = ins[3 * block:3 * block + 3]
        return (mine if own else other)[...] + core[rows, :].astype(jnp.float32)

    straight = summed(0, True).astype(jnp.bfloat16)
    across = summed(1, False).astype(jnp.bfloat16)
    first = lax.axis_index("ka") & 1 == 0
    turn_0[...] = jnp.where(first, across, straight)
    turn_1[...] = jnp.where(first, straight, across)
    cross_0[...] = summed(0, False).astype(jnp.bfloat16)
    cross_2[...] = summed(2, False).astype(jnp.bfloat16)
    mine_1[...] = summed(1, True)
    mine_2[...] = summed(2, True)


def payloads_of(*parts):
    shape = parts[0].shape
    return pl.pallas_call(
        payloads_kernel,
        out_shape=[jax.ShapeDtypeStruct(shape, jnp.bfloat16)] * 4
        + [jax.ShapeDtypeStruct(shape, jnp.float32)] * 2,
        in_specs=[pl.BlockSpec(memory_space=pltpu.VMEM)] * 9,
        out_specs=[pl.BlockSpec(memory_space=pltpu.VMEM)] * 6,
        compiler_params=pltpu.CompilerParams(vmem_limit_bytes=24 * MIB),
        cost_estimate=pl.CostEstimate(
            flops=6 * parts[0].size, bytes_accessed=26 * parts[0].size, transcendentals=0
        ),
    )(*parts)


def on_two_by_four(coeffs, g_cond, g_val, k_plus_q, band_first, norm_factor):
    k_local, bands_c, bands_v, excitons = coeffs.shape
    modes = g_cond.shape[1]
    size = lax.axis_size("ka")
    width = excitons // 4
    me = lax.axis_index("ka")
    core, x, z = me & 1, me >> 1 & 1, me >> 2
    flat = coeffs.reshape(k_local, bands_c * bands_v, excitons)

    pieces = turned_pieces(flat, 0, 1, width)
    rest, _ = lax.optimization_barrier((flat, pieces))
    pieces += turned_pieces(rest, 1, 3, width)
    following = [permute(piece, lambda i: i - 1) for piece in pieces]
    products = products_of(coeffs, g_cond, g_val, band_first)
    products = products.reshape(k_local, modes, bands_c * bands_v, excitons)
    places = jnp.mod(k_plus_q - me * k_local, k_local * size)

    def rows(step, after, sent=True):
        pick = jnp.concatenate((places, jnp.stack((z ^ (3 - step), core, x))))
        pick, _ = lax.optimization_barrier((pick, after))
        mine, other, send = rows_of(pick, flat, following[step], products)
        return mine, other, permute(send, lambda i: i ^ 1) if sent else send

    half = width // 4

    def summed(step, from_core):
        from_core = from_core.astype(jnp.float32)
        return step[0] + from_core[:half], step[1] + from_core[half:]

    def over(value, bits):
        return permute(value.astype(jnp.bfloat16), lambda i: i ^ bits)

    def total_of(value, *arrived):
        for array in arrived:
            value = value + array.astype(jnp.float32)
        return value

    step_0 = rows(0, products)
    step_1 = rows(1, step_0[0])
    step_2 = rows(2, step_1[0])
    core_0, core_1, core_2, following[3] = lax.optimization_barrier(
        (step_0[2], step_1[2], step_2[2], following[3])
    )
    *turns, cross_0, cross_2, mine_1, mine_2 = payloads_of(
        *step_0[:2], core_0, *step_1[:2], core_1, *step_2[:2], core_2
    )
    arrived = [
        permute(turns[turn], lambda i: i ^ (2 if i % 2 == turn else 4)) for turn in range(2)
    ]
    arrived.append(over(cross_0, 6))
    across_2 = over(cross_2, 2)
    mine_3, other_3, send_3 = rows(3, mine_2, False)
    mine_1, _ = lax.optimization_barrier((mine_1, mine_3))
    pair = total_of(mine_1, *arrived)
    mine_2, _ = lax.optimization_barrier((mine_2, pair))
    send_3, _ = lax.optimization_barrier((send_3, pair))
    pair = over(pair, 8)
    near = over(total_of(mine_2, across_2), 4)
    core_3, _ = lax.optimization_barrier((over(send_3, 1), mine_2))
    mine_3, other_3 = summed((mine_3, other_3), core_3)
    mine_3, other_3 = lax.optimization_barrier((mine_3, other_3.astype(jnp.bfloat16)))
    total = lax.optimization_barrier(total_of(mine_3, pair))
    total = total_of(total, over(other_3, 2), near)
    return (total * norm_factor).reshape(width // 4, modes, excitons)


def on_any(coeffs, g_cond, g_val, k_plus_q, band_first, norm_factor):
    k_local, bands_c, bands_v, excitons = coeffs.shape
    modes = g_cond.shape[1]
    size = lax.axis_size("ka")
    depth = bands_c * bands_v
    flat = coeffs.reshape(k_local, depth, excitons)
    blocks = jnp.concatenate((flat, permute(flat, lambda i: i - 1)), 0)
    offsets = jnp.mod(k_plus_q - lax.axis_index("ka") * k_local, k_local * size)
    products = products_of(coeffs, g_cond, g_val, band_first)
    products = products.reshape(k_local, modes, depth, excitons)
    partners = [
        lax.dynamic_index_in_dim(blocks, offsets[k], 0, keepdims=False) for k in range(k_local)
    ]
    running = jnp.einsum(
        "kds,kmdt->smt", jnp.stack(partners), products, preferred_element_type=jnp.float32
    )
    return lax.psum_scatter(running * norm_factor, "ka", scatter_dimension=0, tiled=True)


def shards(coeffs, g_cond, g_val, k_plus_q, band_first):
    k_local, bands_c, bands_v, excitons = coeffs.shape
    size = lax.axis_size("ka")
    norm_factor = 1.0 / math.sqrt(bands_c * bands_v * k_local * size)
    whole_tiles = excitons % (4 * 128) == 0
    plan = on_two_by_four if size == 16 and whole_tiles else on_any
    return plan(coeffs, g_cond, g_val, k_plus_q, band_first, norm_factor)


def solution(mesh):
    in_specs = (
        P(("groups", "ka"), None, None, None),
        P(("groups", "ka"), None, None, None),
        P(("groups", "ka"), None, None, None),
        P(("groups", "ka")),
        P("groups", None),
    )
    out_specs = P(("groups", "ka"), None, None)
    return jax.shard_map(shards, mesh=mesh, in_specs=in_specs, out_specs=out_specs, check_vma=False)
```

```python
import functools
import math

import jax
import jax.numpy as jnp
from jax import lax
from jax.experimental import pallas as pl
from jax.experimental.pallas import tpu as pltpu
from jax.sharding import PartitionSpec as P

MIB = 1024 * 1024


def permute(x, target):
    size = lax.axis_size("ka")
    pairs = [(i, target(i)) for i in range(size)]
    return lax.ppermute(x, "ka", [(i, j % size) for i, j in pairs if j is not None])


def nt_dot(a, b):
    return lax.dot_general(a, b, (((1,), (1,)), ((), ())), preferred_element_type=jnp.float32)


def iotas(rows, cols):
    shape = (rows, cols)
    return lax.broadcasted_iota(jnp.int32, shape, 0), lax.broadcasted_iota(jnp.int32, shape, 1)


def ones_where(condition):
    return jnp.where(condition, 1.0, 0.0).astype(jnp.bfloat16)


PART_C, PART_V = 8, 16


def fill_weights(first_ref, cond_ref, val_ref, we_ref, wh_ref):
    _, modes, bands_c, _ = cond_ref.shape
    bands_v = val_ref.shape[2]
    rows_e, rows_h = bands_c * PART_V, PART_C * bands_v
    row, col = iotas(rows_e, bands_c)
    take = ones_where(row // PART_V == col)
    row, col = iotas(rows_e, rows_e)
    for m in range(modes):
        half = jnp.dot(take, cond_ref[0, m], preferred_element_type=jnp.float32)
        full = nt_dot(half.astype(jnp.bfloat16), take)
        keep = (row % PART_V == col % PART_V) & (row // PART_V >= first_ref[m, 0])
        we_ref[m * rows_e:(m + 1) * rows_e, :] = jnp.where(keep, full, 0.0).astype(jnp.bfloat16)
    row, col = iotas(rows_h, bands_v)
    take = ones_where(row % bands_v == col)
    row, col = iotas(rows_h, rows_h)
    for m in range(modes):
        half = nt_dot(take, val_ref[0, m])
        full = nt_dot(half.astype(jnp.bfloat16), take)
        keep = (row // bands_v == col // bands_v) & (row % bands_v >= first_ref[m, 1])
        wh_ref[m * rows_h:(m + 1) * rows_h, :] = jnp.where(keep, full, 0.0).astype(jnp.bfloat16)


def products_kernel(first_ref, coeffs_ref, cond_ref, val_ref, out_ref, we_ref, wh_ref):
    _, bands_c, bands_v, tile = coeffs_ref.shape
    modes = cond_ref.shape[1]
    rows_e, rows_h = bands_c * PART_V, PART_C * bands_v

    @pl.when(pl.program_id(1) == 0)
    def _():
        fill_weights(first_ref, cond_ref, val_ref, we_ref, wh_ref)

    electron = []
    for h in range(bands_v // PART_V):
        x = coeffs_ref[0, :, h * PART_V:(h + 1) * PART_V, :].reshape(rows_e, tile)
        e = jnp.dot(we_ref[...], x, preferred_element_type=jnp.float32)
        electron.append(e.reshape(modes, bands_c, PART_V, tile))
    for q in range(bands_c // PART_C):
        own = slice(q * PART_C, (q + 1) * PART_C)
        y = coeffs_ref[0, own].reshape(rows_h, tile)
        hole = jnp.dot(wh_ref[...], y, preferred_element_type=jnp.float32)
        hole = hole.reshape(modes, PART_C, bands_v, tile)
        for m in range(modes):
            for h in range(bands_v // PART_V):
                cols = slice(h * PART_V, (h + 1) * PART_V)
                value = electron[h][m, own] - hole[m, :, cols]
                out_ref[0, m, own, cols, :] = value.astype(jnp.bfloat16)


def products_of(coeffs, g_cond, g_val, band_first):
    k_local, bands_c, bands_v, excitons = coeffs.shape
    modes = g_cond.shape[1]
    tile = 256
    rows_e, rows_h = bands_c * PART_V, PART_C * bands_v
    depth = bands_c * bands_v
    return pl.pallas_call(
        products_kernel,
        out_shape=jax.ShapeDtypeStruct((k_local, modes, bands_c, bands_v, excitons), jnp.bfloat16),
        grid=(k_local, excitons // tile),
        in_specs=[
            pl.BlockSpec(memory_space=pltpu.SMEM),
            pl.BlockSpec((1, bands_c, bands_v, tile), lambda k, s: (k, 0, 0, s)),
            pl.BlockSpec((1, modes, bands_c, bands_c), lambda k, s: (k, 0, 0, 0)),
            pl.BlockSpec((1, modes, bands_v, bands_v), lambda k, s: (k, 0, 0, 0)),
        ],
        out_specs=pl.BlockSpec((1, modes, bands_c, bands_v, tile), lambda k, s: (k, 0, 0, 0, s)),
        scratch_shapes=[
            pltpu.VMEM((modes * rows_e, rows_e), jnp.bfloat16),
            pltpu.VMEM((modes * rows_h, rows_h), jnp.bfloat16),
        ],
        compiler_params=pltpu.CompilerParams(vmem_limit_bytes=60 * MIB),
        cost_estimate=pl.CostEstimate(
            flops=2 * k_local * modes * excitons * depth * (rows_e + rows_h),
            bytes_accessed=2 * coeffs.size * (1 + modes),
            transcendentals=0,
        ),
    )(band_first, coeffs, g_cond, g_val)


def turn_kernel(first, coeffs_ref, *refs):
    *out_refs, held, sems = refs
    pieces, k_local, parts, rows, width = held.shape
    size = lax.axis_size("ka")
    behind_z = lax.shift_right_logical(lax.rem(lax.axis_index("ka") + size - 1, size), 2)

    def copy(i, k, p):
        columns = pl.ds(pl.multiple_of((behind_z ^ (3 - first - i)) * width, width), width)
        source = coeffs_ref.at[k, pl.ds(p * rows, rows), columns]
        return pltpu.make_async_copy(source, held.at[i, k, p], sems.at[i, k, p])

    steps = [(i, k, p) for i in range(pieces) for k in range(k_local) for p in range(parts)]
    for step in steps:
        copy(*step).start()
    for step in steps:
        i, k, p = step
        copy(*step).wait()
        out_refs[i][k, :, p * rows:(p + 1) * rows] = held[i, k, p].T


def turned_pieces(flat, first, pieces, width):
    k_local, depth, _ = flat.shape
    parts = 2
    return pl.pallas_call(
        functools.partial(turn_kernel, first),
        out_shape=[jax.ShapeDtypeStruct((k_local, width, depth), jnp.bfloat16)] * pieces,
        in_specs=[pl.BlockSpec(memory_space=pl.ANY)],
        out_specs=[pl.BlockSpec(memory_space=pltpu.VMEM)] * pieces,
        scratch_shapes=[
            pltpu.VMEM((pieces, k_local, parts, depth // parts, width), jnp.bfloat16),
            pltpu.SemaphoreType.DMA((pieces, k_local, parts)),
        ],
        compiler_params=pltpu.CompilerParams(vmem_limit_bytes=60 * MIB),
        cost_estimate=pl.CostEstimate(
            flops=0, bytes_accessed=4 * pieces * k_local * depth * width, transcendentals=0
        ),
    )(flat)


def rows_kernel(pick_ref, own_ref, next_ref, right_ref, mine_ref, other_ref, send_ref, *refs):
    own_held, next_held, held, left, own_sems, next_sems, sems = refs
    k_local, depth, width = own_held.shape
    tiles, _, _, tile = held.shape
    per_mode = right_ref.shape[3] // tile
    core, x = pick_ref[k_local + 1], pick_ref[k_local + 2]
    columns = pl.ds(pl.multiple_of(pick_ref[k_local] * width, width), width)
    near = [pick_ref[k] < k_local for k in range(k_local)]

    def copy_own(k):
        source = own_ref.at[jnp.minimum(pick_ref[k], k_local - 1), :, columns]
        return pltpu.make_async_copy(source, own_held.at[k], own_sems.at[k])

    def copy_next(k):
        source = next_ref.at[jnp.maximum(pick_ref[k] - k_local, 0)]
        return pltpu.make_async_copy(source, next_held.at[k], next_sems.at[k])

    def copy_right(t, k):
        source = right_ref.at[k, t // per_mode, :, pl.ds(t % per_mode * tile, tile)]
        return pltpu.make_async_copy(source, held.at[t, k], sems.at[t, k])

    for k in range(k_local):
        copy_own(k).start()
        copy_next(k).start()
    for t in range(tiles):
        for k in range(k_local):
            copy_right(t, k).start()
    for k in range(k_local):
        copy_own(k).wait()
        copy_next(k).wait()

        @pl.when(near[k])
        def _():
            left[:, k * depth:(k + 1) * depth] = own_held[k].T

        @pl.when(jnp.logical_not(near[k]))
        def _():
            left[:, k * depth:(k + 1) * depth] = next_held[k]

    for t in range(tiles):
        for k in range(k_local):
            copy_right(t, k).wait()
        right = held[t].reshape(k_local * depth, tile)
        total = jnp.dot(left[...], right, preferred_element_type=jnp.float32)
        parts = total.reshape(2, 2, width // 4, tile)
        mine = jnp.where(x == 0, parts[0], parts[1])
        other = jnp.where(x == 0, parts[1], parts[0])
        place = slice(t * tile, (t + 1) * tile)
        mine_ref[:, place] = jnp.where(core == 0, mine[0], mine[1])
        other_ref[:, place] = jnp.where(core == 0, other[0], other[1])
        send_ref[:width // 4, place] = jnp.where(core == 0, mine[1], mine[0]).astype(jnp.bfloat16)
        send_ref[width // 4:, place] = jnp.where(core == 0, other[1], other[0]).astype(jnp.bfloat16)


def rows_of(pick, own, following, products):
    k_local, width, depth = following.shape
    modes, excitons = products.shape[1], products.shape[3]
    columns, tile = modes * excitons, 512
    tiles = columns // tile
    return pl.pallas_call(
        rows_kernel,
        out_shape=[
            jax.ShapeDtypeStruct((width // 4, columns), jnp.float32),
            jax.ShapeDtypeStruct((width // 4, columns), jnp.float32),
            jax.ShapeDtypeStruct((width // 2, columns), jnp.bfloat16),
        ],
        in_specs=[pl.BlockSpec(memory_space=pltpu.SMEM)]
        + [pl.BlockSpec(memory_space=pl.ANY)] * 3,
        out_specs=[pl.BlockSpec(memory_space=pltpu.VMEM)] * 3,
        scratch_shapes=[
            pltpu.VMEM((k_local, depth, width), jnp.bfloat16),
            pltpu.VMEM((k_local, width, depth), jnp.bfloat16),
            pltpu.VMEM((tiles, k_local, depth, tile), jnp.bfloat16),
            pltpu.VMEM((width, k_local * depth), jnp.bfloat16),
            pltpu.SemaphoreType.DMA((k_local,)),
            pltpu.SemaphoreType.DMA((k_local,)),
            pltpu.SemaphoreType.DMA((tiles, k_local)),
        ],
        compiler_params=pltpu.CompilerParams(vmem_limit_bytes=50 * MIB),
        cost_estimate=pl.CostEstimate(
            flops=2 * k_local * depth * width * columns,
            bytes_accessed=2 * k_local * depth * columns,
            transcendentals=0,
        ),
    )(pick, own, following, products)


def payloads_kernel(*refs):
    ins, (far_0, far_1, across, near_0, near_1, mine_1) = refs[:9], refs[9:]
    half = across.shape[0]

    def summed(block, own):
        mine, other, core = ins[3 * block:3 * block + 3]
        rows = slice(0, half) if own else slice(half, 2 * half)
        return (mine if own else other)[...] + core[rows, :].astype(jnp.float32)

    far_0[...] = summed(0, True).astype(jnp.bfloat16)
    far_1[...] = summed(0, False).astype(jnp.bfloat16)
    across[...] = summed(1, False).astype(jnp.bfloat16)
    near_0[...] = summed(2, True).astype(jnp.bfloat16)
    near_1[...] = summed(2, False).astype(jnp.bfloat16)
    mine_1[...] = summed(1, True)


def payloads_of(*parts):
    shape = parts[0].shape
    return pl.pallas_call(
        payloads_kernel,
        out_shape=[jax.ShapeDtypeStruct(shape, jnp.bfloat16)] * 5
        + [jax.ShapeDtypeStruct(shape, jnp.float32)],
        in_specs=[pl.BlockSpec(memory_space=pltpu.VMEM)] * 9,
        out_specs=[pl.BlockSpec(memory_space=pltpu.VMEM)] * 6,
        compiler_params=pltpu.CompilerParams(vmem_limit_bytes=24 * MIB),
        cost_estimate=pl.CostEstimate(
            flops=6 * parts[0].size, bytes_accessed=26 * parts[0].size, transcendentals=0
        ),
    )(*parts)


def close_kernel(factor, mine_ref, core_ref, *refs):
    *parts, out_ref = refs
    half, modes, excitons = out_ref.shape
    for m in range(modes):
        columns = slice(m * excitons, (m + 1) * excitons)
        total = mine_ref[:, columns] + core_ref[:half, columns].astype(jnp.float32)
        for ref in parts:
            total = total + ref[:, columns].astype(jnp.float32)
        out_ref[:, m, :] = total * factor


def closed(modes, factor, *parts):
    rows, columns = parts[0].shape
    return pl.pallas_call(
        functools.partial(close_kernel, factor),
        out_shape=jax.ShapeDtypeStruct((rows, modes, columns // modes), jnp.float32),
        in_specs=[pl.BlockSpec(memory_space=pltpu.VMEM)] * len(parts),
        out_specs=pl.BlockSpec(memory_space=pltpu.VMEM),
        compiler_params=pltpu.CompilerParams(vmem_limit_bytes=24 * MIB),
        cost_estimate=pl.CostEstimate(
            flops=5 * parts[0].size, bytes_accessed=16 * parts[0].size, transcendentals=0
        ),
    )(*parts)


def on_two_by_four(coeffs, g_cond, g_val, k_plus_q, band_first, norm_factor):
    k_local, bands_c, bands_v, excitons = coeffs.shape
    modes = g_cond.shape[1]
    size = lax.axis_size("ka")
    width = excitons // 4
    me = lax.axis_index("ka")
    core, x, z = me & 1, me >> 1 & 1, me >> 2
    flat = coeffs.reshape(k_local, bands_c * bands_v, excitons)

    pieces = turned_pieces(flat, 0, 1, width)
    rest, _ = lax.optimization_barrier((flat, pieces))
    pieces += turned_pieces(rest, 1, 3, width)
    following = [permute(piece, lambda i: i - 1) for piece in pieces]
    products = products_of(coeffs, g_cond, g_val, band_first)
    products = products.reshape(k_local, modes, bands_c * bands_v, excitons)
    places = jnp.mod(k_plus_q - me * k_local, k_local * size)

    def rows(step, after):
        pick = jnp.concatenate((places, jnp.stack((z ^ (3 - step), core, x))))
        pick, _ = lax.optimization_barrier((pick, after))
        mine, other, send = rows_of(pick, flat, following[step], products)
        return mine, other, permute(send, lambda i: i ^ 1)

    half = width // 4

    def over(value, bits):
        return permute(value.astype(jnp.bfloat16), lambda i: i ^ bits)

    def total_of(value, *arrived):
        for array in arrived:
            value = value + array.astype(jnp.float32)
        return value

    step_0 = rows(0, products)
    step_1 = rows(1, step_0[0])
    step_2 = rows(2, step_1[0])
    core_0, core_1, core_2, following[3] = lax.optimization_barrier(
        (step_0[2], step_1[2], step_2[2], following[3])
    )
    *sends, mine_1 = payloads_of(
        *step_0[:2], core_0, *step_1[:2], core_1, *step_2[:2], core_2
    )
    step_3 = rows(3, sends)
    far = over(sends[0], 4), over(sends[1], 6)
    across_1 = over(sends[2], 2)
    near = over(sends[3], 4), over(sends[4], 6)
    mine_1, _ = lax.optimization_barrier((mine_1, step_3[0]))
    pair = over(total_of(mine_1, across_1, *far), 8)
    mine_3, other_3, core_3 = step_3
    across_3 = over(other_3 + core_3[half:].astype(jnp.float32), 2)
    return closed(modes, norm_factor, mine_3, core_3, across_3, pair, *near)


def on_any(coeffs, g_cond, g_val, k_plus_q, band_first, norm_factor):
    k_local, bands_c, bands_v, excitons = coeffs.shape
    modes = g_cond.shape[1]
    size = lax.axis_size("ka")
    depth = bands_c * bands_v
    flat = coeffs.reshape(k_local, depth, excitons)
    blocks = jnp.concatenate((flat, permute(flat, lambda i: i - 1)), 0)
    offsets = jnp.mod(k_plus_q - lax.axis_index("ka") * k_local, k_local * size)
    products = products_of(coeffs, g_cond, g_val, band_first)
    products = products.reshape(k_local, modes, depth, excitons)
    partners = [
        lax.dynamic_index_in_dim(blocks, offsets[k], 0, keepdims=False) for k in range(k_local)
    ]
    running = jnp.einsum(
        "kds,kmdt->smt", jnp.stack(partners), products, preferred_element_type=jnp.float32
    )
    return lax.psum_scatter(running * norm_factor, "ka", scatter_dimension=0, tiled=True)


def shards(coeffs, g_cond, g_val, k_plus_q, band_first):
    k_local, bands_c, bands_v, excitons = coeffs.shape
    size = lax.axis_size("ka")
    norm_factor = 1.0 / math.sqrt(bands_c * bands_v * k_local * size)
    whole_tiles = excitons % (4 * 128) == 0
    plan = on_two_by_four if size == 16 and whole_tiles else on_any
    return plan(coeffs, g_cond, g_val, k_plus_q, band_first, norm_factor)


def solution(mesh):
    in_specs = (
        P(("groups", "ka"), None, None, None),
        P(("groups", "ka"), None, None, None),
        P(("groups", "ka"), None, None, None),
        P(("groups", "ka")),
        P("groups", None),
    )
    out_specs = P(("groups", "ka"), None, None)
    return jax.shard_map(shards, mesh=mesh, in_specs=in_specs, out_specs=out_specs, check_vma=False)
```

```python
import functools
import math

import jax
import jax.numpy as jnp
from jax import lax
from jax.experimental import pallas as pl
from jax.experimental.pallas import tpu as pltpu
from jax.sharding import PartitionSpec as P

MIB = 1024 * 1024


def permute(x, target):
    size = lax.axis_size("ka")
    pairs = [(i, target(i)) for i in range(size)]
    return lax.ppermute(x, "ka", [(i, j % size) for i, j in pairs if j is not None])


def nt_dot(a, b):
    return lax.dot_general(a, b, (((1,), (1,)), ((), ())), preferred_element_type=jnp.float32)


def iotas(rows, cols):
    shape = (rows, cols)
    return lax.broadcasted_iota(jnp.int32, shape, 0), lax.broadcasted_iota(jnp.int32, shape, 1)


def ones_where(condition):
    return jnp.where(condition, 1.0, 0.0).astype(jnp.bfloat16)


PART_C, PART_V = 8, 16


def fill_weights(first_ref, cond_ref, val_ref, we_ref, wh_ref):
    _, modes, bands_c, _ = cond_ref.shape
    bands_v = val_ref.shape[2]
    rows_e, rows_h = bands_c * PART_V, PART_C * bands_v
    row, col = iotas(rows_e, bands_c)
    take = ones_where(row // PART_V == col)
    row, col = iotas(rows_e, rows_e)
    for m in range(modes):
        half = jnp.dot(take, cond_ref[0, m], preferred_element_type=jnp.float32)
        full = nt_dot(half.astype(jnp.bfloat16), take)
        keep = (row % PART_V == col % PART_V) & (row // PART_V >= first_ref[m, 0])
        we_ref[m * rows_e:(m + 1) * rows_e, :] = jnp.where(keep, full, 0.0).astype(jnp.bfloat16)
    row, col = iotas(rows_h, bands_v)
    take = ones_where(row % bands_v == col)
    row, col = iotas(rows_h, rows_h)
    for m in range(modes):
        half = nt_dot(take, val_ref[0, m])
        full = nt_dot(half.astype(jnp.bfloat16), take)
        keep = (row // bands_v == col // bands_v) & (row % bands_v >= first_ref[m, 1])
        wh_ref[m * rows_h:(m + 1) * rows_h, :] = jnp.where(keep, full, 0.0).astype(jnp.bfloat16)


def products_kernel(first_ref, coeffs_ref, cond_ref, val_ref, out_ref, we_ref, wh_ref):
    _, bands_c, bands_v, tile = coeffs_ref.shape
    modes = cond_ref.shape[1]
    rows_e, rows_h = bands_c * PART_V, PART_C * bands_v

    @pl.when(pl.program_id(1) == 0)
    def _():
        fill_weights(first_ref, cond_ref, val_ref, we_ref, wh_ref)

    electron = []
    for h in range(bands_v // PART_V):
        x = coeffs_ref[0, :, h * PART_V:(h + 1) * PART_V, :].reshape(rows_e, tile)
        e = jnp.dot(we_ref[...], x, preferred_element_type=jnp.float32)
        electron.append(e.reshape(modes, bands_c, PART_V, tile))
    for q in range(bands_c // PART_C):
        own = slice(q * PART_C, (q + 1) * PART_C)
        y = coeffs_ref[0, own].reshape(rows_h, tile)
        hole = jnp.dot(wh_ref[...], y, preferred_element_type=jnp.float32)
        hole = hole.reshape(modes, PART_C, bands_v, tile)
        for m in range(modes):
            for h in range(bands_v // PART_V):
                cols = slice(h * PART_V, (h + 1) * PART_V)
                value = electron[h][m, own] - hole[m, :, cols]
                out_ref[0, m, own, cols, :] = value.astype(jnp.bfloat16)


def products_of(coeffs, g_cond, g_val, band_first):
    k_local, bands_c, bands_v, excitons = coeffs.shape
    modes = g_cond.shape[1]
    tile = 256
    rows_e, rows_h = bands_c * PART_V, PART_C * bands_v
    depth = bands_c * bands_v
    return pl.pallas_call(
        products_kernel,
        out_shape=jax.ShapeDtypeStruct((k_local, modes, bands_c, bands_v, excitons), jnp.bfloat16),
        grid=(k_local, excitons // tile),
        in_specs=[
            pl.BlockSpec(memory_space=pltpu.SMEM),
            pl.BlockSpec((1, bands_c, bands_v, tile), lambda k, s: (k, 0, 0, s)),
            pl.BlockSpec((1, modes, bands_c, bands_c), lambda k, s: (k, 0, 0, 0)),
            pl.BlockSpec((1, modes, bands_v, bands_v), lambda k, s: (k, 0, 0, 0)),
        ],
        out_specs=pl.BlockSpec((1, modes, bands_c, bands_v, tile), lambda k, s: (k, 0, 0, 0, s)),
        scratch_shapes=[
            pltpu.VMEM((modes * rows_e, rows_e), jnp.bfloat16),
            pltpu.VMEM((modes * rows_h, rows_h), jnp.bfloat16),
        ],
        compiler_params=pltpu.CompilerParams(vmem_limit_bytes=60 * MIB),
        cost_estimate=pl.CostEstimate(
            flops=2 * k_local * modes * excitons * depth * (rows_e + rows_h),
            bytes_accessed=2 * coeffs.size * (1 + modes),
            transcendentals=0,
        ),
    )(band_first, coeffs, g_cond, g_val)


def turn_kernel(first, coeffs_ref, *refs):
    *out_refs, held, sems = refs
    pieces, k_local, parts, rows, width = held.shape
    size = lax.axis_size("ka")
    behind_z = lax.shift_right_logical(lax.rem(lax.axis_index("ka") + size - 1, size), 2)

    def copy(i, k, p):
        columns = pl.ds(pl.multiple_of((behind_z ^ (3 - first - i)) * width, width), width)
        source = coeffs_ref.at[k, pl.ds(p * rows, rows), columns]
        return pltpu.make_async_copy(source, held.at[i, k, p], sems.at[i, k, p])

    steps = [(i, k, p) for i in range(pieces) for k in range(k_local) for p in range(parts)]
    for step in steps:
        copy(*step).start()
    for step in steps:
        i, k, p = step
        copy(*step).wait()
        out_refs[i][k, :, p * rows:(p + 1) * rows] = held[i, k, p].T


def turned_pieces(flat, first, pieces, width):
    k_local, depth, _ = flat.shape
    parts = 2
    return pl.pallas_call(
        functools.partial(turn_kernel, first),
        out_shape=[jax.ShapeDtypeStruct((k_local, width, depth), jnp.bfloat16)] * pieces,
        in_specs=[pl.BlockSpec(memory_space=pl.ANY)],
        out_specs=[pl.BlockSpec(memory_space=pltpu.VMEM)] * pieces,
        scratch_shapes=[
            pltpu.VMEM((pieces, k_local, parts, depth // parts, width), jnp.bfloat16),
            pltpu.SemaphoreType.DMA((pieces, k_local, parts)),
        ],
        compiler_params=pltpu.CompilerParams(vmem_limit_bytes=60 * MIB),
        cost_estimate=pl.CostEstimate(
            flops=0, bytes_accessed=4 * pieces * k_local * depth * width, transcendentals=0
        ),
    )(flat)


def rows_kernel(pick_ref, own_ref, next_ref, right_ref, mine_ref, other_ref, send_ref, *refs):
    own_held, next_held, held, left, own_sems, next_sems, sems = refs
    k_local, depth, width = own_held.shape
    tiles, _, _, tile = held.shape
    per_mode = right_ref.shape[3] // tile
    core, x = pick_ref[k_local + 1], pick_ref[k_local + 2]
    columns = pl.ds(pl.multiple_of(pick_ref[k_local] * width, width), width)
    near = [pick_ref[k] < k_local for k in range(k_local)]

    def copy_own(k):
        source = own_ref.at[jnp.minimum(pick_ref[k], k_local - 1), :, columns]
        return pltpu.make_async_copy(source, own_held.at[k], own_sems.at[k])

    def copy_next(k):
        source = next_ref.at[jnp.maximum(pick_ref[k] - k_local, 0)]
        return pltpu.make_async_copy(source, next_held.at[k], next_sems.at[k])

    def copy_right(t, k):
        source = right_ref.at[k, t // per_mode, :, pl.ds(t % per_mode * tile, tile)]
        return pltpu.make_async_copy(source, held.at[t, k], sems.at[t, k])

    for k in range(k_local):
        copy_own(k).start()
        copy_next(k).start()
    for t in range(tiles):
        for k in range(k_local):
            copy_right(t, k).start()
    for k in range(k_local):
        copy_own(k).wait()
        copy_next(k).wait()

        @pl.when(near[k])
        def _():
            left[:, k * depth:(k + 1) * depth] = own_held[k].T

        @pl.when(jnp.logical_not(near[k]))
        def _():
            left[:, k * depth:(k + 1) * depth] = next_held[k]

    for t in range(tiles):
        for k in range(k_local):
            copy_right(t, k).wait()
        right = held[t].reshape(k_local * depth, tile)
        total = jnp.dot(left[...], right, preferred_element_type=jnp.float32)
        parts = total.reshape(2, 2, width // 4, tile)
        mine = jnp.where(x == 0, parts[0], parts[1])
        other = jnp.where(x == 0, parts[1], parts[0])
        place = slice(t * tile, (t + 1) * tile)
        mine_ref[:, place] = jnp.where(core == 0, mine[0], mine[1])
        other_ref[:, place] = jnp.where(core == 0, other[0], other[1])
        send_ref[:width // 4, place] = jnp.where(core == 0, mine[1], mine[0]).astype(jnp.bfloat16)
        send_ref[width // 4:, place] = jnp.where(core == 0, other[1], other[0]).astype(jnp.bfloat16)


def rows_of(pick, own, following, products):
    k_local, width, depth = following.shape
    modes, excitons = products.shape[1], products.shape[3]
    columns, tile = modes * excitons, 512
    tiles = columns // tile
    return pl.pallas_call(
        rows_kernel,
        out_shape=[
            jax.ShapeDtypeStruct((width // 4, columns), jnp.float32),
            jax.ShapeDtypeStruct((width // 4, columns), jnp.float32),
            jax.ShapeDtypeStruct((width // 2, columns), jnp.bfloat16),
        ],
        in_specs=[pl.BlockSpec(memory_space=pltpu.SMEM)]
        + [pl.BlockSpec(memory_space=pl.ANY)] * 3,
        out_specs=[pl.BlockSpec(memory_space=pltpu.VMEM)] * 3,
        scratch_shapes=[
            pltpu.VMEM((k_local, depth, width), jnp.bfloat16),
            pltpu.VMEM((k_local, width, depth), jnp.bfloat16),
            pltpu.VMEM((tiles, k_local, depth, tile), jnp.bfloat16),
            pltpu.VMEM((width, k_local * depth), jnp.bfloat16),
            pltpu.SemaphoreType.DMA((k_local,)),
            pltpu.SemaphoreType.DMA((k_local,)),
            pltpu.SemaphoreType.DMA((tiles, k_local)),
        ],
        compiler_params=pltpu.CompilerParams(vmem_limit_bytes=50 * MIB),
        cost_estimate=pl.CostEstimate(
            flops=2 * k_local * depth * width * columns,
            bytes_accessed=2 * k_local * depth * columns,
            transcendentals=0,
        ),
    )(pick, own, following, products)


def payloads_kernel(*refs):
    ins, (turn_0, turn_1, far_1, near_0, near_1, mine_1) = refs[:9], refs[9:]
    half = turn_0.shape[0]

    def summed(block, own):
        mine, other, core = ins[3 * block:3 * block + 3]
        rows = slice(0, half) if own else slice(half, 2 * half)
        return (mine if own else other)[...] + core[rows, :].astype(jnp.float32)

    far_0 = summed(0, True).astype(jnp.bfloat16)
    across = summed(1, False).astype(jnp.bfloat16)
    first = lax.axis_index("ka") & 1 == 0
    turn_0[...] = jnp.where(first, across, far_0)
    turn_1[...] = jnp.where(first, far_0, across)
    far_1[...] = summed(0, False).astype(jnp.bfloat16)
    near_0[...] = summed(2, True).astype(jnp.bfloat16)
    near_1[...] = summed(2, False).astype(jnp.bfloat16)
    mine_1[...] = summed(1, True)


def payloads_of(*parts):
    shape = parts[0].shape
    return pl.pallas_call(
        payloads_kernel,
        out_shape=[jax.ShapeDtypeStruct(shape, jnp.bfloat16)] * 5
        + [jax.ShapeDtypeStruct(shape, jnp.float32)],
        in_specs=[pl.BlockSpec(memory_space=pltpu.VMEM)] * 9,
        out_specs=[pl.BlockSpec(memory_space=pltpu.VMEM)] * 6,
        compiler_params=pltpu.CompilerParams(vmem_limit_bytes=24 * MIB),
        cost_estimate=pl.CostEstimate(
            flops=6 * parts[0].size, bytes_accessed=26 * parts[0].size, transcendentals=0
        ),
    )(*parts)


def close_kernel(factor, mine_ref, core_ref, *refs):
    *parts, out_ref = refs
    half, modes, excitons = out_ref.shape
    for m in range(modes):
        columns = slice(m * excitons, (m + 1) * excitons)
        total = mine_ref[:, columns] + core_ref[:half, columns].astype(jnp.float32)
        for ref in parts:
            total = total + ref[:, columns].astype(jnp.float32)
        out_ref[:, m, :] = total * factor


def closed(modes, factor, *parts):
    rows, columns = parts[0].shape
    return pl.pallas_call(
        functools.partial(close_kernel, factor),
        out_shape=jax.ShapeDtypeStruct((rows, modes, columns // modes), jnp.float32),
        in_specs=[pl.BlockSpec(memory_space=pltpu.VMEM)] * len(parts),
        out_specs=pl.BlockSpec(memory_space=pltpu.VMEM),
        compiler_params=pltpu.CompilerParams(vmem_limit_bytes=24 * MIB),
        cost_estimate=pl.CostEstimate(
            flops=5 * parts[0].size, bytes_accessed=16 * parts[0].size, transcendentals=0
        ),
    )(*parts)


def on_two_by_four(coeffs, g_cond, g_val, k_plus_q, band_first, norm_factor):
    k_local, bands_c, bands_v, excitons = coeffs.shape
    modes = g_cond.shape[1]
    size = lax.axis_size("ka")
    width = excitons // 4
    me = lax.axis_index("ka")
    core, x, z = me & 1, me >> 1 & 1, me >> 2
    flat = coeffs.reshape(k_local, bands_c * bands_v, excitons)

    pieces = turned_pieces(flat, 0, 1, width)
    rest, _ = lax.optimization_barrier((flat, pieces))
    pieces += turned_pieces(rest, 1, 3, width)
    following = [permute(piece, lambda i: i - 1) for piece in pieces]
    products = products_of(coeffs, g_cond, g_val, band_first)
    products = products.reshape(k_local, modes, bands_c * bands_v, excitons)
    places = jnp.mod(k_plus_q - me * k_local, k_local * size)

    def rows(step, after):
        pick = jnp.concatenate((places, jnp.stack((z ^ (3 - step), core, x))))
        pick, _ = lax.optimization_barrier((pick, after))
        mine, other, send = rows_of(pick, flat, following[step], products)
        return mine, other, permute(send, lambda i: i ^ 1)

    half = width // 4

    def over(value, bits):
        return permute(value.astype(jnp.bfloat16), lambda i: i ^ bits)

    def total_of(value, *arrived):
        for array in arrived:
            value = value + array.astype(jnp.float32)
        return value

    step_0 = rows(0, products)
    step_1 = rows(1, step_0[0])
    step_2 = rows(2, step_1[0])
    core_0, core_1, core_2, following[3] = lax.optimization_barrier(
        (step_0[2], step_1[2], step_2[2], following[3])
    )
    *sends, mine_1 = payloads_of(
        *step_0[:2], core_0, *step_1[:2], core_1, *step_2[:2], core_2
    )
    step_3 = rows(3, sends)
    arrived = [
        permute(sends[turn], lambda i: i ^ (2 if i % 2 == turn else 4)) for turn in range(2)
    ]
    arrived.append(over(sends[2], 6))
    near = over(sends[3], 4), over(sends[4], 6)
    mine_1, _ = lax.optimization_barrier((mine_1, step_3[0]))
    pair = over(total_of(mine_1, *arrived), 8)
    mine_3, other_3, core_3 = step_3
    across_3 = over(other_3 + core_3[half:].astype(jnp.float32), 2)
    return closed(modes, norm_factor, mine_3, core_3, across_3, pair, *near)


def on_any(coeffs, g_cond, g_val, k_plus_q, band_first, norm_factor):
    k_local, bands_c, bands_v, excitons = coeffs.shape
    modes = g_cond.shape[1]
    size = lax.axis_size("ka")
    depth = bands_c * bands_v
    flat = coeffs.reshape(k_local, depth, excitons)
    blocks = jnp.concatenate((flat, permute(flat, lambda i: i - 1)), 0)
    offsets = jnp.mod(k_plus_q - lax.axis_index("ka") * k_local, k_local * size)
    products = products_of(coeffs, g_cond, g_val, band_first)
    products = products.reshape(k_local, modes, depth, excitons)
    partners = [
        lax.dynamic_index_in_dim(blocks, offsets[k], 0, keepdims=False) for k in range(k_local)
    ]
    running = jnp.einsum(
        "kds,kmdt->smt", jnp.stack(partners), products, preferred_element_type=jnp.float32
    )
    return lax.psum_scatter(running * norm_factor, "ka", scatter_dimension=0, tiled=True)


def shards(coeffs, g_cond, g_val, k_plus_q, band_first):
    k_local, bands_c, bands_v, excitons = coeffs.shape
    size = lax.axis_size("ka")
    norm_factor = 1.0 / math.sqrt(bands_c * bands_v * k_local * size)
    whole_tiles = excitons % (4 * 128) == 0
    plan = on_two_by_four if size == 16 and whole_tiles else on_any
    return plan(coeffs, g_cond, g_val, k_plus_q, band_first, norm_factor)


def solution(mesh):
    in_specs = (
        P(("groups", "ka"), None, None, None),
        P(("groups", "ka"), None, None, None),
        P(("groups", "ka"), None, None, None),
        P(("groups", "ka")),
        P("groups", None),
    )
    out_specs = P(("groups", "ka"), None, None)
    return jax.shard_map(shards, mesh=mesh, in_specs=in_specs, out_specs=out_specs, check_vma=False)
```

```python
import functools
import math

import jax
import jax.numpy as jnp
from jax import lax
from jax.experimental import pallas as pl
from jax.experimental.pallas import tpu as pltpu
from jax.sharding import PartitionSpec as P

MIB = 1024 * 1024


def permute(x, target):
    size = lax.axis_size("ka")
    pairs = [(i, target(i)) for i in range(size)]
    return lax.ppermute(x, "ka", [(i, j % size) for i, j in pairs if j is not None])


def nt_dot(a, b):
    return lax.dot_general(a, b, (((1,), (1,)), ((), ())), preferred_element_type=jnp.float32)


def iotas(rows, cols):
    shape = (rows, cols)
    return lax.broadcasted_iota(jnp.int32, shape, 0), lax.broadcasted_iota(jnp.int32, shape, 1)


def ones_where(condition):
    return jnp.where(condition, 1.0, 0.0).astype(jnp.bfloat16)


PART_C, PART_V = 8, 16


def fill_weights(first_ref, cond_ref, val_ref, we_ref, wh_ref):
    _, modes, bands_c, _ = cond_ref.shape
    bands_v = val_ref.shape[2]
    rows_e, rows_h = bands_c * PART_V, PART_C * bands_v
    row, col = iotas(rows_e, bands_c)
    take = ones_where(row // PART_V == col)
    row, col = iotas(rows_e, rows_e)
    for m in range(modes):
        half = jnp.dot(take, cond_ref[0, m], preferred_element_type=jnp.float32)
        full = nt_dot(half.astype(jnp.bfloat16), take)
        keep = (row % PART_V == col % PART_V) & (row // PART_V >= first_ref[m, 0])
        we_ref[m * rows_e:(m + 1) * rows_e, :] = jnp.where(keep, full, 0.0).astype(jnp.bfloat16)
    row, col = iotas(rows_h, bands_v)
    take = ones_where(row % bands_v == col)
    row, col = iotas(rows_h, rows_h)
    for m in range(modes):
        half = nt_dot(take, val_ref[0, m])
        full = nt_dot(half.astype(jnp.bfloat16), take)
        keep = (row // bands_v == col // bands_v) & (row % bands_v >= first_ref[m, 1])
        wh_ref[m * rows_h:(m + 1) * rows_h, :] = jnp.where(keep, full, 0.0).astype(jnp.bfloat16)


def products_kernel(first_ref, coeffs_ref, cond_ref, val_ref, out_ref, we_ref, wh_ref):
    _, bands_c, bands_v, tile = coeffs_ref.shape
    modes = cond_ref.shape[1]
    rows_e, rows_h = bands_c * PART_V, PART_C * bands_v

    @pl.when(pl.program_id(1) == 0)
    def _():
        fill_weights(first_ref, cond_ref, val_ref, we_ref, wh_ref)

    electron = []
    for h in range(bands_v // PART_V):
        x = coeffs_ref[0, :, h * PART_V:(h + 1) * PART_V, :].reshape(rows_e, tile)
        e = jnp.dot(we_ref[...], x, preferred_element_type=jnp.float32)
        electron.append(e.reshape(modes, bands_c, PART_V, tile))
    for q in range(bands_c // PART_C):
        own = slice(q * PART_C, (q + 1) * PART_C)
        y = coeffs_ref[0, own].reshape(rows_h, tile)
        hole = jnp.dot(wh_ref[...], y, preferred_element_type=jnp.float32)
        hole = hole.reshape(modes, PART_C, bands_v, tile)
        for m in range(modes):
            for h in range(bands_v // PART_V):
                cols = slice(h * PART_V, (h + 1) * PART_V)
                value = electron[h][m, own] - hole[m, :, cols]
                out_ref[0, m, own, cols, :] = value.astype(jnp.bfloat16)


def products_of(coeffs, g_cond, g_val, band_first):
    k_local, bands_c, bands_v, excitons = coeffs.shape
    modes = g_cond.shape[1]
    tile = 256
    rows_e, rows_h = bands_c * PART_V, PART_C * bands_v
    depth = bands_c * bands_v
    return pl.pallas_call(
        products_kernel,
        out_shape=jax.ShapeDtypeStruct((k_local, modes, bands_c, bands_v, excitons), jnp.bfloat16),
        grid=(k_local, excitons // tile),
        in_specs=[
            pl.BlockSpec(memory_space=pltpu.SMEM),
            pl.BlockSpec((1, bands_c, bands_v, tile), lambda k, s: (k, 0, 0, s)),
            pl.BlockSpec((1, modes, bands_c, bands_c), lambda k, s: (k, 0, 0, 0)),
            pl.BlockSpec((1, modes, bands_v, bands_v), lambda k, s: (k, 0, 0, 0)),
        ],
        out_specs=pl.BlockSpec((1, modes, bands_c, bands_v, tile), lambda k, s: (k, 0, 0, 0, s)),
        scratch_shapes=[
            pltpu.VMEM((modes * rows_e, rows_e), jnp.bfloat16),
            pltpu.VMEM((modes * rows_h, rows_h), jnp.bfloat16),
        ],
        compiler_params=pltpu.CompilerParams(vmem_limit_bytes=60 * MIB),
        cost_estimate=pl.CostEstimate(
            flops=2 * k_local * modes * excitons * depth * (rows_e + rows_h),
            bytes_accessed=2 * coeffs.size * (1 + modes),
            transcendentals=0,
        ),
    )(band_first, coeffs, g_cond, g_val)


def columns_of(step, width):
    size = lax.axis_size("ka")
    behind_z = lax.shift_right_logical(lax.rem(lax.axis_index("ka") + size - 1, size), 2)
    return pl.ds(pl.multiple_of((behind_z ^ (3 - step)) * width, width), width)


def cut_kernel(coeffs_ref, out_ref, sems):
    k_local, parts = sems.shape
    _, depth, width = out_ref.shape
    columns, count = columns_of(0, width), depth // parts
    copies = []
    for k in range(k_local):
        for p in range(parts):
            rows = pl.ds(p * count, count)
            copies.append(
                pltpu.make_async_copy(
                    coeffs_ref.at[k, rows, columns], out_ref.at[k, rows], sems.at[k, p]
                )
            )
    for copy in copies:
        copy.start()
    for copy in copies:
        copy.wait()


def cut_piece(flat, width):
    k_local, depth, _ = flat.shape
    return pl.pallas_call(
        cut_kernel,
        out_shape=jax.ShapeDtypeStruct((k_local, depth, width), jnp.bfloat16),
        in_specs=[pl.BlockSpec(memory_space=pl.ANY)],
        out_specs=pl.BlockSpec(memory_space=pl.ANY),
        scratch_shapes=[pltpu.SemaphoreType.DMA((k_local, 4))],
        compiler_params=pltpu.CompilerParams(vmem_limit_bytes=60 * MIB),
        cost_estimate=pl.CostEstimate(
            flops=0, bytes_accessed=4 * k_local * depth * width, transcendentals=0
        ),
    )(flat)


def turn_kernel(coeffs_ref, *refs):
    *out_refs, held, sems = refs
    pieces, k_local, parts, rows, width = held.shape

    def copy(i, k, p):
        columns = columns_of(1 + i, width)
        source = coeffs_ref.at[k, pl.ds(p * rows, rows), columns]
        return pltpu.make_async_copy(source, held.at[i, k, p], sems.at[i, k, p])

    steps = [(i, k, p) for i in range(pieces) for k in range(k_local) for p in range(parts)]
    for step in steps:
        copy(*step).start()
    for step in steps:
        i, k, p = step
        copy(*step).wait()
        out_refs[i][k, :, p * rows:(p + 1) * rows] = held[i, k, p].T


def turned_pieces(flat, pieces, width):
    k_local, depth, _ = flat.shape
    parts = 2
    return pl.pallas_call(
        turn_kernel,
        out_shape=[jax.ShapeDtypeStruct((k_local, width, depth), jnp.bfloat16)] * pieces,
        in_specs=[pl.BlockSpec(memory_space=pl.ANY)],
        out_specs=[pl.BlockSpec(memory_space=pltpu.VMEM)] * pieces,
        scratch_shapes=[
            pltpu.VMEM((pieces, k_local, parts, depth // parts, width), jnp.bfloat16),
            pltpu.SemaphoreType.DMA((pieces, k_local, parts)),
        ],
        compiler_params=pltpu.CompilerParams(vmem_limit_bytes=60 * MIB),
        cost_estimate=pl.CostEstimate(
            flops=0, bytes_accessed=4 * pieces * k_local * depth * width, transcendentals=0
        ),
    )(flat)


def rows_kernel(turned, pick_ref, own_ref, next_ref, right_ref, mine_ref, other_ref, send_ref, *refs):
    own_held, next_held, held, left, own_sems, next_sems, sems = refs
    k_local, depth, width = own_held.shape
    tiles, _, _, tile = held.shape
    per_mode = right_ref.shape[3] // tile
    core, x = pick_ref[k_local + 1], pick_ref[k_local + 2]
    columns = pl.ds(pl.multiple_of(pick_ref[k_local] * width, width), width)
    near = [pick_ref[k] < k_local for k in range(k_local)]

    def copy_own(k):
        source = own_ref.at[jnp.minimum(pick_ref[k], k_local - 1), :, columns]
        return pltpu.make_async_copy(source, own_held.at[k], own_sems.at[k])

    def copy_next(k):
        source = next_ref.at[jnp.maximum(pick_ref[k] - k_local, 0)]
        return pltpu.make_async_copy(source, next_held.at[k], next_sems.at[k])

    def copy_right(t, k):
        source = right_ref.at[k, t // per_mode, :, pl.ds(t % per_mode * tile, tile)]
        return pltpu.make_async_copy(source, held.at[t, k], sems.at[t, k])

    for k in range(k_local):
        copy_own(k).start()
        copy_next(k).start()
    for t in range(tiles):
        for k in range(k_local):
            copy_right(t, k).start()
    for k in range(k_local):
        copy_own(k).wait()
        copy_next(k).wait()

        @pl.when(near[k])
        def _():
            left[:, k * depth:(k + 1) * depth] = own_held[k].T

        @pl.when(jnp.logical_not(near[k]))
        def _():
            left[:, k * depth:(k + 1) * depth] = next_held[k] if turned else next_held[k].T

    for t in range(tiles):
        for k in range(k_local):
            copy_right(t, k).wait()
        right = held[t].reshape(k_local * depth, tile)
        total = jnp.dot(left[...], right, preferred_element_type=jnp.float32)
        parts = total.reshape(2, 2, width // 4, tile)
        mine = jnp.where(x == 0, parts[0], parts[1])
        other = jnp.where(x == 0, parts[1], parts[0])
        place = slice(t * tile, (t + 1) * tile)
        mine_ref[:, place] = jnp.where(core == 0, mine[0], mine[1])
        other_ref[:, place] = jnp.where(core == 0, other[0], other[1])
        send_ref[:width // 4, place] = jnp.where(core == 0, mine[1], mine[0]).astype(jnp.bfloat16)
        send_ref[width // 4:, place] = jnp.where(core == 0, other[1], other[0]).astype(jnp.bfloat16)


def rows_of(pick, own, following, products, turned):
    k_local, depth = own.shape[:2]
    width = following.shape[1 if turned else 2]
    modes, excitons = products.shape[1], products.shape[3]
    columns, tile = modes * excitons, 512
    tiles = columns // tile
    return pl.pallas_call(
        functools.partial(rows_kernel, turned),
        out_shape=[
            jax.ShapeDtypeStruct((width // 4, columns), jnp.float32),
            jax.ShapeDtypeStruct((width // 4, columns), jnp.float32),
            jax.ShapeDtypeStruct((width // 2, columns), jnp.bfloat16),
        ],
        in_specs=[pl.BlockSpec(memory_space=pltpu.SMEM)]
        + [pl.BlockSpec(memory_space=pl.ANY)] * 3,
        out_specs=[pl.BlockSpec(memory_space=pltpu.VMEM)] * 3,
        scratch_shapes=[
            pltpu.VMEM((k_local, depth, width), jnp.bfloat16),
            pltpu.VMEM(following.shape, jnp.bfloat16),
            pltpu.VMEM((tiles, k_local, depth, tile), jnp.bfloat16),
            pltpu.VMEM((width, k_local * depth), jnp.bfloat16),
            pltpu.SemaphoreType.DMA((k_local,)),
            pltpu.SemaphoreType.DMA((k_local,)),
            pltpu.SemaphoreType.DMA((tiles, k_local)),
        ],
        compiler_params=pltpu.CompilerParams(vmem_limit_bytes=50 * MIB),
        cost_estimate=pl.CostEstimate(
            flops=2 * k_local * depth * width * columns,
            bytes_accessed=2 * k_local * depth * columns,
            transcendentals=0,
        ),
    )(pick, own, following, products)


def payloads_kernel(*refs):
    ins, (far_0, far_1, across, near_0, near_1, mine_1) = refs[:9], refs[9:]
    half = across.shape[0]

    def summed(block, own):
        mine, other, core = ins[3 * block:3 * block + 3]
        rows = slice(0, half) if own else slice(half, 2 * half)
        return (mine if own else other)[...] + core[rows, :].astype(jnp.float32)

    far_0[...] = summed(0, True).astype(jnp.bfloat16)
    far_1[...] = summed(0, False).astype(jnp.bfloat16)
    across[...] = summed(1, False).astype(jnp.bfloat16)
    near_0[...] = summed(2, True).astype(jnp.bfloat16)
    near_1[...] = summed(2, False).astype(jnp.bfloat16)
    mine_1[...] = summed(1, True)


def payloads_of(*parts):
    shape = parts[0].shape
    return pl.pallas_call(
        payloads_kernel,
        out_shape=[jax.ShapeDtypeStruct(shape, jnp.bfloat16)] * 5
        + [jax.ShapeDtypeStruct(shape, jnp.float32)],
        in_specs=[pl.BlockSpec(memory_space=pltpu.VMEM)] * 9,
        out_specs=[pl.BlockSpec(memory_space=pltpu.VMEM)] * 6,
        compiler_params=pltpu.CompilerParams(vmem_limit_bytes=24 * MIB),
        cost_estimate=pl.CostEstimate(
            flops=6 * parts[0].size, bytes_accessed=26 * parts[0].size, transcendentals=0
        ),
    )(*parts)


def close_kernel(factor, mine_ref, core_ref, *refs):
    *parts, out_ref = refs
    half, modes, excitons = out_ref.shape
    for m in range(modes):
        columns = slice(m * excitons, (m + 1) * excitons)
        total = mine_ref[:, columns] + core_ref[:half, columns].astype(jnp.float32)
        for ref in parts:
            total = total + ref[:, columns].astype(jnp.float32)
        out_ref[:, m, :] = total * factor


def closed(modes, factor, *parts):
    rows, columns = parts[0].shape
    return pl.pallas_call(
        functools.partial(close_kernel, factor),
        out_shape=jax.ShapeDtypeStruct((rows, modes, columns // modes), jnp.float32),
        in_specs=[pl.BlockSpec(memory_space=pltpu.VMEM)] * len(parts),
        out_specs=pl.BlockSpec(memory_space=pltpu.VMEM),
        compiler_params=pltpu.CompilerParams(vmem_limit_bytes=24 * MIB),
        cost_estimate=pl.CostEstimate(
            flops=5 * parts[0].size, bytes_accessed=16 * parts[0].size, transcendentals=0
        ),
    )(*parts)


def on_two_by_four(coeffs, g_cond, g_val, k_plus_q, band_first, norm_factor):
    k_local, bands_c, bands_v, excitons = coeffs.shape
    modes = g_cond.shape[1]
    size = lax.axis_size("ka")
    width = excitons // 4
    me = lax.axis_index("ka")
    core, x, z = me & 1, me >> 1 & 1, me >> 2
    flat = coeffs.reshape(k_local, bands_c * bands_v, excitons)

    pieces = [cut_piece(flat, width)]
    rest, _ = lax.optimization_barrier((flat, pieces))
    pieces += turned_pieces(rest, 3, width)
    following = [permute(piece, lambda i: i - 1) for piece in pieces]
    products = products_of(coeffs, g_cond, g_val, band_first)
    products = products.reshape(k_local, modes, bands_c * bands_v, excitons)
    places = jnp.mod(k_plus_q - me * k_local, k_local * size)

    def rows(step, after):
        pick = jnp.concatenate((places, jnp.stack((z ^ (3 - step), core, x))))
        pick, _ = lax.optimization_barrier((pick, after))
        mine, other, send = rows_of(pick, flat, following[step], products, step > 0)
        return mine, other, permute(send, lambda i: i ^ 1)

    half = width // 4

    def over(value, bits):
        return permute(value.astype(jnp.bfloat16), lambda i: i ^ bits)

    def total_of(value, *arrived):
        for array in arrived:
            value = value + array.astype(jnp.float32)
        return value

    step_0 = rows(0, products)
    step_1 = rows(1, step_0[0])
    step_2 = rows(2, step_1[0])
    core_0, core_1, core_2, following[3] = lax.optimization_barrier(
        (step_0[2], step_1[2], step_2[2], following[3])
    )
    *sends, mine_1 = payloads_of(
        *step_0[:2], core_0, *step_1[:2], core_1, *step_2[:2], core_2
    )
    step_3 = rows(3, sends)
    far = over(sends[0], 4), over(sends[1], 6)
    across_1 = over(sends[2], 2)
    near = over(sends[3], 4), over(sends[4], 6)
    mine_1, _ = lax.optimization_barrier((mine_1, step_3[0]))
    pair = over(total_of(mine_1, across_1, *far), 8)
    mine_3, other_3, core_3 = step_3
    across_3 = over(other_3 + core_3[half:].astype(jnp.float32), 2)
    return closed(modes, norm_factor, mine_3, core_3, across_3, pair, *near)


def on_any(coeffs, g_cond, g_val, k_plus_q, band_first, norm_factor):
    k_local, bands_c, bands_v, excitons = coeffs.shape
    modes = g_cond.shape[1]
    size = lax.axis_size("ka")
    depth = bands_c * bands_v
    flat = coeffs.reshape(k_local, depth, excitons)
    blocks = jnp.concatenate((flat, permute(flat, lambda i: i - 1)), 0)
    offsets = jnp.mod(k_plus_q - lax.axis_index("ka") * k_local, k_local * size)
    products = products_of(coeffs, g_cond, g_val, band_first)
    products = products.reshape(k_local, modes, depth, excitons)
    partners = [
        lax.dynamic_index_in_dim(blocks, offsets[k], 0, keepdims=False) for k in range(k_local)
    ]
    running = jnp.einsum(
        "kds,kmdt->smt", jnp.stack(partners), products, preferred_element_type=jnp.float32
    )
    return lax.psum_scatter(running * norm_factor, "ka", scatter_dimension=0, tiled=True)


def shards(coeffs, g_cond, g_val, k_plus_q, band_first):
    k_local, bands_c, bands_v, excitons = coeffs.shape
    size = lax.axis_size("ka")
    norm_factor = 1.0 / math.sqrt(bands_c * bands_v * k_local * size)
    whole_tiles = excitons % (4 * 128) == 0
    plan = on_two_by_four if size == 16 and whole_tiles else on_any
    return plan(coeffs, g_cond, g_val, k_plus_q, band_first, norm_factor)


def solution(mesh):
    in_specs = (
        P(("groups", "ka"), None, None, None),
        P(("groups", "ka"), None, None, None),
        P(("groups", "ka"), None, None, None),
        P(("groups", "ka")),
        P("groups", None),
    )
    out_specs = P(("groups", "ka"), None, None)
    return jax.shard_map(shards, mesh=mesh, in_specs=in_specs, out_specs=out_specs, check_vma=False)
```

```python
import functools
import math

import jax
import jax.numpy as jnp
from jax import lax
from jax.experimental import pallas as pl
from jax.experimental.pallas import tpu as pltpu
from jax.sharding import PartitionSpec as P

MIB = 1024 * 1024


def permute(x, target):
    size = lax.axis_size("ka")
    pairs = [(i, target(i)) for i in range(size)]
    return lax.ppermute(x, "ka", [(i, j % size) for i, j in pairs if j is not None])


def nt_dot(a, b):
    return lax.dot_general(a, b, (((1,), (1,)), ((), ())), preferred_element_type=jnp.float32)


def iotas(rows, cols):
    shape = (rows, cols)
    return lax.broadcasted_iota(jnp.int32, shape, 0), lax.broadcasted_iota(jnp.int32, shape, 1)


def ones_where(condition):
    return jnp.where(condition, 1.0, 0.0).astype(jnp.bfloat16)


PART_C, PART_V = 8, 16


def fill_weights(first_ref, cond_ref, val_ref, we_ref, wh_ref):
    _, modes, bands_c, _ = cond_ref.shape
    bands_v = val_ref.shape[2]
    rows_e, rows_h = bands_c * PART_V, PART_C * bands_v
    row, col = iotas(rows_e, bands_c)
    take = ones_where(row // PART_V == col)
    row, col = iotas(rows_e, rows_e)
    for m in range(modes):
        half = jnp.dot(take, cond_ref[0, m], preferred_element_type=jnp.float32)
        full = nt_dot(half.astype(jnp.bfloat16), take)
        keep = (row % PART_V == col % PART_V) & (row // PART_V >= first_ref[m, 0])
        we_ref[m * rows_e:(m + 1) * rows_e, :] = jnp.where(keep, full, 0.0).astype(jnp.bfloat16)
    row, col = iotas(rows_h, bands_v)
    take = ones_where(row % bands_v == col)
    row, col = iotas(rows_h, rows_h)
    for m in range(modes):
        half = nt_dot(take, val_ref[0, m])
        full = nt_dot(half.astype(jnp.bfloat16), take)
        keep = (row // bands_v == col // bands_v) & (row % bands_v >= first_ref[m, 1])
        wh_ref[m * rows_h:(m + 1) * rows_h, :] = jnp.where(keep, full, 0.0).astype(jnp.bfloat16)


def products_kernel(first_ref, coeffs_ref, cond_ref, val_ref, out_ref, we_ref, wh_ref):
    _, bands_c, bands_v, tile = coeffs_ref.shape
    modes = cond_ref.shape[1]
    rows_e, rows_h = bands_c * PART_V, PART_C * bands_v

    @pl.when(pl.program_id(1) == 0)
    def _():
        fill_weights(first_ref, cond_ref, val_ref, we_ref, wh_ref)

    electron = []
    for h in range(bands_v // PART_V):
        x = coeffs_ref[0, :, h * PART_V:(h + 1) * PART_V, :].reshape(rows_e, tile)
        e = jnp.dot(we_ref[...], x, preferred_element_type=jnp.float32)
        electron.append(e.reshape(modes, bands_c, PART_V, tile))
    for q in range(bands_c // PART_C):
        own = slice(q * PART_C, (q + 1) * PART_C)
        y = coeffs_ref[0, own].reshape(rows_h, tile)
        hole = jnp.dot(wh_ref[...], y, preferred_element_type=jnp.float32)
        hole = hole.reshape(modes, PART_C, bands_v, tile)
        for m in range(modes):
            for h in range(bands_v // PART_V):
                cols = slice(h * PART_V, (h + 1) * PART_V)
                value = electron[h][m, own] - hole[m, :, cols]
                out_ref[0, m, own, cols, :] = value.astype(jnp.bfloat16)


def products_of(coeffs, g_cond, g_val, band_first):
    k_local, bands_c, bands_v, excitons = coeffs.shape
    modes = g_cond.shape[1]
    tile = 256
    rows_e, rows_h = bands_c * PART_V, PART_C * bands_v
    depth = bands_c * bands_v
    return pl.pallas_call(
        products_kernel,
        out_shape=jax.ShapeDtypeStruct((k_local, modes, bands_c, bands_v, excitons), jnp.bfloat16),
        grid=(k_local, excitons // tile),
        in_specs=[
            pl.BlockSpec(memory_space=pltpu.SMEM),
            pl.BlockSpec((1, bands_c, bands_v, tile), lambda k, s: (k, 0, 0, s)),
            pl.BlockSpec((1, modes, bands_c, bands_c), lambda k, s: (k, 0, 0, 0)),
            pl.BlockSpec((1, modes, bands_v, bands_v), lambda k, s: (k, 0, 0, 0)),
        ],
        out_specs=pl.BlockSpec((1, modes, bands_c, bands_v, tile), lambda k, s: (k, 0, 0, 0, s)),
        scratch_shapes=[
            pltpu.VMEM((modes * rows_e, rows_e), jnp.bfloat16),
            pltpu.VMEM((modes * rows_h, rows_h), jnp.bfloat16),
        ],
        compiler_params=pltpu.CompilerParams(vmem_limit_bytes=60 * MIB),
        cost_estimate=pl.CostEstimate(
            flops=2 * k_local * modes * excitons * depth * (rows_e + rows_h),
            bytes_accessed=2 * coeffs.size * (1 + modes),
            transcendentals=0,
        ),
    )(band_first, coeffs, g_cond, g_val)


def columns_of(step, width):
    size = lax.axis_size("ka")
    behind_z = lax.shift_right_logical(lax.rem(lax.axis_index("ka") + size - 1, size), 2)
    return pl.ds(pl.multiple_of((behind_z ^ (3 - step)) * width, width), width)


def cut_kernel(coeffs_ref, out_ref, held, sems, out_sems):
    k_local, parts, rows, width = held.shape
    columns = columns_of(0, width)
    steps = [(k, p) for k in range(k_local) for p in range(parts)]

    def copy_in(k, p):
        source = coeffs_ref.at[k, pl.ds(p * rows, rows), columns]
        return pltpu.make_async_copy(source, held.at[k, p], sems.at[k, p])

    def copy_out(k, p):
        target = out_ref.at[k, pl.ds(p * rows, rows)]
        return pltpu.make_async_copy(held.at[k, p], target, out_sems.at[k, p])

    for step in steps:
        copy_in(*step).start()
    for step in steps:
        copy_in(*step).wait()
        copy_out(*step).start()
    for step in steps:
        copy_out(*step).wait()


def cut_piece(flat, width):
    k_local, depth, _ = flat.shape
    parts = 4
    return pl.pallas_call(
        cut_kernel,
        out_shape=jax.ShapeDtypeStruct((k_local, depth, width), jnp.bfloat16),
        in_specs=[pl.BlockSpec(memory_space=pl.ANY)],
        out_specs=pl.BlockSpec(memory_space=pl.ANY),
        scratch_shapes=[
            pltpu.VMEM((k_local, parts, depth // parts, width), jnp.bfloat16),
            pltpu.SemaphoreType.DMA((k_local, parts)),
            pltpu.SemaphoreType.DMA((k_local, parts)),
        ],
        compiler_params=pltpu.CompilerParams(vmem_limit_bytes=60 * MIB),
        cost_estimate=pl.CostEstimate(
            flops=0, bytes_accessed=4 * k_local * depth * width, transcendentals=0
        ),
    )(flat)


def turn_kernel(coeffs_ref, *refs):
    *out_refs, held, sems = refs
    pieces, k_local, parts, rows, width = held.shape

    def copy(i, k, p):
        columns = columns_of(1 + i, width)
        source = coeffs_ref.at[k, pl.ds(p * rows, rows), columns]
        return pltpu.make_async_copy(source, held.at[i, k, p], sems.at[i, k, p])

    steps = [(i, k, p) for i in range(pieces) for k in range(k_local) for p in range(parts)]
    for step in steps:
        copy(*step).start()
    for step in steps:
        i, k, p = step
        copy(*step).wait()
        out_refs[i][k, :, p * rows:(p + 1) * rows] = held[i, k, p].T


def turned_pieces(flat, pieces, width):
    k_local, depth, _ = flat.shape
    parts = 2
    return pl.pallas_call(
        turn_kernel,
        out_shape=[jax.ShapeDtypeStruct((k_local, width, depth), jnp.bfloat16)] * pieces,
        in_specs=[pl.BlockSpec(memory_space=pl.ANY)],
        out_specs=[pl.BlockSpec(memory_space=pltpu.VMEM)] * pieces,
        scratch_shapes=[
            pltpu.VMEM((pieces, k_local, parts, depth // parts, width), jnp.bfloat16),
            pltpu.SemaphoreType.DMA((pieces, k_local, parts)),
        ],
        compiler_params=pltpu.CompilerParams(vmem_limit_bytes=60 * MIB),
        cost_estimate=pl.CostEstimate(
            flops=0, bytes_accessed=4 * pieces * k_local * depth * width, transcendentals=0
        ),
    )(flat)


def rows_kernel(turned, pick_ref, own_ref, next_ref, right_ref, mine_ref, other_ref, send_ref, *refs):
    own_held, next_held, held, left, own_sems, next_sems, sems = refs
    k_local, depth, width = own_held.shape
    tiles, _, _, tile = held.shape
    per_mode = right_ref.shape[3] // tile
    core, x = pick_ref[k_local + 1], pick_ref[k_local + 2]
    columns = pl.ds(pl.multiple_of(pick_ref[k_local] * width, width), width)
    near = [pick_ref[k] < k_local for k in range(k_local)]

    def copy_own(k):
        source = own_ref.at[jnp.minimum(pick_ref[k], k_local - 1), :, columns]
        return pltpu.make_async_copy(source, own_held.at[k], own_sems.at[k])

    def copy_next(k):
        source = next_ref.at[jnp.maximum(pick_ref[k] - k_local, 0)]
        return pltpu.make_async_copy(source, next_held.at[k], next_sems.at[k])

    def copy_right(t, k):
        source = right_ref.at[k, t // per_mode, :, pl.ds(t % per_mode * tile, tile)]
        return pltpu.make_async_copy(source, held.at[t, k], sems.at[t, k])

    for k in range(k_local):
        copy_own(k).start()
        copy_next(k).start()
    for t in range(tiles):
        for k in range(k_local):
            copy_right(t, k).start()
    for k in range(k_local):
        copy_own(k).wait()
        copy_next(k).wait()

        @pl.when(near[k])
        def _():
            left[:, k * depth:(k + 1) * depth] = own_held[k].T

        @pl.when(jnp.logical_not(near[k]))
        def _():
            left[:, k * depth:(k + 1) * depth] = next_held[k] if turned else next_held[k].T

    for t in range(tiles):
        for k in range(k_local):
            copy_right(t, k).wait()
        right = held[t].reshape(k_local * depth, tile)
        total = jnp.dot(left[...], right, preferred_element_type=jnp.float32)
        parts = total.reshape(2, 2, width // 4, tile)
        mine = jnp.where(x == 0, parts[0], parts[1])
        other = jnp.where(x == 0, parts[1], parts[0])
        place = slice(t * tile, (t + 1) * tile)
        mine_ref[:, place] = jnp.where(core == 0, mine[0], mine[1])
        other_ref[:, place] = jnp.where(core == 0, other[0], other[1])
        send_ref[:width // 4, place] = jnp.where(core == 0, mine[1], mine[0]).astype(jnp.bfloat16)
        send_ref[width // 4:, place] = jnp.where(core == 0, other[1], other[0]).astype(jnp.bfloat16)


def rows_of(pick, own, following, products, turned):
    k_local, depth = own.shape[:2]
    width = following.shape[1 if turned else 2]
    modes, excitons = products.shape[1], products.shape[3]
    columns, tile = modes * excitons, 512
    tiles = columns // tile
    return pl.pallas_call(
        functools.partial(rows_kernel, turned),
        out_shape=[
            jax.ShapeDtypeStruct((width // 4, columns), jnp.float32),
            jax.ShapeDtypeStruct((width // 4, columns), jnp.float32),
            jax.ShapeDtypeStruct((width // 2, columns), jnp.bfloat16),
        ],
        in_specs=[pl.BlockSpec(memory_space=pltpu.SMEM)]
        + [pl.BlockSpec(memory_space=pl.ANY)] * 3,
        out_specs=[pl.BlockSpec(memory_space=pltpu.VMEM)] * 3,
        scratch_shapes=[
            pltpu.VMEM((k_local, depth, width), jnp.bfloat16),
            pltpu.VMEM(following.shape, jnp.bfloat16),
            pltpu.VMEM((tiles, k_local, depth, tile), jnp.bfloat16),
            pltpu.VMEM((width, k_local * depth), jnp.bfloat16),
            pltpu.SemaphoreType.DMA((k_local,)),
            pltpu.SemaphoreType.DMA((k_local,)),
            pltpu.SemaphoreType.DMA((tiles, k_local)),
        ],
        compiler_params=pltpu.CompilerParams(vmem_limit_bytes=50 * MIB),
        cost_estimate=pl.CostEstimate(
            flops=2 * k_local * depth * width * columns,
            bytes_accessed=2 * k_local * depth * columns,
            transcendentals=0,
        ),
    )(pick, own, following, products)


def payloads_kernel(*refs):
    ins, (far_0, far_1, across, near_0, near_1, mine_1) = refs[:9], refs[9:]
    half = across.shape[0]

    def summed(block, own):
        mine, other, core = ins[3 * block:3 * block + 3]
        rows = slice(0, half) if own else slice(half, 2 * half)
        return (mine if own else other)[...] + core[rows, :].astype(jnp.float32)

    far_0[...] = summed(0, True).astype(jnp.bfloat16)
    far_1[...] = summed(0, False).astype(jnp.bfloat16)
    across[...] = summed(1, False).astype(jnp.bfloat16)
    near_0[...] = summed(2, True).astype(jnp.bfloat16)
    near_1[...] = summed(2, False).astype(jnp.bfloat16)
    mine_1[...] = summed(1, True)


def payloads_of(*parts):
    shape = parts[0].shape
    return pl.pallas_call(
        payloads_kernel,
        out_shape=[jax.ShapeDtypeStruct(shape, jnp.bfloat16)] * 5
        + [jax.ShapeDtypeStruct(shape, jnp.float32)],
        in_specs=[pl.BlockSpec(memory_space=pltpu.VMEM)] * 9,
        out_specs=[pl.BlockSpec(memory_space=pltpu.VMEM)] * 6,
        compiler_params=pltpu.CompilerParams(vmem_limit_bytes=24 * MIB),
        cost_estimate=pl.CostEstimate(
            flops=6 * parts[0].size, bytes_accessed=26 * parts[0].size, transcendentals=0
        ),
    )(*parts)


def close_kernel(factor, mine_ref, core_ref, *refs):
    *parts, out_ref = refs
    half, modes, excitons = out_ref.shape
    for m in range(modes):
        columns = slice(m * excitons, (m + 1) * excitons)
        total = mine_ref[:, columns] + core_ref[:half, columns].astype(jnp.float32)
        for ref in parts:
            total = total + ref[:, columns].astype(jnp.float32)
        out_ref[:, m, :] = total * factor


def closed(modes, factor, *parts):
    rows, columns = parts[0].shape
    return pl.pallas_call(
        functools.partial(close_kernel, factor),
        out_shape=jax.ShapeDtypeStruct((rows, modes, columns // modes), jnp.float32),
        in_specs=[pl.BlockSpec(memory_space=pltpu.VMEM)] * len(parts),
        out_specs=pl.BlockSpec(memory_space=pltpu.VMEM),
        compiler_params=pltpu.CompilerParams(vmem_limit_bytes=24 * MIB),
        cost_estimate=pl.CostEstimate(
            flops=5 * parts[0].size, bytes_accessed=16 * parts[0].size, transcendentals=0
        ),
    )(*parts)


def on_two_by_four(coeffs, g_cond, g_val, k_plus_q, band_first, norm_factor):
    k_local, bands_c, bands_v, excitons = coeffs.shape
    modes = g_cond.shape[1]
    size = lax.axis_size("ka")
    width = excitons // 4
    me = lax.axis_index("ka")
    core, x, z = me & 1, me >> 1 & 1, me >> 2
    flat = coeffs.reshape(k_local, bands_c * bands_v, excitons)

    pieces = [cut_piece(flat, width)]
    rest, _ = lax.optimization_barrier((flat, pieces))
    pieces += turned_pieces(rest, 3, width)
    following = [permute(piece, lambda i: i - 1) for piece in pieces]
    products = products_of(coeffs, g_cond, g_val, band_first)
    products = products.reshape(k_local, modes, bands_c * bands_v, excitons)
    places = jnp.mod(k_plus_q - me * k_local, k_local * size)

    def rows(step, after):
        pick = jnp.concatenate((places, jnp.stack((z ^ (3 - step), core, x))))
        pick, _ = lax.optimization_barrier((pick, after))
        mine, other, send = rows_of(pick, flat, following[step], products, step > 0)
        return mine, other, permute(send, lambda i: i ^ 1)

    half = width // 4

    def over(value, bits):
        return permute(value.astype(jnp.bfloat16), lambda i: i ^ bits)

    def total_of(value, *arrived):
        for array in arrived:
            value = value + array.astype(jnp.float32)
        return value

    step_0 = rows(0, products)
    step_1 = rows(1, step_0[0])
    step_2 = rows(2, step_1[0])
    core_0, core_1, core_2, following[3] = lax.optimization_barrier(
        (step_0[2], step_1[2], step_2[2], following[3])
    )
    *sends, mine_1 = payloads_of(
        *step_0[:2], core_0, *step_1[:2], core_1, *step_2[:2], core_2
    )
    step_3 = rows(3, sends)
    far = over(sends[0], 4), over(sends[1], 6)
    across_1 = over(sends[2], 2)
    near = over(sends[3], 4), over(sends[4], 6)
    mine_1, _ = lax.optimization_barrier((mine_1, step_3[0]))
    pair = over(total_of(mine_1, across_1, *far), 8)
    mine_3, other_3, core_3 = step_3
    across_3 = over(other_3 + core_3[half:].astype(jnp.float32), 2)
    return closed(modes, norm_factor, mine_3, core_3, across_3, pair, *near)


def on_any(coeffs, g_cond, g_val, k_plus_q, band_first, norm_factor):
    k_local, bands_c, bands_v, excitons = coeffs.shape
    modes = g_cond.shape[1]
    size = lax.axis_size("ka")
    depth = bands_c * bands_v
    flat = coeffs.reshape(k_local, depth, excitons)
    blocks = jnp.concatenate((flat, permute(flat, lambda i: i - 1)), 0)
    offsets = jnp.mod(k_plus_q - lax.axis_index("ka") * k_local, k_local * size)
    products = products_of(coeffs, g_cond, g_val, band_first)
    products = products.reshape(k_local, modes, depth, excitons)
    partners = [
        lax.dynamic_index_in_dim(blocks, offsets[k], 0, keepdims=False) for k in range(k_local)
    ]
    running = jnp.einsum(
        "kds,kmdt->smt", jnp.stack(partners), products, preferred_element_type=jnp.float32
    )
    return lax.psum_scatter(running * norm_factor, "ka", scatter_dimension=0, tiled=True)


def shards(coeffs, g_cond, g_val, k_plus_q, band_first):
    k_local, bands_c, bands_v, excitons = coeffs.shape
    size = lax.axis_size("ka")
    norm_factor = 1.0 / math.sqrt(bands_c * bands_v * k_local * size)
    whole_tiles = excitons % (4 * 128) == 0
    plan = on_two_by_four if size == 16 and whole_tiles else on_any
    return plan(coeffs, g_cond, g_val, k_plus_q, band_first, norm_factor)


def solution(mesh):
    in_specs = (
        P(("groups", "ka"), None, None, None),
        P(("groups", "ka"), None, None, None),
        P(("groups", "ka"), None, None, None),
        P(("groups", "ka")),
        P("groups", None),
    )
    out_specs = P(("groups", "ka"), None, None)
    return jax.shard_map(shards, mesh=mesh, in_specs=in_specs, out_specs=out_specs, check_vma=False)
```

```python
import functools
import math

import jax
import jax.numpy as jnp
from jax import lax
from jax.experimental import pallas as pl
from jax.experimental.pallas import tpu as pltpu
from jax.sharding import PartitionSpec as P

MIB = 1024 * 1024


def permute(x, target):
    size = lax.axis_size("ka")
    pairs = [(i, target(i)) for i in range(size)]
    return lax.ppermute(x, "ka", [(i, j % size) for i, j in pairs if j is not None])


def nt_dot(a, b):
    return lax.dot_general(a, b, (((1,), (1,)), ((), ())), preferred_element_type=jnp.float32)


def iotas(rows, cols):
    shape = (rows, cols)
    return lax.broadcasted_iota(jnp.int32, shape, 0), lax.broadcasted_iota(jnp.int32, shape, 1)


def ones_where(condition):
    return jnp.where(condition, 1.0, 0.0).astype(jnp.bfloat16)


PART_C, PART_V = 8, 16


def fill_weights(first_ref, cond_ref, val_ref, we_ref, wh_ref):
    _, modes, bands_c, _ = cond_ref.shape
    bands_v = val_ref.shape[2]
    rows_e, rows_h = bands_c * PART_V, PART_C * bands_v
    row, col = iotas(rows_e, bands_c)
    take = ones_where(row // PART_V == col)
    row, col = iotas(rows_e, rows_e)
    for m in range(modes):
        half = jnp.dot(take, cond_ref[0, m], preferred_element_type=jnp.float32)
        full = nt_dot(half.astype(jnp.bfloat16), take)
        keep = (row % PART_V == col % PART_V) & (row // PART_V >= first_ref[m, 0])
        we_ref[m * rows_e:(m + 1) * rows_e, :] = jnp.where(keep, full, 0.0).astype(jnp.bfloat16)
    row, col = iotas(rows_h, bands_v)
    take = ones_where(row % bands_v == col)
    row, col = iotas(rows_h, rows_h)
    for m in range(modes):
        half = nt_dot(take, val_ref[0, m])
        full = nt_dot(half.astype(jnp.bfloat16), take)
        keep = (row // bands_v == col // bands_v) & (row % bands_v >= first_ref[m, 1])
        wh_ref[m * rows_h:(m + 1) * rows_h, :] = jnp.where(keep, full, 0.0).astype(jnp.bfloat16)


def products_kernel(first_ref, coeffs_ref, cond_ref, val_ref, out_ref, we_ref, wh_ref):
    _, bands_c, bands_v, tile = coeffs_ref.shape
    modes = cond_ref.shape[1]
    rows_e, rows_h = bands_c * PART_V, PART_C * bands_v

    @pl.when(pl.program_id(1) == 0)
    def _():
        fill_weights(first_ref, cond_ref, val_ref, we_ref, wh_ref)

    electron = []
    for h in range(bands_v // PART_V):
        x = coeffs_ref[0, :, h * PART_V:(h + 1) * PART_V, :].reshape(rows_e, tile)
        e = jnp.dot(we_ref[...], x, preferred_element_type=jnp.float32)
        electron.append(e.reshape(modes, bands_c, PART_V, tile))
    for q in range(bands_c // PART_C):
        own = slice(q * PART_C, (q + 1) * PART_C)
        y = coeffs_ref[0, own].reshape(rows_h, tile)
        hole = jnp.dot(wh_ref[...], y, preferred_element_type=jnp.float32)
        hole = hole.reshape(modes, PART_C, bands_v, tile)
        for m in range(modes):
            for h in range(bands_v // PART_V):
                cols = slice(h * PART_V, (h + 1) * PART_V)
                value = electron[h][m, own] - hole[m, :, cols]
                out_ref[0, m, own, cols, :] = value.astype(jnp.bfloat16)


def products_of(coeffs, g_cond, g_val, band_first):
    k_local, bands_c, bands_v, excitons = coeffs.shape
    modes = g_cond.shape[1]
    tile = 256
    rows_e, rows_h = bands_c * PART_V, PART_C * bands_v
    depth = bands_c * bands_v
    return pl.pallas_call(
        products_kernel,
        out_shape=jax.ShapeDtypeStruct((k_local, modes, bands_c, bands_v, excitons), jnp.bfloat16),
        grid=(k_local, excitons // tile),
        in_specs=[
            pl.BlockSpec(memory_space=pltpu.SMEM),
            pl.BlockSpec((1, bands_c, bands_v, tile), lambda k, s: (k, 0, 0, s)),
            pl.BlockSpec((1, modes, bands_c, bands_c), lambda k, s: (k, 0, 0, 0)),
            pl.BlockSpec((1, modes, bands_v, bands_v), lambda k, s: (k, 0, 0, 0)),
        ],
        out_specs=pl.BlockSpec((1, modes, bands_c, bands_v, tile), lambda k, s: (k, 0, 0, 0, s)),
        scratch_shapes=[
            pltpu.VMEM((modes * rows_e, rows_e), jnp.bfloat16),
            pltpu.VMEM((modes * rows_h, rows_h), jnp.bfloat16),
        ],
        compiler_params=pltpu.CompilerParams(vmem_limit_bytes=60 * MIB),
        cost_estimate=pl.CostEstimate(
            flops=2 * k_local * modes * excitons * depth * (rows_e + rows_h),
            bytes_accessed=2 * coeffs.size * (1 + modes),
            transcendentals=0,
        ),
    )(band_first, coeffs, g_cond, g_val)


def columns_of(step, width):
    size = lax.axis_size("ka")
    behind_z = lax.shift_right_logical(lax.rem(lax.axis_index("ka") + size - 1, size), 2)
    return pl.ds(pl.multiple_of((behind_z ^ (3 - step)) * width, width), width)


def cut_kernel(coeffs_ref, out_ref, held, sems, out_sems):
    k_local, parts, rows, width = held.shape
    columns = columns_of(0, width)
    steps = [(k, p) for k in range(k_local) for p in range(parts)]

    def copy_in(k, p):
        source = coeffs_ref.at[k, pl.ds(p * rows, rows), columns]
        return pltpu.make_async_copy(source, held.at[k, p], sems.at[k, p])

    def copy_out(k, p):
        target = out_ref.at[k, pl.ds(p * rows, rows)]
        return pltpu.make_async_copy(held.at[k, p], target, out_sems.at[k, p])

    for step in steps:
        copy_in(*step).start()
    for step in steps:
        copy_in(*step).wait()
        copy_out(*step).start()
    for step in steps:
        copy_out(*step).wait()


def cut_piece(flat, width):
    k_local, depth, _ = flat.shape
    parts = 4
    return pl.pallas_call(
        cut_kernel,
        out_shape=jax.ShapeDtypeStruct((k_local, depth, width), jnp.bfloat16),
        in_specs=[pl.BlockSpec(memory_space=pl.ANY)],
        out_specs=pl.BlockSpec(memory_space=pl.ANY),
        scratch_shapes=[
            pltpu.VMEM((k_local, parts, depth // parts, width), jnp.bfloat16),
            pltpu.SemaphoreType.DMA((k_local, parts)),
            pltpu.SemaphoreType.DMA((k_local, parts)),
        ],
        compiler_params=pltpu.CompilerParams(vmem_limit_bytes=60 * MIB),
        cost_estimate=pl.CostEstimate(
            flops=0, bytes_accessed=4 * k_local * depth * width, transcendentals=0
        ),
    )(flat)


def turn_kernel(coeffs_ref, *refs):
    *out_refs, held, sems = refs
    pieces, k_local, parts, rows, width = held.shape

    def copy(i, k, p):
        columns = columns_of(1 + i, width)
        source = coeffs_ref.at[k, pl.ds(p * rows, rows), columns]
        return pltpu.make_async_copy(source, held.at[i, k, p], sems.at[i, k, p])

    steps = [(i, k, p) for i in range(pieces) for k in range(k_local) for p in range(parts)]
    for step in steps:
        copy(*step).start()
    for step in steps:
        i, k, p = step
        copy(*step).wait()
        out_refs[i][k, :, p * rows:(p + 1) * rows] = held[i, k, p].T


def turned_pieces(flat, pieces, width):
    k_local, depth, _ = flat.shape
    parts = 2
    return pl.pallas_call(
        turn_kernel,
        out_shape=[jax.ShapeDtypeStruct((k_local, width, depth), jnp.bfloat16)] * pieces,
        in_specs=[pl.BlockSpec(memory_space=pl.ANY)],
        out_specs=[pl.BlockSpec(memory_space=pltpu.VMEM)] * pieces,
        scratch_shapes=[
            pltpu.VMEM((pieces, k_local, parts, depth // parts, width), jnp.bfloat16),
            pltpu.SemaphoreType.DMA((pieces, k_local, parts)),
        ],
        compiler_params=pltpu.CompilerParams(vmem_limit_bytes=60 * MIB),
        cost_estimate=pl.CostEstimate(
            flops=0, bytes_accessed=4 * pieces * k_local * depth * width, transcendentals=0
        ),
    )(flat)


def rows_kernel(turned, pick_ref, own_ref, next_ref, right_ref, mine_ref, other_ref, send_ref, *refs):
    own_held, next_held, held, left, own_sems, next_sems, sems = refs
    k_local, depth, width = own_held.shape
    tiles, _, _, tile = held.shape
    per_mode = right_ref.shape[3] // tile
    core, x = pick_ref[k_local + 1], pick_ref[k_local + 2]
    columns = pl.ds(pl.multiple_of(pick_ref[k_local] * width, width), width)
    near = [pick_ref[k] < k_local for k in range(k_local)]

    def copy_own(k):
        source = own_ref.at[jnp.minimum(pick_ref[k], k_local - 1), :, columns]
        return pltpu.make_async_copy(source, own_held.at[k], own_sems.at[k])

    def copy_next(k):
        source = next_ref.at[jnp.maximum(pick_ref[k] - k_local, 0)]
        return pltpu.make_async_copy(source, next_held.at[k], next_sems.at[k])

    def copy_right(t, k):
        source = right_ref.at[k, t // per_mode, :, pl.ds(t % per_mode * tile, tile)]
        return pltpu.make_async_copy(source, held.at[t, k], sems.at[t, k])

    for k in range(k_local):
        copy_own(k).start()
        copy_next(k).start()
    for t in range(tiles):
        for k in range(k_local):
            copy_right(t, k).start()
    for k in range(k_local):
        copy_own(k).wait()
        copy_next(k).wait()

        @pl.when(near[k])
        def _():
            left[:, k * depth:(k + 1) * depth] = own_held[k].T

        @pl.when(jnp.logical_not(near[k]))
        def _():
            left[:, k * depth:(k + 1) * depth] = next_held[k] if turned else next_held[k].T

    for t in range(tiles):
        for k in range(k_local):
            copy_right(t, k).wait()
        right = held[t].reshape(k_local * depth, tile)
        total = jnp.dot(left[...], right, preferred_element_type=jnp.float32)
        parts = total.reshape(2, 2, width // 4, tile)
        mine = jnp.where(x == 0, parts[0], parts[1])
        other = jnp.where(x == 0, parts[1], parts[0])
        place = slice(t * tile, (t + 1) * tile)
        mine_ref[:, place] = jnp.where(core == 0, mine[0], mine[1])
        other_ref[:, place] = jnp.where(core == 0, other[0], other[1])
        send_ref[:width // 4, place] = jnp.where(core == 0, mine[1], mine[0]).astype(jnp.bfloat16)
        send_ref[width // 4:, place] = jnp.where(core == 0, other[1], other[0]).astype(jnp.bfloat16)


def rows_of(pick, own, following, products, turned):
    k_local, depth = own.shape[:2]
    width = following.shape[1 if turned else 2]
    modes, excitons = products.shape[1], products.shape[3]
    columns, tile = modes * excitons, 512
    tiles = columns // tile
    return pl.pallas_call(
        functools.partial(rows_kernel, turned),
        out_shape=[
            jax.ShapeDtypeStruct((width // 4, columns), jnp.float32),
            jax.ShapeDtypeStruct((width // 4, columns), jnp.float32),
            jax.ShapeDtypeStruct((width // 2, columns), jnp.bfloat16),
        ],
        in_specs=[pl.BlockSpec(memory_space=pltpu.SMEM)]
        + [pl.BlockSpec(memory_space=pl.ANY)] * 3,
        out_specs=[pl.BlockSpec(memory_space=pltpu.VMEM)] * 3,
        scratch_shapes=[
            pltpu.VMEM((k_local, depth, width), jnp.bfloat16),
            pltpu.VMEM(following.shape, jnp.bfloat16),
            pltpu.VMEM((tiles, k_local, depth, tile), jnp.bfloat16),
            pltpu.VMEM((width, k_local * depth), jnp.bfloat16),
            pltpu.SemaphoreType.DMA((k_local,)),
            pltpu.SemaphoreType.DMA((k_local,)),
            pltpu.SemaphoreType.DMA((tiles, k_local)),
        ],
        compiler_params=pltpu.CompilerParams(vmem_limit_bytes=50 * MIB),
        cost_estimate=pl.CostEstimate(
            flops=2 * k_local * depth * width * columns,
            bytes_accessed=2 * k_local * depth * columns,
            transcendentals=0,
        ),
    )(pick, own, following, products)


def payloads_kernel(*refs):
    ins, (turn_0, turn_1, far_0, near_0, near_1, mine_1) = refs[:9], refs[9:]
    half = turn_0.shape[0]

    def summed(block, own):
        mine, other, core = ins[3 * block:3 * block + 3]
        rows = slice(0, half) if own else slice(half, 2 * half)
        return (mine if own else other)[...] + core[rows, :].astype(jnp.float32)

    far_1 = summed(0, False).astype(jnp.bfloat16)
    across = summed(1, False).astype(jnp.bfloat16)
    first = lax.axis_index("ka") & 1 == 0
    turn_0[...] = jnp.where(first, across, far_1)
    turn_1[...] = jnp.where(first, far_1, across)
    far_0[...] = summed(0, True).astype(jnp.bfloat16)
    near_0[...] = summed(2, True).astype(jnp.bfloat16)
    near_1[...] = summed(2, False).astype(jnp.bfloat16)
    mine_1[...] = summed(1, True)


def payloads_of(*parts):
    shape = parts[0].shape
    return pl.pallas_call(
        payloads_kernel,
        out_shape=[jax.ShapeDtypeStruct(shape, jnp.bfloat16)] * 5
        + [jax.ShapeDtypeStruct(shape, jnp.float32)],
        in_specs=[pl.BlockSpec(memory_space=pltpu.VMEM)] * 9,
        out_specs=[pl.BlockSpec(memory_space=pltpu.VMEM)] * 6,
        compiler_params=pltpu.CompilerParams(vmem_limit_bytes=24 * MIB),
        cost_estimate=pl.CostEstimate(
            flops=6 * parts[0].size, bytes_accessed=26 * parts[0].size, transcendentals=0
        ),
    )(*parts)


def close_kernel(factor, mine_ref, core_ref, *refs):
    *parts, out_ref = refs
    half, modes, excitons = out_ref.shape
    for m in range(modes):
        columns = slice(m * excitons, (m + 1) * excitons)
        total = mine_ref[:, columns] + core_ref[:half, columns].astype(jnp.float32)
        for ref in parts:
            total = total + ref[:, columns].astype(jnp.float32)
        out_ref[:, m, :] = total * factor


def closed(modes, factor, *parts):
    rows, columns = parts[0].shape
    return pl.pallas_call(
        functools.partial(close_kernel, factor),
        out_shape=jax.ShapeDtypeStruct((rows, modes, columns // modes), jnp.float32),
        in_specs=[pl.BlockSpec(memory_space=pltpu.VMEM)] * len(parts),
        out_specs=pl.BlockSpec(memory_space=pltpu.VMEM),
        compiler_params=pltpu.CompilerParams(vmem_limit_bytes=24 * MIB),
        cost_estimate=pl.CostEstimate(
            flops=5 * parts[0].size, bytes_accessed=16 * parts[0].size, transcendentals=0
        ),
    )(*parts)


def on_two_by_four(coeffs, g_cond, g_val, k_plus_q, band_first, norm_factor):
    k_local, bands_c, bands_v, excitons = coeffs.shape
    modes = g_cond.shape[1]
    size = lax.axis_size("ka")
    width = excitons // 4
    me = lax.axis_index("ka")
    core, x, z = me & 1, me >> 1 & 1, me >> 2
    flat = coeffs.reshape(k_local, bands_c * bands_v, excitons)

    pieces = [cut_piece(flat, width)]
    rest, _ = lax.optimization_barrier((flat, pieces))
    pieces += turned_pieces(rest, 3, width)
    following = [permute(piece, lambda i: i - 1) for piece in pieces]
    products = products_of(coeffs, g_cond, g_val, band_first)
    products = products.reshape(k_local, modes, bands_c * bands_v, excitons)
    places = jnp.mod(k_plus_q - me * k_local, k_local * size)

    def rows(step, after):
        pick = jnp.concatenate((places, jnp.stack((z ^ (3 - step), core, x))))
        pick, _ = lax.optimization_barrier((pick, after))
        mine, other, send = rows_of(pick, flat, following[step], products, step > 0)
        return mine, other, permute(send, lambda i: i ^ 1)

    half = width // 4

    def over(value, bits):
        return permute(value.astype(jnp.bfloat16), lambda i: i ^ bits)

    def total_of(value, *arrived):
        for array in arrived:
            value = value + array.astype(jnp.float32)
        return value

    step_0 = rows(0, products)
    step_1 = rows(1, step_0[0])
    step_2 = rows(2, step_1[0])
    core_0, core_1, core_2, following[3] = lax.optimization_barrier(
        (step_0[2], step_1[2], step_2[2], following[3])
    )
    *sends, mine_1 = payloads_of(
        *step_0[:2], core_0, *step_1[:2], core_1, *step_2[:2], core_2
    )
    step_3 = rows(3, sends)
    arrived = [
        permute(sends[turn], lambda i: i ^ (2 if i % 2 == turn else 6)) for turn in range(2)
    ]
    arrived.append(over(sends[2], 4))
    near = over(sends[3], 4), over(sends[4], 6)
    mine_1, _ = lax.optimization_barrier((mine_1, step_3[0]))
    pair = over(total_of(mine_1, *arrived), 8)
    mine_3, other_3, core_3 = step_3
    across_3 = over(other_3 + core_3[half:].astype(jnp.float32), 2)
    return closed(modes, norm_factor, mine_3, core_3, across_3, pair, *near)


def on_any(coeffs, g_cond, g_val, k_plus_q, band_first, norm_factor):
    k_local, bands_c, bands_v, excitons = coeffs.shape
    modes = g_cond.shape[1]
    size = lax.axis_size("ka")
    depth = bands_c * bands_v
    flat = coeffs.reshape(k_local, depth, excitons)
    blocks = jnp.concatenate((flat, permute(flat, lambda i: i - 1)), 0)
    offsets = jnp.mod(k_plus_q - lax.axis_index("ka") * k_local, k_local * size)
    products = products_of(coeffs, g_cond, g_val, band_first)
    products = products.reshape(k_local, modes, depth, excitons)
    partners = [
        lax.dynamic_index_in_dim(blocks, offsets[k], 0, keepdims=False) for k in range(k_local)
    ]
    running = jnp.einsum(
        "kds,kmdt->smt", jnp.stack(partners), products, preferred_element_type=jnp.float32
    )
    return lax.psum_scatter(running * norm_factor, "ka", scatter_dimension=0, tiled=True)


def shards(coeffs, g_cond, g_val, k_plus_q, band_first):
    k_local, bands_c, bands_v, excitons = coeffs.shape
    size = lax.axis_size("ka")
    norm_factor = 1.0 / math.sqrt(bands_c * bands_v * k_local * size)
    whole_tiles = excitons % (4 * 128) == 0
    plan = on_two_by_four if size == 16 and whole_tiles else on_any
    return plan(coeffs, g_cond, g_val, k_plus_q, band_first, norm_factor)


def solution(mesh):
    in_specs = (
        P(("groups", "ka"), None, None, None),
        P(("groups", "ka"), None, None, None),
        P(("groups", "ka"), None, None, None),
        P(("groups", "ka")),
        P("groups", None),
    )
    out_specs = P(("groups", "ka"), None, None)
    return jax.shard_map(shards, mesh=mesh, in_specs=in_specs, out_specs=out_specs, check_vma=False)
```

```python
import functools
import math

import jax
import jax.numpy as jnp
from jax import lax
from jax.experimental import pallas as pl
from jax.experimental.pallas import tpu as pltpu
from jax.sharding import PartitionSpec as P

MIB = 1024 * 1024


def permute(x, target):
    size = lax.axis_size("ka")
    pairs = [(i, target(i)) for i in range(size)]
    return lax.ppermute(x, "ka", [(i, j % size) for i, j in pairs if j is not None])


def nt_dot(a, b):
    return lax.dot_general(a, b, (((1,), (1,)), ((), ())), preferred_element_type=jnp.float32)


def iotas(rows, cols):
    shape = (rows, cols)
    return lax.broadcasted_iota(jnp.int32, shape, 0), lax.broadcasted_iota(jnp.int32, shape, 1)


def ones_where(condition):
    return jnp.where(condition, 1.0, 0.0).astype(jnp.bfloat16)


PART_C, PART_V = 8, 16


def fill_weights(first_ref, cond_ref, val_ref, we_ref, wh_ref):
    _, modes, bands_c, _ = cond_ref.shape
    bands_v = val_ref.shape[2]
    rows_e, rows_h = bands_c * PART_V, PART_C * bands_v
    row, col = iotas(rows_e, bands_c)
    take = ones_where(row // PART_V == col)
    row, col = iotas(rows_e, rows_e)
    for m in range(modes):
        half = jnp.dot(take, cond_ref[0, m], preferred_element_type=jnp.float32)
        full = nt_dot(half.astype(jnp.bfloat16), take)
        keep = (row % PART_V == col % PART_V) & (row // PART_V >= first_ref[m, 0])
        we_ref[m * rows_e:(m + 1) * rows_e, :] = jnp.where(keep, full, 0.0).astype(jnp.bfloat16)
    row, col = iotas(rows_h, bands_v)
    take = ones_where(row % bands_v == col)
    row, col = iotas(rows_h, rows_h)
    for m in range(modes):
        half = nt_dot(take, val_ref[0, m])
        full = nt_dot(half.astype(jnp.bfloat16), take)
        keep = (row // bands_v == col // bands_v) & (row % bands_v >= first_ref[m, 1])
        wh_ref[m * rows_h:(m + 1) * rows_h, :] = jnp.where(keep, full, 0.0).astype(jnp.bfloat16)


def products_kernel(first_ref, coeffs_ref, cond_ref, val_ref, out_ref, we_ref, wh_ref):
    _, bands_c, bands_v, tile = coeffs_ref.shape
    modes = cond_ref.shape[1]
    rows_e, rows_h = bands_c * PART_V, PART_C * bands_v

    @pl.when(pl.program_id(1) == 0)
    def _():
        fill_weights(first_ref, cond_ref, val_ref, we_ref, wh_ref)

    electron = []
    for h in range(bands_v // PART_V):
        x = coeffs_ref[0, :, h * PART_V:(h + 1) * PART_V, :].reshape(rows_e, tile)
        e = jnp.dot(we_ref[...], x, preferred_element_type=jnp.float32)
        electron.append(e.reshape(modes, bands_c, PART_V, tile))
    for q in range(bands_c // PART_C):
        own = slice(q * PART_C, (q + 1) * PART_C)
        y = coeffs_ref[0, own].reshape(rows_h, tile)
        hole = jnp.dot(wh_ref[...], y, preferred_element_type=jnp.float32)
        hole = hole.reshape(modes, PART_C, bands_v, tile)
        for m in range(modes):
            for h in range(bands_v // PART_V):
                cols = slice(h * PART_V, (h + 1) * PART_V)
                value = electron[h][m, own] - hole[m, :, cols]
                out_ref[0, m, own, cols, :] = value.astype(jnp.bfloat16)


def products_of(coeffs, g_cond, g_val, band_first):
    k_local, bands_c, bands_v, excitons = coeffs.shape
    modes = g_cond.shape[1]
    tile = 256
    rows_e, rows_h = bands_c * PART_V, PART_C * bands_v
    depth = bands_c * bands_v
    return pl.pallas_call(
        products_kernel,
        out_shape=jax.ShapeDtypeStruct((k_local, modes, bands_c, bands_v, excitons), jnp.bfloat16),
        grid=(k_local, excitons // tile),
        in_specs=[
            pl.BlockSpec(memory_space=pltpu.SMEM),
            pl.BlockSpec((1, bands_c, bands_v, tile), lambda k, s: (k, 0, 0, s)),
            pl.BlockSpec((1, modes, bands_c, bands_c), lambda k, s: (k, 0, 0, 0)),
            pl.BlockSpec((1, modes, bands_v, bands_v), lambda k, s: (k, 0, 0, 0)),
        ],
        out_specs=pl.BlockSpec((1, modes, bands_c, bands_v, tile), lambda k, s: (k, 0, 0, 0, s)),
        scratch_shapes=[
            pltpu.VMEM((modes * rows_e, rows_e), jnp.bfloat16),
            pltpu.VMEM((modes * rows_h, rows_h), jnp.bfloat16),
        ],
        compiler_params=pltpu.CompilerParams(vmem_limit_bytes=60 * MIB),
        cost_estimate=pl.CostEstimate(
            flops=2 * k_local * modes * excitons * depth * (rows_e + rows_h),
            bytes_accessed=2 * coeffs.size * (1 + modes),
            transcendentals=0,
        ),
    )(band_first, coeffs, g_cond, g_val)


def columns_of(step, width):
    size = lax.axis_size("ka")
    behind_z = lax.shift_right_logical(lax.rem(lax.axis_index("ka") + size - 1, size), 2)
    return pl.ds(pl.multiple_of((behind_z ^ (3 - step)) * width, width), width)


def cut_kernel(coeffs_ref, out_ref, held, sems, out_sems):
    k_local, parts, rows, width = held.shape
    columns = columns_of(0, width)
    steps = [(k, p) for k in range(k_local) for p in range(parts)]

    def copy_in(k, p):
        source = coeffs_ref.at[k, pl.ds(p * rows, rows), columns]
        return pltpu.make_async_copy(source, held.at[k, p], sems.at[k, p])

    def copy_out(k, p):
        target = out_ref.at[k, pl.ds(p * rows, rows)]
        return pltpu.make_async_copy(held.at[k, p], target, out_sems.at[k, p])

    for step in steps:
        copy_in(*step).start()
    for step in steps:
        copy_in(*step).wait()
        copy_out(*step).start()
    for step in steps:
        copy_out(*step).wait()


def cut_piece(flat, width):
    k_local, depth, _ = flat.shape
    parts = 4
    return pl.pallas_call(
        cut_kernel,
        out_shape=jax.ShapeDtypeStruct((k_local, depth, width), jnp.bfloat16),
        in_specs=[pl.BlockSpec(memory_space=pl.ANY)],
        out_specs=pl.BlockSpec(memory_space=pl.ANY),
        scratch_shapes=[
            pltpu.VMEM((k_local, parts, depth // parts, width), jnp.bfloat16),
            pltpu.SemaphoreType.DMA((k_local, parts)),
            pltpu.SemaphoreType.DMA((k_local, parts)),
        ],
        compiler_params=pltpu.CompilerParams(vmem_limit_bytes=60 * MIB),
        cost_estimate=pl.CostEstimate(
            flops=0, bytes_accessed=4 * k_local * depth * width, transcendentals=0
        ),
    )(flat)


def turn_kernel(coeffs_ref, *refs):
    *out_refs, held, sems = refs
    pieces, k_local, parts, rows, width = held.shape

    def copy(i, k, p):
        columns = columns_of(1 + i, width)
        source = coeffs_ref.at[k, pl.ds(p * rows, rows), columns]
        return pltpu.make_async_copy(source, held.at[i, k, p], sems.at[i, k, p])

    steps = [(i, k, p) for i in range(pieces) for k in range(k_local) for p in range(parts)]
    for step in steps:
        copy(*step).start()
    for step in steps:
        i, k, p = step
        copy(*step).wait()
        out_refs[i][k, :, p * rows:(p + 1) * rows] = held[i, k, p].T


def turned_pieces(flat, pieces, width):
    k_local, depth, _ = flat.shape
    parts = 2
    return pl.pallas_call(
        turn_kernel,
        out_shape=[jax.ShapeDtypeStruct((k_local, width, depth), jnp.bfloat16)] * pieces,
        in_specs=[pl.BlockSpec(memory_space=pl.ANY)],
        out_specs=[pl.BlockSpec(memory_space=pltpu.VMEM)] * pieces,
        scratch_shapes=[
            pltpu.VMEM((pieces, k_local, parts, depth // parts, width), jnp.bfloat16),
            pltpu.SemaphoreType.DMA((pieces, k_local, parts)),
        ],
        compiler_params=pltpu.CompilerParams(vmem_limit_bytes=60 * MIB),
        cost_estimate=pl.CostEstimate(
            flops=0, bytes_accessed=4 * pieces * k_local * depth * width, transcendentals=0
        ),
    )(flat)


def rows_kernel(turned, pick_ref, own_ref, next_ref, right_ref, mine_ref, other_ref, send_ref, *refs):
    own_held, next_held, held, left, own_sems, next_sems, sems = refs
    k_local, depth, width = own_held.shape
    tiles, _, _, tile = held.shape
    per_mode = right_ref.shape[3] // tile
    core, x = pick_ref[k_local + 1], pick_ref[k_local + 2]
    columns = pl.ds(pl.multiple_of(pick_ref[k_local] * width, width), width)
    near = [pick_ref[k] < k_local for k in range(k_local)]

    def copy_own(k):
        source = own_ref.at[jnp.minimum(pick_ref[k], k_local - 1), :, columns]
        return pltpu.make_async_copy(source, own_held.at[k], own_sems.at[k])

    def copy_next(k):
        source = next_ref.at[jnp.maximum(pick_ref[k] - k_local, 0)]
        return pltpu.make_async_copy(source, next_held.at[k], next_sems.at[k])

    def copy_right(t, k):
        source = right_ref.at[k, t // per_mode, :, pl.ds(t % per_mode * tile, tile)]
        return pltpu.make_async_copy(source, held.at[t, k], sems.at[t, k])

    for k in range(k_local):
        copy_own(k).start()
        copy_next(k).start()
    for t in range(tiles):
        for k in range(k_local):
            copy_right(t, k).start()
    for k in range(k_local):
        copy_own(k).wait()
        copy_next(k).wait()

        @pl.when(near[k])
        def _():
            left[:, k * depth:(k + 1) * depth] = own_held[k].T

        @pl.when(jnp.logical_not(near[k]))
        def _():
            left[:, k * depth:(k + 1) * depth] = next_held[k] if turned else next_held[k].T

    for t in range(tiles):
        for k in range(k_local):
            copy_right(t, k).wait()
        right = held[t].reshape(k_local * depth, tile)
        total = jnp.dot(left[...], right, preferred_element_type=jnp.float32)
        parts = total.reshape(2, 2, width // 4, tile)
        mine = jnp.where(x == 0, parts[0], parts[1])
        other = jnp.where(x == 0, parts[1], parts[0])
        place = slice(t * tile, (t + 1) * tile)
        mine_ref[:, place] = jnp.where(core == 0, mine[0], mine[1])
        other_ref[:, place] = jnp.where(core == 0, other[0], other[1])
        send_ref[:width // 4, place] = jnp.where(core == 0, mine[1], mine[0]).astype(jnp.bfloat16)
        send_ref[width // 4:, place] = jnp.where(core == 0, other[1], other[0]).astype(jnp.bfloat16)


def rows_of(pick, own, following, products, turned):
    k_local, depth = own.shape[:2]
    width = following.shape[1 if turned else 2]
    modes, excitons = products.shape[1], products.shape[3]
    columns, tile = modes * excitons, 512
    tiles = columns // tile
    return pl.pallas_call(
        functools.partial(rows_kernel, turned),
        out_shape=[
            jax.ShapeDtypeStruct((width // 4, columns), jnp.float32),
            jax.ShapeDtypeStruct((width // 4, columns), jnp.float32),
            jax.ShapeDtypeStruct((width // 2, columns), jnp.bfloat16),
        ],
        in_specs=[pl.BlockSpec(memory_space=pltpu.SMEM)]
        + [pl.BlockSpec(memory_space=pl.ANY)] * 3,
        out_specs=[pl.BlockSpec(memory_space=pltpu.VMEM)] * 3,
        scratch_shapes=[
            pltpu.VMEM((k_local, depth, width), jnp.bfloat16),
            pltpu.VMEM(following.shape, jnp.bfloat16),
            pltpu.VMEM((tiles, k_local, depth, tile), jnp.bfloat16),
            pltpu.VMEM((width, k_local * depth), jnp.bfloat16),
            pltpu.SemaphoreType.DMA((k_local,)),
            pltpu.SemaphoreType.DMA((k_local,)),
            pltpu.SemaphoreType.DMA((tiles, k_local)),
        ],
        compiler_params=pltpu.CompilerParams(vmem_limit_bytes=50 * MIB),
        cost_estimate=pl.CostEstimate(
            flops=2 * k_local * depth * width * columns,
            bytes_accessed=2 * k_local * depth * columns,
            transcendentals=0,
        ),
    )(pick, own, following, products)


def payloads_kernel(*refs):
    ins, (turn_0, turn_1, far_0, near_0, near_1, mine_1) = refs[:9], refs[9:]
    half = turn_0.shape[0]

    def summed(block, own):
        mine, other, core = ins[3 * block:3 * block + 3]
        rows = slice(0, half) if own else slice(half, 2 * half)
        return (mine if own else other)[...] + core[rows, :].astype(jnp.float32)

    far_1 = summed(0, False).astype(jnp.bfloat16)
    across = summed(1, False).astype(jnp.bfloat16)
    first = lax.axis_index("ka") & 1 == 0
    turn_0[...] = jnp.where(first, across, far_1)
    turn_1[...] = jnp.where(first, far_1, across)
    far_0[...] = summed(0, True).astype(jnp.bfloat16)
    near_0[...] = summed(2, True).astype(jnp.bfloat16)
    near_1[...] = summed(2, False).astype(jnp.bfloat16)
    mine_1[...] = summed(1, True)


def payloads_of(*parts):
    shape = parts[0].shape
    return pl.pallas_call(
        payloads_kernel,
        out_shape=[jax.ShapeDtypeStruct(shape, jnp.bfloat16)] * 5
        + [jax.ShapeDtypeStruct(shape, jnp.float32)],
        in_specs=[pl.BlockSpec(memory_space=pltpu.VMEM)] * 9,
        out_specs=[pl.BlockSpec(memory_space=pltpu.VMEM)] * 6,
        compiler_params=pltpu.CompilerParams(vmem_limit_bytes=24 * MIB),
        cost_estimate=pl.CostEstimate(
            flops=6 * parts[0].size, bytes_accessed=26 * parts[0].size, transcendentals=0
        ),
    )(*parts)


def close_kernel(factor, mine_ref, core_ref, *refs):
    *parts, out_ref = refs
    half, modes, excitons = out_ref.shape
    for m in range(modes):
        columns = slice(m * excitons, (m + 1) * excitons)
        total = mine_ref[:, columns] + core_ref[:half, columns].astype(jnp.float32)
        for ref in parts:
            total = total + ref[:, columns].astype(jnp.float32)
        out_ref[:, m, :] = total * factor


def closed(modes, factor, *parts):
    rows, columns = parts[0].shape
    return pl.pallas_call(
        functools.partial(close_kernel, factor),
        out_shape=jax.ShapeDtypeStruct((rows, modes, columns // modes), jnp.float32),
        in_specs=[pl.BlockSpec(memory_space=pltpu.VMEM)] * len(parts),
        out_specs=pl.BlockSpec(memory_space=pltpu.VMEM),
        compiler_params=pltpu.CompilerParams(vmem_limit_bytes=24 * MIB),
        cost_estimate=pl.CostEstimate(
            flops=5 * parts[0].size, bytes_accessed=16 * parts[0].size, transcendentals=0
        ),
    )(*parts)


def on_two_by_four(coeffs, g_cond, g_val, k_plus_q, band_first, norm_factor):
    k_local, bands_c, bands_v, excitons = coeffs.shape
    modes = g_cond.shape[1]
    size = lax.axis_size("ka")
    width = excitons // 4
    me = lax.axis_index("ka")
    core, x, z = me & 1, me >> 1 & 1, me >> 2
    flat = coeffs.reshape(k_local, bands_c * bands_v, excitons)

    pieces = [cut_piece(flat, width)]
    rest, _ = lax.optimization_barrier((flat, pieces))
    pieces += turned_pieces(rest, 3, width)
    following = [permute(piece, lambda i: i - 1) for piece in pieces]
    products = products_of(coeffs, g_cond, g_val, band_first)
    products = products.reshape(k_local, modes, bands_c * bands_v, excitons)
    places = jnp.mod(k_plus_q - me * k_local, k_local * size)

    def rows(step, after):
        pick = jnp.concatenate((places, jnp.stack((z ^ (3 - step), core, x))))
        pick, _ = lax.optimization_barrier((pick, after))
        mine, other, send = rows_of(pick, flat, following[step], products, step > 0)
        return mine, other, permute(send, lambda i: i ^ 1)

    half = width // 4

    def over(value, bits):
        return permute(value.astype(jnp.bfloat16), lambda i: i ^ bits)

    def total_of(value, *arrived):
        for array in arrived:
            value = value + array.astype(jnp.float32)
        return value

    step_0 = rows(0, products)
    step_1 = rows(1, step_0[0])
    step_2 = rows(2, step_1[0])
    core_0, core_1, core_2, following[3] = lax.optimization_barrier(
        (step_0[2], step_1[2], step_2[2], following[3])
    )
    *sends, mine_1 = payloads_of(
        *step_0[:2], core_0, *step_1[:2], core_1, *step_2[:2], core_2
    )
    step_3 = rows(3, sends)
    arrived = [
        permute(sends[turn], lambda i: i ^ (2 if i % 2 == turn else 6)) for turn in range(2)
    ]
    arrived.append(over(sends[2], 4))
    mine_1, _ = lax.optimization_barrier((mine_1, step_3[0]))
    pair = total_of(mine_1, *arrived)
    cross_2, _ = lax.optimization_barrier((sends[4], pair))
    pair = over(pair, 8)
    near = over(sends[3], 4), over(cross_2, 6)
    mine_3, other_3, core_3 = step_3
    across_3 = over(other_3 + core_3[half:].astype(jnp.float32), 2)
    return closed(modes, norm_factor, mine_3, core_3, across_3, pair, *near)


def on_any(coeffs, g_cond, g_val, k_plus_q, band_first, norm_factor):
    k_local, bands_c, bands_v, excitons = coeffs.shape
    modes = g_cond.shape[1]
    size = lax.axis_size("ka")
    depth = bands_c * bands_v
    flat = coeffs.reshape(k_local, depth, excitons)
    blocks = jnp.concatenate((flat, permute(flat, lambda i: i - 1)), 0)
    offsets = jnp.mod(k_plus_q - lax.axis_index("ka") * k_local, k_local * size)
    products = products_of(coeffs, g_cond, g_val, band_first)
    products = products.reshape(k_local, modes, depth, excitons)
    partners = [
        lax.dynamic_index_in_dim(blocks, offsets[k], 0, keepdims=False) for k in range(k_local)
    ]
    running = jnp.einsum(
        "kds,kmdt->smt", jnp.stack(partners), products, preferred_element_type=jnp.float32
    )
    return lax.psum_scatter(running * norm_factor, "ka", scatter_dimension=0, tiled=True)


def shards(coeffs, g_cond, g_val, k_plus_q, band_first):
    k_local, bands_c, bands_v, excitons = coeffs.shape
    size = lax.axis_size("ka")
    norm_factor = 1.0 / math.sqrt(bands_c * bands_v * k_local * size)
    whole_tiles = excitons % (4 * 128) == 0
    plan = on_two_by_four if size == 16 and whole_tiles else on_any
    return plan(coeffs, g_cond, g_val, k_plus_q, band_first, norm_factor)


def solution(mesh):
    in_specs = (
        P(("groups", "ka"), None, None, None),
        P(("groups", "ka"), None, None, None),
        P(("groups", "ka"), None, None, None),
        P(("groups", "ka")),
        P("groups", None),
    )
    out_specs = P(("groups", "ka"), None, None)
    return jax.shard_map(shards, mesh=mesh, in_specs=in_specs, out_specs=out_specs, check_vma=False)
```

```python
import functools
import math

import jax
import jax.numpy as jnp
from jax import lax
from jax.experimental import pallas as pl
from jax.experimental.pallas import tpu as pltpu
from jax.sharding import PartitionSpec as P

MIB = 1024 * 1024


def permute(x, target):
    size = lax.axis_size("ka")
    pairs = [(i, target(i)) for i in range(size)]
    return lax.ppermute(x, "ka", [(i, j % size) for i, j in pairs if j is not None])


def nt_dot(a, b):
    return lax.dot_general(a, b, (((1,), (1,)), ((), ())), preferred_element_type=jnp.float32)


def iotas(rows, cols):
    shape = (rows, cols)
    return lax.broadcasted_iota(jnp.int32, shape, 0), lax.broadcasted_iota(jnp.int32, shape, 1)


def ones_where(condition):
    return jnp.where(condition, 1.0, 0.0).astype(jnp.bfloat16)


PART_C, PART_V = 8, 16


def fill_weights(first_ref, cond_ref, val_ref, we_ref, wh_ref):
    _, modes, bands_c, _ = cond_ref.shape
    bands_v = val_ref.shape[2]
    rows_e, rows_h = bands_c * PART_V, PART_C * bands_v
    row, col = iotas(rows_e, bands_c)
    take = ones_where(row // PART_V == col)
    row, col = iotas(rows_e, rows_e)
    for m in range(modes):
        half = jnp.dot(take, cond_ref[0, m], preferred_element_type=jnp.float32)
        full = nt_dot(half.astype(jnp.bfloat16), take)
        keep = (row % PART_V == col % PART_V) & (row // PART_V >= first_ref[m, 0])
        we_ref[m * rows_e:(m + 1) * rows_e, :] = jnp.where(keep, full, 0.0).astype(jnp.bfloat16)
    row, col = iotas(rows_h, bands_v)
    take = ones_where(row % bands_v == col)
    row, col = iotas(rows_h, rows_h)
    for m in range(modes):
        half = nt_dot(take, val_ref[0, m])
        full = nt_dot(half.astype(jnp.bfloat16), take)
        keep = (row // bands_v == col // bands_v) & (row % bands_v >= first_ref[m, 1])
        wh_ref[m * rows_h:(m + 1) * rows_h, :] = jnp.where(keep, full, 0.0).astype(jnp.bfloat16)


def products_kernel(first_ref, coeffs_ref, cond_ref, val_ref, out_ref, we_ref, wh_ref):
    _, bands_c, bands_v, tile = coeffs_ref.shape
    modes = cond_ref.shape[1]
    rows_e, rows_h = bands_c * PART_V, PART_C * bands_v

    @pl.when(pl.program_id(1) == 0)
    def _():
        fill_weights(first_ref, cond_ref, val_ref, we_ref, wh_ref)

    electron = []
    for h in range(bands_v // PART_V):
        x = coeffs_ref[0, :, h * PART_V:(h + 1) * PART_V, :].reshape(rows_e, tile)
        e = jnp.dot(we_ref[...], x, preferred_element_type=jnp.float32)
        electron.append(e.reshape(modes, bands_c, PART_V, tile))
    for q in range(bands_c // PART_C):
        own = slice(q * PART_C, (q + 1) * PART_C)
        y = coeffs_ref[0, own].reshape(rows_h, tile)
        hole = jnp.dot(wh_ref[...], y, preferred_element_type=jnp.float32)
        hole = hole.reshape(modes, PART_C, bands_v, tile)
        for m in range(modes):
            for h in range(bands_v // PART_V):
                cols = slice(h * PART_V, (h + 1) * PART_V)
                value = electron[h][m, own] - hole[m, :, cols]
                out_ref[0, m, own, cols, :] = value.astype(jnp.bfloat16)


def products_of(coeffs, g_cond, g_val, band_first):
    k_local, bands_c, bands_v, excitons = coeffs.shape
    modes = g_cond.shape[1]
    tile = 256
    rows_e, rows_h = bands_c * PART_V, PART_C * bands_v
    depth = bands_c * bands_v
    return pl.pallas_call(
        products_kernel,
        out_shape=jax.ShapeDtypeStruct((k_local, modes, bands_c, bands_v, excitons), jnp.bfloat16),
        grid=(k_local, excitons // tile),
        in_specs=[
            pl.BlockSpec(memory_space=pltpu.SMEM),
            pl.BlockSpec((1, bands_c, bands_v, tile), lambda k, s: (k, 0, 0, s)),
            pl.BlockSpec((1, modes, bands_c, bands_c), lambda k, s: (k, 0, 0, 0)),
            pl.BlockSpec((1, modes, bands_v, bands_v), lambda k, s: (k, 0, 0, 0)),
        ],
        out_specs=pl.BlockSpec((1, modes, bands_c, bands_v, tile), lambda k, s: (k, 0, 0, 0, s)),
        scratch_shapes=[
            pltpu.VMEM((modes * rows_e, rows_e), jnp.bfloat16),
            pltpu.VMEM((modes * rows_h, rows_h), jnp.bfloat16),
        ],
        compiler_params=pltpu.CompilerParams(vmem_limit_bytes=60 * MIB),
        cost_estimate=pl.CostEstimate(
            flops=2 * k_local * modes * excitons * depth * (rows_e + rows_h),
            bytes_accessed=2 * coeffs.size * (1 + modes),
            transcendentals=0,
        ),
    )(band_first, coeffs, g_cond, g_val)


def columns_of(step, width):
    size = lax.axis_size("ka")
    behind_z = lax.shift_right_logical(lax.rem(lax.axis_index("ka") + size - 1, size), 2)
    return pl.ds(pl.multiple_of((behind_z ^ (3 - step)) * width, width), width)


def cut_kernel(coeffs_ref, out_ref, held, sems, out_sems):
    k_local, parts, rows, width = held.shape
    columns = columns_of(0, width)
    steps = [(k, p) for k in range(k_local) for p in range(parts)]

    def copy_in(k, p):
        source = coeffs_ref.at[k, pl.ds(p * rows, rows), columns]
        return pltpu.make_async_copy(source, held.at[k, p], sems.at[k, p])

    def copy_out(k, p):
        target = out_ref.at[k, pl.ds(p * rows, rows)]
        return pltpu.make_async_copy(held.at[k, p], target, out_sems.at[k, p])

    for step in steps:
        copy_in(*step).start()
    for step in steps:
        copy_in(*step).wait()
        copy_out(*step).start()
    for step in steps:
        copy_out(*step).wait()


def cut_piece(flat, width):
    k_local, depth, _ = flat.shape
    parts = 4
    return pl.pallas_call(
        cut_kernel,
        out_shape=jax.ShapeDtypeStruct((k_local, depth, width), jnp.bfloat16),
        in_specs=[pl.BlockSpec(memory_space=pl.ANY)],
        out_specs=pl.BlockSpec(memory_space=pl.ANY),
        scratch_shapes=[
            pltpu.VMEM((k_local, parts, depth // parts, width), jnp.bfloat16),
            pltpu.SemaphoreType.DMA((k_local, parts)),
            pltpu.SemaphoreType.DMA((k_local, parts)),
        ],
        compiler_params=pltpu.CompilerParams(vmem_limit_bytes=60 * MIB),
        cost_estimate=pl.CostEstimate(
            flops=0, bytes_accessed=4 * k_local * depth * width, transcendentals=0
        ),
    )(flat)


def turn_kernel(coeffs_ref, *refs):
    *out_refs, held, sems = refs
    pieces, k_local, parts, rows, width = held.shape

    def copy(i, k, p):
        columns = columns_of(1 + i, width)
        source = coeffs_ref.at[k, pl.ds(p * rows, rows), columns]
        return pltpu.make_async_copy(source, held.at[i, k, p], sems.at[i, k, p])

    steps = [(i, k, p) for i in range(pieces) for k in range(k_local) for p in range(parts)]
    for step in steps:
        copy(*step).start()
    for step in steps:
        i, k, p = step
        copy(*step).wait()
        out_refs[i][k, :, p * rows:(p + 1) * rows] = held[i, k, p].T


def turned_pieces(flat, pieces, width):
    k_local, depth, _ = flat.shape
    parts = 2
    return pl.pallas_call(
        turn_kernel,
        out_shape=[jax.ShapeDtypeStruct((k_local, width, depth), jnp.bfloat16)] * pieces,
        in_specs=[pl.BlockSpec(memory_space=pl.ANY)],
        out_specs=[pl.BlockSpec(memory_space=pltpu.VMEM)] * pieces,
        scratch_shapes=[
            pltpu.VMEM((pieces, k_local, parts, depth // parts, width), jnp.bfloat16),
            pltpu.SemaphoreType.DMA((pieces, k_local, parts)),
        ],
        compiler_params=pltpu.CompilerParams(vmem_limit_bytes=60 * MIB),
        cost_estimate=pl.CostEstimate(
            flops=0, bytes_accessed=4 * pieces * k_local * depth * width, transcendentals=0
        ),
    )(flat)


def rows_kernel(turned, pick_ref, own_ref, next_ref, right_ref, mine_ref, other_ref, send_ref, *refs):
    own_held, next_held, held, left, own_sems, next_sems, sems = refs
    k_local, depth, width = own_held.shape
    tiles, _, _, tile = held.shape
    per_mode = right_ref.shape[3] // tile
    core, x = pick_ref[k_local + 1], pick_ref[k_local + 2]
    columns = pl.ds(pl.multiple_of(pick_ref[k_local] * width, width), width)
    near = [pick_ref[k] < k_local for k in range(k_local)]

    def copy_own(k):
        source = own_ref.at[jnp.minimum(pick_ref[k], k_local - 1), :, columns]
        return pltpu.make_async_copy(source, own_held.at[k], own_sems.at[k])

    def copy_next(k):
        source = next_ref.at[jnp.maximum(pick_ref[k] - k_local, 0)]
        return pltpu.make_async_copy(source, next_held.at[k], next_sems.at[k])

    def copy_right(t, k):
        source = right_ref.at[k, t // per_mode, :, pl.ds(t % per_mode * tile, tile)]
        return pltpu.make_async_copy(source, held.at[t, k], sems.at[t, k])

    for k in range(k_local):
        copy_own(k).start()
        copy_next(k).start()
    for t in range(tiles):
        for k in range(k_local):
            copy_right(t, k).start()
    for k in range(k_local):
        copy_own(k).wait()
        copy_next(k).wait()

        @pl.when(near[k])
        def _():
            left[:, k * depth:(k + 1) * depth] = own_held[k].T

        @pl.when(jnp.logical_not(near[k]))
        def _():
            left[:, k * depth:(k + 1) * depth] = next_held[k] if turned else next_held[k].T

    for t in range(tiles):
        for k in range(k_local):
            copy_right(t, k).wait()
        right = held[t].reshape(k_local * depth, tile)
        total = jnp.dot(left[...], right, preferred_element_type=jnp.float32)
        parts = total.reshape(2, 2, width // 4, tile)
        mine = jnp.where(x == 0, parts[0], parts[1])
        other = jnp.where(x == 0, parts[1], parts[0])
        place = slice(t * tile, (t + 1) * tile)
        mine_ref[:, place] = jnp.where(core == 0, mine[0], mine[1])
        other_ref[:, place] = jnp.where(core == 0, other[0], other[1])
        send_ref[:width // 4, place] = jnp.where(core == 0, mine[1], mine[0]).astype(jnp.bfloat16)
        send_ref[width // 4:, place] = jnp.where(core == 0, other[1], other[0]).astype(jnp.bfloat16)


def rows_of(pick, own, following, products, turned):
    k_local, depth = own.shape[:2]
    width = following.shape[1 if turned else 2]
    modes, excitons = products.shape[1], products.shape[3]
    columns, tile = modes * excitons, 512
    tiles = columns // tile
    return pl.pallas_call(
        functools.partial(rows_kernel, turned),
        out_shape=[
            jax.ShapeDtypeStruct((width // 4, columns), jnp.float32),
            jax.ShapeDtypeStruct((width // 4, columns), jnp.float32),
            jax.ShapeDtypeStruct((width // 2, columns), jnp.bfloat16),
        ],
        in_specs=[pl.BlockSpec(memory_space=pltpu.SMEM)]
        + [pl.BlockSpec(memory_space=pl.ANY)] * 3,
        out_specs=[pl.BlockSpec(memory_space=pltpu.VMEM)] * 3,
        scratch_shapes=[
            pltpu.VMEM((k_local, depth, width), jnp.bfloat16),
            pltpu.VMEM(following.shape, jnp.bfloat16),
            pltpu.VMEM((tiles, k_local, depth, tile), jnp.bfloat16),
            pltpu.VMEM((width, k_local * depth), jnp.bfloat16),
            pltpu.SemaphoreType.DMA((k_local,)),
            pltpu.SemaphoreType.DMA((k_local,)),
            pltpu.SemaphoreType.DMA((tiles, k_local)),
        ],
        compiler_params=pltpu.CompilerParams(vmem_limit_bytes=50 * MIB),
        cost_estimate=pl.CostEstimate(
            flops=2 * k_local * depth * width * columns,
            bytes_accessed=2 * k_local * depth * columns,
            transcendentals=0,
        ),
    )(pick, own, following, products)


def payloads_kernel(*refs):
    ins, (far_0, far_1, across, near_0, near_1, mine_1) = refs[:9], refs[9:]
    half = across.shape[0]

    def summed(block, own):
        mine, other, core = ins[3 * block:3 * block + 3]
        rows = slice(0, half) if own else slice(half, 2 * half)
        return (mine if own else other)[...] + core[rows, :].astype(jnp.float32)

    far_0[...] = summed(0, True).astype(jnp.bfloat16)
    far_1[...] = summed(0, False).astype(jnp.bfloat16)
    across[...] = summed(1, False).astype(jnp.bfloat16)
    near_0[...] = summed(2, True).astype(jnp.bfloat16)
    near_1[...] = summed(2, False).astype(jnp.bfloat16)
    mine_1[...] = summed(1, True)


def payloads_of(*parts):
    shape = parts[0].shape
    return pl.pallas_call(
        payloads_kernel,
        out_shape=[jax.ShapeDtypeStruct(shape, jnp.bfloat16)] * 5
        + [jax.ShapeDtypeStruct(shape, jnp.float32)],
        in_specs=[pl.BlockSpec(memory_space=pltpu.VMEM)] * 9,
        out_specs=[pl.BlockSpec(memory_space=pltpu.VMEM)] * 6,
        compiler_params=pltpu.CompilerParams(vmem_limit_bytes=24 * MIB),
        cost_estimate=pl.CostEstimate(
            flops=6 * parts[0].size, bytes_accessed=26 * parts[0].size, transcendentals=0
        ),
    )(*parts)


def close_kernel(factor, mine_ref, core_ref, *refs):
    *parts, out_ref = refs
    half, modes, excitons = out_ref.shape
    for m in range(modes):
        columns = slice(m * excitons, (m + 1) * excitons)
        total = mine_ref[:, columns] + core_ref[:half, columns].astype(jnp.float32)
        for ref in parts:
            total = total + ref[:, columns].astype(jnp.float32)
        out_ref[:, m, :] = total * factor


def closed(modes, factor, *parts):
    rows, columns = parts[0].shape
    return pl.pallas_call(
        functools.partial(close_kernel, factor),
        out_shape=jax.ShapeDtypeStruct((rows, modes, columns // modes), jnp.float32),
        in_specs=[pl.BlockSpec(memory_space=pltpu.VMEM)] * len(parts),
        out_specs=pl.BlockSpec(memory_space=pltpu.VMEM),
        compiler_params=pltpu.CompilerParams(vmem_limit_bytes=24 * MIB),
        cost_estimate=pl.CostEstimate(
            flops=5 * parts[0].size, bytes_accessed=16 * parts[0].size, transcendentals=0
        ),
    )(*parts)


def on_two_by_four(coeffs, g_cond, g_val, k_plus_q, band_first, norm_factor):
    k_local, bands_c, bands_v, excitons = coeffs.shape
    modes = g_cond.shape[1]
    size = lax.axis_size("ka")
    width = excitons // 4
    me = lax.axis_index("ka")
    core, x, z = me & 1, me >> 1 & 1, me >> 2
    flat = coeffs.reshape(k_local, bands_c * bands_v, excitons)

    pieces = [cut_piece(flat, width)]
    rest, _ = lax.optimization_barrier((flat, pieces))
    pieces += turned_pieces(rest, 3, width)
    following = [permute(piece, lambda i: i - 1) for piece in pieces]
    products = products_of(coeffs, g_cond, g_val, band_first)
    products = products.reshape(k_local, modes, bands_c * bands_v, excitons)
    places = jnp.mod(k_plus_q - me * k_local, k_local * size)

    def rows(step, after):
        pick = jnp.concatenate((places, jnp.stack((z ^ (3 - step), core, x))))
        pick, _ = lax.optimization_barrier((pick, after))
        mine, other, send = rows_of(pick, flat, following[step], products, step > 0)
        return mine, other, permute(send, lambda i: i ^ 1)

    half = width // 4

    def over(value, bits):
        return permute(value.astype(jnp.bfloat16), lambda i: i ^ bits)

    def total_of(value, *arrived):
        for array in arrived:
            value = value + array.astype(jnp.float32)
        return value

    step_0 = rows(0, products)
    step_1 = rows(1, step_0[0])
    step_2 = rows(2, step_1[0])
    core_0, core_1, core_2, following[3] = lax.optimization_barrier(
        (step_0[2], step_1[2], step_2[2], following[3])
    )
    *sends, mine_1 = payloads_of(
        *step_0[:2], core_0, *step_1[:2], core_1, *step_2[:2], core_2
    )
    step_3 = rows(3, sends)
    far = over(sends[0], 4), over(sends[1], 6)
    across_1 = over(sends[2], 2)
    near = over(sends[3], 4), over(sends[4], 6)
    mine_1, _ = lax.optimization_barrier((mine_1, step_3[0]))
    mine_1 = lax.optimization_barrier(total_of(mine_1, across_1))
    pair = over(total_of(mine_1, *far), 8)
    mine_3, other_3, core_3 = step_3
    across_3 = over(other_3 + core_3[half:].astype(jnp.float32), 2)
    return closed(modes, norm_factor, mine_3, core_3, across_3, pair, *near)


def on_any(coeffs, g_cond, g_val, k_plus_q, band_first, norm_factor):
    k_local, bands_c, bands_v, excitons = coeffs.shape
    modes = g_cond.shape[1]
    size = lax.axis_size("ka")
    depth = bands_c * bands_v
    flat = coeffs.reshape(k_local, depth, excitons)
    blocks = jnp.concatenate((flat, permute(flat, lambda i: i - 1)), 0)
    offsets = jnp.mod(k_plus_q - lax.axis_index("ka") * k_local, k_local * size)
    products = products_of(coeffs, g_cond, g_val, band_first)
    products = products.reshape(k_local, modes, depth, excitons)
    partners = [
        lax.dynamic_index_in_dim(blocks, offsets[k], 0, keepdims=False) for k in range(k_local)
    ]
    running = jnp.einsum(
        "kds,kmdt->smt", jnp.stack(partners), products, preferred_element_type=jnp.float32
    )
    return lax.psum_scatter(running * norm_factor, "ka", scatter_dimension=0, tiled=True)


def shards(coeffs, g_cond, g_val, k_plus_q, band_first):
    k_local, bands_c, bands_v, excitons = coeffs.shape
    size = lax.axis_size("ka")
    norm_factor = 1.0 / math.sqrt(bands_c * bands_v * k_local * size)
    whole_tiles = excitons % (4 * 128) == 0
    plan = on_two_by_four if size == 16 and whole_tiles else on_any
    return plan(coeffs, g_cond, g_val, k_plus_q, band_first, norm_factor)


def solution(mesh):
    in_specs = (
        P(("groups", "ka"), None, None, None),
        P(("groups", "ka"), None, None, None),
        P(("groups", "ka"), None, None, None),
        P(("groups", "ka")),
        P("groups", None),
    )
    out_specs = P(("groups", "ka"), None, None)
    return jax.shard_map(shards, mesh=mesh, in_specs=in_specs, out_specs=out_specs, check_vma=False)
```
